32 devices in a mesh: ctx: 16 (over z, y, core), tp: 2 (over x).
Axes of the slice: x: 2, y: 2, z: 4, core: 2. Of those that a mesh axis runs over, the one named last changes fastest.
Arguments:
- tokens: bfloat16 [4, 2048, 1536], P(None, 'ctx'), may hold values from -6 to 6
- output_cotangent: bfloat16 [4, 2048, 1536], P(None, 'ctx'), may hold values from -6 to 6
- segment_ids: int32 [4, 2048], replicated, may hold values from 0 to 255, as said below
- variant: int32 [4], replicated, may hold values from 0 to 7
- attn_gain: float32 [1536], replicated, may hold values from 0.1 to 1.9
- ffn_gain: float32 [1536], replicated, may hold values from 0.1 to 1.9
- q_gain: float32 [64], replicated, may hold values from 0.1 to 1.9
- k_gain: float32 [64], replicated, may hold values from 0.1 to 1.9
- query_matrix: bfloat16 [1536, 1536], P(None, 'tp'), may hold values from -0.15625 to 0.15625
- key_matrix: bfloat16 [1536, 512], P(None, 'tp'), may hold values from -0.15625 to 0.15625
- value_matrix: bfloat16 [1536, 512], P(None, 'tp'), may hold values from -0.15625 to 0.15625
- output_matrix: bfloat16 [1536, 1536], P('tp'), may hold values from -1.25 to 1.25
- gate_matrix: bfloat16 [1536, 6912], P(None, 'tp'), may hold values from -0.15625 to 0.15625
- up_matrix: bfloat16 [1536, 6912], P(None, 'tp'), may hold values from -0.15625 to 0.15625
- down_matrix: bfloat16 [6912, 1536], P('tp'), may hold values from -0.078125 to 0.078125
- query_input_factor: bfloat16 [128, 1536], replicated, may hold values from -0.15625 to 0.15625
- query_output_factor: bfloat16 [128, 1536], P(None, 'tp'), may hold values from -0.75 to 0.75
- key_input_factor: bfloat16 [128, 1536], replicated, may hold values from -0.15625 to 0.15625
- key_output_factor: bfloat16 [128, 512], P(None, 'tp'), may hold values from -0.75 to 0.75
- value_input_factor: bfloat16 [128, 1536], replicated, may hold values from -0.15625 to 0.15625
- value_output_factor: bfloat16 [128, 512], P(None, 'tp'), may hold values from -0.75 to 0.75
- output_input_factor: bfloat16 [128, 1536], P(None, 'tp'), may hold values from -0.15625 to 0.15625
- output_output_factor: bfloat16 [128, 1536], replicated, may hold values from -3 to 3
- gate_input_factor: bfloat16 [128, 1536], replicated, may hold values from -0.15625 to 0.15625
- gate_output_factor: bfloat16 [128, 6912], P(None, 'tp'), may hold values from -0.75 to 0.75
- up_input_factor: bfloat16 [128, 1536], replicated, may hold values from -0.15625 to 0.15625
- up_output_factor: bfloat16 [128, 6912], P(None, 'tp'), may hold values from -0.75 to 0.75
- down_input_factor: bfloat16 [128, 6912], P(None, 'tp'), may hold values from -0.078125 to 0.078125
- down_output_factor: bfloat16 [128, 1536], replicated, may hold values from -0.75 to 0.75
Outputs:
- block_result: bfloat16 [4, 2048, 1536], P(None, 'ctx')
- input_grad: bfloat16 [4, 2048, 1536], P(None, 'ctx')
- grad_a_query: float32 [128, 1536], P('ctx')
- grad_b_query: float32 [128, 1536], P('ctx', 'tp')
- grad_a_key: float32 [128, 1536], P('ctx')
- grad_b_key: float32 [128, 512], P('ctx', 'tp')
- grad_a_value: float32 [128, 1536], P('ctx')
- grad_b_value: float32 [128, 512], P('ctx', 'tp')
- grad_a_out: float32 [128, 1536], P('ctx', 'tp')
- grad_b_out: float32 [128, 1536], P('ctx')
- grad_a_gate: float32 [128, 1536], P('ctx')
- grad_b_gate: float32 [128, 6912], P('ctx', 'tp')
- grad_a_up: float32 [128, 1536], P('ctx')
- grad_b_up: float32 [128, 6912], P('ctx', 'tp')
- grad_a_down: float32 [128, 6912], P('ctx', 'tp')
- grad_b_down: float32 [128, 1536], P('ctx')
The draws below stay inside these ranges and needn't reach their ends.
Inputs may be any that keep to these rules, and one draw needn't show every extreme that they name: `segment_ids`: in each sequence the ids start at 0, never fall, and rise by at most one from a position to the next; in every draw at least one sequence is a single document, and some sequence reaches the largest id 2048 // 8 - 1.
All inputs are finite; a program needn't handle non-finite values.
Results may differ from the reference program's by a relative error of at most 0.025.
Values may be sent and summed in bfloat16 or wider, within the bound.
A program may use at most 320 MiB of HBM per device.

```python
import jax
import jax.numpy as jnp
from jax import lax

D = 1536
HEADS = 24
KV_HEADS = 8
HEAD_DIM = 64
FF = 6912
VARIANTS = 8
RANK = 16
SEQS = 4
SEQ_ROWS = 128
LEN = 2048


def draw_segment_ids(key, part):
    key = jax.random.fold_in(key, 17)
    level_key, tick_key, whole_key = jax.random.split(key, 3)
    levels = jax.random.randint(level_key, (SEQS, LEN // 32, 1), 0, 4)
    limits = jnp.left_shift(jnp.int32(4), 3 * levels)
    tick_values = jax.random.randint(tick_key, (SEQS, LEN // 32, 32), 0, 1 << 30)
    starts = (jnp.remainder(tick_values, limits) == 0).reshape(SEQS, LEN)
    chosen = jax.random.randint(whole_key, (), 0, SEQS)
    busy = jnp.remainder(chosen + 1, SEQS)
    seq_index = jnp.arange(SEQS, dtype=jnp.int32)[:, None]
    pos_index = jnp.arange(LEN, dtype=jnp.int32)[None, :]
    forced = (seq_index == busy) & (jnp.remainder(pos_index, 4) == 0) & (pos_index < LEN // 2)
    starts = (starts | forced) & (seq_index != chosen) & (pos_index > 0)
    counted = jnp.cumsum(starts.astype(jnp.int32), axis=1).astype(jnp.int32)
    return jnp.minimum(counted, LEN // 8 - 1).astype(jnp.int32)


def plant(values, key, low, largest):
    longest = values.shape.index(max(values.shape))
    spots = []
    for shift in (0, 1):
        where = [jax.random.randint(jax.random.fold_in(key, axis), (), 0, length) for axis, length in enumerate(values.shape)]
        where[longest] = (where[longest] + shift) % values.shape[longest]
        spots.append(tuple(where))
    return values.at[spots[0]].set(low).at[spots[1]].set(largest)


def shard_levels(key, shape, cuts, smallest, largest):
    loudness = 1.0
    for position, blocks in cuts:
        steps = jax.random.uniform(jax.random.fold_in(jax.random.fold_in(key, 6), position), (blocks,), jnp.float32, smallest / len(cuts), largest / len(cuts))
        loudness = loudness * jnp.repeat(jnp.exp(steps), shape[position] // blocks).reshape((-1,) + (1,) * (len(shape) - 1 - position))
    return loudness


def scatter_about(stream_key, dims, scale, reach, shards=(), kind=jnp.bfloat16):
    gain = shard_levels(stream_key, dims, shards, -0.22, 0.18) if shards else 1.0
    values = jax.random.normal(stream_key, dims, jnp.float32) * scale * gain
    return jnp.minimum(jnp.maximum(values, -reach), reach).astype(kind)


def setup_inputs(seed: int = 0) -> dict:
    arg_keys = jax.random.split(jax.random.key(seed), 30)
    return {
        "tokens": scatter_about(arg_keys[0], (SEQS, LEN, D), 1.0, 6.0, ((1, 16),)),
        "output_cotangent": scatter_about(arg_keys[1], (SEQS, LEN, D), 1.0, 6.0, ((1, 16),)),
        "segment_ids": draw_segment_ids(jax.random.fold_in(arg_keys[29], 71), 0),
        "variant": plant(jax.random.randint(arg_keys[3], (SEQS,), 0, VARIANTS), jax.random.fold_in(arg_keys[3], 1), 0, VARIANTS - 1).astype(jnp.int32),
        "attn_gain": jnp.clip(1.0 + 0.18 * jax.random.normal(arg_keys[4], (D,), jnp.float32), 0.1, 1.9),
        "ffn_gain": jnp.clip(1.0 + 0.18 * jax.random.normal(arg_keys[5], (D,), jnp.float32), 0.1, 1.9),
        "q_gain": jnp.clip(1.0 + 0.18 * jax.random.normal(arg_keys[6], (HEAD_DIM,), jnp.float32), 0.1, 1.9),
        "k_gain": jnp.clip(1.0 + 0.18 * jax.random.normal(arg_keys[7], (HEAD_DIM,), jnp.float32), 0.1, 1.9),
        "query_matrix": scatter_about(arg_keys[8], (D, HEADS * HEAD_DIM), D ** -0.5, 0.15625, ((1, 2),)),
        "key_matrix": scatter_about(arg_keys[9], (D, KV_HEADS * HEAD_DIM), D ** -0.5, 0.15625, ((1, 2),)),
        "value_matrix": scatter_about(arg_keys[10], (D, KV_HEADS * HEAD_DIM), D ** -0.5, 0.15625, ((1, 2),)),
        "output_matrix": scatter_about(arg_keys[11], (HEADS * HEAD_DIM, D), (HEADS * HEAD_DIM // 64) ** -0.5, 1.25, ((0, 2),)),
        "gate_matrix": scatter_about(arg_keys[12], (D, FF), D ** -0.5, 0.15625, ((1, 2),)),
        "up_matrix": scatter_about(arg_keys[13], (D, FF), D ** -0.5, 0.15625, ((1, 2),)),
        "down_matrix": scatter_about(arg_keys[14], (FF, D), FF ** -0.5, 0.078125, ((0, 2),)),
        "query_input_factor": scatter_about(arg_keys[15], (VARIANTS * RANK, D), D ** -0.5, 0.15625),
        "query_output_factor": scatter_about(arg_keys[16], (VARIANTS * RANK, HEADS * HEAD_DIM), (4 * RANK) ** -0.5, 0.75, ((1, 2),)),
        "key_input_factor": scatter_about(arg_keys[17], (VARIANTS * RANK, D), D ** -0.5, 0.15625),
        "key_output_factor": scatter_about(arg_keys[18], (VARIANTS * RANK, KV_HEADS * HEAD_DIM), (4 * RANK) ** -0.5, 0.75, ((1, 2),)),
        "value_input_factor": scatter_about(arg_keys[19], (VARIANTS * RANK, D), D ** -0.5, 0.15625),
        "value_output_factor": scatter_about(arg_keys[20], (VARIANTS * RANK, KV_HEADS * HEAD_DIM), (4 * RANK) ** -0.5, 0.75, ((1, 2),)),
        "output_input_factor": scatter_about(arg_keys[21], (VARIANTS * RANK, HEADS * HEAD_DIM), (HEADS * HEAD_DIM) ** -0.5, 0.15625, ((1, 2),)),
        "output_output_factor": scatter_about(arg_keys[22], (VARIANTS * RANK, D), (RANK // 4) ** -0.5, 3.0),
        "gate_input_factor": scatter_about(arg_keys[23], (VARIANTS * RANK, D), D ** -0.5, 0.15625),
        "gate_output_factor": scatter_about(arg_keys[24], (VARIANTS * RANK, FF), (4 * RANK) ** -0.5, 0.75, ((1, 2),)),
        "up_input_factor": scatter_about(arg_keys[25], (VARIANTS * RANK, D), D ** -0.5, 0.15625),
        "up_output_factor": scatter_about(arg_keys[26], (VARIANTS * RANK, FF), (4 * RANK) ** -0.5, 0.75, ((1, 2),)),
        "down_input_factor": scatter_about(arg_keys[27], (VARIANTS * RANK, FF), FF ** -0.5, 0.078125, ((1, 2),)),
        "down_output_factor": scatter_about(arg_keys[28], (VARIANTS * RANK, D), (4 * RANK) ** -0.5, 0.75),
    }


EPSILON = 1e-05
THETA_BASE = 1000000.0
ADAPTER_SCALE = 2.0
MASKED_SCORE = -1e+30
FULL_PRECISION = lax.Precision.HIGHEST

@jax.custom_vjp
def low(v):
    return lax.optimization_barrier(v.astype(jnp.bfloat16)).astype(jnp.float32)

@jax.custom_vjp
def low_back(v):
    return v

def low_keep(v):
    return (low(v), None)

def low_pass(kept, grad):
    return (grad,)

def back_keep(v):
    return (v, None)

def back_low(kept, grad):
    return (low(grad),)
low.defvjp(low_keep, low_pass)
low_back.defvjp(back_keep, back_low)

def norm_rows(values, gains):
    return values * lax.rsqrt(lax.optimization_barrier(jnp.mean(values * values, axis=-1, keepdims=True)) + EPSILON) * gains

def rotate(values, positions):
    halfway = values.shape[-1] // 2
    frequencies = THETA_BASE ** (-jnp.arange(halfway, dtype=jnp.float32) * 2.0 / values.shape[-1])
    angles = positions.astype(jnp.float32)[:, None] * frequencies[None, :]
    cosine_table = jnp.cos(angles)[:, None, :]
    sine_table = jnp.sin(angles)[:, None, :]
    leading = values[..., :halfway]
    trailing = values[..., halfway:]
    return jnp.concatenate([leading * cosine_table - trailing * sine_table, trailing * cosine_table + leading * sine_table], axis=-1)

def apply_projection(input_rows, weight_tuple):
    return jnp.einsum('cgt,tr->cgr', input_rows, weight_tuple, precision=FULL_PRECISION)

def adapter(input_rows, lowrank_factor_input, factor_out, pick_variant):
    hidden_rows = jnp.einsum('pou,hu->poh', input_rows, lowrank_factor_input, precision=FULL_PRECISION) * pick_variant
    return ADAPTER_SCALE * jnp.einsum('slr,re->sle', low_back(low(hidden_rows)), factor_out, precision=FULL_PRECISION)

def attend(queries, keys, values, segments):
    seq_length, head_count, head_width = queries.shape
    key_heads = keys.shape[1]
    group_size = head_count // key_heads
    block_rows = 4 * SEQ_ROWS
    key_positions = jnp.arange(seq_length, dtype=jnp.int32)

    def one_block(block_index):
        first_row = (block_index * block_rows).astype(jnp.int32)
        query_block = lax.dynamic_slice_in_dim(queries, first_row, block_rows, 0).reshape(block_rows, key_heads, group_size, head_width)
        block_segs = lax.dynamic_slice_in_dim(segments, first_row, block_rows, 0)
        block_positions = first_row + jnp.arange(block_rows, dtype=jnp.int32)
        scores = low_back(jnp.einsum('qkgd,nkd->kgqn', query_block, keys, precision=FULL_PRECISION) * head_width ** (-0.5))
        allowed = (block_segs[:, None] == segments[None, :]) & (block_positions[:, None] >= key_positions[None, :])
        masked = jnp.where(allowed[None, None], scores, MASKED_SCORE)
        shifted = jnp.exp(masked - lax.optimization_barrier(jnp.max(masked, axis=-1, keepdims=True)))
        attention_weights = low(shifted / lax.optimization_barrier(jnp.sum(shifted, axis=-1, keepdims=True)))
        combined = jnp.einsum('kgqn,nkd->qkgd', attention_weights, values, precision=FULL_PRECISION)
        return combined.reshape(block_rows, head_count * head_width)
    blocks = lax.map(jax.checkpoint(one_block), jnp.arange(seq_length // block_rows, dtype=jnp.int32))
    return blocks.reshape(seq_length, head_count * head_width)

def reference(tokens, output_cotangent, segment_ids, variant, attn_gain, ffn_gain, q_gain, k_gain, query_matrix, key_matrix, value_matrix, output_matrix, gate_matrix, up_matrix, down_matrix, query_input_factor, query_output_factor, key_input_factor, key_output_factor, value_input_factor, value_output_factor, output_input_factor, output_output_factor, gate_input_factor, gate_output_factor, up_input_factor, up_output_factor, down_input_factor, down_output_factor):
    sequences, seq_length, model_width = tokens.shape
    positions = jnp.arange(seq_length, dtype=jnp.int32)
    stacked = query_input_factor.shape[0]
    pick_variant = ((jnp.arange(stacked, dtype=jnp.int32) // RANK)[None, :] == variant[:, None]).astype(jnp.float32)[:, None, :]
    query_weights = query_matrix.astype(jnp.float32)
    key_weights = key_matrix.astype(jnp.float32)
    value_weights = value_matrix.astype(jnp.float32)
    out_weights = output_matrix.astype(jnp.float32)
    gate_weights = gate_matrix.astype(jnp.float32)
    up_weights = up_matrix.astype(jnp.float32)
    down_weights = down_matrix.astype(jnp.float32)

    def forward(input_rows, factors):
        query_in, query_out, key_in, key_out, value_in, value_out, out_in, out_out, gate_in, gate_out, up_in, up_out, down_in, down_out = factors
        first_normed = low(norm_rows(input_rows, attn_gain))
        query_before = low_back(apply_projection(first_normed, query_weights) + adapter(first_normed, query_in, query_out, pick_variant))
        key_before = low_back(apply_projection(first_normed, key_weights) + adapter(first_normed, key_in, key_out, pick_variant))
        value_before = apply_projection(first_normed, value_weights) + adapter(first_normed, value_in, value_out, pick_variant)
        query_heads = rotate(norm_rows(query_before.reshape(sequences, seq_length, HEADS, HEAD_DIM), q_gain), positions)
        key_rotated = rotate(norm_rows(key_before.reshape(sequences, seq_length, KV_HEADS, HEAD_DIM), k_gain), positions)
        query_low = low(low_back(query_heads))
        key_low = low(low_back(key_rotated))
        value_low = low(low_back(value_before.reshape(sequences, seq_length, KV_HEADS, HEAD_DIM)))
        attention = low(low_back(jax.vmap(attend)(query_low, key_low, value_low, segment_ids)))
        branch = low_back(apply_projection(attention, out_weights) + adapter(attention, out_in, out_out, pick_variant))
        residual_middle = input_rows + branch
        second_normed = low(norm_rows(residual_middle, ffn_gain))
        gate_before = low_back(apply_projection(second_normed, gate_weights) + adapter(second_normed, gate_in, gate_out, pick_variant))
        up_before = low_back(apply_projection(second_normed, up_weights) + adapter(second_normed, up_in, up_out, pick_variant))
        hidden_rows = low(gate_before / (1.0 + jnp.exp(-gate_before)) * up_before)
        return residual_middle + apply_projection(hidden_rows, down_weights) + adapter(hidden_rows, down_in, down_out, pick_variant)
    factors = tuple((lowrank_factor.astype(jnp.float32) for lowrank_factor in (query_input_factor, query_output_factor, key_input_factor, key_output_factor, value_input_factor, value_output_factor, output_input_factor, output_output_factor, gate_input_factor, gate_output_factor, up_input_factor, up_output_factor, down_input_factor, down_output_factor)))
    result, pullback = jax.vjp(forward, tokens.astype(jnp.float32), factors)
    d_inputs, d_factors = pullback(output_cotangent.astype(jnp.float32))
    return (result.astype(jnp.bfloat16), d_inputs.astype(jnp.bfloat16), d_factors[0], d_factors[1], d_factors[2], d_factors[3], d_factors[4], d_factors[5], d_factors[6], d_factors[7], d_factors[8], d_factors[9], d_factors[10], d_factors[11], d_factors[12], d_factors[13])
```

```python
import functools, jax, jax.numpy as jnp
from jax import lax
from jax.experimental import pallas as pl
from jax.experimental.pallas import tpu as pltpu
from jax.sharding import PartitionSpec as P

HEAD_DIM = 64
LOG2E = 1.4426950408889634
KEY_TILE = 256


def tile_bounds(tile, stride, part):
    first = (2 * tile) * stride + part
    last = (2 * tile + 1) * stride + part
    return first, last


def allowed_pairs(seg_rows, seq, first, last, key_tile, group):
    lanes = lax.broadcasted_iota(jnp.int32, (1, 128), 1)
    q_pos = jnp.concatenate([first * 128 + lanes, last * 128 + lanes], axis=1)
    q_seg = jnp.concatenate(
        [seg_rows[seq, block] for block in (first, last)], axis=1
    )
    k_seg = jnp.concatenate(
        [jnp.transpose(jnp.broadcast_to(seg_rows[seq, 2 * key_tile + b], (128, 128))) for b in (0, 1)], axis=0
    )
    k_seg = jnp.concatenate([k_seg, k_seg], axis=1)
    k_pos = key_tile * 256 + lax.broadcasted_iota(jnp.int32, (256, 256), 0)
    allowed = (k_seg == jnp.broadcast_to(q_seg, (256, 256))) & (k_pos <= jnp.broadcast_to(q_pos, (256, 256)))
    return jnp.concatenate([allowed] * group, axis=1)


def tile_kind(seg_smem, seq, first, last, key_tile):
    key_low = seg_smem[seq, key_tile * 256]
    key_high = seg_smem[seq, key_tile * 256 + 255]
    q_low = seg_smem[seq, first * 128]
    q_high = seg_smem[seq, last * 128 + 127]
    needed = key_high >= q_low
    plain = (key_low == q_high) & (2 * key_tile + 1 < first)
    return needed, plain


def heads_side_by_side(ref, tile, group, offset=0):
    return jnp.concatenate(
        [ref[2 * tile + b, offset + h * HEAD_DIM : offset + (h + 1) * HEAD_DIM, :] for h in range(group) for b in (0, 1)], axis=1
    )


def attn_fwd_kernel(stride, group, units_per_seq, unit_ref, seg_smem, seg_rows, q_ref, kv_ref, o_ref, of_ref, lse_ref, kb, vt, acc):
    unit, part = unit_ref[0], unit_ref[1]
    seq = unit // units_per_seq
    key_tiles = kv_ref.shape[0] // 2
    q_tiles = q_ref.shape[0] // 2
    width = group * 256

    def load(j, _):
        for b in (0, 1):
            kb[j, b * 128 : (b + 1) * 128, :] = jnp.transpose(kv_ref[2 * j + b, :HEAD_DIM, :])
            vt[j, :HEAD_DIM, b * 128 : (b + 1) * 128] = kv_ref[2 * j + b, HEAD_DIM:, :]
        vt[j, HEAD_DIM:, :] = jnp.ones((16, 256), jnp.bfloat16)
        return 0

    lax.fori_loop(0, key_tiles, load, 0)

    def q_step(i, _):
        first, last = tile_bounds(i, stride, part)
        qt = heads_side_by_side(q_ref, i, group)
        acc[...] = jnp.zeros_like(acc)

        def k_step(j, _):
            needed, plain = tile_kind(seg_smem, seq, first, last, j)

            def weigh(masked):
                s = jnp.dot(kb[j], qt, preferred_element_type=jnp.float32)
                p = jnp.exp2(s * (LOG2E * HEAD_DIM**-0.5))
                if masked:
                    p = jnp.where(allowed_pairs(seg_rows, seq, first, last, j, group), p, 0.0)
                acc[...] += jnp.dot(vt[j], p.astype(jnp.bfloat16), preferred_element_type=jnp.float32)

            @pl.when(needed & plain)
            def _():
                weigh(False)

            @pl.when(needed & jnp.logical_not(plain))
            def _():
                weigh(True)

            return 0

        lax.fori_loop(0, last // 2 + 1, k_step, 0)
        total = acc[HEAD_DIM : HEAD_DIM + 1, :]
        lse_ref[i] = jnp.broadcast_to(jnp.log2(total), (8, width))
        out = acc[:HEAD_DIM, :] / total
        for h in range(group):
            for b in (0, 1):
                piece = out[:, h * 256 + b * 128 : h * 256 + (b + 1) * 128]
                of_ref[2 * i + b, h * HEAD_DIM : (h + 1) * HEAD_DIM, :] = piece
                o_ref[2 * i + b, h * HEAD_DIM : (h + 1) * HEAD_DIM, :] = piece.astype(jnp.bfloat16)
        return 0

    lax.fori_loop(0, q_tiles, q_step, 0)


def attn_bwd_kernel(
    stride, group, units_per_seq, unit_ref, seg_smem, seg_rows, q_ref, kv_ref, do_ref, of_ref, lse_ref,
    dq_ref, dkv_ref, qt, q3, dot_t, do3, delta, dqt,
):
    unit, part = unit_ref[0], unit_ref[1]
    seq = unit // units_per_seq
    key_tiles = kv_ref.shape[0] // 2
    q_tiles = q_ref.shape[0] // 2
    width = group * 256

    def load(i, _):
        for h in range(group):
            for b in (0, 1):
                rows = slice(h * HEAD_DIM, (h + 1) * HEAD_DIM)
                lanes = slice(h * 256 + b * 128, h * 256 + (b + 1) * 128)
                q = q_ref[2 * i + b, rows, :]
                g = do_ref[2 * i + b, rows, :]
                qt[i, :, lanes] = q
                q3[i, lanes, :] = jnp.transpose(q)
                dot_t[i, :, lanes] = g
                do3[i, lanes, :] = jnp.transpose(g)
                d = jnp.sum(g.astype(jnp.float32) * of_ref[2 * i + b, rows, :], axis=0, keepdims=True)
                delta[i, :, lanes] = jnp.broadcast_to(d, (8, 128))
        dqt[i] = jnp.zeros((HEAD_DIM, width), jnp.float32)
        return 0

    lax.fori_loop(0, q_tiles, load, 0)

    def k_step(j, _):
        kt = jnp.concatenate([kv_ref[2 * j + b, :HEAD_DIM, :] for b in (0, 1)], axis=1)
        vt = jnp.concatenate([kv_ref[2 * j + b, HEAD_DIM:, :] for b in (0, 1)], axis=1)
        kb = jnp.transpose(kt)
        vb = jnp.transpose(vt)

        def q_step(i, state):
            first, last = tile_bounds(i, stride, part)
            needed, plain = tile_kind(seg_smem, seq, first, last, j)

            def terms(masked, dk, dv):
                s = jnp.dot(kb, qt[i], preferred_element_type=jnp.float32)
                p = jnp.exp2(s * (LOG2E * HEAD_DIM**-0.5) - lse_ref[i, 0:1, :])
                if masked:
                    p = jnp.where(allowed_pairs(seg_rows, seq, first, last, j, group), p, 0.0)
                dp = jnp.dot(vb, dot_t[i], preferred_element_type=jnp.float32)
                ds = (p * (dp - delta[i, 0:1, :])).astype(jnp.bfloat16)
                dv = dv + jnp.dot(p.astype(jnp.bfloat16), do3[i], preferred_element_type=jnp.float32)
                dk = dk + jnp.dot(ds, q3[i], preferred_element_type=jnp.float32)
                dqt[i] += jnp.dot(kt, ds, preferred_element_type=jnp.float32)
                return dk, dv

            kind = jnp.where(needed, jnp.where(plain, 1, 2), 0)
            return lax.switch(
                kind, [lambda a, b: (a, b), functools.partial(terms, False), functools.partial(terms, True)], *state
            )

        zero = jnp.zeros((256, HEAD_DIM), jnp.float32)
        start = jnp.maximum((2 * j - part + stride - 1) // stride, 0) // 2
        dk, dv = lax.fori_loop(start, q_tiles, q_step, (zero, zero))
        for b in (0, 1):
            rows = slice(b * 128, (b + 1) * 128)
            dkv_ref[2 * j + b, :HEAD_DIM, :] = jnp.transpose(dk[rows] * HEAD_DIM**-0.5).astype(jnp.bfloat16)
            dkv_ref[2 * j + b, HEAD_DIM:, :] = jnp.transpose(dv[rows]).astype(jnp.bfloat16)
        return 0

    lax.fori_loop(0, key_tiles, k_step, 0)

    def store(i, _):
        for h in range(group):
            for b in (0, 1):
                piece = dqt[i, :, h * 256 + b * 128 : h * 256 + (b + 1) * 128]
                dq_ref[2 * i + b, h * HEAD_DIM : (h + 1) * HEAD_DIM, :] = (piece * HEAD_DIM**-0.5).astype(jnp.bfloat16)
        return 0

    lax.fori_loop(0, q_tiles, store, 0)


SMEM = pl.BlockSpec(memory_space=pltpu.SMEM)
VM = pl.BlockSpec(memory_space=pltpu.VMEM)


def attn_fwd(unit, segs, q, kv, stride, units_per_seq):
    blocks, qrows, _ = q.shape
    group = qrows // HEAD_DIM
    tiles, ktiles, width = blocks // 2, kv.shape[0] // 2, group * 256
    return pl.pallas_call(
        functools.partial(attn_fwd_kernel, stride, group, units_per_seq),
        out_shape=(
            jax.ShapeDtypeStruct(q.shape, jnp.bfloat16),
            jax.ShapeDtypeStruct(q.shape, jnp.float32),
            jax.ShapeDtypeStruct((tiles, 8, width), jnp.float32),
        ),
        in_specs=[SMEM, SMEM, VM, VM, VM],
        out_specs=(VM, VM, VM),
        scratch_shapes=[
            pltpu.VMEM((ktiles, 256, HEAD_DIM), jnp.bfloat16),
            pltpu.VMEM((ktiles, HEAD_DIM + 16, 256), jnp.bfloat16),
            pltpu.VMEM((HEAD_DIM + 16, width), jnp.float32),
        ],
        compiler_params=pltpu.CompilerParams(vmem_limit_bytes=56 * 2**20),
        name="attention_forward",
    )(unit, segs, segs.reshape(segs.shape[0], -1, 1, 128), q, kv)


def attn_bwd(unit, segs, q, kv, do, of, lse, stride, units_per_seq):
    blocks, qrows, _ = q.shape
    group = qrows // HEAD_DIM
    tiles, ktiles, width = blocks // 2, kv.shape[0] // 2, group * 256
    return pl.pallas_call(
        functools.partial(attn_bwd_kernel, stride, group, units_per_seq),
        out_shape=(jax.ShapeDtypeStruct(q.shape, jnp.bfloat16), jax.ShapeDtypeStruct(kv.shape, jnp.bfloat16)),
        in_specs=[SMEM, SMEM, VM, VM, VM, VM, VM, VM],
        out_specs=(VM, VM),
        scratch_shapes=[
            pltpu.VMEM((tiles, HEAD_DIM, width), jnp.bfloat16),
            pltpu.VMEM((tiles, width, HEAD_DIM), jnp.bfloat16),
            pltpu.VMEM((tiles, HEAD_DIM, width), jnp.bfloat16),
            pltpu.VMEM((tiles, width, HEAD_DIM), jnp.bfloat16),
            pltpu.VMEM((tiles, 8, width), jnp.float32),
            pltpu.VMEM((tiles, HEAD_DIM, width), jnp.float32),
        ],
        compiler_params=pltpu.CompilerParams(vmem_limit_bytes=56 * 2**20),
        name="attention_backward",
    )(unit, segs, segs.reshape(segs.shape[0], -1, 1, 128), q, kv, do, of, lse)


NT = (((1,), (1,)), ((), ()))


def mm(a, b):
    return jnp.dot(a, b, preferred_element_type=jnp.float32)


def mm_nt(a, b):
    return lax.dot_general(a, b, NT, preferred_element_type=jnp.float32)


def ffn_kernel(
    chunk, n2_ref, cot_ref, mask_ref, ag_ref, au_ref, bd_ref, wg_ref, wu_ref, wd_ref, bg_ref, bu_ref, ad_ref,
    down_ref, dn2_ref, gbg_ref, gbu_ref, gad_ref,
    hg, hu, dhd, hgt, hut, dhdt, down_acc, hdown_acc, dn2_acc, dhg_acc, dhu_acc, d_gate, d_up, hidden,
):
    step = pl.program_id(0)
    rows = n2_ref.shape[0]

    @pl.when(step == 0)
    def _():
        mask = mask_ref[...]
        hg[...] = (mm_nt(n2_ref[...], ag_ref[...]) * mask).astype(jnp.bfloat16)
        hu[...] = (mm_nt(n2_ref[...], au_ref[...]) * mask).astype(jnp.bfloat16)
        dhd[...] = (mm_nt(cot_ref[...], bd_ref[...]) * (2.0 * mask)).astype(jnp.bfloat16)
        hgt[...] = jnp.transpose(hg[...]) * 2
        hut[...] = jnp.transpose(hu[...]) * 2
        dhdt[...] = jnp.transpose(dhd[...])
        down_acc[...] = jnp.zeros_like(down_acc)
        hdown_acc[...] = jnp.zeros_like(hdown_acc)
        dn2_acc[...] = jnp.zeros_like(dn2_acc)
        dhg_acc[...] = jnp.zeros_like(dhg_acc)
        dhu_acc[...] = jnp.zeros_like(dhu_acc)

    def one(r, _):
        rs = pl.ds(pl.multiple_of(r * chunk, chunk), chunk)
        n2 = n2_ref[rs, :]
        cot = cot_ref[rs, :]
        gate = mm(n2, wg_ref[...]) + mm(hg[rs, :] * 2, bg_ref[...])
        up = mm(n2, wu_ref[...]) + mm(hu[rs, :] * 2, bu_ref[...])
        sg = 1.0 / (1.0 + jnp.exp(-gate))
        silu = gate * sg
        hid = (silu * up).astype(jnp.bfloat16)
        hidden[rs, :] = hid
        dh = mm_nt(cot, wd_ref[...]) + mm(dhd[rs, :], ad_ref[...])
        dg = (dh * up * sg * (1.0 + gate * (1.0 - sg))).astype(jnp.bfloat16)
        du = (dh * silu).astype(jnp.bfloat16)
        d_gate[rs, :] = dg
        d_up[rs, :] = du
        down_acc[rs, :] += mm(hid, wd_ref[...])
        hdown_acc[rs, :] += mm_nt(hid, ad_ref[...])
        dn2_acc[rs, :] += mm_nt(dg, wg_ref[...]) + mm_nt(du, wu_ref[...])
        dhg_acc[rs, :] += mm_nt(dg, bg_ref[...])
        dhu_acc[rs, :] += mm_nt(du, bu_ref[...])
        return 0

    lax.fori_loop(0, rows // chunk, one, 0)
    gbg_ref[...] = mm(hgt[...], d_gate[...]).astype(gbg_ref.dtype)
    gbu_ref[...] = mm(hut[...], d_up[...]).astype(gbu_ref.dtype)
    gad_ref[...] = mm(dhdt[...], hidden[...]).astype(gad_ref.dtype)

    @pl.when(step == pl.num_programs(0) - 1)
    def _():
        width, rank = n2_ref.shape[1], ag_ref.shape[0]
        down_ref[:, :width] = down_acc[...].astype(jnp.bfloat16)
        down_ref[:, width:] = hdown_acc[...].astype(jnp.bfloat16)
        dn2_ref[:, :width] = dn2_acc[...].astype(jnp.bfloat16)
        dn2_ref[:, width : width + rank] = (dhg_acc[...] * 2).astype(jnp.bfloat16)
        dn2_ref[:, width + rank :] = (dhu_acc[...] * 2).astype(jnp.bfloat16)


def ffn(n2, cot, mask, ag, au, bd, wg, wu, wd, bg, bu, ad, tile=1152, chunk=256):
    rows, width = n2.shape
    rank = ag.shape[0]
    units = wg.shape[1]
    tile = min(tile, units)
    fixed = lambda shape: pl.BlockSpec(shape, lambda f: (0, 0))
    cols = lambda height: pl.BlockSpec((height, tile), lambda f: (0, f))
    bf = jnp.bfloat16
    out = lambda shape: jax.ShapeDtypeStruct(shape, bf)
    f32 = jnp.float32
    return pl.pallas_call(
        functools.partial(ffn_kernel, chunk),
        grid=(units // tile,),
        out_shape=(
            out((rows, width + rank)), out((rows, width + 2 * rank)),
            out((rank, units)), out((rank, units)), out((rank, units)),
        ),
        in_specs=[
            fixed((rows, width)), fixed((rows, width)), fixed((rows, rank)),
            fixed((rank, width)), fixed((rank, width)), fixed((rank, width)),
            cols(width), cols(width), pl.BlockSpec((tile, width), lambda f: (f, 0)),
            cols(rank), cols(rank), cols(rank),
        ],
        out_specs=(
            fixed((rows, width + rank)), fixed((rows, width + 2 * rank)),
            cols(rank), cols(rank), cols(rank),
        ),
        scratch_shapes=[
            pltpu.VMEM((rows, rank), bf), pltpu.VMEM((rows, rank), bf), pltpu.VMEM((rows, rank), bf),
            pltpu.VMEM((rank, rows), bf), pltpu.VMEM((rank, rows), bf), pltpu.VMEM((rank, rows), bf),
            pltpu.VMEM((rows, width), f32), pltpu.VMEM((rows, rank), f32), pltpu.VMEM((rows, width), f32),
            pltpu.VMEM((rows, rank), f32), pltpu.VMEM((rows, rank), f32),
            pltpu.VMEM((rows, tile), bf), pltpu.VMEM((rows, tile), bf), pltpu.VMEM((rows, tile), bf),
        ],
        compiler_params=pltpu.CompilerParams(vmem_limit_bytes=60 * 2**20),
        name="feed_forward",
    )(n2, cot, mask, ag, au, bd, wg, wu, wd, bg, bu, ad)


MESH = pl.DeviceIdType.MESH


def exchange_kernel(count, parts, kinds, *refs):
    n = len(kinds)
    xs, outs = refs[:n], refs[n : 2 * n]
    sends, recvs, locals_ = refs[2 * n : 3 * n], refs[3 * n : 4 * n], refs[4 * n]
    me = lax.axis_index("ctx")
    barrier = pltpu.get_barrier_semaphore()
    step = 1 if "full" in kinds else parts
    peers = count // step - 1

    def greet(k, _):
        other = lax.rem(me + k * step, count)
        pl.semaphore_signal(barrier, inc=1, device_id={"ctx": other}, device_id_type=MESH)
        return 0

    lax.fori_loop(1, peers + 1, greet, 0)

    def block(kind, x, device):
        if kind == "class" or x.shape[0] != count:
            return device // parts
        return device

    def slot(kind, device):
        return device // parts if kind == "class" else device

    def copy(i, target, place):
        kind = kinds[i]
        return pltpu.make_async_remote_copy(
            src_ref=xs[i].at[block(kind, xs[i], target)],
            dst_ref=outs[i].at[slot(kind, place)],
            send_sem=sends[i].at[slot(kind, target)],
            recv_sem=recvs[i].at[slot(kind, place)],
            device_id={"ctx": target},
            device_id_type=MESH,
        )

    own = [
        pltpu.make_async_copy(xs[i].at[block(kinds[i], xs[i], me)], outs[i].at[slot(kinds[i], me)], locals_.at[i])
        for i in range(n)
    ]
    for c in own:
        c.start()
    pl.semaphore_wait(barrier, peers)
    for i in range(n):
        hop = 1 if kinds[i] == "full" else parts

        def send(k, _, i=i, hop=hop):
            copy(i, lax.rem(me + k * hop, count), me).start()
            return 0

        lax.fori_loop(1, count // hop, send, 0)
    for i in range(n):
        hop = 1 if kinds[i] == "full" else parts

        def finish(k, _, i=i, hop=hop):
            other = lax.rem(me + k * hop, count)
            copy(i, other, me).wait_send()
            copy(i, other, other).wait_recv()
            return 0

        lax.fori_loop(1, count // hop, finish, 0)
    for c in own:
        c.wait()


def exchange(arrays, kinds, count, parts, collective_id, name):
    n = len(arrays)
    members = [count // parts if kind == "class" else count for kind in kinds]
    anywhere = pl.BlockSpec(memory_space=pl.ANY)
    return pl.pallas_call(
        functools.partial(exchange_kernel, count, parts, kinds),
        out_shape=tuple(jax.ShapeDtypeStruct((k,) + a.shape[1:], a.dtype) for k, a in zip(members, arrays)),
        in_specs=[anywhere] * n,
        out_specs=(anywhere,) * n,
        scratch_shapes=[pltpu.SemaphoreType.DMA((k,)) for k in members] * 2 + [pltpu.SemaphoreType.DMA((n,))],
        compiler_params=pltpu.CompilerParams(collective_id=collective_id, has_side_effects=True),
        name=name,
    )(*arrays)


RANK = 16
EPSILON = 1e-05
THETA_BASE = 1000000.0
BF = jnp.bfloat16
F32 = jnp.float32


def norm_rows(values, gains):
    return values * lax.rsqrt(jnp.mean(values * values, axis=-1, keepdims=True) + EPSILON) * gains


def norm_rows_back(values, gains, cotangent):
    scale = lax.rsqrt(jnp.mean(values * values, axis=-1, keepdims=True) + EPSILON)
    unit = values * scale
    weighted = cotangent * gains
    return scale * (weighted - unit * jnp.mean(weighted * unit, axis=-1, keepdims=True))


def rotary_tables(positions):
    half = HEAD_DIM // 2
    frequencies = THETA_BASE ** (-jnp.arange(half, dtype=F32) * 2.0 / HEAD_DIM)
    angles = frequencies[:, None] * positions.astype(F32)[None, :]
    return jnp.cos(angles), jnp.sin(angles)


def turn(values, cosine, sine):
    a, b = jnp.split(values, 2, axis=-2)
    return jnp.concatenate([a * cosine - b * sine, b * cosine + a * sine], axis=-2)


def head_prepare(values, gains, tables):
    sequences, width, rows = values.shape
    heads = values.reshape(sequences, width // HEAD_DIM, HEAD_DIM, rows)
    scale = lax.rsqrt(jnp.mean(heads * heads, axis=2, keepdims=True) + EPSILON)
    return turn(heads * scale * gains[:, None], *tables).astype(BF)


def head_prepare_back(values, gains, tables, cotangent):
    sequences, width, rows = values.shape
    heads = values.reshape(sequences, width // HEAD_DIM, HEAD_DIM, rows)
    scale = lax.rsqrt(jnp.mean(heads * heads, axis=2, keepdims=True) + EPSILON)
    unit = heads * scale
    cosine, sine = tables
    weighted = turn(cotangent.reshape(heads.shape).astype(F32), cosine, -sine) * gains[:, None]
    back = scale * (weighted - unit * jnp.mean(weighted * unit, axis=2, keepdims=True))
    return back.reshape(values.shape).astype(BF)


def ein(spec, a, b):
    return jnp.einsum(spec, a, b, preferred_element_type=F32)


def swap(values):
    return lax.ppermute(values, "tp", [(0, 1), (1, 0)])


def reduce_scatter_rows(grads, count):
    rows, columns = grads.shape
    index = lax.axis_index("ctx")
    held = grads.reshape(count, rows // count, columns)
    bit = 1
    while bit < count:
        mine = (index // bit) % 2
        pairs = held.reshape(held.shape[0] // 2, 2, held.shape[1], columns)
        kept = lax.dynamic_index_in_dim(pairs, mine, 1, keepdims=False)
        sent = lax.dynamic_index_in_dim(pairs, 1 - mine, 1, keepdims=False).astype(BF)
        held = kept.astype(F32) + lax.ppermute(sent, "ctx", [(i, i ^ bit) for i in range(count)]).astype(F32)
        bit *= 2
    return held[0]


def local(
    tokens, output_cotangent, segment_ids, variant, attn_gain, ffn_gain, q_gain, k_gain,
    query_matrix, key_matrix, value_matrix, output_matrix, gate_matrix, up_matrix, down_matrix,
    query_input_factor, query_output_factor, key_input_factor, key_output_factor,
    value_input_factor, value_output_factor, output_input_factor, output_output_factor,
    gate_input_factor, gate_output_factor, up_input_factor, up_output_factor,
    down_input_factor, down_output_factor,
):
    sequences, rows_here, model_width = tokens.shape
    count = lax.axis_size("ctx")
    index = lax.axis_index("ctx")
    half = lax.axis_index("tp")
    key_heads = key_matrix.shape[1] // HEAD_DIM
    group = query_matrix.shape[1] // key_matrix.shape[1]
    units = sequences * key_heads
    parts = count // units
    unit = jnp.stack([index // parts, index % parts]).astype(jnp.int32)
    stacked = query_input_factor.shape[0]
    pick = ((jnp.arange(stacked, dtype=jnp.int32) // RANK)[None, :] == variant[:, None]).astype(F32)[:, None, :]
    tables = rotary_tables(index * rows_here + jnp.arange(rows_here, dtype=jnp.int32))

    output_matrix_other = swap(output_matrix)
    output_input_other = swap(output_input_factor)

    x = tokens.astype(F32)
    n1 = norm_rows(x, attn_gain).astype(BF)

    def low(rows, factor):
        return (ein("spd,rd->spr", rows, factor) * pick).astype(BF)

    h_query, h_key, h_value = (low(n1, f) for f in (query_input_factor, key_input_factor, value_input_factor))

    def project(hidden, matrix, factor):
        return ein("spd,de->sep", n1, matrix) + 2.0 * ein("spr,re->sep", hidden, factor)

    q_pre = project(h_query, query_matrix, query_output_factor)
    k_pre = project(h_key, key_matrix, key_output_factor)
    v_pre = project(h_value, value_matrix, value_output_factor)
    queries = head_prepare(q_pre, q_gain, tables).reshape(units, group * HEAD_DIM, rows_here)
    keys = head_prepare(k_pre, k_gain, tables).reshape(units, HEAD_DIM, rows_here)
    values = v_pre.astype(BF).reshape(units, HEAD_DIM, rows_here)
    q_all, kv_all = exchange(
        (queries, jnp.concatenate([keys, values], axis=1)), ("class", "full"), count, parts, 0, "send_qkv"
    )
    o_all, o_wide, lse = attn_fwd(unit, segment_ids, q_all, kv_all, parts, key_heads)
    (attn,) = exchange((o_all,), ("class",), count, parts, 1, "send_attn")
    attn = attn.reshape(sequences, key_heads * group * HEAD_DIM, rows_here)
    attn_other = swap(attn)

    out_sum = ein("sep,ed->spd", attn, output_matrix) + ein("sep,ed->spd", attn_other, output_matrix_other)
    h_out = ein("sep,re->spr", attn, output_input_factor) + ein("sep,re->spr", attn_other, output_input_other)
    h_out = (h_out * pick).astype(BF)
    mid = x + (out_sum + 2.0 * ein("spr,rd->spd", h_out, output_output_factor))
    n2 = norm_rows(mid, ffn_gain).astype(BF)

    halves = []
    cut = sequences // 2
    for part in (slice(0, cut), slice(cut, sequences)):
        flat = lambda a: a[part].reshape(-1, a.shape[-1])
        mask = jnp.broadcast_to(pick[part], (cut, rows_here, stacked)).reshape(-1, stacked)
        down, back, gb_gate, gb_up, ga_down = ffn(
            flat(n2), flat(output_cotangent), mask, gate_input_factor, up_input_factor, down_output_factor,
            gate_matrix, up_matrix, down_matrix, gate_output_factor, up_output_factor, down_input_factor,
        )
        shape = lambda a: a.reshape(cut, rows_here, -1).astype(F32)
        halves.append((shape(down), shape(swap(down)), shape(back), shape(swap(back)), gb_gate, gb_up, ga_down))
    gb_gate, gb_up, ga_down = (halves[0][i].astype(F32) + halves[1][i].astype(F32) for i in (4, 5, 6))

    def mine(a):
        return lax.dynamic_slice_in_dim(a, half * (model_width // 2), model_width // 2, a.ndim - 1)

    def grad(hidden, rows):
        return ein("spr,spe->re", hidden, rows)

    back = jnp.concatenate([h[2] + h[3] for h in halves], axis=0)
    dh_gate = (back[..., model_width : model_width + stacked] * pick).astype(BF)
    dh_up = (back[..., model_width + stacked :] * pick).astype(BF)
    d_n2 = back[..., :model_width] + ein("spr,rd->spd", dh_gate, gate_input_factor)
    d_n2 = d_n2 + ein("spr,rd->spd", dh_up, up_input_factor)
    d_mid = output_cotangent.astype(F32) + norm_rows_back(mid, ffn_gain, d_n2)
    d_branch = d_mid.astype(BF)
    dh_out = (2.0 * ein("spd,rd->spr", d_branch, output_output_factor) * pick).astype(BF)
    d_attn = ein("spd,ed->sep", d_branch, output_matrix) + ein("spr,re->sep", dh_out, output_input_factor)
    d_attn = d_attn.astype(BF).reshape(units, group * HEAD_DIM, rows_here)
    (do_all,) = exchange((d_attn,), ("class",), count, parts, 2, "send_d_attn")
    dq_all, dkv_all = attn_bwd(unit, segment_ids, q_all, kv_all, do_all, o_wide, lse, parts, key_heads)
    dq, dkv = exchange((dq_all, dkv_all), ("class", "full"), count, parts, 3, "send_dqkv")

    down = jnp.concatenate([h[0] + h[1] for h in halves], axis=0)
    h_down = (down[..., model_width:] * pick).astype(BF)
    block_result = mid + (down[..., :model_width] + 2.0 * ein("spr,rd->spd", h_down, down_output_factor))
    n2_mine, cot_mine, branch_mine = mine(n2), mine(output_cotangent), mine(d_branch)
    first = [
        2.0 * grad(h_down, cot_mine),
        grad(dh_gate, n2_mine),
        grad(dh_up, n2_mine),
        2.0 * grad(h_out, branch_mine),
        ein("spr,sep->re", dh_out, attn),
        gb_gate, gb_up, ga_down,
    ]
    first = reduce_scatter_rows(jnp.concatenate(first, axis=1), count)

    dq = dq.reshape(sequences, -1, rows_here)
    dkv = dkv.reshape(sequences, key_heads, parts, 2, HEAD_DIM, rows_here)
    dkv = jnp.sum(dkv.astype(F32), axis=2).astype(BF)
    d_v_pre = dkv[:, :, 1].reshape(sequences, -1, rows_here)
    d_q_pre = head_prepare_back(q_pre, q_gain, tables, dq)
    d_k_pre = head_prepare_back(k_pre, k_gain, tables, dkv[:, :, 0].reshape(sequences, -1, rows_here))
    partial = (
        ein("sep,de->spd", d_q_pre, query_matrix)
        + ein("sep,de->spd", d_k_pre, key_matrix)
        + ein("sep,de->spd", d_v_pre, value_matrix)
    )
    partial = jnp.concatenate(
        [
            partial,
            2.0 * ein("sep,re->spr", d_q_pre, query_output_factor),
            2.0 * ein("sep,re->spr", d_k_pre, key_output_factor),
            2.0 * ein("sep,re->spr", d_v_pre, value_output_factor),
        ],
        axis=-1,
    ).astype(BF)
    whole = partial.astype(F32) + swap(partial).astype(F32)
    dh_query, dh_key, dh_value = (
        (whole[..., model_width + i * stacked : model_width + (i + 1) * stacked] * pick).astype(BF) for i in range(3)
    )
    d_n1 = whole[..., :model_width] + ein("spr,rd->spd", dh_query, query_input_factor)
    d_n1 = d_n1 + ein("spr,rd->spd", dh_key, key_input_factor)
    d_n1 = d_n1 + ein("spr,rd->spd", dh_value, value_input_factor)
    input_grad = (d_mid + norm_rows_back(x, attn_gain, d_n1)).astype(BF)
    n1_mine = mine(n1)
    second = [
        grad(dh_query, n1_mine),
        grad(dh_key, n1_mine),
        grad(dh_value, n1_mine),
        2.0 * ein("spr,sep->re", h_query, d_q_pre),
        2.0 * ein("spr,sep->re", h_key, d_k_pre),
        2.0 * ein("spr,sep->re", h_value, d_v_pre),
    ]
    second = reduce_scatter_rows(jnp.concatenate(second, axis=1), count)

    w = model_width // 2
    shared = jnp.concatenate([first[:, : 4 * w], second[:, : 3 * w]], axis=1)
    other = swap(shared)
    both = jnp.where(half == 0, jnp.stack([shared, other], 1), jnp.stack([other, shared], 1))
    gb_down, ga_gate, ga_up, gb_out, ga_query, ga_key, ga_value = (
        both[:, :, i * w : (i + 1) * w].reshape(-1, model_width) for i in range(7)
    )
    units_here = gate_matrix.shape[1]
    qw, kw = query_matrix.shape[1], key_matrix.shape[1]
    ga_out, gb_gate, gb_up, ga_down = jnp.split(first[:, 4 * w :], [qw, qw + units_here, qw + 2 * units_here], axis=1)
    gb_query, gb_key, gb_value = jnp.split(second[:, 3 * w :], [qw, qw + kw], axis=1)
    return (
        block_result.astype(BF), input_grad, ga_query, gb_query, ga_key, gb_key, ga_value, gb_value,
        ga_out, gb_out, ga_gate, gb_gate, ga_up, gb_up, ga_down, gb_down,
    )


def solution(mesh):
    rows, whole, columns = P(None, "ctx", None), P(), P(None, "tp")
    owned, owned_half = P("ctx", None), P("ctx", "tp")
    return jax.shard_map(
        local,
        mesh=mesh,
        in_specs=(rows, rows) + (whole,) * 6
        + (columns, columns, columns, P("tp", None), columns, columns, P("tp", None))
        + (whole, columns) * 3 + (columns, whole) + (whole, columns) * 2 + (columns, whole),
        out_specs=(
            rows, rows, owned, owned_half, owned, owned_half, owned, owned_half,
            owned_half, owned, owned, owned_half, owned, owned_half, owned_half, owned,
        ),
        check_vma=False,
    )
```

```python
import functools, jax, jax.numpy as jnp
from jax import lax
from jax.experimental import pallas as pl
from jax.experimental.pallas import tpu as pltpu
from jax.sharding import PartitionSpec as P

HEAD_DIM = 64
LOG2E = 1.4426950408889634
KEY_TILE = 256


def tile_bounds(tile, stride, part):
    first = (2 * tile) * stride + part
    last = (2 * tile + 1) * stride + part
    return first, last


def allowed_pairs(seg_rows, seq, first, last, key_tile, group):
    lanes = lax.broadcasted_iota(jnp.int32, (1, 128), 1)
    q_pos = jnp.concatenate([first * 128 + lanes, last * 128 + lanes], axis=1)
    q_seg = jnp.concatenate(
        [seg_rows[block] for block in (first, last)], axis=1
    )
    k_seg = jnp.concatenate(
        [jnp.transpose(jnp.broadcast_to(seg_rows[2 * key_tile + b], (128, 128))) for b in (0, 1)], axis=0
    )
    k_seg = jnp.concatenate([k_seg, k_seg], axis=1)
    k_pos = key_tile * 256 + lax.broadcasted_iota(jnp.int32, (256, 256), 0)
    allowed = (k_seg == jnp.broadcast_to(q_seg, (256, 256))) & (k_pos <= jnp.broadcast_to(q_pos, (256, 256)))
    return jnp.concatenate([allowed] * group, axis=1)


def load_segments(seg_ref, seq, seg_rows):
    sequences, length = seg_ref.shape
    number = lax.broadcasted_iota(jnp.int32, (sequences, length), 0)
    row = jnp.sum(jnp.where(number == seq, seg_ref[...], 0), axis=0, keepdims=True)
    for b in range(length // 128):
        seg_rows[b] = row[:, b * 128 : (b + 1) * 128]


def tile_kind(seg_smem, seq, first, last, key_tile):
    key_low = seg_smem[seq, key_tile * 256]
    key_high = seg_smem[seq, key_tile * 256 + 255]
    q_low = seg_smem[seq, first * 128]
    q_high = seg_smem[seq, last * 128 + 127]
    needed = key_high >= q_low
    plain = (key_low == q_high) & (2 * key_tile + 1 < first)
    return needed, plain


def heads_side_by_side(ref, tile, group, offset=0):
    return jnp.concatenate(
        [ref[2 * tile + b, offset + h * HEAD_DIM : offset + (h + 1) * HEAD_DIM, :] for h in range(group) for b in (0, 1)], axis=1
    )


def attn_fwd_kernel(stride, group, units_per_seq, seg_smem, seg_ref, q_ref, kv_ref, o_ref, of_ref, lse_ref, kb, vt, acc, seg_rows):
    unit, part = lax.axis_index("ctx") // stride, lax.rem(lax.axis_index("ctx"), stride)
    seq = unit // units_per_seq
    load_segments(seg_ref, seq, seg_rows)
    key_tiles = kv_ref.shape[0] // 2
    q_tiles = q_ref.shape[0] // 2
    width = group * 256

    def load(j, _):
        for b in (0, 1):
            kb[j, b * 128 : (b + 1) * 128, :] = jnp.transpose(kv_ref[2 * j + b, :HEAD_DIM, :])
            vt[j, :HEAD_DIM, b * 128 : (b + 1) * 128] = kv_ref[2 * j + b, HEAD_DIM:, :]
        vt[j, HEAD_DIM:, :] = jnp.ones((16, 256), jnp.bfloat16)
        return 0

    lax.fori_loop(0, key_tiles, load, 0)

    def q_step(i, _):
        first, last = tile_bounds(i, stride, part)
        qt = heads_side_by_side(q_ref, i, group)
        acc[...] = jnp.zeros_like(acc)

        def k_step(j, _):
            needed, plain = tile_kind(seg_smem, seq, first, last, j)

            def weigh(masked):
                s = jnp.dot(kb[j], qt, preferred_element_type=jnp.float32)
                p = jnp.exp2(s * (LOG2E * HEAD_DIM**-0.5))
                if masked:
                    p = jnp.where(allowed_pairs(seg_rows, seq, first, last, j, group), p, 0.0)
                acc[...] += jnp.dot(vt[j], p.astype(jnp.bfloat16), preferred_element_type=jnp.float32)

            @pl.when(needed & plain)
            def _():
                weigh(False)

            @pl.when(needed & jnp.logical_not(plain))
            def _():
                weigh(True)

            return 0

        lax.fori_loop(0, last // 2 + 1, k_step, 0)
        total = acc[HEAD_DIM : HEAD_DIM + 1, :]
        lse_ref[i] = jnp.broadcast_to(jnp.log2(total), (8, width))
        out = acc[:HEAD_DIM, :] / total
        for h in range(group):
            for b in (0, 1):
                piece = out[:, h * 256 + b * 128 : h * 256 + (b + 1) * 128]
                of_ref[2 * i + b, h * HEAD_DIM : (h + 1) * HEAD_DIM, :] = piece
                o_ref[2 * i + b, h * HEAD_DIM : (h + 1) * HEAD_DIM, :] = piece.astype(jnp.bfloat16)
        return 0

    lax.fori_loop(0, q_tiles, q_step, 0)


def attn_bwd_kernel(
    stride, group, units_per_seq, seg_smem, seg_ref, q_ref, kv_ref, do_ref, of_ref, lse_ref,
    dq_ref, dkv_ref, qt, q3, dot_t, do3, delta, dqt, seg_rows,
):
    unit, part = lax.axis_index("ctx") // stride, lax.rem(lax.axis_index("ctx"), stride)
    seq = unit // units_per_seq
    load_segments(seg_ref, seq, seg_rows)
    key_tiles = kv_ref.shape[0] // 2
    q_tiles = q_ref.shape[0] // 2
    width = group * 256

    def load(i, _):
        for h in range(group):
            for b in (0, 1):
                rows = slice(h * HEAD_DIM, (h + 1) * HEAD_DIM)
                lanes = slice(h * 256 + b * 128, h * 256 + (b + 1) * 128)
                q = q_ref[2 * i + b, rows, :]
                g = do_ref[2 * i + b, rows, :]
                qt[i, :, lanes] = q
                q3[i, lanes, :] = jnp.transpose(q)
                dot_t[i, :, lanes] = g
                do3[i, lanes, :] = jnp.transpose(g)
                d = jnp.sum(g.astype(jnp.float32) * of_ref[2 * i + b, rows, :], axis=0, keepdims=True)
                delta[i, :, lanes] = jnp.broadcast_to(d, (8, 128))
        dqt[i] = jnp.zeros((HEAD_DIM, width), jnp.float32)
        return 0

    lax.fori_loop(0, q_tiles, load, 0)

    def k_step(j, _):
        kt = jnp.concatenate([kv_ref[2 * j + b, :HEAD_DIM, :] for b in (0, 1)], axis=1)
        vt = jnp.concatenate([kv_ref[2 * j + b, HEAD_DIM:, :] for b in (0, 1)], axis=1)
        kb = jnp.transpose(kt)
        vb = jnp.transpose(vt)

        def q_step(i, state):
            first, last = tile_bounds(i, stride, part)
            needed, plain = tile_kind(seg_smem, seq, first, last, j)

            def terms(masked, dk, dv):
                s = jnp.dot(kb, qt[i], preferred_element_type=jnp.float32)
                p = jnp.exp2(s * (LOG2E * HEAD_DIM**-0.5) - lse_ref[i, 0:1, :])
                if masked:
                    p = jnp.where(allowed_pairs(seg_rows, seq, first, last, j, group), p, 0.0)
                dp = jnp.dot(vb, dot_t[i], preferred_element_type=jnp.float32)
                ds = (p * (dp - delta[i, 0:1, :])).astype(jnp.bfloat16)
                dv = dv + jnp.dot(p.astype(jnp.bfloat16), do3[i], preferred_element_type=jnp.float32)
                dk = dk + jnp.dot(ds, q3[i], preferred_element_type=jnp.float32)
                dqt[i] += jnp.dot(kt, ds, preferred_element_type=jnp.float32)
                return dk, dv

            kind = jnp.where(needed, jnp.where(plain, 1, 2), 0)
            return lax.switch(
                kind, [lambda a, b: (a, b), functools.partial(terms, False), functools.partial(terms, True)], *state
            )

        zero = jnp.zeros((256, HEAD_DIM), jnp.float32)
        start = jnp.maximum((2 * j - part + stride - 1) // stride, 0) // 2
        dk, dv = lax.fori_loop(start, q_tiles, q_step, (zero, zero))
        for b in (0, 1):
            rows = slice(b * 128, (b + 1) * 128)
            dkv_ref[2 * j + b, :HEAD_DIM, :] = jnp.transpose(dk[rows] * HEAD_DIM**-0.5).astype(jnp.bfloat16)
            dkv_ref[2 * j + b, HEAD_DIM:, :] = jnp.transpose(dv[rows]).astype(jnp.bfloat16)
        return 0

    lax.fori_loop(0, key_tiles, k_step, 0)

    def store(i, _):
        for h in range(group):
            for b in (0, 1):
                piece = dqt[i, :, h * 256 + b * 128 : h * 256 + (b + 1) * 128]
                dq_ref[2 * i + b, h * HEAD_DIM : (h + 1) * HEAD_DIM, :] = (piece * HEAD_DIM**-0.5).astype(jnp.bfloat16)
        return 0

    lax.fori_loop(0, q_tiles, store, 0)


SMEM = pl.BlockSpec(memory_space=pltpu.SMEM)
VM = pl.BlockSpec(memory_space=pltpu.VMEM)


def attn_fwd(segs, q, kv, stride, units_per_seq):
    blocks, qrows, _ = q.shape
    group = qrows // HEAD_DIM
    tiles, ktiles, width = blocks // 2, kv.shape[0] // 2, group * 256
    return pl.pallas_call(
        functools.partial(attn_fwd_kernel, stride, group, units_per_seq),
        out_shape=(
            jax.ShapeDtypeStruct(q.shape, jnp.bfloat16),
            jax.ShapeDtypeStruct(q.shape, jnp.float32),
            jax.ShapeDtypeStruct((tiles, 8, width), jnp.float32),
        ),
        in_specs=[SMEM, VM, VM, VM],
        out_specs=(VM, VM, VM),
        scratch_shapes=[
            pltpu.VMEM((ktiles, 256, HEAD_DIM), jnp.bfloat16),
            pltpu.VMEM((ktiles, HEAD_DIM + 16, 256), jnp.bfloat16),
            pltpu.VMEM((HEAD_DIM + 16, width), jnp.float32),
            pltpu.VMEM((kv.shape[0], 1, 128), jnp.int32),
        ],
        compiler_params=pltpu.CompilerParams(vmem_limit_bytes=56 * 2**20),
        cost_estimate=pl.CostEstimate(flops=2 * 128 * blocks * qrows * kv.shape[0] * 128, bytes_accessed=4 * q.size, transcendentals=0),
        name="attention_forward",
    )(segs, segs, q, kv)


def attn_bwd(segs, q, kv, do, of, lse, stride, units_per_seq):
    blocks, qrows, _ = q.shape
    group = qrows // HEAD_DIM
    tiles, ktiles, width = blocks // 2, kv.shape[0] // 2, group * 256
    return pl.pallas_call(
        functools.partial(attn_bwd_kernel, stride, group, units_per_seq),
        out_shape=(jax.ShapeDtypeStruct(q.shape, jnp.bfloat16), jax.ShapeDtypeStruct(kv.shape, jnp.bfloat16)),
        in_specs=[SMEM, VM, VM, VM, VM, VM, VM],
        out_specs=(VM, VM),
        scratch_shapes=[
            pltpu.VMEM((tiles, HEAD_DIM, width), jnp.bfloat16),
            pltpu.VMEM((tiles, width, HEAD_DIM), jnp.bfloat16),
            pltpu.VMEM((tiles, HEAD_DIM, width), jnp.bfloat16),
            pltpu.VMEM((tiles, width, HEAD_DIM), jnp.bfloat16),
            pltpu.VMEM((tiles, 8, width), jnp.float32),
            pltpu.VMEM((tiles, HEAD_DIM, width), jnp.float32),
            pltpu.VMEM((kv.shape[0], 1, 128), jnp.int32),
        ],
        compiler_params=pltpu.CompilerParams(vmem_limit_bytes=56 * 2**20),
        cost_estimate=pl.CostEstimate(flops=5 * 128 * blocks * qrows * kv.shape[0] * 128, bytes_accessed=4 * q.size, transcendentals=0),
        name="attention_backward",
    )(segs, segs, q, kv, do, of, lse)

RANK = 16
EPSILON = 1e-05
THETA_BASE = 1000000.0
BF = jnp.bfloat16
F32 = jnp.float32
NT = (((1,), (1,)), ((), ()))
BIG = pltpu.CompilerParams(vmem_limit_bytes=60 * 2**20)


def cost(rows, width, columns, products, moved):
    return pl.CostEstimate(flops=2 * products * rows * width * columns, bytes_accessed=moved, transcendentals=0)

ANYWHERE = pl.BlockSpec(memory_space=pl.ANY)


def mm(a, b):
    return jnp.dot(a, b, preferred_element_type=F32)


def mm_nt(a, b):
    return lax.dot_general(a, b, NT, preferred_element_type=F32)


def shape(dims, kind):
    return jax.ShapeDtypeStruct(dims, kind)


def own_rows(ref, variant):
    return ref[pl.ds(pl.multiple_of(variant * RANK, RANK), RANK), :]


def norm_back(u, gain, c):
    scale = lax.rsqrt(jnp.mean(u * u, axis=-1, keepdims=True) + EPSILON)
    y = u * scale
    w = c * gain
    return scale * (w - y * jnp.mean(w * y, axis=-1, keepdims=True))


def turn(values, cosine, sine):
    half = HEAD_DIM // 2
    a, b = values[:, :half], values[:, half:]
    return jnp.concatenate([a * cosine - b * sine, b * cosine + a * sine], axis=1)


def rank_halves(blocks):
    return jnp.concatenate([b[: RANK // 2] for b in blocks] + [b[RANK // 2 :] for b in blocks], axis=0)


def spread(blocks):
    wide = []
    for i, b in enumerate(blocks):
        zero = jnp.zeros_like(b)
        wide.append(jnp.concatenate([b if i == j else zero for j in range(len(blocks))], axis=1))
    return rank_halves(wide)


def column(ref):
    return jnp.transpose(jnp.broadcast_to(ref[...][None, :], (128, ref.shape[0])))


def project_kernel(
    variant, x_ref, gain_ref, wq, wk, wv, aq, ak, av, bq, bk, bv, qg_ref, kg_ref, cos_ref, sin_ref,
    n1_ref, h_ref, pre_ref, q_ref, kv_ref, ac_ref, bc_ref, gains_ref, pick_ref, n1_s,
):
    sequences, rows, width = x_ref.shape
    qw, kw = wq.shape[1], wk.shape[1]
    heads_q, heads_k = qw // HEAD_DIM, kw // HEAD_DIM
    cosine, sine = cos_ref[...], sin_ref[...]
    qg, kg = column(qg_ref), column(kg_ref)
    gains_ref[0], gains_ref[1] = qg, kg
    gain = gain_ref[...][None, :]
    for v in range(pick_ref.shape[0]):
        for s in range(sequences):
            pick_ref[v, s] = jnp.full((8, 128), jnp.where(variant[s] == v, 1.0, 0.0), F32)

    def prepare(t, gains):
        heads = t.reshape(t.shape[0] // HEAD_DIM, HEAD_DIM, rows)
        scale = lax.rsqrt(jnp.mean(heads * heads, axis=1, keepdims=True) + EPSILON)
        return turn(heads * scale * gains, cosine, sine).astype(BF)

    def pair(p, _):
        for i in (0, 1):
            x = x_ref[2 * p + i].astype(F32)
            scale = lax.rsqrt(jnp.mean(x * x, axis=-1, keepdims=True) + EPSILON)
            n1 = (x * scale * gain).astype(BF)
            n1_ref[2 * p + i] = n1
            n1_s[i * rows : (i + 1) * rows, :] = n1
        n1 = n1_s[...]
        base = [mm(n1, w[...]) for w in (wq, wk, wv)]
        for i in (0, 1):
            s = 2 * p + i
            v = variant[s]
            half = slice(i * rows, (i + 1) * rows)
            a = jnp.concatenate([own_rows(f, v) for f in (aq, ak, av)], axis=0)
            b = [own_rows(f, v) for f in (bq, bk, bv)]
            ac_ref[s] = a
            bc_ref[s] = jnp.concatenate(b, axis=1)
            h = mm_nt(n1_s[half, :], a).astype(BF)
            h_ref[s] = jnp.concatenate([h, jnp.zeros((rows, 128 - 3 * RANK), BF)], axis=1)
            h2 = h * 2
            q, k, val = (
                jnp.transpose(base[n][half] + mm(h2[:, n * RANK : (n + 1) * RANK], b[n])) for n in range(3)
            )
            pre_ref[s, :qw, :] = q
            pre_ref[s, qw:, :] = k
            group = heads_q // heads_k
            q = prepare(q, qg).reshape(heads_k, group * HEAD_DIM, rows)
            k = prepare(k, kg)
            val = val.astype(BF).reshape(heads_k, HEAD_DIM, rows)
            q_ref[pl.ds(s * heads_k, heads_k)] = q
            kv_ref[pl.ds(s * heads_k, heads_k), :HEAD_DIM, :] = k
            kv_ref[pl.ds(s * heads_k, heads_k), HEAD_DIM:, :] = val
        return 0

    lax.fori_loop(0, sequences // 2, pair, 0)


def project(variant, x, gain, weights, ins, outs, qg, kg, tables):
    sequences, rows, width = x.shape
    qw, kw = weights[0].shape[1], weights[1].shape[1]
    units = sequences * kw // HEAD_DIM
    return pl.pallas_call(
        project_kernel,
        out_shape=(
            shape(x.shape, BF), shape((sequences, rows, 128), BF), shape((sequences, qw + kw, rows), F32),
            shape((units, qw // kw * HEAD_DIM, rows), BF), shape((units, 2 * HEAD_DIM, rows), BF),
            shape((sequences, 3 * RANK, width), BF), shape((sequences, RANK, qw + 2 * kw), BF),
            shape((2, HEAD_DIM, rows), F32), shape((ins[0].shape[0] // RANK, sequences, 8, 128), F32),
        ),
        in_specs=[SMEM] + [VM] * 15,
        out_specs=(VM,) * 9,
        scratch_shapes=[pltpu.VMEM((2 * rows, width), BF)],
        compiler_params=BIG,
        cost_estimate=cost(sequences * rows, width, qw + 2 * kw, 1, 12 * sequences * rows * width),
        name="project",
    )(variant, x, gain, *weights, *ins, *outs, qg, kg, *tables)


def middle_kernel(variant, x_ref, gain_ref, attn, attn_x, wo, wo_x, ao, ao_x, bo, mid_ref, n2_ref, h_ref, lhs, lhs_x):
    sequences, rows, width = x_ref.shape

    def pair(p, _):
        for i in (0, 1):
            half = slice(i * rows, (i + 1) * rows)
            lhs[half, :] = jnp.transpose(attn[2 * p + i])
            lhs_x[half, :] = jnp.transpose(attn_x[2 * p + i])
        out = mm(lhs[...], wo[...]) + mm(lhs_x[...], wo_x[...])
        for i in (0, 1):
            s = 2 * p + i
            v = variant[s]
            half = slice(i * rows, (i + 1) * rows)
            h = (mm_nt(lhs[half, :], own_rows(ao, v)) + mm_nt(lhs_x[half, :], own_rows(ao_x, v))).astype(BF)
            h_ref[s] = jnp.concatenate([h, jnp.zeros((rows, 128 - RANK), BF)], axis=1)
            mid = x_ref[s].astype(F32) + (out[half] + mm(h * 2, own_rows(bo, v)))
            mid_ref[s] = mid
            scale = lax.rsqrt(jnp.mean(mid * mid, axis=-1, keepdims=True) + EPSILON)
            n2_ref[s] = (mid * scale * gain_ref[...][None, :]).astype(BF)
        return 0

    lax.fori_loop(0, sequences // 2, pair, 0)


def middle(variant, x, gain, attn, attn_x, wo, wo_x, ao, ao_x, bo):
    sequences, rows, width = x.shape
    inner = attn.shape[1]
    return pl.pallas_call(
        middle_kernel,
        out_shape=(shape(x.shape, F32), shape(x.shape, BF), shape((sequences, rows, 128), BF)),
        in_specs=[SMEM] + [VM] * 9,
        out_specs=(VM,) * 3,
        scratch_shapes=[pltpu.VMEM((2 * rows, inner), BF), pltpu.VMEM((2 * rows, inner), BF)],
        compiler_params=BIG,
        cost_estimate=cost(sequences * rows, width, inner, 2, 12 * sequences * rows * width),
        name="middle",
    )(variant, x, gain, attn, attn_x, wo, wo_x, ao, ao_x, bo)


def feed_kernel(
    first, variant, n2_ref, cot_ref, ag, au, bd, wg_ref, wu_ref, wd_ref, bg_ref, bu_ref, ad_ref,
    back_ref, h_ref, hidden_ref, dgate_ref, dup_ref, hg, hu, dhd, dn2_acc, dhg_acc, dhu_acc,
):
    step = pl.program_id(0)
    rows, width = n2_ref.shape
    seqs = rows // 128
    ranks = seqs * RANK
    keep = lax.broadcasted_iota(jnp.int32, (rows, ranks), 0) // 128 == (
        lax.broadcasted_iota(jnp.int32, (rows, ranks), 1) // RANK
    )

    def gather(ref):
        return jnp.concatenate([own_rows(ref, variant[first + i]) for i in range(seqs)], axis=0)

    def compact(a):
        a = jnp.where(keep, a, 0.0)
        return sum(a[:, i * RANK : (i + 1) * RANK] for i in range(seqs))

    @pl.when(step == 0)
    def _():
        g = jnp.where(keep, mm_nt(n2_ref[...], gather(ag)), 0.0)
        u = jnp.where(keep, mm_nt(n2_ref[...], gather(au)), 0.0)
        d = jnp.where(keep, mm_nt(cot_ref[...], gather(bd)) * 2.0, 0.0)
        hg[...] = (g * 2.0).astype(BF)
        hu[...] = (u * 2.0).astype(BF)
        dhd[...] = d.astype(BF)
        h_ref[...] = jnp.concatenate(
            [compact(g), compact(u), compact(d), jnp.zeros((rows, 128 - 3 * RANK), F32)], axis=1
        ).astype(BF)
        dn2_acc[...] = jnp.zeros_like(dn2_acc)
        dhg_acc[...] = jnp.zeros_like(dhg_acc)
        dhu_acc[...] = jnp.zeros_like(dhu_acc)

    n2 = n2_ref[...]
    bg, bu, ad = gather(bg_ref), gather(bu_ref), gather(ad_ref)
    gate = mm(n2, wg_ref[...]) + mm(hg[...], bg)
    up = mm(n2, wu_ref[...]) + mm(hu[...], bu)
    sg = 1.0 / (1.0 + jnp.exp(-gate))
    silu = gate * sg
    hidden_ref[...] = (silu * up).astype(BF)
    dh = mm_nt(cot_ref[...], wd_ref[...]) + mm(dhd[...], ad)
    dg = (dh * up * sg * (1.0 + gate * (1.0 - sg))).astype(BF)
    du = (dh * silu).astype(BF)
    dgate_ref[...] = dg
    dup_ref[...] = du
    dn2_acc[...] += mm_nt(dg, wg_ref[...]) + mm_nt(du, wu_ref[...])
    dhg_acc[...] += mm_nt(dg, bg)
    dhu_acc[...] += mm_nt(du, bu)

    @pl.when(step == pl.num_programs(0) - 1)
    def _():
        back_ref[:, :width] = dn2_acc[...].astype(BF)
        back_ref[:, width:] = jnp.concatenate(
            [compact(dhg_acc[...]) * 2, compact(dhu_acc[...]) * 2, jnp.zeros((rows, 128 - 2 * RANK), F32)], axis=1
        ).astype(BF)


def feed_tile(units):
    return 1152 if units % 1152 == 0 else units


def feed(index, parts, variant, n2, cot, ag, au, bd, wg, wu, wd, bg, bu, ad):
    rows, width = n2.shape[0] // parts, n2.shape[1]
    stacked, units = bg.shape
    tile = feed_tile(units)
    ranks = rows // 128 * RANK
    part = pl.BlockSpec((rows, width), lambda f: (index, 0))
    fixed = lambda dims: pl.BlockSpec(dims, lambda f: (0, 0))
    cols = lambda height: pl.BlockSpec((height, tile), lambda f: (0, f))
    return pl.pallas_call(
        functools.partial(feed_kernel, index * rows // 128),
        grid=(units // tile,),
        out_shape=(shape((rows, width + 128), BF), shape((rows, 128), BF)) + (shape((rows, units), BF),) * 3,
        in_specs=[SMEM, part, part] + [fixed((stacked, width))] * 3
        + [cols(width), cols(width), pl.BlockSpec((tile, width), lambda f: (f, 0))] + [cols(stacked)] * 3,
        out_specs=(fixed((rows, width + 128)), fixed((rows, 128))) + (cols(rows),) * 3,
        scratch_shapes=[pltpu.VMEM((rows, ranks), BF)] * 3
        + [pltpu.VMEM((rows, width), F32), pltpu.VMEM((rows, ranks), F32), pltpu.VMEM((rows, ranks), F32)],
        compiler_params=BIG,
        cost_estimate=cost(rows, width, units, 5, 6 * width * units),
        name="feed_forward",
    )(variant, n2, cot, ag, au, bd, wg, wu, wd, bg, bu, ad)


def down_kernel(variant, *refs):
    (h_a, hidden_a, dgate_a, dup_a), (h_b, hidden_b, dgate_b, dup_b) = refs[:4], refs[4:8]
    wd_ref, ad_ref, down_ref, grads_ref, hs, acc, hacc = refs[8:]
    step = pl.program_id(0)
    part = hidden_a.shape[0]
    width, tile = wd_ref.shape[1], wd_ref.shape[0]
    seqs = 2 * part // 128

    @pl.when(step == 0)
    def _():
        turned = [jnp.transpose(r[i * 128 : (i + 1) * 128, :].astype(F32)) for r in (h_a, h_b) for i in range(seqs // 2)]
        for n, factor in enumerate((2.0, 2.0, 1.0)):
            hs[n] = (spread([t[n * RANK : (n + 1) * RANK] for t in turned]) * factor).astype(BF)
        acc[...] = jnp.zeros_like(acc)
        hacc[...] = jnp.zeros_like(hacc)

    for c, hidden in enumerate((hidden_a, hidden_b)):
        acc[c * part : (c + 1) * part] += mm(hidden[...], wd_ref[...])
        for i in range(seqs // 2):
            rows = slice(i * 128, (i + 1) * 128)
            own = own_rows(ad_ref, variant[c * (seqs // 2) + i])
            hacc[c * part + i * 128 : c * part + (i + 1) * 128, :RANK] += mm_nt(hidden[rows], own)
    for n, (a, b) in enumerate(((dgate_a, dgate_b), (dup_a, dup_b), (hidden_a, hidden_b))):
        grad = mm(hs[n, :, :part], a[...]) + mm(hs[n, :, part:], b[...])
        grads_ref[:, n * tile : (n + 1) * tile] = grad.astype(BF)

    @pl.when(step == pl.num_programs(0) - 1)
    def _():
        down_ref[:, :width] = acc[...].astype(BF)
        down_ref[:, width:] = hacc[...].astype(BF)


def down_part(variant, fed_a, fed_b, wd, ad):
    part, units = fed_a[1].shape
    rows = 2 * part
    stacked, width = ad.shape[0], wd.shape[1]
    tile = feed_tile(units)
    ranks = rows // 128 * RANK
    fixed = lambda dims: pl.BlockSpec(dims, lambda f: (0, 0))
    cols = lambda height, n=1: pl.BlockSpec((height, n * tile), lambda f: (0, f))
    return pl.pallas_call(
        down_kernel,
        grid=(units // tile,),
        out_shape=(shape((rows, width + 128), BF), shape((ranks, 3 * units), BF)),
        in_specs=[SMEM] + [fixed((part, 128)), cols(part), cols(part), cols(part)] * 2
        + [pl.BlockSpec((tile, width), lambda f: (f, 0)), cols(stacked)],
        out_specs=(fixed((rows, width + 128)), cols(ranks, 3)),
        scratch_shapes=[pltpu.VMEM((3, ranks, rows), BF), pltpu.VMEM((rows, width), F32), pltpu.VMEM((rows, 128), F32)],
        compiler_params=BIG,
        cost_estimate=cost(rows, width, units, 1, 2 * width * units),
        name="feed_down",
    )(variant, *fed_a, *fed_b, wd, ad)


def turn_back_kernel(
    variant, mid_ref, n2_ref, cot_ref, back_a, back_ax, back_b, back_bx, hout_ref, attn_ref, gain_ref, ag, au, bo, ao, wo,
    dmid_ref, dattn_ref, grads_ref, branch_s, hidden_s,
):
    sequences, rows, width = mid_ref.shape
    half = pl.multiple_of(lax.axis_index("tp") * (width // 2), width // 2)
    mine = pl.ds(half, width // 2)
    gain = gain_ref[...][None, :]
    cut = sequences // 2
    sums = ((back_a, back_ax), (back_b, back_bx))
    blocks = []
    for s in range(sequences):
        v = variant[s]
        own, other = (r[s % cut * rows : (s % cut + 1) * rows, :].astype(F32) for r in sums[s // cut])
        whole = own + other
        dh = whole[:, width : width + 2 * RANK].astype(BF)
        c = whole[:, :width] + mm(dh, jnp.concatenate([own_rows(ag, v), own_rows(au, v)], axis=0))
        d_mid = cot_ref[s].astype(F32) + norm_back(mid_ref[s], gain, c)
        dmid_ref[s] = d_mid
        here = slice(s * rows, (s + 1) * rows)
        branch_s[here, :] = d_mid.astype(BF)
        dho = (mm_nt(branch_s[here, :], own_rows(bo, v)) * 2.0).astype(BF)
        hidden_s[here, :] = mm(dho, own_rows(ao, v))
        wide = jnp.concatenate([dh, dho, hout_ref[s][:, :RANK] * 2, jnp.zeros((rows, 128 - 4 * RANK), BF)], axis=1)
        t = jnp.transpose(wide.astype(F32)).astype(BF)
        blocks.append(
            jnp.concatenate(
                [
                    mm_nt(t[2 * RANK : 3 * RANK], attn_ref[s]),
                    mm(t[:RANK], n2_ref[s, :, mine]),
                    mm(t[RANK : 2 * RANK], n2_ref[s, :, mine]),
                    mm(t[3 * RANK : 4 * RANK], branch_s[here, mine]),
                ],
                axis=1,
            )
        )
    grads_ref[...] = rank_halves(blocks).astype(BF)
    for p in range(sequences // 2):
        d_attn = mm_nt(branch_s[2 * p * rows : 2 * (p + 1) * rows, :], wo[...]) + hidden_s[2 * p * rows : 2 * (p + 1) * rows, :]
        for i in (0, 1):
            dattn_ref[2 * p + i] = jnp.transpose(d_attn[i * rows : (i + 1) * rows]).astype(BF)


def turn_back(variant, mid, n2, cot, backs, hout, attn, gain, ag, au, bo, ao, wo):
    sequences, rows, width = mid.shape
    inner = wo.shape[0]
    return pl.pallas_call(
        turn_back_kernel,
        out_shape=(
            shape(mid.shape, F32), shape((sequences, inner, rows), BF),
            shape((sequences * RANK, inner + 3 * (width // 2)), BF),
        ),
        in_specs=[SMEM] + [VM] * 15,
        out_specs=(VM,) * 3,
        scratch_shapes=[pltpu.VMEM((sequences * rows, width), BF), pltpu.VMEM((sequences * rows, inner), F32)],
        compiler_params=BIG,
        cost_estimate=cost(sequences * rows, width, inner, 1, 20 * sequences * rows * width),
        name="turn_back",
    )(variant, mid, n2, cot, *backs, hout, attn, gain, ag, au, bo, ao, wo)


def result_kernel(variant, mid_ref, down_ref, down_x_ref, cot_ref, bd, out_ref, grads_ref):
    sequences, rows, width = mid_ref.shape
    mine = pl.ds(pl.multiple_of(lax.axis_index("tp") * (width // 2), width // 2), width // 2)
    blocks = []
    for s in range(sequences):
        v = variant[s]
        whole = down_ref[s].astype(F32) + down_x_ref[s].astype(F32)
        h = whole[:, width : width + RANK].astype(BF) * 2
        out_ref[s] = (mid_ref[s] + (whole[:, :width] + mm(h, own_rows(bd, v)))).astype(BF)
        t = jnp.transpose(jnp.concatenate([h, jnp.zeros((rows, 128 - RANK), BF)], axis=1).astype(F32)).astype(BF)
        blocks.append(mm(t[:RANK], cot_ref[s, :, mine]))
    grads_ref[...] = rank_halves(blocks).astype(BF)


def result(variant, mid, down, down_x, cot, bd):
    sequences, rows, width = mid.shape
    return pl.pallas_call(
        result_kernel,
        out_shape=(shape(mid.shape, BF), shape((sequences * RANK, width // 2), BF)),
        in_specs=[SMEM] + [VM] * 5,
        out_specs=(VM,) * 2,
        compiler_params=BIG,
        cost_estimate=cost(sequences * rows, width, 16, 2, 12 * sequences * rows * width),
        name="block_result",
    )(variant, mid, down, down_x, cot, bd)


MESH = pl.DeviceIdType.MESH


def exchange_kernel(count, parts, kinds, *refs):
    n = len(kinds)
    xs, outs = refs[:n], refs[n : 2 * n]
    sends, recvs, locals_ = refs[2 * n : 3 * n], refs[3 * n : 4 * n], refs[4 * n]
    me = lax.axis_index("ctx")
    barrier = pltpu.get_barrier_semaphore()
    step = 1 if "full" in kinds else parts
    peers = count // step - 1

    def greet(k, _):
        other = lax.rem(me + k * step, count)
        pl.semaphore_signal(barrier, inc=1, device_id={"ctx": other}, device_id_type=MESH)
        return 0

    lax.fori_loop(1, peers + 1, greet, 0)

    def block(kind, x, device):
        if kind == "class" or x.shape[0] != count:
            return device // parts
        return device

    def slot(kind, device):
        return device // parts if kind == "class" else device

    def copy(i, target, place):
        kind = kinds[i]
        return pltpu.make_async_remote_copy(
            src_ref=xs[i].at[block(kind, xs[i], target)],
            dst_ref=outs[i].at[slot(kind, place)],
            send_sem=sends[i].at[slot(kind, target)],
            recv_sem=recvs[i].at[slot(kind, place)],
            device_id={"ctx": target},
            device_id_type=MESH,
        )

    own = [
        pltpu.make_async_copy(xs[i].at[block(kinds[i], xs[i], me)], outs[i].at[slot(kinds[i], me)], locals_.at[i])
        for i in range(n)
    ]
    for c in own:
        c.start()
    pl.semaphore_wait(barrier, peers)
    for i in range(n):
        hop = 1 if kinds[i] == "full" else parts

        def send(k, _, i=i, hop=hop):
            copy(i, lax.rem(me + k * hop, count), me).start()
            return 0

        lax.fori_loop(1, count // hop, send, 0)
    for i in range(n):
        hop = 1 if kinds[i] == "full" else parts

        def finish(k, _, i=i, hop=hop):
            other = lax.rem(me + k * hop, count)
            copy(i, other, me).wait_send()
            copy(i, other, other).wait_recv()
            return 0

        lax.fori_loop(1, count // hop, finish, 0)
    for c in own:
        c.wait()


def exchange(arrays, kinds, count, parts, collective_id, name):
    n = len(arrays)
    members = [count // parts if kind == "class" else count for kind in kinds]
    anywhere = pl.BlockSpec(memory_space=pl.ANY)
    return pl.pallas_call(
        functools.partial(exchange_kernel, count, parts, kinds),
        out_shape=tuple(jax.ShapeDtypeStruct((k,) + a.shape[1:], a.dtype) for k, a in zip(members, arrays)),
        in_specs=[anywhere] * n,
        out_specs=(anywhere,) * n,
        scratch_shapes=[pltpu.SemaphoreType.DMA((k,)) for k in members] * 2 + [pltpu.SemaphoreType.DMA((n,))],
        compiler_params=pltpu.CompilerParams(collective_id=collective_id, has_side_effects=True),
        name=name,
    )(*arrays)


def home_kernel(count, parts, x, o, ox, send, recv, xsend, xrecv, own):
    me = lax.axis_index("ctx")
    unit = me // parts
    units = count // parts
    across = {"tp": 1 - lax.axis_index("tp")}
    barrier = pltpu.get_barrier_semaphore()

    def greet(k, _):
        pl.semaphore_signal(barrier, inc=1, device_id={"ctx": lax.rem(me + k * parts, count)}, device_id_type=MESH)
        return 0

    lax.fori_loop(1, units, greet, 0)
    pl.semaphore_signal(barrier, inc=1, device_id=across, device_id_type=MESH)
    kept = pltpu.make_async_copy(x.at[unit], o.at[unit], own)
    kept.start()
    pl.semaphore_wait(barrier, units)

    def copy(target, place):
        return pltpu.make_async_remote_copy(
            src_ref=x.at[target // parts], dst_ref=o.at[place // parts], send_sem=send.at[target // parts],
            recv_sem=recv.at[place // parts], device_id={"ctx": target}, device_id_type=MESH,
        )

    def pass_on(source, slot):
        return pltpu.make_async_remote_copy(
            src_ref=source.at[slot], dst_ref=ox.at[slot], send_sem=xsend.at[slot], recv_sem=xrecv.at[slot],
            device_id=across, device_id_type=MESH,
        )

    def start(k, _):
        copy(lax.rem(me + k * parts, count), me).start()
        return 0

    lax.fori_loop(1, units, start, 0)
    pass_on(x, unit).start()

    def relay(k, _):
        other = lax.rem(me + count - k * parts, count)
        copy(other, other).wait_recv()
        pass_on(o, other // parts).start()
        return 0

    lax.fori_loop(1, units, relay, 0)

    def finish(k, _):
        other = lax.rem(me + k * parts, count)
        copy(other, me).wait_send()
        return 0

    lax.fori_loop(1, units, finish, 0)

    def finish_across(k, _):
        pass_on(o, k).wait_send()
        pass_on(o, k).wait_recv()
        return 0

    lax.fori_loop(0, units, finish_across, 0)
    kept.wait()


def send_home(x, count, parts, collective_id):
    units = count // parts
    dma = pltpu.SemaphoreType.DMA
    return pl.pallas_call(
        functools.partial(home_kernel, count, parts),
        out_shape=(shape(x.shape, x.dtype),) * 2,
        in_specs=[ANYWHERE],
        out_specs=(ANYWHERE,) * 2,
        scratch_shapes=[dma((units,))] * 4 + [dma],
        compiler_params=pltpu.CompilerParams(collective_id=collective_id, has_side_effects=True),
        name="send_attn",
    )(x)


def finish_kernel(reduce, count, widths, shared, *refs):
    refs = list(refs)
    take = lambda n: [refs.pop(0) for _ in range(n)]
    dq_ref, dkv_ref, pre_ref, h_ref, gains, cos_ref, sin_ref, gain_ref, bc_ref, pick_ref = take(10)
    far = take(7)
    grads = take(3) if reduce else []
    (out_ref,) = take(1)
    gout = take(4) if reduce else take(1)
    x, d_mid, n1, wq, wk, wv, ac = near = take(7)
    d_n, gb, dh_own, dh_other, dh_sum, sbuf, rbuf, gq = take(8)
    near_sems, dh_send, dh_recv, xsend, xrecv = take(5)
    sequences, inner, rows = dq_ref.shape
    width = out_ref.shape[2]
    kw = wk.shape[1]
    half_rows = sequences * RANK // 2
    me = lax.axis_index("ctx")
    across = {"tp": 1 - lax.axis_index("tp")}
    mine = pl.ds(pl.multiple_of(lax.axis_index("tp") * (width // 2), width // 2), width // 2)

    def remote(source, target, send, recv, device):
        return pltpu.make_async_remote_copy(
            src_ref=source, dst_ref=target, send_sem=send, recv_sem=recv, device_id=device, device_id_type=MESH
        )

    loads = [pltpu.make_async_copy(f, n, near_sems.at[i]) for i, (f, n) in enumerate(zip(far, near))]
    barrier = pltpu.get_barrier_semaphore()
    pl.semaphore_signal(barrier, inc=1, device_id=across, device_id_type=MESH)
    peers = 1
    if reduce:
        planes, plane_ins, fin_outs, fin_ins = take(2), take(2), take(2), take(2)
        own, core_in = take(2)
        own_sems, core_send, core_recv = take(3)
        plane_send, plane_recv, fin_send, fin_recv = take(4)
        (last_sems,) = take(1)
        chips = count // 2
        chip, core = me // 2, lax.rem(me, 2)
        twin = {"ctx": 2 * chip + 1 - core}
        pl.semaphore_signal(barrier, inc=1, device_id=twin, device_id_type=MESH)

        def at_chip(k):
            return lax.rem(chip + k, chips)

        def greet(k, _):
            pl.semaphore_signal(barrier, inc=1, device_id={"ctx": 2 * at_chip(k) + core}, device_id_type=MESH)
            return 0

        lax.fori_loop(1, chips, greet, 0)
        peers += chips

        def part_of(ref, who):
            size = ref.shape[0] // 2
            return ref.at[pl.ds(pl.multiple_of(who * size, 16), size), :]

        known, w_qkv = sum(widths[:3]), widths[3]
        own_loads, to_twin, at = [], [], 0
        for i, ref in enumerate(grads):
            place = slice(at, at + widths[i])
            at += widths[i]
            own_loads.append(pltpu.make_async_copy(part_of(ref, core), own.at[:, place], own_sems.at[i]))
            to_twin.append(
                remote(part_of(ref, 1 - core), core_in.at[:, place], core_send.at[i], core_recv.at[i], twin)
            )
        to_twin.append(remote(gq.at[1 - core], core_in.at[:, known : known + w_qkv], core_send.at[3], core_recv.at[3], twin))
        for c in own_loads:
            c.start()
    for i in (3, 4, 5, 2, 6, 0, 1):
        loads[i].start()
    pl.semaphore_wait(barrier, peers)
    if reduce:
        for c in to_twin[:3]:
            c.start()

    cosine, sine = cos_ref[...], sin_ref[...]
    heads_k = kw // HEAD_DIM
    cuts = (slice(0, inner), slice(inner, inner + kw), slice(inner + kw, inner + 2 * kw))

    def prepare_back(pre, gains, c):
        u = pre.reshape(pre.shape[0] // HEAD_DIM, HEAD_DIM, rows)
        scale = lax.rsqrt(jnp.mean(u * u, axis=1, keepdims=True) + EPSILON)
        y = u * scale
        w = turn(c.reshape(u.shape).astype(F32), cosine, -sine) * gains
        return (scale * (w - y * jnp.mean(w * y, axis=1, keepdims=True))).reshape(pre.shape)

    def first_step(s):
        dkv = dkv_ref[s * heads_k : (s + 1) * heads_k].astype(F32)
        dkv = jnp.sum(dkv, axis=1).astype(BF) if dkv.shape[1] > 1 else dkv[:, 0].astype(BF)
        d_q = prepare_back(pre_ref[s, :inner, :], gains[0], dq_ref[s])
        d_k = prepare_back(pre_ref[s, inner:, :], gains[1], dkv[:, :HEAD_DIM, :].reshape(kw, rows))
        d_v = dkv[:, HEAD_DIM:, :].reshape(kw, rows).astype(F32)
        d = jnp.transpose(jnp.concatenate([d_q, d_k, d_v], axis=0)).astype(BF)
        d_n[s] = d
        dh = [mm_nt(d[:, c], bc_ref[s, :, c]) * 2.0 for c in cuts]
        dh_own[s] = jnp.concatenate(dh + [jnp.zeros((rows, 128 - 3 * RANK), F32)], axis=1).astype(BF)
        t = (jnp.transpose(h_ref[s].astype(F32)) * 2.0).astype(BF)
        gb[s] = jnp.concatenate([mm(t[i * RANK : (i + 1) * RANK], d[:, c]) for i, c in enumerate(cuts)], axis=1)

    def part_copy(s):
        return remote(sbuf.at[s], rbuf.at[s], xsend.at[s], xrecv.at[s], across)

    dh_copies = []

    def send_pair(p):
        pair = pl.ds(2 * p, 2)
        first_step(2 * p)
        first_step(2 * p + 1)
        dh_copies.append(remote(dh_own.at[pair], dh_other.at[pair], dh_send.at[p], dh_recv.at[p], across))
        dh_copies[-1].start()
        if p == 0:
            for i in (3, 4, 5):
                loads[i].wait()
        d = jnp.concatenate([d_n[2 * p], d_n[2 * p + 1]], axis=0)
        part = mm_nt(d[:, cuts[0]], wq[...]) + mm_nt(d[:, cuts[1]], wk[...]) + mm_nt(d[:, cuts[2]], wv[...])
        for i in (0, 1):
            sbuf[2 * p + i] = part[i * rows : (i + 1) * rows].astype(BF)
            part_copy(2 * p + i).start()

    def plane_copy(g, k, slot):
        chunk = planes[g].shape[1] // chips
        return remote(
            planes[g].at[:, pl.ds(pl.multiple_of(k * chunk, 128), chunk)], plane_ins[g].at[slot],
            plane_send.at[g, k], plane_recv.at[g, slot], {"ctx": 2 * k + core},
        )

    def fin_copy(g, k, slot):
        return remote(
            fin_outs[g].at[k], fin_ins[g].at[slot], fin_send.at[g, k], fin_recv.at[g, slot], {"ctx": 2 * k + core}
        )

    def each_chip(step):
        def body(k, _):
            step(at_chip(k))
            return 0

        lax.fori_loop(1, chips, body, 0)

    def to_plane(g):
        chunk = planes[g].shape[1] // chips
        each_chip(lambda k: plane_copy(g, k, chip).start())
        plane_ins[g][chip] = planes[g][:, pl.ds(pl.multiple_of(chip * chunk, 128), chunk)]

    def to_owners(g):
        each_chip(lambda k: plane_copy(g, k, k).wait_recv())
        total = plane_ins[g][0].astype(F32)
        for k in range(1, chips):
            total = total + plane_ins[g][k].astype(F32)
        chunk, per = total.shape[1], RANK // 2
        for k in range(chips):
            row = jnp.zeros((per, chunk), F32)
            for s in range(sequences):
                row = row + total[s * per : (s + 1) * per] * pick_ref[k, s][:, :1]
            fin_outs[g][k] = jnp.concatenate([row[:, : chunk // 2], row[:, chunk // 2 :]], axis=0).astype(BF)
        each_chip(lambda k: fin_copy(g, k, chip).start())
        fin_ins[g][chip] = fin_outs[g][chip]

    def rows_in(g):
        each_chip(lambda k: fin_copy(g, k, k).wait_recv())
        rows_ref, per = gout[g], RANK // 2
        chunk = rows_ref.shape[1] // chips
        for k in range(chips):
            block = fin_ins[g][k].astype(F32)
            rows_ref[:, k * chunk : k * chunk + chunk // 2] = block[:per]
            rows_ref[:, k * chunk + chunk // 2 : (k + 1) * chunk] = block[per:]
        copy = remote(
            rows_ref.at[:, shared[g][0] : shared[g][1]], gout[2 + g], last_sems.at[g], last_sems.at[2 + g], across
        )
        copy.start()
        return copy

    def last_step(s):
        part_copy(s).wait_recv()
        c = sbuf[s].astype(F32) + rbuf[s].astype(F32) + mm(dh_sum[s][:, : 3 * RANK], ac[s])
        out_ref[s] = (d_mid[s] + norm_back(x[s].astype(F32), gain_ref[...][None, :], c)).astype(BF)

    pairs = sequences // 2
    send_pair(0)
    if reduce:
        for c in own_loads:
            c.wait()
        for c in to_twin[:3]:
            c.wait_recv()
        planes[0][:, :known] = (own[...].astype(F32) + core_in[:, :known].astype(F32)).astype(BF)
        if planes[0].shape[1] > known:
            planes[0][:, known:] = jnp.zeros((half_rows, planes[0].shape[1] - known), BF)
        to_plane(0)
    for p in range(1, pairs):
        send_pair(p)
    loads[2].wait()
    blocks = []
    for s in range(sequences):
        if s % 2 == 0:
            dh_copies[s // 2].wait_recv()
        dh = (dh_own[s].astype(F32) + dh_other[s].astype(F32)).astype(BF)
        dh_sum[s] = dh
        t = jnp.transpose(dh.astype(F32)).astype(BF)
        wide = mm(t[: 3 * RANK], n1[s, :, mine])
        blocks.append(jnp.concatenate([wide[i * RANK : (i + 1) * RANK] for i in range(3)] + [gb[s]], axis=1))
    everything = rank_halves(blocks)
    for b in (0, 1):
        gq[b] = everything[b * half_rows : (b + 1) * half_rows].astype(BF)
    if reduce:
        to_twin[3].start()
    for i in (6, 0, 1):
        loads[i].wait()
    if reduce:
        to_owners(0)
        to_twin[3].wait_recv()
        planes[1][:, :w_qkv] = (gq[core].astype(F32) + core_in[:, known : known + w_qkv].astype(F32)).astype(BF)
        if planes[1].shape[1] > w_qkv:
            planes[1][:, w_qkv:] = jnp.zeros((half_rows, planes[1].shape[1] - w_qkv), BF)
        to_plane(1)
        last_step(0)
        to_owners(1)
        shared_copies = [rows_in(0)]
        last_step(1)
        shared_copies.append(rows_in(1))
        for s in range(2, sequences):
            last_step(s)
        for c in shared_copies:
            c.wait()
        for c in to_twin:
            c.wait_send()
        for g in (0, 1):
            each_chip(lambda k, g=g: plane_copy(g, k, chip).wait_send())
            each_chip(lambda k, g=g: fin_copy(g, k, chip).wait_send())
    else:
        for s in range(sequences):
            last_step(s)
        gout[0][...] = gq[...]
    for c in dh_copies:
        c.wait_send()
    for s in range(sequences):
        part_copy(s).wait_send()


def finish(reduce, count, dq, dkv, pre, h, gains, tables, gain, bc, pick, x, d_mid, n1, weights, ac, grads, shared, collective_id):
    sequences, rows, width = x.shape
    inner, kw = weights[0].shape[1], weights[1].shape[1]
    w_qkv = 3 * (width // 2) + inner + 2 * kw
    half_rows = sequences * RANK // 2
    dma = pltpu.SemaphoreType.DMA
    far = (x, d_mid, n1) + tuple(weights) + (ac,)
    widths = ()
    gshape = (shape((2, half_rows, w_qkv), BF),)
    scratch = [pltpu.VMEM(a.shape, a.dtype) for a in far]
    scratch += [
        pltpu.VMEM((sequences, rows, inner + 2 * kw), BF),
        pltpu.VMEM((sequences, RANK, inner + 2 * kw), F32),
        pltpu.VMEM((sequences, rows, 128), BF),
        pltpu.VMEM((sequences, rows, 128), BF),
        pltpu.VMEM((sequences, rows, 128), BF),
        pltpu.VMEM(x.shape, BF),
        pltpu.VMEM(x.shape, BF),
        pltpu.VMEM((2, half_rows, w_qkv), BF),
        dma((7,)), dma((sequences // 2,)), dma((sequences // 2,)), dma((sequences,)), dma((sequences,)),
    ]
    extra = ()
    if reduce:
        chips = count // 2
        widths = tuple(g.shape[1] for g in grads) + (w_qkv,)
        padded = [-(-n // (256 * chips)) * 256 * chips for n in (sum(widths[:3]), w_qkv)]
        gshape = tuple(shape((RANK // 2, n), F32) for n in padded)
        gshape += tuple(shape((RANK // 2, b - a), F32) for a, b in shared)
        scratch += [pltpu.VMEM((half_rows, n), BF) for n in padded]
        scratch += [pltpu.VMEM((chips, half_rows, n // chips), BF) for n in padded]
        scratch += [pltpu.VMEM((chips, RANK, n // chips // 2), BF) for n in padded] * 2
        scratch += [
            pltpu.VMEM((half_rows, sum(widths[:3])), BF),
            pltpu.VMEM((half_rows, sum(widths)), BF),
            dma((3,)), dma((4,)), dma((4,)),
        ]
        scratch += [dma((2, chips))] * 4 + [dma((4,))]
        extra = tuple(grads)
    return pl.pallas_call(
        functools.partial(finish_kernel, reduce, count, widths, shared),
        out_shape=(shape(x.shape, BF),) + gshape,
        in_specs=[VM] * 10 + [ANYWHERE] * (7 + len(extra)),
        out_specs=(VM,) * (1 + len(gshape)),
        scratch_shapes=scratch,
        compiler_params=pltpu.CompilerParams(
            collective_id=collective_id, has_side_effects=True, vmem_limit_bytes=60 * 2**20
        ),
        name="finish",
    )(dq, dkv, pre, h, gains, *tables, gain, bc, pick, *far, *extra)


def unpack_kernel(hidden_units, tile, inner, kw, first, second, first_x, second_x, *outs):
    ga_query, gb_query, ga_key, gb_key, ga_value, gb_value, ga_out, gb_out, ga_gate, gb_gate, ga_up, gb_up, ga_down, gb_down = outs
    width = ga_query.shape[1]
    w = width // 2
    lower = lax.axis_index("tp") == 0
    for f in range(hidden_units // tile):
        for n, out in enumerate((gb_gate, gb_up, ga_down)):
            out[:, f * tile : (f + 1) * tile] = first[:, (3 * f + n) * tile : (3 * f + n + 1) * tile]
    at = 3 * hidden_units
    ga_out[...] = first[:, at : at + inner]

    def join(out, own, own_at, other, i):
        a = own[:, own_at + i * w : own_at + (i + 1) * w]
        b = other[:, i * w : (i + 1) * w]
        out[:, :w] = jnp.where(lower, a, b)
        out[:, w:] = jnp.where(lower, b, a)

    for i, out in enumerate((ga_gate, ga_up, gb_out, gb_down)):
        join(out, first, at + inner, first_x, i)
    for i, out in enumerate((ga_query, ga_key, ga_value)):
        join(out, second, 0, second_x, i)
    at = 3 * w
    gb_query[...] = second[:, at : at + inner]
    gb_key[...] = second[:, at + inner : at + inner + kw]
    gb_value[...] = second[:, at + inner + kw : at + inner + 2 * kw]


def unpack(first, second, first_x, second_x, width, hidden_units, tile, inner, kw):
    sizes = (width, inner, width, kw, width, kw, inner, width, width, hidden_units, width, hidden_units, hidden_units, width)
    return pl.pallas_call(
        functools.partial(unpack_kernel, hidden_units, tile, inner, kw),
        out_shape=tuple(shape((first.shape[0], n), F32) for n in sizes),
        in_specs=[VM] * 4,
        out_specs=(VM,) * 14,
        name="unpack",
    )(first, second, first_x, second_x)


def rotary_tables(positions):
    half = HEAD_DIM // 2
    frequencies = THETA_BASE ** (-jnp.arange(half, dtype=F32) * 2.0 / HEAD_DIM)
    angles = frequencies[:, None] * positions.astype(F32)[None, :]
    return jnp.cos(angles), jnp.sin(angles)


def swap(values):
    return lax.ppermute(values, "tp", [(0, 1), (1, 0)])


def reduce_scatter_rows(grads, count):
    rows, columns = grads.shape
    index = lax.axis_index("ctx")
    held = grads.reshape(count, rows // count, columns)
    bit = 1
    while bit < count:
        mine = (index // bit) % 2
        pairs = held.reshape(held.shape[0] // 2, 2, held.shape[1], columns)
        kept = lax.dynamic_index_in_dim(pairs, mine, 1, keepdims=False)
        sent = lax.dynamic_index_in_dim(pairs, 1 - mine, 1, keepdims=False).astype(BF)
        held = kept.astype(F32) + lax.ppermute(sent, "ctx", [(i, i ^ bit) for i in range(count)]).astype(F32)
        bit *= 2
    return held[0]


def local(
    tokens, output_cotangent, segment_ids, variant, attn_gain, ffn_gain, q_gain, k_gain,
    query_matrix, key_matrix, value_matrix, output_matrix, gate_matrix, up_matrix, down_matrix,
    query_input_factor, query_output_factor, key_input_factor, key_output_factor,
    value_input_factor, value_output_factor, output_input_factor, output_output_factor,
    gate_input_factor, gate_output_factor, up_input_factor, up_output_factor,
    down_input_factor, down_output_factor,
):
    sequences, rows_here, width = tokens.shape
    count = lax.axis_size("ctx")
    index = lax.axis_index("ctx")
    inner, kw = query_matrix.shape[1], key_matrix.shape[1]
    key_heads = kw // HEAD_DIM
    units = sequences * key_heads
    parts = count // units
    stacked = query_input_factor.shape[0]
    reduce_here = stacked // count == RANK // 2
    tables = rotary_tables(index * rows_here + jnp.arange(rows_here, dtype=jnp.int32))
    weights = (query_matrix, key_matrix, value_matrix)
    ins = (query_input_factor, key_input_factor, value_input_factor)
    outs = (query_output_factor, key_output_factor, value_output_factor)

    output_matrix_other = swap(output_matrix)
    output_input_other = swap(output_input_factor)

    n1, h_one, pre, queries, keys_values, ac, bc, gains, pick = project(
        variant, tokens, attn_gain, weights, ins, outs, q_gain, k_gain, tables
    )
    q_all, kv_all = exchange((queries, keys_values), ("class", "full"), count, parts, 0, "send_qkv")
    o_all, o_wide, lse = attn_fwd(segment_ids, q_all, kv_all, parts, key_heads)
    attn, attn_other = (a.reshape(sequences, inner, rows_here) for a in send_home(o_all, count, parts, 1))
    mid, n2, h_out = middle(
        variant, tokens, ffn_gain, attn, attn_other, output_matrix, output_matrix_other,
        output_input_factor, output_input_other, output_output_factor,
    )

    flat = lambda a: a.reshape(sequences * rows_here, -1)
    by_seq = lambda a: a.reshape(sequences, rows_here, -1)
    fed = [
        feed(
            i, 2, variant, flat(n2), flat(output_cotangent), gate_input_factor, up_input_factor, down_output_factor,
            gate_matrix, up_matrix, down_matrix, gate_output_factor, up_output_factor, down_input_factor,
        )
        for i in (0, 1)
    ]
    backs = [b for f in fed for b in (f[0], swap(f[0]))]
    down, g_ffn = down_part(variant, fed[0][1:], fed[1][1:], down_matrix, down_input_factor)
    d_mid, d_attn, g_mid = turn_back(
        variant, mid, n2, output_cotangent, backs, h_out, attn, ffn_gain, gate_input_factor, up_input_factor,
        output_output_factor, output_input_factor, output_matrix,
    )
    d_attn = d_attn.reshape(queries.shape)
    d_attn, down = lax.optimization_barrier((d_attn, down))
    down_other = swap(down)
    (do_all,) = exchange((d_attn,), ("class",), count, parts, 2, "send_d_attn")
    dq_all, dkv_all = attn_bwd(segment_ids, q_all, kv_all, do_all, o_wide, lse, parts, key_heads)
    block_result, g_down = result(variant, mid, by_seq(down), by_seq(down_other), output_cotangent, down_output_factor)
    dq, dkv = exchange((dq_all, dkv_all), ("class", "full"), count, parts, 3, "send_dqkv")

    w = width // 2
    hidden_units = gate_matrix.shape[1]
    tile = feed_tile(hidden_units)
    at = 3 * hidden_units + inner
    shared = ((at, at + 4 * w), (0, 3 * w))
    ends = finish(
        reduce_here, count, dq.reshape(sequences, inner, rows_here), dkv.reshape(units, parts, 2 * HEAD_DIM, rows_here),
        pre, h_one, gains, tables, attn_gain, bc, pick, tokens, d_mid, n1, weights, ac,
        (g_ffn, g_mid, g_down), shared, 4,
    )
    if reduce_here:
        owned = ends[1:]
    else:
        per = RANK // 2
        pick = (jnp.arange(stacked // RANK, dtype=jnp.int32)[:, None] == variant[None, :]).astype(F32)
        owned, other = [], []
        for grads, (low, high) in zip((jnp.concatenate([g_ffn, g_mid, g_down], axis=1), ends[1]), shared):
            grads = grads.reshape(2, sequences, per, -1).astype(F32)
            dense = jnp.sum(pick[:, None, :, None, None] * grads[None], axis=2)
            owned.append(reduce_scatter_rows(dense.reshape(stacked, -1), count))
            other.append(swap(owned[-1][:, low:high]))
        owned = owned + other
    return (block_result, ends[0]) + tuple(unpack(*owned, width, hidden_units, tile, inner, kw))


def solution(mesh):
    rows, whole, columns = P(None, "ctx", None), P(), P(None, "tp")
    owned, owned_half = P("ctx", None), P("ctx", "tp")
    return jax.shard_map(
        local,
        mesh=mesh,
        in_specs=(rows, rows) + (whole,) * 6
        + (columns, columns, columns, P("tp", None), columns, columns, P("tp", None))
        + (whole, columns) * 3 + (columns, whole) + (whole, columns) * 2 + (columns, whole),
        out_specs=(
            rows, rows, owned, owned_half, owned, owned_half, owned, owned_half,
            owned_half, owned, owned, owned_half, owned, owned_half, owned_half, owned,
        ),
        check_vma=False,
    )
```

```python
import functools, jax, jax.numpy as jnp
from jax import lax
from jax.experimental import pallas as pl
from jax.experimental.pallas import tpu as pltpu
from jax.sharding import PartitionSpec as P

HEAD_DIM = 64
LOG2E = 1.4426950408889634
MESH = pl.DeviceIdType.MESH
SMEM = pl.BlockSpec(memory_space=pltpu.SMEM)
VM = pl.BlockSpec(memory_space=pltpu.VMEM)
RANK = 16
EPSILON = 1e-05
THETA_BASE = 1000000.0
BF = jnp.bfloat16
F32 = jnp.float32
NT = (((1,), (1,)), ((), ()))
BIG = pltpu.CompilerParams(vmem_limit_bytes=60 * 2**20)


def cost(rows, width, columns, products, moved):
    return pl.CostEstimate(flops=2 * products * rows * width * columns, bytes_accessed=moved, transcendentals=0)

ANYWHERE = pl.BlockSpec(memory_space=pl.ANY)


def mm(a, b):
    return jnp.dot(a, b, preferred_element_type=F32)


def mm_nt(a, b):
    return lax.dot_general(a, b, NT, preferred_element_type=F32)


def shape(dims, kind):
    return jax.ShapeDtypeStruct(dims, kind)


def remote(source, target, send, recv, device):
    return pltpu.make_async_remote_copy(
        src_ref=source, dst_ref=target, send_sem=send, recv_sem=recv, device_id=device, device_id_type=MESH
    )


def own_rows(ref, variant):
    return ref[pl.ds(pl.multiple_of(variant * RANK, RANK), RANK), :]


def norm_back(u, gain, c):
    scale = lax.rsqrt(jnp.mean(u * u, axis=-1, keepdims=True) + EPSILON)
    y = u * scale
    w = c * gain
    return scale * (w - y * jnp.mean(w * y, axis=-1, keepdims=True))


def turn(values, cosine, sine):
    half = HEAD_DIM // 2
    a, b = values[:, :half], values[:, half:]
    return jnp.concatenate([a * cosine - b * sine, b * cosine + a * sine], axis=1)


def rank_halves(blocks):
    return jnp.concatenate([b[: RANK // 2] for b in blocks] + [b[RANK // 2 :] for b in blocks], axis=0)


def column(ref):
    return jnp.transpose(jnp.broadcast_to(ref[...][None, :], (128, ref.shape[0])))


def project_kernel(
    variant, x_ref, gain_ref, wq, wk, wv, aq, ak, av, bq, bk, bv, qg_ref, kg_ref, cos_ref, sin_ref, *refs,
):
    n1_ref, h_ref, pre_ref, q_ref, kv_ref, ac_ref, bc_ref, gains_ref, pick_ref = refs[6:15]
    n1_s, sems = refs[21:]
    picks = [
        pltpu.make_async_copy(
            refs[n].at[pl.ds(pl.multiple_of(variant[s] * RANK, RANK), RANK), :],
            refs[15 + n].at[pl.ds(s * RANK, RANK), :], sems.at[n, s],
        )
        for n in range(6)
        for s in range(x_ref.shape[0])
    ]
    for c in picks:
        c.start()
    sequences, rows, width = x_ref.shape
    qw, kw = wq.shape[1], wk.shape[1]
    heads_q, heads_k = qw // HEAD_DIM, kw // HEAD_DIM
    cosine, sine = cos_ref[...], sin_ref[...]
    qg, kg = column(qg_ref), column(kg_ref)
    gains_ref[0], gains_ref[1] = qg, kg
    gain = gain_ref[...][None, :]
    for v in range(pick_ref.shape[0]):
        for s in range(sequences):
            pick_ref[v, s] = jnp.full((8, 128), jnp.where(variant[s] == v, 1.0, 0.0), F32)

    def prepare(t, gains):
        heads = t.reshape(t.shape[0] // HEAD_DIM, HEAD_DIM, rows)
        scale = lax.rsqrt(jnp.mean(heads * heads, axis=1, keepdims=True) + EPSILON)
        return turn(heads * scale * gains, cosine, sine).astype(BF)

    def pair(p, _):
        for i in (0, 1):
            x = x_ref[2 * p + i].astype(F32)
            scale = lax.rsqrt(jnp.mean(x * x, axis=-1, keepdims=True) + EPSILON)
            n1 = (x * scale * gain).astype(BF)
            n1_ref[2 * p + i] = n1
            n1_s[i * rows : (i + 1) * rows, :] = n1
        n1 = n1_s[...]
        base = [mm(n1, w[...]) for w in (wq, wk, wv)]
        for i in (0, 1):
            s = 2 * p + i
            v = variant[s]
            half = slice(i * rows, (i + 1) * rows)
            a = jnp.concatenate([own_rows(f, v) for f in (aq, ak, av)], axis=0)
            b = [own_rows(f, v) for f in (bq, bk, bv)]
            ac_ref[s] = a
            bc_ref[s] = jnp.concatenate(b, axis=1)
            h = mm_nt(n1_s[half, :], a).astype(BF)
            h_ref[s] = jnp.concatenate([h, jnp.zeros((rows, 128 - 3 * RANK), BF)], axis=1)
            h2 = h * 2
            q, k, val = (
                jnp.transpose(base[n][half] + mm(h2[:, n * RANK : (n + 1) * RANK], b[n])) for n in range(3)
            )
            pre_ref[s, :qw, :] = q
            pre_ref[s, qw:, :] = k
            group = heads_q // heads_k
            q = prepare(q, qg).reshape(heads_k, group * HEAD_DIM, rows)
            k = prepare(k, kg)
            val = val.astype(BF).reshape(heads_k, HEAD_DIM, rows)
            q_ref[pl.ds(s * heads_k, heads_k)] = q
            kv_ref[pl.ds(s * heads_k, heads_k), :HEAD_DIM, :] = k
            kv_ref[pl.ds(s * heads_k, heads_k), HEAD_DIM:, :] = val
        return 0

    lax.fori_loop(0, sequences // 2, pair, 0)
    for c in picks:
        c.wait()


def project(variant, x, gain, weights, ins, outs, qg, kg, tables, factors):
    sequences, rows, width = x.shape
    qw, kw = weights[0].shape[1], weights[1].shape[1]
    units = sequences * kw // HEAD_DIM
    return pl.pallas_call(
        project_kernel,
        out_shape=(
            shape(x.shape, BF), shape((sequences, rows, 128), BF), shape((sequences, qw + kw, rows), F32),
            shape((units, qw // kw * HEAD_DIM, rows), BF), shape((units, 2 * HEAD_DIM, rows), BF),
            shape((sequences, 3 * RANK, width), BF), shape((sequences, RANK, qw + 2 * kw), BF),
            shape((2, HEAD_DIM, rows), F32), shape((ins[0].shape[0] // RANK, sequences, 8, 128), F32),
        ) + tuple(shape((sequences * RANK, f.shape[1]), BF) for f in factors),
        in_specs=[SMEM] + [VM] * 15 + [ANYWHERE] * 6,
        out_specs=(VM,) * 15,
        scratch_shapes=[pltpu.VMEM((2 * rows, width), BF), pltpu.SemaphoreType.DMA((6, sequences))],
        compiler_params=BIG,
        cost_estimate=cost(sequences * rows, width, qw + 2 * kw, 1, 12 * sequences * rows * width),
        name="project",
    )(variant, x, gain, *weights, *ins, *outs, qg, kg, *tables, *factors)


def middle_kernel(variant, x_ref, gain_ref, attn, attn_x, wo, wo_x, ao, ao_x, bo, mid_ref, n2_ref, h_ref, lhs, lhs_x):
    sequences, rows, width = x_ref.shape

    def pair(p, _):
        for i in (0, 1):
            half = slice(i * rows, (i + 1) * rows)
            lhs[half, :] = jnp.transpose(attn[2 * p + i])
            lhs_x[half, :] = jnp.transpose(attn_x[2 * p + i])
        out = mm(lhs[...], wo[...]) + mm(lhs_x[...], wo_x[...])
        for i in (0, 1):
            s = 2 * p + i
            v = variant[s]
            half = slice(i * rows, (i + 1) * rows)
            h = (mm_nt(lhs[half, :], own_rows(ao, v)) + mm_nt(lhs_x[half, :], own_rows(ao_x, v))).astype(BF)
            h_ref[s] = jnp.concatenate([h, jnp.zeros((rows, 128 - RANK), BF)], axis=1)
            mid = x_ref[s].astype(F32) + (out[half] + mm(h * 2, own_rows(bo, v)))
            mid_ref[s] = mid
            scale = lax.rsqrt(jnp.mean(mid * mid, axis=-1, keepdims=True) + EPSILON)
            n2_ref[s] = (mid * scale * gain_ref[...][None, :]).astype(BF)
        return 0

    lax.fori_loop(0, sequences // 2, pair, 0)


def middle(variant, x, gain, attn, attn_x, wo, wo_x, ao, ao_x, bo):
    sequences, rows, width = x.shape
    inner = attn.shape[1]
    return pl.pallas_call(
        middle_kernel,
        out_shape=(shape(x.shape, F32), shape(x.shape, BF), shape((sequences, rows, 128), BF)),
        in_specs=[SMEM] + [VM] * 9,
        out_specs=(VM,) * 3,
        scratch_shapes=[pltpu.VMEM((2 * rows, inner), BF), pltpu.VMEM((2 * rows, inner), BF)],
        compiler_params=BIG,
        cost_estimate=cost(sequences * rows, width, inner, 2, 12 * sequences * rows * width),
        name="middle",
    )(variant, x, gain, attn, attn_x, wo, wo_x, ao, ao_x, bo)


def feed_kernel(
    chunks, n2_ref, cot_ref, ag, au, bd, wg_ref, wu_ref, wd_ref, bg_ref, bu_ref, ad_ref,
    back_ref, back_x_ref, down_ref, grads_ref,
    hg, hu, dhd, hs, dn2_acc, dhg_acc, dhu_acc, down_acc, h_acc, hidden_s, dgate_s, dup_s, back_s, down_s,
    send_sems, recv_sems, keep_sems,
):
    step = pl.program_id(0)
    rows, width = n2_ref.shape
    tiles, tile = hidden_s.shape[0], hidden_s.shape[2]
    part = rows // chunks
    seqs = rows // 128
    ranks = seqs * RANK
    chunk, f = step // tiles, lax.rem(step, tiles)
    here = pl.ds(pl.multiple_of(chunk * part, part), part)
    across = {"tp": 1 - lax.axis_index("tp")}

    def keep(first, count):
        row = lax.broadcasted_iota(jnp.int32, (count, ranks), 0) // 128 + first // 128
        return row == lax.broadcasted_iota(jnp.int32, (count, ranks), 1) // RANK

    def compact(a, first=0):
        a = jnp.where(keep(first, a.shape[0]), a, 0.0)
        return sum(a[:, i * RANK : (i + 1) * RANK] for i in range(seqs))

    def copies(c):
        there = pl.ds(c * part, part)
        return (
            remote(back_s.at[there, :], back_x_ref.at[there, :], send_sems.at[c], recv_sems.at[c], across),
            pltpu.make_async_copy(back_s.at[there, :], back_ref.at[there, :], keep_sems.at[c]),
        )

    down_copy = pltpu.make_async_copy(down_s, down_ref, keep_sems.at[chunks])

    @pl.when(step == 0)
    def _():
        barrier = pltpu.get_barrier_semaphore()
        pl.semaphore_signal(barrier, inc=1, device_id=across, device_id_type=MESH)
        pl.semaphore_wait(barrier, 1)
        g = jnp.where(keep(0, rows), mm_nt(n2_ref[...], ag[...]), 0.0)
        u = jnp.where(keep(0, rows), mm_nt(n2_ref[...], au[...]), 0.0)
        d = jnp.where(keep(0, rows), mm_nt(cot_ref[...], bd[...]) * 2.0, 0.0)
        hg[...] = (g * 2.0).astype(BF)
        hu[...] = (u * 2.0).astype(BF)
        dhd[...] = d.astype(BF)
        for n, a in enumerate((g * 2.0, u * 2.0, d)):
            turned = jnp.transpose(jnp.concatenate([a, jnp.zeros((rows, 128 - ranks), F32)], axis=1))
            rows_of = [turned[i * RANK : (i + 1) * RANK] for i in range(seqs)]
            hs[n] = rank_halves(rows_of).astype(BF)
        down_acc[...] = jnp.zeros_like(down_acc)
        h_acc[...] = jnp.zeros_like(h_acc)

    @pl.when((step < chunks * tiles) & (f == 0))
    def _():
        dn2_acc[...] = jnp.zeros_like(dn2_acc)
        dhg_acc[...] = jnp.zeros_like(dhg_acc)
        dhu_acc[...] = jnp.zeros_like(dhu_acc)

    @pl.when(step < chunks * tiles)
    def _():
        n2 = n2_ref[here, :]
        bg, bu, ad = bg_ref[...], bu_ref[...], ad_ref[...]
        gate = mm(n2, wg_ref[...]) + mm(hg[here, :], bg)
        up = mm(n2, wu_ref[...]) + mm(hu[here, :], bu)
        sg = 1.0 / (1.0 + jnp.exp(-gate))
        silu = gate * sg
        hidden_s[f, here, :] = (silu * up).astype(BF)
        dh = mm_nt(cot_ref[here, :], wd_ref[...]) + mm(dhd[here, :], ad)
        dg = (dh * up * sg * (1.0 + gate * (1.0 - sg))).astype(BF)
        du = (dh * silu).astype(BF)
        dgate_s[f, here, :] = dg
        dup_s[f, here, :] = du
        dn2_acc[...] += mm_nt(dg, wg_ref[...]) + mm_nt(du, wu_ref[...])
        dhg_acc[...] += mm_nt(dg, bg)
        dhu_acc[...] += mm_nt(du, bu)

    for c in range(chunks):

        @pl.when(step == (c + 1) * tiles - 1)
        def _():
            there = slice(c * part, (c + 1) * part)
            back_s[there, :width] = dn2_acc[...].astype(BF)
            small = [compact(a[...], c * part) * 2 for a in (dhg_acc, dhu_acc)]
            back_s[there, width:] = jnp.concatenate(small + [jnp.zeros((part, 128 - 2 * RANK), F32)], axis=1).astype(BF)
            for copy in copies(c):
                copy.start()

    @pl.when(step >= chunks * tiles)
    def _():
        hidden = hidden_s[f]
        down_acc[...] += mm(hidden, wd_ref[...])
        h_acc[...] += mm_nt(hidden, ad_ref[...])
        for n, kept in enumerate((dgate_s, dup_s, hidden_s)):
            grads_ref[:, n * tile : (n + 1) * tile] = mm(hs[n], kept[f]).astype(BF)

    @pl.when(step == pl.num_programs(0) - 1)
    def _():
        down_s[:, :width] = down_acc[...].astype(BF)
        down_s[:, width:] = jnp.concatenate([compact(h_acc[...]), jnp.zeros((rows, 128 - RANK), F32)], axis=1).astype(BF)
        down_copy.start()
        for c in range(chunks):
            for copy in copies(c):
                copy.wait()
        down_copy.wait()


def feed_tile(units):
    return 1152 if units % 1152 == 0 else units


def feed(chunks, n2, cot, ag, au, bd, wg, wu, wd, bg, bu, ad, collective_id):
    rows, width = n2.shape
    stacked, units = bg.shape
    tile = feed_tile(units)
    tiles, part, ranks = units // tile, rows // chunks, rows // 128 * RANK
    last = chunks * tiles
    once = lambda dims: pl.BlockSpec(dims, lambda i: (0, 0), pipeline_mode=pl.Buffered(1))
    early = lambda height: pl.BlockSpec((height, tile), lambda i: (0, jnp.where(i < last, lax.rem(i, tiles), tiles - 1)))
    down_rows = pl.BlockSpec((tile, width), lambda i: (lax.rem(i, tiles), 0))
    down_cols = pl.BlockSpec((stacked, tile), lambda i: (0, lax.rem(i, tiles)))
    vm, dma = pltpu.VMEM, pltpu.SemaphoreType.DMA
    wide = shape((rows, width + 128), BF)
    return pl.pallas_call(
        functools.partial(feed_kernel, chunks),
        grid=(last + tiles,),
        out_shape=(wide, wide, wide, shape((ranks, 3 * units), BF)),
        in_specs=[once((rows, width)), once((rows, width))] + [once((stacked, width))] * 3
        + [early(width), early(width), down_rows, early(stacked), early(stacked), down_cols],
        out_specs=(ANYWHERE,) * 3 + (pl.BlockSpec((ranks, 3 * tile), lambda i: (0, jnp.maximum(i - last, 0))),),
        scratch_shapes=[vm((rows, ranks), BF)] * 3
        + [vm((3, ranks, rows), BF), vm((part, width), F32), vm((part, ranks), F32), vm((part, ranks), F32)]
        + [vm((rows, width), F32), vm((rows, ranks), F32)] + [vm((tiles, rows, tile), BF)] * 3
        + [vm((rows, width + 128), BF)] * 2 + [dma((chunks,)), dma((chunks,)), dma((chunks + 1,))],
        compiler_params=pltpu.CompilerParams(
            collective_id=collective_id, has_side_effects=True, vmem_limit_bytes=62 * 2**20
        ),
        cost_estimate=cost(rows, width, units, 6, 12 * width * units),
        name="feed_forward",
    )(n2, cot, ag, au, bd, wg, wu, wd, bg, bu, ad)


def turn_back_kernel(
    variant, mid_ref, n2_ref, cot_ref, back_ref, back_x_ref, hout_ref, attn_ref, gain_ref, ag, au, bo, ao, wo,
    dmid_ref, dattn_ref, grads_ref, branch_s, hidden_s,
):
    sequences, rows, width = mid_ref.shape
    half = pl.multiple_of(lax.axis_index("tp") * (width // 2), width // 2)
    mine = pl.ds(half, width // 2)
    gain = gain_ref[...][None, :]
    blocks = []
    for s in range(sequences):
        v = variant[s]
        whole = back_ref[s].astype(F32) + back_x_ref[s].astype(F32)
        dh = whole[:, width : width + 2 * RANK].astype(BF)
        c = whole[:, :width] + mm(dh, jnp.concatenate([own_rows(ag, v), own_rows(au, v)], axis=0))
        d_mid = cot_ref[s].astype(F32) + norm_back(mid_ref[s], gain, c)
        dmid_ref[s] = d_mid
        here = slice(s * rows, (s + 1) * rows)
        branch_s[here, :] = d_mid.astype(BF)
        dho = (mm_nt(branch_s[here, :], own_rows(bo, v)) * 2.0).astype(BF)
        hidden_s[here, :] = mm(dho, own_rows(ao, v))
        wide = jnp.concatenate([dh, dho, hout_ref[s][:, :RANK] * 2, jnp.zeros((rows, 128 - 4 * RANK), BF)], axis=1)
        t = jnp.transpose(wide.astype(F32)).astype(BF)
        blocks.append(
            jnp.concatenate(
                [
                    mm_nt(t[2 * RANK : 3 * RANK], attn_ref[s]),
                    mm(t[:RANK], n2_ref[s, :, mine]),
                    mm(t[RANK : 2 * RANK], n2_ref[s, :, mine]),
                    mm(t[3 * RANK : 4 * RANK], branch_s[here, mine]),
                ],
                axis=1,
            )
        )
    grads_ref[...] = rank_halves(blocks).astype(BF)
    for p in range(sequences // 2):
        d_attn = mm_nt(branch_s[2 * p * rows : 2 * (p + 1) * rows, :], wo[...]) + hidden_s[2 * p * rows : 2 * (p + 1) * rows, :]
        for i in (0, 1):
            dattn_ref[2 * p + i] = jnp.transpose(d_attn[i * rows : (i + 1) * rows]).astype(BF)


def turn_back(variant, mid, n2, cot, back, back_x, hout, attn, gain, ag, au, bo, ao, wo):
    sequences, rows, width = mid.shape
    inner = wo.shape[0]
    return pl.pallas_call(
        turn_back_kernel,
        out_shape=(
            shape(mid.shape, F32), shape((sequences, inner, rows), BF),
            shape((sequences * RANK, inner + 3 * (width // 2)), BF),
        ),
        in_specs=[SMEM] + [VM] * 13,
        out_specs=(VM,) * 3,
        scratch_shapes=[pltpu.VMEM((sequences * rows, width), BF), pltpu.VMEM((sequences * rows, inner), F32)],
        compiler_params=BIG,
        cost_estimate=cost(sequences * rows, width, inner, 1, 20 * sequences * rows * width),
        name="turn_back",
    )(variant, mid, n2, cot, back, back_x, hout, attn, gain, ag, au, bo, ao, wo)


def result_kernel(variant, mid_ref, down_ref, down_x_ref, cot_ref, bd, out_ref, grads_ref):
    sequences, rows, width = mid_ref.shape
    mine = pl.ds(pl.multiple_of(lax.axis_index("tp") * (width // 2), width // 2), width // 2)
    blocks = []
    for s in range(sequences):
        v = variant[s]
        whole = down_ref[s].astype(F32) + down_x_ref[s].astype(F32)
        h = whole[:, width : width + RANK].astype(BF) * 2
        out_ref[s] = (mid_ref[s] + (whole[:, :width] + mm(h, own_rows(bd, v)))).astype(BF)
        t = jnp.transpose(jnp.concatenate([h, jnp.zeros((rows, 128 - RANK), BF)], axis=1).astype(F32)).astype(BF)
        blocks.append(mm(t[:RANK], cot_ref[s, :, mine]))
    grads_ref[...] = rank_halves(blocks).astype(BF)


def result(variant, mid, down, down_x, cot, bd):
    sequences, rows, width = mid.shape
    return pl.pallas_call(
        result_kernel,
        out_shape=(shape(mid.shape, BF), shape((sequences * RANK, width // 2), BF)),
        in_specs=[SMEM] + [VM] * 5,
        out_specs=(VM,) * 2,
        compiler_params=BIG,
        cost_estimate=cost(sequences * rows, width, 16, 2, 12 * sequences * rows * width),
        name="block_result",
    )(variant, mid, down, down_x, cot, bd)


TILE = 512
BLOCKS = TILE // 128
SUB = 512
SCALE = HEAD_DIM**-0.5


def document_starts(seg_ref, seq, seg_rows, starts):
    sequences, length = seg_ref.shape
    blocks = length // 128
    number = lax.broadcasted_iota(jnp.int32, (sequences, length), 0)
    row = jnp.sum(jnp.where(number == seq, seg_ref[...], 0), axis=0, keepdims=True).astype(F32)
    for b in range(blocks):
        seg_rows[b] = row[:, b * 128 : (b + 1) * 128]
        starts[b] = jnp.zeros((1, 128), jnp.int32)

    def keys(j, _):
        k = jnp.transpose(jnp.broadcast_to(seg_rows[j], (128, 128)))

        def queries(i, _):
            earlier = jnp.where(k < jnp.broadcast_to(seg_rows[i], (128, 128)), 1.0, 0.0)
            starts[i] += jnp.sum(earlier, axis=0, keepdims=True).astype(jnp.int32)
            return 0

        return lax.fori_loop(j, blocks, queries, 0)

    lax.fori_loop(0, blocks, keys, 0)


def query_rows(starts, tile, stride, part):
    lanes = lax.broadcasted_iota(jnp.int32, (1, 128), 1)
    blocks = [(BLOCKS * tile + b) * stride + part for b in range(BLOCKS)]
    position = jnp.concatenate([b * 128 + lanes for b in blocks], axis=1)
    return position, jnp.concatenate([starts[b] for b in blocks], axis=1)


def key_range(tile, stride, part):
    return BLOCKS * tile * stride // BLOCKS + part // BLOCKS, ((BLOCKS * tile + BLOCKS - 1) * stride + part) // BLOCKS + 1


def keep_pairs(p, first, start, position, causal):
    key = lax.broadcasted_iota(jnp.int32, p.shape, 0)
    keep = key >= jnp.broadcast_to(start - first, p.shape)
    if causal:
        keep = keep & (key <= jnp.broadcast_to(position - first, p.shape))
    return jnp.where(keep, p, 0.0)


def across_blocks(ref, tile, rows):
    return jnp.concatenate([ref[BLOCKS * tile + b, rows, :] for b in range(BLOCKS)], axis=1)


def load_keys(kv_ref, kb, vt):
    def load(j, _):
        for b in range(BLOCKS):
            kb[j, b * 128 : (b + 1) * 128, :] = jnp.transpose(kv_ref[BLOCKS * j + b, :HEAD_DIM, :])
            vt[j, :HEAD_DIM, b * 128 : (b + 1) * 128] = kv_ref[BLOCKS * j + b, HEAD_DIM:, :]
        vt[j, HEAD_DIM:, :] = jnp.ones((16, TILE), BF)
        return 0

    lax.fori_loop(0, kv_ref.shape[0] // BLOCKS, load, 0)


def head_forward(h, stride, part, q_ref, starts, kb, vt, acc, of_ref, lse_ref, done):
    rows = pl.ds(h * HEAD_DIM, HEAD_DIM)

    def q_step(i, _):
        position, start = query_rows(starts, i, stride, part)
        qt = across_blocks(q_ref, i, rows)
        acc[...] = jnp.zeros_like(acc)

        def k_step(causal, j, _):
            total = acc[...]
            for c in range(TILE // SUB):
                keys = slice(c * SUB, (c + 1) * SUB)
                p = jnp.exp2(mm(kb[j, keys, :], qt) * (LOG2E * SCALE))
                p = keep_pairs(p, j * TILE + c * SUB, start, position, causal)
                total = total + mm(vt[j, :, keys], p.astype(BF))
            acc[...] = total
            return 0

        whole, end = key_range(i, stride, part)
        lax.fori_loop(0, whole, functools.partial(k_step, False), 0)
        lax.fori_loop(whole, end, functools.partial(k_step, True), 0)
        total = acc[HEAD_DIM : HEAD_DIM + 1, :]
        lse_ref[h, i] = jnp.broadcast_to(jnp.log2(total), (8, TILE))
        out = acc[:HEAD_DIM, :] / total
        for b in range(BLOCKS):
            of_ref[BLOCKS * i + b, rows, :] = out[:, b * 128 : (b + 1) * 128]
        done(i, out.astype(BF))
        return 0

    lax.fori_loop(0, q_ref.shape[0] // BLOCKS, q_step, 0)


def pair_backward(h, i, j, causal, stride, part, qt, q3, dot_t, do3, lse_ref, delta, starts, kb, vb, kt, dqt, dk, dv):
    position, start = query_rows(starts, i, stride, part)
    dq = dqt[h, i]
    for c in range(TILE // SUB):
        keys = slice(c * SUB, (c + 1) * SUB)
        p = jnp.exp2(mm(kb[j, keys, :], qt[h, i]) * (LOG2E * SCALE) - lse_ref[h, i, 0:1, :])
        p = keep_pairs(p, j * TILE + c * SUB, start, position, causal)
        dp = mm(vb[j, keys, :], dot_t[h, i])
        ds = (p * (dp - delta[h, i, 0:1, :])).astype(BF)
        dv[j, keys, :] += mm(p.astype(BF), do3[h, i])
        dk[j, keys, :] += mm(ds, q3[h, i])
        dq = dq + mm(kt[j, :, keys], ds)
    dqt[h, i] = dq


def head_rows(h):
    return pl.ds(h * HEAD_DIM, HEAD_DIM)


def loop(low, high, step):
    def body(k, _):
        step(k)
        return 0

    lax.fori_loop(low, high, body, 0)


def class_copy(count, parts, source, target, send, recv):
    def make(index, sender):
        return remote(
            source(index), target(sender), send.at[index], recv.at[sender],
            {"ctx": index * parts + lax.rem(lax.axis_index("ctx"), parts)},
        )

    return make


def attend_kernel(
    count, parts, units_per_seq, seg_ref, q_ref, kv_ref,
    q_all, kv_all, of_ref, lse_ref, starts, home, home_x,
    q_in, kv_in, o_buf, kb, vt, acc, seg_rows,
    kv_send, kv_recv, q_send, q_recv, o_send, o_recv, x_send, x_recv, own_sems, out_sems,
):
    me = lax.axis_index("ctx")
    units = count // parts
    unit, part = me // parts, lax.rem(me, parts)
    group = q_ref.shape[1] // HEAD_DIM
    across = {"tp": 1 - lax.axis_index("tp")}
    barrier = pltpu.get_barrier_semaphore()
    pl.semaphore_signal(barrier, inc=1, device_id=across, device_id_type=MESH)
    loop(
        1, count,
        lambda k: pl.semaphore_signal(barrier, inc=1, device_id={"ctx": lax.rem(me + k, count)}, device_id_type=MESH),
    )
    own = [pltpu.make_async_copy(kv_ref.at[unit], kv_in.at[me], own_sems.at[0])]
    own.append(pltpu.make_async_copy(q_ref.at[unit], q_in.at[unit], own_sems.at[1]))
    for c in own:
        c.start()
    pl.semaphore_wait(barrier, count)

    def kv_copy(device, sender):
        return remote(
            kv_ref.at[device // parts], kv_in.at[sender], kv_send.at[device], kv_recv.at[sender], {"ctx": device}
        )

    q_copy = [
        class_copy(
            count, parts, lambda i, h=h: q_ref.at[i, head_rows(h), :], lambda i, h=h: q_in.at[i, head_rows(h), :],
            q_send.at[h], q_recv.at[h],
        )
        for h in range(group)
    ]
    o_copy = [
        class_copy(
            count, parts, lambda i, h=h: o_buf.at[h, i], lambda i, h=h: home.at[i, head_rows(h), :],
            o_send.at[h], o_recv.at[h],
        )
        for h in range(group)
    ]

    def x_copy(h, i):
        place = (i, head_rows(h), slice(None))
        return remote(home.at[place], home_x.at[place], x_send.at[h, i], x_recv.at[h, i], across)

    def turn_of(k):
        return lax.rem(unit + k, units)

    loop(1, count, lambda k: kv_copy(lax.rem(me + k, count), me).start())
    for h in range(group):
        loop(1, units, lambda k, h=h: q_copy[h](turn_of(k), unit).start())
    document_starts(seg_ref, unit // units_per_seq, seg_rows, starts)
    for c in own:
        c.wait()
    loop(1, count, lambda k: kv_copy(me, lax.rem(me + k, count)).wait_recv())
    load_keys(kv_in, kb, vt)
    saves = [pltpu.make_async_copy(kv_in, kv_all, out_sems.at[0])]
    saves[0].start()

    def keep_own(h):
        return pltpu.make_async_copy(o_buf.at[h, unit], home.at[unit, head_rows(h), :], own_sems.at[2 + h])

    def pass_on(h):
        keep_own(h).wait()
        x_copy(h, unit).start()

        def relay(k):
            other = turn_of(units - k)
            o_copy[h](unit, other).wait_recv()
            x_copy(h, other).start()

        loop(1, units, relay)

    for h in range(group):
        loop(1, units, lambda k, h=h: q_copy[h](unit, turn_of(k)).wait_recv())
        if h == group - 1:
            saves.append(pltpu.make_async_copy(q_in, q_all, out_sems.at[1]))
            saves[1].start()

        def done(i, out, h=h):
            for b in range(BLOCKS):
                block = BLOCKS * i + b
                o_buf[h, block] = out[:, b * 128 : (b + 1) * 128]

                @pl.when(block == unit)
                def _():
                    keep_own(h).start()

                @pl.when(block != unit)
                def _():
                    o_copy[h](block, unit).start()

        head_forward(h, parts, part, q_in, starts, kb, vt, acc, of_ref, lse_ref, done)
        if h > 0:
            pass_on(h - 1)
    pass_on(group - 1)
    for c in saves:
        c.wait()
    loop(1, count, lambda k: kv_copy(lax.rem(me + k, count), me).wait_send())
    for h in range(group):

        def finish_block(k, h=h):
            q_copy[h](turn_of(k), unit).wait_send()
            o_copy[h](turn_of(k), unit).wait_send()

        loop(1, units, finish_block)

        def finish_across(i, h=h):
            x_copy(h, i).wait_send()
            x_copy(h, i).wait_recv()

        loop(0, units, finish_across)


def attend(segs, q, kv, count, parts, units_per_seq, collective_id):
    units, qrows, _ = q.shape
    group, tiles, ktiles = qrows // HEAD_DIM, units // BLOCKS, count // BLOCKS
    dma, vm = pltpu.SemaphoreType.DMA, pltpu.VMEM
    kv_shape = (count,) + kv.shape[1:]
    return pl.pallas_call(
        functools.partial(attend_kernel, count, parts, units_per_seq),
        out_shape=(
            shape(q.shape, BF), shape(kv_shape, BF), shape(q.shape, F32), shape((group, tiles, 8, TILE), F32),
            shape((count, 1, 128), jnp.int32), shape(q.shape, BF), shape(q.shape, BF),
        ),
        in_specs=[VM, ANYWHERE, ANYWHERE],
        out_specs=(ANYWHERE, ANYWHERE, VM, VM, VM, ANYWHERE, ANYWHERE),
        scratch_shapes=[
            vm(q.shape, BF), vm(kv_shape, BF), vm((group, units, HEAD_DIM, 128), BF), vm((ktiles, TILE, HEAD_DIM), BF),
            vm((ktiles, HEAD_DIM + 16, TILE), BF), vm((HEAD_DIM + 16, TILE), F32), vm((count, 1, 128), F32),
            dma((count,)), dma((count,)),
        ]
        + [dma((group, units))] * 6 + [dma((2 + group,)), dma((2,))],
        compiler_params=pltpu.CompilerParams(
            collective_id=collective_id, has_side_effects=True, vmem_limit_bytes=60 * 2**20
        ),
        name="attend",
    )(segs, q, kv)


def attend_back_kernel(
    count, parts, do_ref, q_all, kv_all, of_ref, lse_ref, starts, dq_home, dkv_home,
    do_in, dq_buf, dkv_buf, kb, vb, kt, qt, q3, dot_t, do3, delta, dqt, dk, dv,
    do_send, do_recv, dq_send, dq_recv, dkv_send, dkv_recv, own_sems,
):
    me = lax.axis_index("ctx")
    units = count // parts
    unit, part = me // parts, lax.rem(me, parts)
    group, tiles, ktiles = q_all.shape[1] // HEAD_DIM, units // BLOCKS, count // BLOCKS
    barrier = pltpu.get_barrier_semaphore()
    loop(
        1, count,
        lambda k: pl.semaphore_signal(barrier, inc=1, device_id={"ctx": lax.rem(me + k, count)}, device_id_type=MESH),
    )
    own_do = pltpu.make_async_copy(do_ref.at[unit], do_in.at[unit], own_sems.at[0])
    own_do.start()
    pl.semaphore_wait(barrier, count - 1)

    def turn_of(k):
        return lax.rem(unit + k, units)

    do_copy = [
        class_copy(
            count, parts, lambda i, h=h: do_ref.at[i, head_rows(h), :], lambda i, h=h: do_in.at[i, head_rows(h), :],
            do_send.at[h], do_recv.at[h],
        )
        for h in range(group)
    ]
    dq_copy = [
        class_copy(
            count, parts, lambda i, h=h: dq_buf.at[h, i], lambda i, h=h: dq_home.at[i, head_rows(h), :],
            dq_send.at[h], dq_recv.at[h],
        )
        for h in range(group)
    ]

    def dkv_copy(device, sender):
        return remote(dkv_buf.at[device], dkv_home.at[sender], dkv_send.at[device], dkv_recv.at[sender], {"ctx": device})

    own_dkv = pltpu.make_async_copy(dkv_buf.at[me], dkv_home.at[me], own_sems.at[1])

    def own_dq(h):
        return pltpu.make_async_copy(dq_buf.at[h, unit], dq_home.at[unit, head_rows(h), :], own_sems.at[2 + h])

    for h in range(group):
        loop(1, units, lambda k, h=h: do_copy[h](turn_of(k), unit).start())

    def load_kv(j):
        for b in range(BLOCKS):
            lanes = slice(b * 128, (b + 1) * 128)
            kt[j, :, lanes] = kv_all[BLOCKS * j + b, :HEAD_DIM, :]
            kb[j, lanes, :] = jnp.transpose(kv_all[BLOCKS * j + b, :HEAD_DIM, :])
            vb[j, lanes, :] = jnp.transpose(kv_all[BLOCKS * j + b, HEAD_DIM:, :])

    def load_q(i):
        for h in range(group):
            for b in range(BLOCKS):
                lanes = slice(b * 128, (b + 1) * 128)
                q = q_all[BLOCKS * i + b, h * HEAD_DIM : (h + 1) * HEAD_DIM, :]
                qt[h, i, :, lanes] = q
                q3[h, i, lanes, :] = jnp.transpose(q)
            dqt[h, i] = jnp.zeros((HEAD_DIM, TILE), F32)

    def load_do(h, i):
        rows = slice(h * HEAD_DIM, (h + 1) * HEAD_DIM)
        for b in range(BLOCKS):
            lanes = slice(b * 128, (b + 1) * 128)
            g = do_in[BLOCKS * i + b, rows, :]
            dot_t[h, i, :, lanes] = g
            do3[h, i, lanes, :] = jnp.transpose(g)
            d = jnp.sum(g.astype(F32) * of_ref[BLOCKS * i + b, rows, :], axis=0, keepdims=True)
            delta[h, i, :, lanes] = jnp.broadcast_to(d, (8, 128))

    loop(0, ktiles, load_kv)
    loop(0, tiles, load_q)

    def last_tile(i):
        return key_range(i, parts, part)[1] - 1

    def run(h, j):
        low = jnp.maximum(BLOCKS * j - part + parts - 1, 0) // (BLOCKS * parts)
        full = jnp.minimum((BLOCKS * (j + 1) - part + BLOCKS * parts - 1) // (BLOCKS * parts), tiles)

        def pair(causal, i):
            pair_backward(
                h, i, j, causal, parts, part, qt, q3, dot_t, do3, lse_ref, delta, starts, kb, vb, kt, dqt, dk, dv
            )

        loop(low, full, functools.partial(pair, True))
        loop(full, tiles, functools.partial(pair, False))

    def emit_keys(j):
        for b in range(BLOCKS):
            rows = slice(b * 128, (b + 1) * 128)
            block = BLOCKS * j + b
            dkv_buf[block, :HEAD_DIM, :] = jnp.transpose(dk[j, rows, :] * SCALE).astype(BF)
            dkv_buf[block, HEAD_DIM:, :] = jnp.transpose(dv[j, rows, :]).astype(BF)

            @pl.when(block == me)
            def _():
                own_dkv.start()

            @pl.when(block != me)
            def _():
                dkv_copy(block, me).start()

    def emit_queries(h, j, i):
        @pl.when(last_tile(i) == j)
        def _():
            for b in range(BLOCKS):
                block = BLOCKS * i + b
                dq_buf[h, block] = (dqt[h, i, :, b * 128 : (b + 1) * 128] * SCALE).astype(BF)

                @pl.when(block == unit)
                def _():
                    own_dq(h).start()

                @pl.when(block != unit)
                def _():
                    dq_copy[h](block, unit).start()

    dk[...] = jnp.zeros_like(dk)
    dv[...] = jnp.zeros_like(dv)
    own_do.wait()
    for h in range(group):
        loop(1, units, lambda k, h=h: do_copy[h](unit, turn_of(k)).wait_recv())
        loop(0, tiles, functools.partial(load_do, h))

        def key_step(j, h=h):
            run(h, j)
            if h == group - 1:
                emit_keys(j)
            loop(0, tiles, functools.partial(emit_queries, h, j))

        loop(0, ktiles, key_step)
    for h in range(group):
        own_dq(h).wait()
    own_dkv.wait()

    def finish_full(k):
        other = lax.rem(me + k, count)
        dkv_copy(other, me).wait_send()
        dkv_copy(me, other).wait_recv()

    loop(1, count, finish_full)

    def finish_class(k):
        other = turn_of(k)
        for h in range(group):
            do_copy[h](other, unit).wait_send()
            dq_copy[h](other, unit).wait_send()
            dq_copy[h](unit, other).wait_recv()

    loop(1, units, finish_class)


def attend_back(do, q, kv, of, lse, starts, count, parts, collective_id):
    units, qrows, _ = q.shape
    group, tiles, ktiles = qrows // HEAD_DIM, units // BLOCKS, count // BLOCKS
    dma, vm = pltpu.SemaphoreType.DMA, pltpu.VMEM
    return pl.pallas_call(
        functools.partial(attend_back_kernel, count, parts),
        out_shape=(shape(q.shape, BF), shape(kv.shape, BF)),
        in_specs=[ANYWHERE] + [VM] * 5,
        out_specs=(ANYWHERE, ANYWHERE),
        scratch_shapes=[vm(q.shape, BF), vm((group, units, HEAD_DIM, 128), BF), vm(kv.shape, BF)]
        + [vm((ktiles, TILE, HEAD_DIM), BF)] * 2 + [vm((ktiles, HEAD_DIM, TILE), BF)]
        + [vm((group, tiles, HEAD_DIM, TILE), BF), vm((group, tiles, TILE, HEAD_DIM), BF)] * 2
        + [vm((group, tiles, 8, TILE), F32), vm((group, tiles, HEAD_DIM, TILE), F32)]
        + [vm((ktiles, TILE, HEAD_DIM), F32)] * 2
        + [dma((group, units))] * 4 + [dma((count,))] * 2 + [dma((2 + group,))],
        compiler_params=pltpu.CompilerParams(
            collective_id=collective_id, has_side_effects=True, vmem_limit_bytes=60 * 2**20
        ),
        name="attend_back",
    )(do, q, kv, of, lse, starts)


def finish_kernel(reduce, count, widths, shared, *refs):
    refs = list(refs)
    take = lambda n: [refs.pop(0) for _ in range(n)]
    dq_ref, dkv_ref, pre_ref, h_ref, gains, cos_ref, sin_ref, gain_ref, bc_ref, pick_ref = take(10)
    far = take(7)
    grads = take(3) if reduce else []
    (out_ref,) = take(1)
    gout = take(4) if reduce else take(1)
    x, d_mid, n1, wq, wk, wv, ac = near = take(7)
    d_n, gb, dh_own, dh_other, dh_sum, sbuf, rbuf, gq = take(8)
    near_sems, dh_send, dh_recv, xsend, xrecv = take(5)
    sequences, inner, rows = dq_ref.shape
    width = out_ref.shape[2]
    kw = wk.shape[1]
    half_rows = sequences * RANK // 2
    me = lax.axis_index("ctx")
    across = {"tp": 1 - lax.axis_index("tp")}
    mine = pl.ds(pl.multiple_of(lax.axis_index("tp") * (width // 2), width // 2), width // 2)

    loads = [pltpu.make_async_copy(f, n, near_sems.at[i]) for i, (f, n) in enumerate(zip(far, near))]
    barrier = pltpu.get_barrier_semaphore()
    pl.semaphore_signal(barrier, inc=1, device_id=across, device_id_type=MESH)
    peers = 1
    if reduce:
        planes, plane_ins, fin_outs, fin_ins = take(2), take(2), take(2), take(2)
        own, core_in = take(2)
        own_sems, core_send, core_recv = take(3)
        plane_send, plane_recv, fin_send, fin_recv = take(4)
        (last_sems,) = take(1)
        chips = count // 2
        chip, core = me // 2, lax.rem(me, 2)
        twin = {"ctx": 2 * chip + 1 - core}
        pl.semaphore_signal(barrier, inc=1, device_id=twin, device_id_type=MESH)

        def at_chip(k):
            return lax.rem(chip + k, chips)

        def greet(k, _):
            pl.semaphore_signal(barrier, inc=1, device_id={"ctx": 2 * at_chip(k) + core}, device_id_type=MESH)
            return 0

        lax.fori_loop(1, chips, greet, 0)
        peers += chips

        def part_of(ref, who):
            size = ref.shape[0] // 2
            return ref.at[pl.ds(pl.multiple_of(who * size, 16), size), :]

        known, w_qkv = sum(widths[:3]), widths[3]
        own_loads, to_twin, at = [], [], 0
        for i, ref in enumerate(grads):
            place = slice(at, at + widths[i])
            at += widths[i]
            own_loads.append(pltpu.make_async_copy(part_of(ref, core), own.at[:, place], own_sems.at[i]))
            to_twin.append(
                remote(part_of(ref, 1 - core), core_in.at[:, place], core_send.at[i], core_recv.at[i], twin)
            )
        to_twin.append(remote(gq.at[1 - core], core_in.at[:, known : known + w_qkv], core_send.at[3], core_recv.at[3], twin))
        for c in own_loads:
            c.start()
    for i in (3, 4, 5, 2, 6, 0, 1):
        loads[i].start()
    pl.semaphore_wait(barrier, peers)
    if reduce:
        for c in to_twin[:3]:
            c.start()

    cosine, sine = cos_ref[...], sin_ref[...]
    heads_k = kw // HEAD_DIM
    cuts = (slice(0, inner), slice(inner, inner + kw), slice(inner + kw, inner + 2 * kw))

    def prepare_back(pre, gains, c):
        u = pre.reshape(pre.shape[0] // HEAD_DIM, HEAD_DIM, rows)
        scale = lax.rsqrt(jnp.mean(u * u, axis=1, keepdims=True) + EPSILON)
        y = u * scale
        w = turn(c.reshape(u.shape).astype(F32), cosine, -sine) * gains
        return (scale * (w - y * jnp.mean(w * y, axis=1, keepdims=True))).reshape(pre.shape)

    def first_step(s):
        dkv = dkv_ref[s * heads_k : (s + 1) * heads_k].astype(F32)
        dkv = jnp.sum(dkv, axis=1).astype(BF) if dkv.shape[1] > 1 else dkv[:, 0].astype(BF)
        d_q = prepare_back(pre_ref[s, :inner, :], gains[0], dq_ref[s])
        d_k = prepare_back(pre_ref[s, inner:, :], gains[1], dkv[:, :HEAD_DIM, :].reshape(kw, rows))
        d_v = dkv[:, HEAD_DIM:, :].reshape(kw, rows).astype(F32)
        d = jnp.transpose(jnp.concatenate([d_q, d_k, d_v], axis=0)).astype(BF)
        d_n[s] = d
        dh = [mm_nt(d[:, c], bc_ref[s, :, c]) * 2.0 for c in cuts]
        dh_own[s] = jnp.concatenate(dh + [jnp.zeros((rows, 128 - 3 * RANK), F32)], axis=1).astype(BF)
        t = (jnp.transpose(h_ref[s].astype(F32)) * 2.0).astype(BF)
        gb[s] = jnp.concatenate([mm(t[i * RANK : (i + 1) * RANK], d[:, c]) for i, c in enumerate(cuts)], axis=1)

    def part_copy(s):
        return remote(sbuf.at[s], rbuf.at[s], xsend.at[s], xrecv.at[s], across)

    dh_copies = []

    def send_pair(p):
        pair = pl.ds(2 * p, 2)
        first_step(2 * p)
        first_step(2 * p + 1)
        dh_copies.append(remote(dh_own.at[pair], dh_other.at[pair], dh_send.at[p], dh_recv.at[p], across))
        dh_copies[-1].start()
        if p == 0:
            for i in (3, 4, 5):
                loads[i].wait()
        d = jnp.concatenate([d_n[2 * p], d_n[2 * p + 1]], axis=0)
        part = mm_nt(d[:, cuts[0]], wq[...]) + mm_nt(d[:, cuts[1]], wk[...]) + mm_nt(d[:, cuts[2]], wv[...])
        for i in (0, 1):
            sbuf[2 * p + i] = part[i * rows : (i + 1) * rows].astype(BF)
            part_copy(2 * p + i).start()

    def plane_copy(g, k, slot):
        chunk = planes[g].shape[1] // chips
        return remote(
            planes[g].at[:, pl.ds(pl.multiple_of(k * chunk, 128), chunk)], plane_ins[g].at[slot],
            plane_send.at[g, k], plane_recv.at[g, slot], {"ctx": 2 * k + core},
        )

    def fin_copy(g, k, slot):
        return remote(
            fin_outs[g].at[k], fin_ins[g].at[slot], fin_send.at[g, k], fin_recv.at[g, slot], {"ctx": 2 * k + core}
        )

    def each_chip(step):
        def body(k, _):
            step(at_chip(k))
            return 0

        lax.fori_loop(1, chips, body, 0)

    def to_plane(g):
        chunk = planes[g].shape[1] // chips
        each_chip(lambda k: plane_copy(g, k, chip).start())
        plane_ins[g][chip] = planes[g][:, pl.ds(pl.multiple_of(chip * chunk, 128), chunk)]

    def to_owners(g):
        each_chip(lambda k: plane_copy(g, k, k).wait_recv())
        total = plane_ins[g][0].astype(F32)
        for k in range(1, chips):
            total = total + plane_ins[g][k].astype(F32)
        chunk, per = total.shape[1], RANK // 2
        for k in range(chips):
            row = jnp.zeros((per, chunk), F32)
            for s in range(sequences):
                row = row + total[s * per : (s + 1) * per] * pick_ref[k, s][:, :1]
            fin_outs[g][k] = jnp.concatenate([row[:, : chunk // 2], row[:, chunk // 2 :]], axis=0).astype(BF)
        each_chip(lambda k: fin_copy(g, k, chip).start())
        fin_ins[g][chip] = fin_outs[g][chip]

    def rows_in(g):
        each_chip(lambda k: fin_copy(g, k, k).wait_recv())
        rows_ref, per = gout[g], RANK // 2
        chunk = rows_ref.shape[1] // chips
        for k in range(chips):
            block = fin_ins[g][k].astype(F32)
            rows_ref[:, k * chunk : k * chunk + chunk // 2] = block[:per]
            rows_ref[:, k * chunk + chunk // 2 : (k + 1) * chunk] = block[per:]
        copy = remote(
            rows_ref.at[:, shared[g][0] : shared[g][1]], gout[2 + g], last_sems.at[g], last_sems.at[2 + g], across
        )
        copy.start()
        return copy

    def last_step(s):
        part_copy(s).wait_recv()
        c = sbuf[s].astype(F32) + rbuf[s].astype(F32) + mm(dh_sum[s][:, : 3 * RANK], ac[s])
        out_ref[s] = (d_mid[s] + norm_back(x[s].astype(F32), gain_ref[...][None, :], c)).astype(BF)

    pairs = sequences // 2
    send_pair(0)
    if reduce:
        for c in own_loads:
            c.wait()
        for c in to_twin[:3]:
            c.wait_recv()
        planes[0][:, :known] = (own[...].astype(F32) + core_in[:, :known].astype(F32)).astype(BF)
        if planes[0].shape[1] > known:
            planes[0][:, known:] = jnp.zeros((half_rows, planes[0].shape[1] - known), BF)
        to_plane(0)
    for p in range(1, pairs):
        send_pair(p)
    loads[2].wait()
    blocks = []
    for s in range(sequences):
        if s % 2 == 0:
            dh_copies[s // 2].wait_recv()
        dh = (dh_own[s].astype(F32) + dh_other[s].astype(F32)).astype(BF)
        dh_sum[s] = dh
        t = jnp.transpose(dh.astype(F32)).astype(BF)
        wide = mm(t[: 3 * RANK], n1[s, :, mine])
        blocks.append(jnp.concatenate([wide[i * RANK : (i + 1) * RANK] for i in range(3)] + [gb[s]], axis=1))
    everything = rank_halves(blocks)
    for b in (0, 1):
        gq[b] = everything[b * half_rows : (b + 1) * half_rows].astype(BF)
    if reduce:
        to_twin[3].start()
    for i in (6, 0, 1):
        loads[i].wait()
    if reduce:
        to_owners(0)
        to_twin[3].wait_recv()
        planes[1][:, :w_qkv] = (gq[core].astype(F32) + core_in[:, known : known + w_qkv].astype(F32)).astype(BF)
        if planes[1].shape[1] > w_qkv:
            planes[1][:, w_qkv:] = jnp.zeros((half_rows, planes[1].shape[1] - w_qkv), BF)
        to_plane(1)
        last_step(0)
        to_owners(1)
        shared_copies = [rows_in(0)]
        last_step(1)
        shared_copies.append(rows_in(1))
        for s in range(2, sequences):
            last_step(s)
        for c in shared_copies:
            c.wait()
        for c in to_twin:
            c.wait_send()
        for g in (0, 1):
            each_chip(lambda k, g=g: plane_copy(g, k, chip).wait_send())
            each_chip(lambda k, g=g: fin_copy(g, k, chip).wait_send())
    else:
        for s in range(sequences):
            last_step(s)
        gout[0][...] = gq[...]
    for c in dh_copies:
        c.wait_send()
    for s in range(sequences):
        part_copy(s).wait_send()


def finish(reduce, count, dq, dkv, pre, h, gains, tables, gain, bc, pick, x, d_mid, n1, weights, ac, grads, shared, collective_id):
    sequences, rows, width = x.shape
    inner, kw = weights[0].shape[1], weights[1].shape[1]
    w_qkv = 3 * (width // 2) + inner + 2 * kw
    half_rows = sequences * RANK // 2
    dma = pltpu.SemaphoreType.DMA
    far = (x, d_mid, n1) + tuple(weights) + (ac,)
    widths = ()
    gshape = (shape((2, half_rows, w_qkv), BF),)
    scratch = [pltpu.VMEM(a.shape, a.dtype) for a in far]
    scratch += [
        pltpu.VMEM((sequences, rows, inner + 2 * kw), BF),
        pltpu.VMEM((sequences, RANK, inner + 2 * kw), F32),
        pltpu.VMEM((sequences, rows, 128), BF),
        pltpu.VMEM((sequences, rows, 128), BF),
        pltpu.VMEM((sequences, rows, 128), BF),
        pltpu.VMEM(x.shape, BF),
        pltpu.VMEM(x.shape, BF),
        pltpu.VMEM((2, half_rows, w_qkv), BF),
        dma((7,)), dma((sequences // 2,)), dma((sequences // 2,)), dma((sequences,)), dma((sequences,)),
    ]
    extra = ()
    if reduce:
        chips = count // 2
        widths = tuple(g.shape[1] for g in grads) + (w_qkv,)
        padded = [-(-n // (256 * chips)) * 256 * chips for n in (sum(widths[:3]), w_qkv)]
        gshape = tuple(shape((RANK // 2, n), F32) for n in padded)
        gshape += tuple(shape((RANK // 2, b - a), F32) for a, b in shared)
        scratch += [pltpu.VMEM((half_rows, n), BF) for n in padded]
        scratch += [pltpu.VMEM((chips, half_rows, n // chips), BF) for n in padded]
        scratch += [pltpu.VMEM((chips, RANK, n // chips // 2), BF) for n in padded] * 2
        scratch += [
            pltpu.VMEM((half_rows, sum(widths[:3])), BF),
            pltpu.VMEM((half_rows, sum(widths)), BF),
            dma((3,)), dma((4,)), dma((4,)),
        ]
        scratch += [dma((2, chips))] * 4 + [dma((4,))]
        extra = tuple(grads)
    return pl.pallas_call(
        functools.partial(finish_kernel, reduce, count, widths, shared),
        out_shape=(shape(x.shape, BF),) + gshape,
        in_specs=[VM] * 10 + [ANYWHERE] * (7 + len(extra)),
        out_specs=(VM,) * (1 + len(gshape)),
        scratch_shapes=scratch,
        compiler_params=pltpu.CompilerParams(
            collective_id=collective_id, has_side_effects=True, vmem_limit_bytes=60 * 2**20
        ),
        name="finish",
    )(dq, dkv, pre, h, gains, *tables, gain, bc, pick, *far, *extra)


def unpack_kernel(hidden_units, tile, inner, kw, first, second, first_x, second_x, *outs):
    ga_query, gb_query, ga_key, gb_key, ga_value, gb_value, ga_out, gb_out, ga_gate, gb_gate, ga_up, gb_up, ga_down, gb_down = outs
    width = ga_query.shape[1]
    w = width // 2
    lower = lax.axis_index("tp") == 0
    for f in range(hidden_units // tile):
        for n, out in enumerate((gb_gate, gb_up, ga_down)):
            out[:, f * tile : (f + 1) * tile] = first[:, (3 * f + n) * tile : (3 * f + n + 1) * tile]
    at = 3 * hidden_units
    ga_out[...] = first[:, at : at + inner]

    def join(out, own, own_at, other, i):
        a = own[:, own_at + i * w : own_at + (i + 1) * w]
        b = other[:, i * w : (i + 1) * w]
        out[:, :w] = jnp.where(lower, a, b)
        out[:, w:] = jnp.where(lower, b, a)

    for i, out in enumerate((ga_gate, ga_up, gb_out, gb_down)):
        join(out, first, at + inner, first_x, i)
    for i, out in enumerate((ga_query, ga_key, ga_value)):
        join(out, second, 0, second_x, i)
    at = 3 * w
    gb_query[...] = second[:, at : at + inner]
    gb_key[...] = second[:, at + inner : at + inner + kw]
    gb_value[...] = second[:, at + inner + kw : at + inner + 2 * kw]


def unpack(first, second, first_x, second_x, width, hidden_units, tile, inner, kw):
    sizes = (width, inner, width, kw, width, kw, inner, width, width, hidden_units, width, hidden_units, hidden_units, width)
    return pl.pallas_call(
        functools.partial(unpack_kernel, hidden_units, tile, inner, kw),
        out_shape=tuple(shape((first.shape[0], n), F32) for n in sizes),
        in_specs=[VM] * 4,
        out_specs=(VM,) * 14,
        name="unpack",
    )(first, second, first_x, second_x)


def rotary_tables(positions):
    half = HEAD_DIM // 2
    frequencies = THETA_BASE ** (-jnp.arange(half, dtype=F32) * 2.0 / HEAD_DIM)
    angles = frequencies[:, None] * positions.astype(F32)[None, :]
    return jnp.cos(angles), jnp.sin(angles)


def swap(values):
    return lax.ppermute(values, "tp", [(0, 1), (1, 0)])


def reduce_scatter_rows(grads, count):
    rows, columns = grads.shape
    index = lax.axis_index("ctx")
    held = grads.reshape(count, rows // count, columns)
    bit = 1
    while bit < count:
        mine = (index // bit) % 2
        pairs = held.reshape(held.shape[0] // 2, 2, held.shape[1], columns)
        kept = lax.dynamic_index_in_dim(pairs, mine, 1, keepdims=False)
        sent = lax.dynamic_index_in_dim(pairs, 1 - mine, 1, keepdims=False).astype(BF)
        held = kept.astype(F32) + lax.ppermute(sent, "ctx", [(i, i ^ bit) for i in range(count)]).astype(F32)
        bit *= 2
    return held[0]


def local(
    tokens, output_cotangent, segment_ids, variant, attn_gain, ffn_gain, q_gain, k_gain,
    query_matrix, key_matrix, value_matrix, output_matrix, gate_matrix, up_matrix, down_matrix,
    query_input_factor, query_output_factor, key_input_factor, key_output_factor,
    value_input_factor, value_output_factor, output_input_factor, output_output_factor,
    gate_input_factor, gate_output_factor, up_input_factor, up_output_factor,
    down_input_factor, down_output_factor,
):
    sequences, rows_here, width = tokens.shape
    count = lax.axis_size("ctx")
    index = lax.axis_index("ctx")
    inner, kw = query_matrix.shape[1], key_matrix.shape[1]
    key_heads = kw // HEAD_DIM
    units = sequences * key_heads
    parts = count // units
    stacked = query_input_factor.shape[0]
    reduce_here = stacked // count == RANK // 2
    tables = rotary_tables(index * rows_here + jnp.arange(rows_here, dtype=jnp.int32))
    weights = (query_matrix, key_matrix, value_matrix)
    ins = (query_input_factor, key_input_factor, value_input_factor)
    outs = (query_output_factor, key_output_factor, value_output_factor)

    output_matrix_other = swap(output_matrix)
    output_input_other = swap(output_input_factor)

    n1, h_one, pre, queries, keys_values, ac, bc, gains, pick, *chosen = project(
        variant, tokens, attn_gain, weights, ins, outs, q_gain, k_gain, tables,
        (gate_input_factor, up_input_factor, down_output_factor, gate_output_factor, up_output_factor, down_input_factor),
    )
    *kept, attn, attn_other = attend(segment_ids, queries, keys_values, count, parts, key_heads, 0)
    attn, attn_other = (a.reshape(sequences, inner, rows_here) for a in (attn, attn_other))
    mid, n2, h_out = middle(
        variant, tokens, ffn_gain, attn, attn_other, output_matrix, output_matrix_other,
        output_input_factor, output_input_other, output_output_factor,
    )

    flat = lambda a: a.reshape(sequences * rows_here, -1)
    by_seq = lambda a: a.reshape(sequences, rows_here, -1)
    back, back_other, down, g_ffn = feed(
        2, flat(n2), flat(output_cotangent), *chosen[:3], gate_matrix, up_matrix, down_matrix, *chosen[3:], 3,
    )
    d_mid, d_attn, g_mid = turn_back(
        variant, mid, n2, output_cotangent, by_seq(back), by_seq(back_other), h_out, attn, ffn_gain,
        gate_input_factor, up_input_factor, output_output_factor, output_input_factor, output_matrix,
    )
    d_attn = d_attn.reshape(queries.shape)
    d_attn, down = lax.optimization_barrier((d_attn, down))
    down_other = swap(down)
    dq, dkv = attend_back(d_attn, *kept, count, parts, 1)
    block_result, g_down = result(variant, mid, by_seq(down), by_seq(down_other), output_cotangent, down_output_factor)

    w = width // 2
    hidden_units = gate_matrix.shape[1]
    tile = feed_tile(hidden_units)
    at = 3 * hidden_units + inner
    shared = ((at, at + 4 * w), (0, 3 * w))
    ends = finish(
        reduce_here, count, dq.reshape(sequences, inner, rows_here), dkv.reshape(units, parts, 2 * HEAD_DIM, rows_here),
        pre, h_one, gains, tables, attn_gain, bc, pick, tokens, d_mid, n1, weights, ac,
        (g_ffn, g_mid, g_down), shared, 2,
    )
    if reduce_here:
        owned = ends[1:]
    else:
        per = RANK // 2
        pick = (jnp.arange(stacked // RANK, dtype=jnp.int32)[:, None] == variant[None, :]).astype(F32)
        owned, other = [], []
        for grads, (low, high) in zip((jnp.concatenate([g_ffn, g_mid, g_down], axis=1), ends[1]), shared):
            grads = grads.reshape(2, sequences, per, -1).astype(F32)
            dense = jnp.sum(pick[:, None, :, None, None] * grads[None], axis=2)
            owned.append(reduce_scatter_rows(dense.reshape(stacked, -1), count))
            other.append(swap(owned[-1][:, low:high]))
        owned = owned + other
    return (block_result, ends[0]) + tuple(unpack(*owned, width, hidden_units, tile, inner, kw))


def solution(mesh):
    rows, whole, columns = P(None, "ctx", None), P(), P(None, "tp")
    owned, owned_half = P("ctx", None), P("ctx", "tp")
    return jax.shard_map(
        local,
        mesh=mesh,
        in_specs=(rows, rows) + (whole,) * 6
        + (columns, columns, columns, P("tp", None), columns, columns, P("tp", None))
        + (whole, columns) * 3 + (columns, whole) + (whole, columns) * 2 + (columns, whole),
        out_specs=(
            rows, rows, owned, owned_half, owned, owned_half, owned, owned_half,
            owned_half, owned, owned, owned_half, owned, owned_half, owned_half, owned,
        ),
        check_vma=False,
    )
```

```python
import functools, jax, jax.numpy as jnp
from jax import lax
from jax.experimental import pallas as pl
from jax.experimental.pallas import tpu as pltpu
from jax.sharding import PartitionSpec as P

HEAD_DIM = 64
LOG2E = 1.4426950408889634
MESH = pl.DeviceIdType.MESH
SMEM = pl.BlockSpec(memory_space=pltpu.SMEM)
VM = pl.BlockSpec(memory_space=pltpu.VMEM)
RANK = 16
EPSILON = 1e-05
THETA_BASE = 1000000.0
BF = jnp.bfloat16
F32 = jnp.float32
NT = (((1,), (1,)), ((), ()))
BIG = pltpu.CompilerParams(vmem_limit_bytes=60 * 2**20)


def cost(rows, width, columns, products, moved):
    return pl.CostEstimate(flops=2 * products * rows * width * columns, bytes_accessed=moved, transcendentals=0)

ANYWHERE = pl.BlockSpec(memory_space=pl.ANY)


def mm(a, b):
    return jnp.dot(a, b, preferred_element_type=F32)


def mm_nt(a, b):
    return lax.dot_general(a, b, NT, preferred_element_type=F32)


def shape(dims, kind):
    return jax.ShapeDtypeStruct(dims, kind)


def remote(source, target, send, recv, device):
    return pltpu.make_async_remote_copy(
        src_ref=source, dst_ref=target, send_sem=send, recv_sem=recv, device_id=device, device_id_type=MESH
    )


def own_rows(ref, variant):
    return ref[pl.ds(pl.multiple_of(variant * RANK, RANK), RANK), :]


def norm_back(u, gain, c):
    scale = lax.rsqrt(jnp.mean(u * u, axis=-1, keepdims=True) + EPSILON)
    y = u * scale
    w = c * gain
    return scale * (w - y * jnp.mean(w * y, axis=-1, keepdims=True))


def turn(values, cosine, sine):
    half = HEAD_DIM // 2
    a, b = values[:, :half], values[:, half:]
    return jnp.concatenate([a * cosine - b * sine, b * cosine + a * sine], axis=1)


def rank_halves(blocks):
    return jnp.concatenate([b[: RANK // 2] for b in blocks] + [b[RANK // 2 :] for b in blocks], axis=0)


def column(ref):
    return jnp.transpose(jnp.broadcast_to(ref[...][None, :], (128, ref.shape[0])))


def project_kernel(
    variant, x_ref, gain_ref, wq, wk, wv, aq, ak, av, bq, bk, bv, qg_ref, kg_ref, cos_ref, sin_ref, *refs,
):
    n1_ref, h_ref, pre_ref, q_ref, kv_ref, ac_ref, bc_ref, gains_ref, pick_ref = refs[8:17]
    n1_s, sems = refs[25:]
    step = pl.program_id(0)
    sequences = pick_ref.shape[1]
    rows, width = x_ref.shape[1:]
    qw, kw = wq.shape[1], wk.shape[1]
    heads_q, heads_k = qw // HEAD_DIM, kw // HEAD_DIM
    cosine, sine = cos_ref[...], sin_ref[...]
    qg, kg = column(qg_ref), column(kg_ref)
    gain = gain_ref[...][None, :]
    picks = [
        pltpu.make_async_copy(
            refs[n].at[pl.ds(pl.multiple_of(variant[s] * RANK, RANK), RANK), :],
            refs[17 + n].at[pl.ds(s * RANK, RANK), :], sems.at[n, s],
        )
        for n in range(8)
        for s in range(sequences)
    ]

    @pl.when(step == 0)
    def _():
        for c in picks:
            c.start()
        gains_ref[0], gains_ref[1] = qg, kg
        for v in range(pick_ref.shape[0]):
            for s in range(sequences):
                pick_ref[v, s] = jnp.full((8, 128), jnp.where(variant[s] == v, 1.0, 0.0), F32)

    def prepare(t, gains):
        heads = t.reshape(t.shape[0] // HEAD_DIM, HEAD_DIM, rows)
        scale = lax.rsqrt(jnp.mean(heads * heads, axis=1, keepdims=True) + EPSILON)
        return turn(heads * scale * gains, cosine, sine).astype(BF)

    for i in (0, 1):
        x = x_ref[i].astype(F32)
        scale = lax.rsqrt(jnp.mean(x * x, axis=-1, keepdims=True) + EPSILON)
        n1 = (x * scale * gain).astype(BF)
        n1_ref[i] = n1
        n1_s[i * rows : (i + 1) * rows, :] = n1
    n1 = n1_s[...]
    base = [mm(n1, w[...]) for w in (wq, wk, wv)]
    for i in (0, 1):
        v = variant[2 * step + i]
        half = slice(i * rows, (i + 1) * rows)
        a = jnp.concatenate([own_rows(f, v) for f in (aq, ak, av)], axis=0)
        b = [own_rows(f, v) for f in (bq, bk, bv)]
        ac_ref[i] = a
        bc_ref[i] = jnp.concatenate(b, axis=1)
        h = mm_nt(n1_s[half, :], a).astype(BF)
        h_ref[i] = jnp.concatenate([h, jnp.zeros((rows, 128 - 3 * RANK), BF)], axis=1)
        h2 = h * 2
        q, k, val = (
            jnp.transpose(base[n][half] + mm(h2[:, n * RANK : (n + 1) * RANK], b[n])) for n in range(3)
        )
        pre_ref[i, :qw, :] = q
        pre_ref[i, qw:, :] = k
        group = heads_q // heads_k
        q_ref[i * heads_k : (i + 1) * heads_k] = prepare(q, qg).reshape(heads_k, group * HEAD_DIM, rows)
        kv_ref[i * heads_k : (i + 1) * heads_k, :HEAD_DIM, :] = prepare(k, kg)
        kv_ref[i * heads_k : (i + 1) * heads_k, HEAD_DIM:, :] = val.astype(BF).reshape(heads_k, HEAD_DIM, rows)

    @pl.when(step == pl.num_programs(0) - 1)
    def _():
        for c in picks:
            c.wait()


def whole(array):
    return pl.BlockSpec(array.shape, lambda i: (0,) * len(array.shape), pipeline_mode=pl.Buffered(1))


def stepped(dims, per):
    return pl.BlockSpec((per,) + tuple(dims[1:]), lambda i: (i,) + (0,) * (len(dims) - 1))


def project(variant, x, gain, weights, ins, outs, qg, kg, tables, factors):
    sequences, rows, width = x.shape
    qw, kw = weights[0].shape[1], weights[1].shape[1]
    heads = kw // HEAD_DIM
    units = sequences * heads
    by_step = (
        (x.shape, BF, 2), ((sequences, rows, 128), BF, 2), ((sequences, qw + kw, rows), F32, 2),
        ((units, qw // kw * HEAD_DIM, rows), BF, 2 * heads), ((units, 2 * HEAD_DIM, rows), BF, 2 * heads),
        ((sequences, 3 * RANK, width), BF, 2), ((sequences, RANK, qw + 2 * kw), BF, 2),
    )
    at_once = (shape((2, HEAD_DIM, rows), F32), shape((ins[0].shape[0] // RANK, sequences, 8, 128), F32))
    at_once += tuple(shape((sequences * RANK, f.shape[1]), BF) for f in factors)
    same = (gain, *weights, *ins, *outs, qg, kg, *tables)
    return pl.pallas_call(
        project_kernel,
        grid=(sequences // 2,),
        out_shape=tuple(shape(dims, kind) for dims, kind, _ in by_step) + at_once,
        in_specs=[SMEM, stepped(x.shape, 2)] + [whole(a) for a in same] + [ANYWHERE] * 8,
        out_specs=tuple(stepped(dims, per) for dims, _, per in by_step) + tuple(whole(a) for a in at_once),
        scratch_shapes=[pltpu.VMEM((2 * rows, width), BF), pltpu.SemaphoreType.DMA((8, sequences))],
        compiler_params=BIG,
        cost_estimate=cost(sequences * rows, width, qw + 2 * kw, 1, 12 * sequences * rows * width),
        name="project",
    )(variant, x, *same, *factors)


def middle_kernel(variant, x_ref, attn, attn_x, gain_ref, wo, wo_x, ao, ao_x, bo, mid_ref, n2_ref, h_ref, lhs, lhs_x):
    step = pl.program_id(0)
    rows, width = x_ref.shape[1:]
    for i in (0, 1):
        half = slice(i * rows, (i + 1) * rows)
        lhs[half, :] = jnp.transpose(attn[i])
        lhs_x[half, :] = jnp.transpose(attn_x[i])
    out = mm(lhs[...], wo[...]) + mm(lhs_x[...], wo_x[...])
    for i in (0, 1):
        v = variant[2 * step + i]
        half = slice(i * rows, (i + 1) * rows)
        h = (mm_nt(lhs[half, :], own_rows(ao, v)) + mm_nt(lhs_x[half, :], own_rows(ao_x, v))).astype(BF)
        h_ref[i] = jnp.concatenate([h, jnp.zeros((rows, 128 - RANK), BF)], axis=1)
        mid = x_ref[i].astype(F32) + (out[half] + mm(h * 2, own_rows(bo, v)))
        mid_ref[i] = mid
        scale = lax.rsqrt(jnp.mean(mid * mid, axis=-1, keepdims=True) + EPSILON)
        n2_ref[i] = (mid * scale * gain_ref[...][None, :]).astype(BF)


def middle(variant, x, attn, attn_x, gain, wo, wo_x, ao, ao_x, bo):
    sequences, rows, width = x.shape
    inner = attn.shape[1]
    same = (gain, wo, wo_x, ao, ao_x, bo)
    outs = ((x.shape, F32), (x.shape, BF), ((sequences, rows, 128), BF))
    return pl.pallas_call(
        middle_kernel,
        grid=(sequences // 2,),
        out_shape=tuple(shape(dims, kind) for dims, kind in outs),
        in_specs=[SMEM] + [stepped(a.shape, 2) for a in (x, attn, attn_x)] + [whole(a) for a in same],
        out_specs=tuple(stepped(dims, 2) for dims, _ in outs),
        scratch_shapes=[pltpu.VMEM((2 * rows, inner), BF), pltpu.VMEM((2 * rows, inner), BF)],
        compiler_params=BIG,
        cost_estimate=cost(sequences * rows, width, inner, 2, 12 * sequences * rows * width),
        name="middle",
    )(variant, x, attn, attn_x, *same)


def own_ranks(first, rows, ranks):
    row = lax.broadcasted_iota(jnp.int32, (rows, ranks), 0) // 128 + first // 128
    return row == lax.broadcasted_iota(jnp.int32, (rows, ranks), 1) // RANK


def feed_kernel(
    cuts, n2_ref, dhd_ref, ag, au, bo, ao, wo, gain_ref, wg_ref, wu_ref, wd_ref, bg_ref, bu_ref, ad_ref, dh_ref,
    mid_ref, cot_ref, hout_ref, attn_ref,
    grads_ref, down_ref, dmid_ref, dattn_ref, more_ref,
    hg, hu, hs, dn2_acc, dhg_acc, dhu_acc, down_acc, h_acc, hidden_s, dgate_s, dup_s, back_s, back_x, branch_s, more_s,
    send_sems, recv_sems,
):
    step = pl.program_id(0)
    rows, width = n2_ref.shape
    tiles, tile = hidden_s.shape[0], hidden_s.shape[2]
    seqs = rows // 128
    ranks = seqs * RANK
    chunks = len(cuts) - 1
    last = chunks * tiles
    f = lax.rem(step, tiles)
    across = {"tp": 1 - lax.axis_index("tp")}

    def compact(a, first=0):
        a = jnp.where(own_ranks(first, *a.shape), a, 0.0)
        return sum(a[:, i * RANK : (i + 1) * RANK] for i in range(seqs))

    def copy(c):
        there = pl.ds(cuts[c], cuts[c + 1] - cuts[c])
        return remote(back_s.at[there, :], back_x.at[there, :], send_sems.at[c], recv_sems.at[c], across)

    @pl.when(step == 0)
    def _():
        barrier = pltpu.get_barrier_semaphore()
        pl.semaphore_signal(barrier, inc=1, device_id=across, device_id_type=MESH)
        pl.semaphore_wait(barrier, 1)
        kept = own_ranks(0, rows, ranks)
        g = jnp.where(kept, mm_nt(n2_ref[...], ag[...]) * 2.0, 0.0)
        u = jnp.where(kept, mm_nt(n2_ref[...], au[...]) * 2.0, 0.0)
        hg[...] = g.astype(BF)
        hu[...] = u.astype(BF)
        for n, a in enumerate((g, u, dhd_ref[...].astype(F32))):
            turned = jnp.transpose(jnp.concatenate([a, jnp.zeros((rows, 128 - ranks), F32)], axis=1))
            rows_of = [turned[i * RANK : (i + 1) * RANK] for i in range(seqs)]
            hs[n] = rank_halves(rows_of).astype(BF)
        down_acc[...] = jnp.zeros_like(down_acc)
        h_acc[...] = jnp.zeros_like(h_acc)

    for c in range(chunks):
        first, part = cuts[c], cuts[c + 1] - cuts[c]
        here, top = slice(first, first + part), slice(0, part)

        @pl.when((step >= c * tiles) & (step < (c + 1) * tiles))
        def _(here=here, top=top):
            n2 = n2_ref[here, :]
            bg, bu = bg_ref[...], bu_ref[...]
            gate = mm(n2, wg_ref[...]) + mm(hg[here, :], bg)
            up = mm(n2, wu_ref[...]) + mm(hu[here, :], bu)
            sg = 1.0 / (1.0 + jnp.exp(-gate))
            silu = gate * sg
            hidden_s[f, here, :] = (silu * up).astype(BF)
            dh = dh_ref[here, :].astype(F32)
            dg = (dh * up * sg * (1.0 + gate * (1.0 - sg))).astype(BF)
            du = (dh * silu).astype(BF)
            dgate_s[f, here, :] = dg
            dup_s[f, here, :] = du
            terms = (
                (dn2_acc, mm_nt(dg, wg_ref[...]) + mm_nt(du, wu_ref[...])), (dhg_acc, mm_nt(dg, bg)), (dhu_acc, mm_nt(du, bu))
            )
            for acc, term in terms:
                acc[top, :] = jnp.where(f == 0, term, acc[top, :] + term)

        @pl.when(step == (c + 1) * tiles - 1)
        def _(c=c, here=here, top=top, first=first, part=part):
            back_s[here, :width] = dn2_acc[top, :].astype(BF)
            small = [compact(a[top, :], first) * 2 for a in (dhg_acc, dhu_acc)]
            back_s[here, width:] = jnp.concatenate(small + [jnp.zeros((part, 128 - 2 * RANK), F32)], axis=1).astype(BF)
            copy(c).start()

    @pl.when((step >= last) & (step < last + tiles))
    def _():
        hidden = hidden_s[f]
        down_acc[...] += mm(hidden, wd_ref[...])
        h_acc[...] += mm_nt(hidden, ad_ref[...])
        for n, kept in enumerate((dgate_s, dup_s, hidden_s)):
            grads_ref[:, n * tile : (n + 1) * tile] = mm(hs[n], kept[f]).astype(BF)

    for c in range(chunks):

        @pl.when(step == last + tiles + cuts[c] // 128)
        def _(c=c):
            copy(c).wait()

    @pl.when(step >= last + tiles)
    def _():
        s = step - last - tiles
        here = pl.ds(pl.multiple_of(s * 128, 128), 128)
        own = pl.ds(pl.multiple_of(s * RANK, RANK), RANK)
        mine = pl.ds(pl.multiple_of(lax.axis_index("tp") * (width // 2), width // 2), width // 2)
        down_ref[0, :, :width] = down_acc[here, :].astype(BF)
        h = jnp.where(own_ranks(s * 128, 128, ranks), h_acc[here, :], 0.0)
        h = sum(h[:, i * RANK : (i + 1) * RANK] for i in range(seqs))
        down_ref[0, :, width:] = jnp.concatenate([h, jnp.zeros((128, 128 - RANK), F32)], axis=1).astype(BF)
        total = back_s[here, :].astype(F32) + back_x[here, :].astype(F32)
        dh = total[:, width : width + 2 * RANK].astype(BF)
        c = total[:, :width] + mm(dh, jnp.concatenate([ag[own, :], au[own, :]], axis=0))
        d_mid = cot_ref[0].astype(F32) + norm_back(mid_ref[0], gain_ref[...][None, :], c)
        dmid_ref[0] = d_mid
        branch_s[...] = d_mid.astype(BF)
        dho = (mm_nt(branch_s[...], bo[own, :]) * 2.0).astype(BF)
        d_attn = mm_nt(branch_s[...], wo[...]) + mm(dho, ao[own, :])
        dattn_ref[0] = jnp.transpose(d_attn).astype(BF)
        wide = jnp.concatenate([dh, dho, hout_ref[0][:, :RANK] * 2, jnp.zeros((128, 128 - 4 * RANK), BF)], axis=1)
        t = jnp.transpose(wide.astype(F32)).astype(BF)
        both = mm(t[: 2 * RANK], n2_ref[here, mine])
        more_s[s] = jnp.concatenate(
            [
                mm_nt(t[2 * RANK : 3 * RANK], attn_ref[0]), both[:RANK], both[RANK:],
                mm(t[3 * RANK : 4 * RANK], branch_s[:, mine]),
            ],
            axis=1,
        )

    @pl.when(step == pl.num_programs(0) - 1)
    def _():
        more_ref[...] = rank_halves([more_s[i] for i in range(seqs)]).astype(BF)


def feed_tile(units):
    return 1152 if units % 1152 == 0 else units


def feed(cuts, n2, dhd, ag, au, bo, ao, wo, gain, wg, wu, wd, bg, bu, ad, dh, mid, cot, hout, attn, collective_id):
    rows, width = n2.shape
    stacked, units = bg.shape
    inner = wo.shape[0]
    tile = feed_tile(units)
    chunks, part = len(cuts) - 1, max(b - a for a, b in zip(cuts, cuts[1:]))
    seqs, tiles, ranks = rows // 128, units // tile, rows // 128 * RANK
    last = chunks * tiles
    early = lambda height: pl.BlockSpec((height, tile), lambda i: (0, jnp.where(i < last, lax.rem(i, tiles), tiles - 1)))
    late = lambda i: jnp.clip(i - last, 0, tiles - 1)
    by_seq = lambda dims: pl.BlockSpec((1,) + dims[1:], lambda i: (jnp.maximum(i - last - tiles, 0), 0, 0))
    vm, dma = pltpu.VMEM, pltpu.SemaphoreType.DMA
    more = shape((ranks, inner + 3 * (width // 2)), BF)
    wide = (seqs, 128, width + 128)
    return pl.pallas_call(
        functools.partial(feed_kernel, cuts),
        grid=(last + tiles + seqs,),
        out_shape=(shape((ranks, 3 * units), BF), shape(wide, BF), shape(mid.shape, F32), shape(attn.shape, BF), more),
        in_specs=[whole(a) for a in (n2, dhd, ag, au, bo, ao, wo, gain)]
        + [early(width), early(width), pl.BlockSpec((tile, width), lambda i: (late(i), 0)), early(stacked), early(stacked)]
        + [pl.BlockSpec((stacked, tile), lambda i: (0, late(i))), early(rows)]
        + [by_seq(a.shape) for a in (mid, cot, hout, attn)],
        out_specs=(
            pl.BlockSpec((ranks, 3 * tile), lambda i: (0, late(i))), by_seq(wide), by_seq(mid.shape), by_seq(attn.shape),
            whole(more),
        ),
        scratch_shapes=[vm((rows, ranks), BF)] * 2
        + [vm((3, ranks, rows), BF), vm((part, width), F32), vm((part, ranks), F32), vm((part, ranks), F32)]
        + [vm((rows, width), F32), vm((rows, ranks), F32)] + [vm((tiles, rows, tile), BF)] * 3
        + [vm((rows, width + 128), BF)] * 2 + [vm((128, width), BF), vm((seqs, RANK, more.shape[1]), F32)]
        + [dma((chunks,)), dma((chunks,))],
        compiler_params=pltpu.CompilerParams(
            collective_id=collective_id, has_side_effects=True, vmem_limit_bytes=63 * 2**20
        ),
        cost_estimate=cost(rows, width, units, 5, 12 * width * units),
        name="feed_forward",
    )(n2, dhd, ag, au, bo, ao, wo, gain, wg, wu, wd, bg, bu, ad, dh, mid, cot, hout, attn)


TILE = 512
BLOCKS = TILE // 128
SUB = 512
SCALE = HEAD_DIM**-0.5


def document_starts(seg_ref, seq, seg_rows, starts):
    sequences, length = seg_ref.shape
    blocks = length // 128
    number = lax.broadcasted_iota(jnp.int32, (sequences, length), 0)
    row = jnp.sum(jnp.where(number == seq, seg_ref[...], 0), axis=0, keepdims=True).astype(F32)
    for b in range(blocks):
        seg_rows[b] = row[:, b * 128 : (b + 1) * 128]
        starts[b] = jnp.zeros((1, 128), jnp.int32)

    def keys(j, _):
        k = jnp.transpose(jnp.broadcast_to(seg_rows[j], (128, 128)))

        def queries(i, _):
            earlier = jnp.where(k < jnp.broadcast_to(seg_rows[i], (128, 128)), 1.0, 0.0)
            starts[i] += jnp.sum(earlier, axis=0, keepdims=True).astype(jnp.int32)
            return 0

        return lax.fori_loop(j, blocks, queries, 0)

    lax.fori_loop(0, blocks, keys, 0)


def query_rows(starts, tile, stride, part):
    lanes = lax.broadcasted_iota(jnp.int32, (1, 128), 1)
    blocks = [(BLOCKS * tile + b) * stride + part for b in range(BLOCKS)]
    position = jnp.concatenate([b * 128 + lanes for b in blocks], axis=1)
    return position, jnp.concatenate([starts[b] for b in blocks], axis=1)


def key_range(tile, stride, part):
    return BLOCKS * tile * stride // BLOCKS + part // BLOCKS, ((BLOCKS * tile + BLOCKS - 1) * stride + part) // BLOCKS + 1


def keep_pairs(p, first, start, position, causal):
    key = lax.broadcasted_iota(jnp.int32, p.shape, 0)
    keep = key >= jnp.broadcast_to(start - first, p.shape)
    if causal:
        keep = keep & (key <= jnp.broadcast_to(position - first, p.shape))
    return jnp.where(keep, p, 0.0)


def across_blocks(ref, tile, rows):
    return jnp.concatenate([ref[BLOCKS * tile + b, rows, :] for b in range(BLOCKS)], axis=1)


def load_keys(kv_ref, kb, vt):
    def load(j, _):
        for b in range(BLOCKS):
            kb[j, b * 128 : (b + 1) * 128, :] = jnp.transpose(kv_ref[BLOCKS * j + b, :HEAD_DIM, :])
            vt[j, :HEAD_DIM, b * 128 : (b + 1) * 128] = kv_ref[BLOCKS * j + b, HEAD_DIM:, :]
        vt[j, HEAD_DIM:, :] = jnp.ones((16, TILE), BF)
        return 0

    lax.fori_loop(0, kv_ref.shape[0] // BLOCKS, load, 0)


def head_forward(h, stride, part, q_ref, starts, kb, vt, acc, of_ref, lse_ref, done):
    rows = pl.ds(h * HEAD_DIM, HEAD_DIM)

    def q_step(i, _):
        position, start = query_rows(starts, i, stride, part)
        qt = across_blocks(q_ref, i, rows)
        acc[...] = jnp.zeros_like(acc)

        def k_step(causal, j, _):
            total = acc[...]
            for c in range(TILE // SUB):
                keys = slice(c * SUB, (c + 1) * SUB)
                p = jnp.exp2(mm(kb[j, keys, :], qt) * (LOG2E * SCALE))
                p = keep_pairs(p, j * TILE + c * SUB, start, position, causal)
                total = total + mm(vt[j, :, keys], p.astype(BF))
            acc[...] = total
            return 0

        whole, end = key_range(i, stride, part)
        lax.fori_loop(0, whole, functools.partial(k_step, False), 0)
        lax.fori_loop(whole, end, functools.partial(k_step, True), 0)
        total = acc[HEAD_DIM : HEAD_DIM + 1, :]
        lse_ref[h, i] = jnp.broadcast_to(jnp.log2(total), (8, TILE))
        out = acc[:HEAD_DIM, :] / total
        for b in range(BLOCKS):
            of_ref[BLOCKS * i + b, rows, :] = out[:, b * 128 : (b + 1) * 128]
        done(i, out.astype(BF))
        return 0

    lax.fori_loop(0, q_ref.shape[0] // BLOCKS, q_step, 0)


def pair_backward(h, i, j, causal, stride, part, qt, q3, dot_t, do3, lse_ref, delta, starts, kb, vb, kt, dqt, dk, dv):
    position, start = query_rows(starts, i, stride, part)
    dq = dqt[h, i]
    for c in range(TILE // SUB):
        keys = slice(c * SUB, (c + 1) * SUB)
        p = jnp.exp2(mm(kb[j, keys, :], qt[h, i]) * (LOG2E * SCALE) - lse_ref[h, i, 0:1, :])
        p = keep_pairs(p, j * TILE + c * SUB, start, position, causal)
        dp = mm(vb[j, keys, :], dot_t[h, i])
        ds = (p * (dp - delta[h, i, 0:1, :])).astype(BF)
        dv[j, keys, :] += mm(p.astype(BF), do3[h, i])
        dk[j, keys, :] += mm(ds, q3[h, i])
        dq = dq + mm(kt[j, :, keys], ds)
    dqt[h, i] = dq


def head_rows(h):
    return pl.ds(h * HEAD_DIM, HEAD_DIM)


def loop(low, high, step):
    def body(k, _):
        step(k)
        return 0

    lax.fori_loop(low, high, body, 0)


def class_copy(count, parts, source, target, send, recv):
    def make(index, sender):
        return remote(
            source(index), target(sender), send.at[index], recv.at[sender],
            {"ctx": index * parts + lax.rem(lax.axis_index("ctx"), parts)},
        )

    return make


def attend_kernel(
    count, parts, units_per_seq, seg_ref, q_ref, kv_ref, cot_ref, bd_ref, ad_ref, wd_ref,
    q_all, kv_all, of_ref, lse_ref, starts, dhd_ref, home, home_x, dh_ref,
    cot_s, wd_s, dh_s, spare_sems, q_in, kv_in, o_buf, kb, vt, acc, seg_rows,
    kv_send, kv_recv, q_send, q_recv, o_send, o_recv, x_send, x_recv, own_sems, out_sems,
):
    me = lax.axis_index("ctx")
    units = count // parts
    unit, part = me // parts, lax.rem(me, parts)
    group = q_ref.shape[1] // HEAD_DIM
    across = {"tp": 1 - lax.axis_index("tp")}
    barrier = pltpu.get_barrier_semaphore()
    pl.semaphore_signal(barrier, inc=1, device_id=across, device_id_type=MESH)
    loop(
        1, count,
        lambda k: pl.semaphore_signal(barrier, inc=1, device_id={"ctx": lax.rem(me + k, count)}, device_id_type=MESH),
    )
    own = [pltpu.make_async_copy(kv_ref.at[unit], kv_in.at[me], own_sems.at[0])]
    own.append(pltpu.make_async_copy(q_ref.at[unit], q_in.at[unit], own_sems.at[1]))
    for c in own:
        c.start()
    tiles, tile = wd_s.shape[0], wd_s.shape[1]
    loads = [pltpu.make_async_copy(cot_ref, cot_s, spare_sems.at[0])]
    for f in range(tiles):
        rows = pl.ds(f * tile, tile)
        loads.append(pltpu.make_async_copy(wd_ref.at[rows, :], wd_s.at[f], spare_sems.at[1 + f]))
    for c in loads:
        c.start()
    pl.semaphore_wait(barrier, count)

    def kv_copy(device, sender):
        return remote(
            kv_ref.at[device // parts], kv_in.at[sender], kv_send.at[device], kv_recv.at[sender], {"ctx": device}
        )

    q_copy = [
        class_copy(
            count, parts, lambda i, h=h: q_ref.at[i, head_rows(h), :], lambda i, h=h: q_in.at[i, head_rows(h), :],
            q_send.at[h], q_recv.at[h],
        )
        for h in range(group)
    ]
    o_copy = [
        class_copy(
            count, parts, lambda i, h=h: o_buf.at[h, i], lambda i, h=h: home.at[i, head_rows(h), :],
            o_send.at[h], o_recv.at[h],
        )
        for h in range(group)
    ]

    def x_copy(h, i):
        place = (i, head_rows(h), slice(None))
        return remote(home.at[place], home_x.at[place], x_send.at[h, i], x_recv.at[h, i], across)

    def turn_of(k):
        return lax.rem(unit + k, units)

    loop(1, count, lambda k: kv_copy(lax.rem(me + k, count), me).start())
    for h in range(group):
        loop(1, units, lambda k, h=h: q_copy[h](turn_of(k), unit).start())
    document_starts(seg_ref, unit // units_per_seq, seg_rows, starts)
    loads[0].wait()
    dhd_ref[...] = jnp.where(own_ranks(0, *dhd_ref.shape), mm_nt(cot_s[...], bd_ref[...]) * 2.0, 0.0).astype(BF)
    saves = []
    for f in range(tiles):
        loads[1 + f].wait()
        columns = slice(f * tile, (f + 1) * tile)
        dh_s[:, columns] = (mm_nt(cot_s[...], wd_s[f]) + mm(dhd_ref[...], ad_ref[:, columns])).astype(BF)
        saves.append(pltpu.make_async_copy(dh_s.at[:, columns], dh_ref.at[:, columns], spare_sems.at[1 + tiles + f]))
        saves[-1].start()
    for c in own:
        c.wait()
    loop(1, count, lambda k: kv_copy(me, lax.rem(me + k, count)).wait_recv())
    load_keys(kv_in, kb, vt)
    saves.append(pltpu.make_async_copy(kv_in, kv_all, out_sems.at[0]))
    saves[-1].start()

    def keep_own(h):
        return pltpu.make_async_copy(o_buf.at[h, unit], home.at[unit, head_rows(h), :], own_sems.at[2 + h])

    def pass_on(h):
        keep_own(h).wait()
        x_copy(h, unit).start()

        def relay(k):
            other = turn_of(units - k)
            o_copy[h](unit, other).wait_recv()
            x_copy(h, other).start()

        loop(1, units, relay)

    for h in range(group):
        loop(1, units, lambda k, h=h: q_copy[h](unit, turn_of(k)).wait_recv())
        if h == group - 1:
            saves.append(pltpu.make_async_copy(q_in, q_all, out_sems.at[1]))
            saves[-1].start()

        def done(i, out, h=h):
            for b in range(BLOCKS):
                block = BLOCKS * i + b
                o_buf[h, block] = out[:, b * 128 : (b + 1) * 128]

                @pl.when(block == unit)
                def _():
                    keep_own(h).start()

                @pl.when(block != unit)
                def _():
                    o_copy[h](block, unit).start()

        head_forward(h, parts, part, q_in, starts, kb, vt, acc, of_ref, lse_ref, done)
        if h > 0:
            pass_on(h - 1)
    pass_on(group - 1)
    for c in saves:
        c.wait()
    loop(1, count, lambda k: kv_copy(lax.rem(me + k, count), me).wait_send())
    for h in range(group):

        def finish_block(k, h=h):
            q_copy[h](turn_of(k), unit).wait_send()
            o_copy[h](turn_of(k), unit).wait_send()

        loop(1, units, finish_block)

        def finish_across(i, h=h):
            x_copy(h, i).wait_send()
            x_copy(h, i).wait_recv()

        loop(0, units, finish_across)


def attend(segs, q, kv, cot, bd, ad, wd, count, parts, units_per_seq, collective_id):
    units, qrows, _ = q.shape
    group, tiles, ktiles = qrows // HEAD_DIM, units // BLOCKS, count // BLOCKS
    dma, vm = pltpu.SemaphoreType.DMA, pltpu.VMEM
    kv_shape = (count,) + kv.shape[1:]
    hidden_units, tile = wd.shape[0], feed_tile(wd.shape[0])
    spare = hidden_units // tile
    return pl.pallas_call(
        functools.partial(attend_kernel, count, parts, units_per_seq),
        out_shape=(
            shape(q.shape, BF), shape(kv_shape, BF), shape(q.shape, F32), shape((group, tiles, 8, TILE), F32),
            shape((count, 1, 128), jnp.int32), shape((cot.shape[0], bd.shape[0]), BF), shape(q.shape, BF),
            shape(q.shape, BF), shape((cot.shape[0], hidden_units), BF),
        ),
        in_specs=[VM, ANYWHERE, ANYWHERE, ANYWHERE, VM, VM, ANYWHERE],
        out_specs=(ANYWHERE, ANYWHERE, VM, VM, VM, VM, ANYWHERE, ANYWHERE, ANYWHERE),
        scratch_shapes=[
            vm(cot.shape, BF), vm((spare, tile, wd.shape[1]), BF), vm((cot.shape[0], hidden_units), BF),
            dma((1 + 2 * spare,)),
            vm(q.shape, BF), vm(kv_shape, BF), vm((group, units, HEAD_DIM, 128), BF), vm((ktiles, TILE, HEAD_DIM), BF),
            vm((ktiles, HEAD_DIM + 16, TILE), BF), vm((HEAD_DIM + 16, TILE), F32), vm((count, 1, 128), F32),
            dma((count,)), dma((count,)),
        ]
        + [dma((group, units))] * 6 + [dma((2 + group,)), dma((2,))],
        compiler_params=pltpu.CompilerParams(
            collective_id=collective_id, has_side_effects=True, vmem_limit_bytes=60 * 2**20
        ),
        name="attend",
    )(segs, q, kv, cot, bd, ad, wd)


def owner_rows(total, pick_ref, k, sequences):
    per = RANK // 2
    row = jnp.zeros((per, total.shape[1]), F32)
    for s in range(sequences):
        row = row + total[s * per : (s + 1) * per] * pick_ref[k, s][:, :1]
    half = total.shape[1] // 2
    return jnp.concatenate([row[:, :half], row[:, half:]], axis=0).astype(BF)


def unfold_rows(rows_ref, at, block):
    per, half = RANK // 2, block.shape[1]
    rows_ref[:, at : at + half] = block[:per].astype(F32)
    rows_ref[:, at + half : at + 2 * half] = block[per:].astype(F32)


class EarlyReduction:
    def __init__(self, me, grads, y_sum, own, core_in, plane, y_in, loads, twin_sends, twin_recvs, y_sems):
        self.y_sum, self.own, self.core_in, self.plane, self.y_in = y_sum, own, core_in, plane, y_in
        chip, core = me // 2, lax.rem(me, 2)
        self.y = lax.rem(chip, 2)
        self.loads, self.to_twin, at = [], [], 0
        for i, ref in enumerate(grads):
            size, place = ref.shape[0] // 2, slice(at, at + ref.shape[1])
            at += ref.shape[1]
            half = lambda who, ref=ref, size=size: ref.at[pl.ds(pl.multiple_of(who * size, 16), size), :]
            self.loads.append(pltpu.make_async_copy(half(core), own.at[:, place], loads.at[i]))
            twin = {"ctx": 2 * chip + 1 - core}
            self.to_twin.append(remote(half(1 - core), core_in.at[:, place], twin_sends.at[i], twin_recvs.at[i], twin))
        self.known, self.width = at, plane.shape[1] // 2
        self.to_y = remote(
            plane.at[:, pl.ds(pl.multiple_of((1 - self.y) * self.width, 128), self.width)], y_in, y_sems.at[0],
            y_sems.at[1], {"ctx": 2 * (chip + 1 - 2 * self.y) + core},
        )

    def begin(self):
        for c in self.loads + self.to_twin:
            c.start()

    def over_cores(self):
        for c in self.loads:
            c.wait()
        for c in self.to_twin:
            c.wait_recv()
        self.plane[:, : self.known] = (self.own[...].astype(F32) + self.core_in[...].astype(F32)).astype(BF)
        rest = self.plane.shape[1] - self.known
        if rest:
            self.plane[:, self.known :] = jnp.zeros((self.plane.shape[0], rest), BF)
        self.to_y.start()

    def over_y(self):
        self.to_y.wait()
        mine = self.plane[:, pl.ds(pl.multiple_of(self.y * self.width, 128), self.width)]
        self.y_sum[...] = (mine.astype(F32) + self.y_in[...].astype(F32)).astype(BF)
        for c in self.to_twin:
            c.wait_send()


def early_scratch(grads, total):
    vm, dma = pltpu.VMEM, pltpu.SemaphoreType.DMA
    rows, known = grads[0].shape[0] // 2, sum(g.shape[1] for g in grads)
    return [vm((rows, known), BF), vm((rows, known), BF), vm((rows, total), BF), vm((rows, total // 2), BF)] + [dma((2,))] * 4


def padded(columns, chips):
    return -(-columns // (256 * chips)) * 256 * chips


def attend_back_kernel(count, parts, reduce, do_ref, q_all, kv_all, of_ref, lse_ref, starts, *refs):
    refs = list(refs)
    take = lambda n: [refs.pop(0) for _ in range(n)]
    grads = take(2) if reduce else []
    dq_home, dkv_home = take(2)
    early = EarlyReduction(lax.axis_index("ctx"), grads, *take(9)) if reduce else None
    attend_back_body(
        count, parts, early,
        do_ref, q_all, kv_all, of_ref, lse_ref, starts, dq_home, dkv_home, *refs,
    )


def attend_back_body(
    count, parts, early, do_ref, q_all, kv_all, of_ref, lse_ref, starts, dq_home, dkv_home,
    do_in, dq_buf, dkv_buf, kb, vb, kt, qt, q3, dot_t, do3, delta, dqt, dk, dv,
    do_send, do_recv, dq_send, dq_recv, dkv_send, dkv_recv, own_sems,
):
    me = lax.axis_index("ctx")
    units = count // parts
    unit, part = me // parts, lax.rem(me, parts)
    group, tiles, ktiles = q_all.shape[1] // HEAD_DIM, units // BLOCKS, count // BLOCKS
    barrier = pltpu.get_barrier_semaphore()
    loop(
        1, count,
        lambda k: pl.semaphore_signal(barrier, inc=1, device_id={"ctx": lax.rem(me + k, count)}, device_id_type=MESH),
    )
    own_do = pltpu.make_async_copy(do_ref.at[unit], do_in.at[unit], own_sems.at[0])
    own_do.start()
    pl.semaphore_wait(barrier, count - 1)
    if early:
        early.begin()

    def turn_of(k):
        return lax.rem(unit + k, units)

    do_copy = [
        class_copy(
            count, parts, lambda i, h=h: do_ref.at[i, head_rows(h), :], lambda i, h=h: do_in.at[i, head_rows(h), :],
            do_send.at[h], do_recv.at[h],
        )
        for h in range(group)
    ]
    dq_copy = [
        class_copy(
            count, parts, lambda i, h=h: dq_buf.at[h, i], lambda i, h=h: dq_home.at[i, head_rows(h), :],
            dq_send.at[h], dq_recv.at[h],
        )
        for h in range(group)
    ]

    def dkv_copy(device, sender):
        return remote(dkv_buf.at[device], dkv_home.at[sender], dkv_send.at[device], dkv_recv.at[sender], {"ctx": device})

    own_dkv = pltpu.make_async_copy(dkv_buf.at[me], dkv_home.at[me], own_sems.at[1])

    def own_dq(h):
        return pltpu.make_async_copy(dq_buf.at[h, unit], dq_home.at[unit, head_rows(h), :], own_sems.at[2 + h])

    for h in range(group):
        loop(1, units, lambda k, h=h: do_copy[h](turn_of(k), unit).start())

    def load_kv(j):
        for b in range(BLOCKS):
            lanes = slice(b * 128, (b + 1) * 128)
            kt[j, :, lanes] = kv_all[BLOCKS * j + b, :HEAD_DIM, :]
            kb[j, lanes, :] = jnp.transpose(kv_all[BLOCKS * j + b, :HEAD_DIM, :])
            vb[j, lanes, :] = jnp.transpose(kv_all[BLOCKS * j + b, HEAD_DIM:, :])

    def load_q(i):
        for h in range(group):
            for b in range(BLOCKS):
                lanes = slice(b * 128, (b + 1) * 128)
                q = q_all[BLOCKS * i + b, h * HEAD_DIM : (h + 1) * HEAD_DIM, :]
                qt[h, i, :, lanes] = q
                q3[h, i, lanes, :] = jnp.transpose(q)
            dqt[h, i] = jnp.zeros((HEAD_DIM, TILE), F32)

    def load_do(h, i):
        rows = slice(h * HEAD_DIM, (h + 1) * HEAD_DIM)
        for b in range(BLOCKS):
            lanes = slice(b * 128, (b + 1) * 128)
            g = do_in[BLOCKS * i + b, rows, :]
            dot_t[h, i, :, lanes] = g
            do3[h, i, lanes, :] = jnp.transpose(g)
            d = jnp.sum(g.astype(F32) * of_ref[BLOCKS * i + b, rows, :], axis=0, keepdims=True)
            delta[h, i, :, lanes] = jnp.broadcast_to(d, (8, 128))

    loop(0, ktiles, load_kv)
    loop(0, tiles, load_q)

    def last_tile(i):
        return key_range(i, parts, part)[1] - 1

    def run(h, j):
        low = jnp.maximum(BLOCKS * j - part + parts - 1, 0) // (BLOCKS * parts)
        full = jnp.minimum((BLOCKS * (j + 1) - part + BLOCKS * parts - 1) // (BLOCKS * parts), tiles)

        def pair(causal, i):
            pair_backward(
                h, i, j, causal, parts, part, qt, q3, dot_t, do3, lse_ref, delta, starts, kb, vb, kt, dqt, dk, dv
            )

        loop(low, full, functools.partial(pair, True))
        loop(full, tiles, functools.partial(pair, False))

    def emit_keys(j):
        for b in range(BLOCKS):
            rows = slice(b * 128, (b + 1) * 128)
            block = BLOCKS * j + b
            dkv_buf[block, :HEAD_DIM, :] = jnp.transpose(dk[j, rows, :] * SCALE).astype(BF)
            dkv_buf[block, HEAD_DIM:, :] = jnp.transpose(dv[j, rows, :]).astype(BF)

            @pl.when(block == me)
            def _():
                own_dkv.start()

            @pl.when(block != me)
            def _():
                dkv_copy(block, me).start()

    def emit_queries(h, j, i):
        @pl.when(last_tile(i) == j)
        def _():
            for b in range(BLOCKS):
                block = BLOCKS * i + b
                dq_buf[h, block] = (dqt[h, i, :, b * 128 : (b + 1) * 128] * SCALE).astype(BF)

                @pl.when(block == unit)
                def _():
                    own_dq(h).start()

                @pl.when(block != unit)
                def _():
                    dq_copy[h](block, unit).start()

    dk[...] = jnp.zeros_like(dk)
    dv[...] = jnp.zeros_like(dv)
    own_do.wait()
    if early:
        early.over_cores()
    for h in range(group):
        loop(1, units, lambda k, h=h: do_copy[h](unit, turn_of(k)).wait_recv())
        loop(0, tiles, functools.partial(load_do, h))

        def key_step(j, h=h):
            run(h, j)
            if h == group - 1:
                emit_keys(j)
            loop(0, tiles, functools.partial(emit_queries, h, j))

        loop(0, ktiles, key_step)
        if early and h == 1:
            early.over_y()
    for h in range(group):
        own_dq(h).wait()
    own_dkv.wait()

    def finish_full(k):
        other = lax.rem(me + k, count)
        dkv_copy(other, me).wait_send()
        dkv_copy(me, other).wait_recv()

    loop(1, count, finish_full)

    def finish_class(k):
        other = turn_of(k)
        for h in range(group):
            do_copy[h](other, unit).wait_send()
            dq_copy[h](other, unit).wait_send()
            dq_copy[h](unit, other).wait_recv()

    loop(1, units, finish_class)


def attend_back(do, q, kv, of, lse, starts, early, count, parts, collective_id):
    units, qrows, _ = q.shape
    group, tiles, ktiles = qrows // HEAD_DIM, units // BLOCKS, count // BLOCKS
    dma, vm = pltpu.SemaphoreType.DMA, pltpu.VMEM
    sums, scratch = (), []
    if early:
        total = padded(sum(g.shape[1] for g in early), count // 2)
        sums = (shape((early[0].shape[0] // 2, total // 2), BF),)
        scratch = early_scratch(early, total)
    return pl.pallas_call(
        functools.partial(attend_back_kernel, count, parts, bool(early)),
        out_shape=(shape(q.shape, BF), shape(kv.shape, BF)) + sums,
        in_specs=[ANYWHERE] + [VM] * 5 + [ANYWHERE] * len(early),
        out_specs=(ANYWHERE, ANYWHERE) + (VM,) * len(sums),
        scratch_shapes=scratch + [vm(q.shape, BF), vm((group, units, HEAD_DIM, 128), BF), vm(kv.shape, BF)]
        + [vm((ktiles, TILE, HEAD_DIM), BF)] * 2 + [vm((ktiles, HEAD_DIM, TILE), BF)]
        + [vm((group, tiles, HEAD_DIM, TILE), BF), vm((group, tiles, TILE, HEAD_DIM), BF)] * 2
        + [vm((group, tiles, 8, TILE), F32), vm((group, tiles, HEAD_DIM, TILE), F32)]
        + [vm((ktiles, TILE, HEAD_DIM), F32)] * 2
        + [dma((group, units))] * 4 + [dma((count,))] * 2 + [dma((2 + group,))],
        compiler_params=pltpu.CompilerParams(
            collective_id=collective_id, has_side_effects=True, vmem_limit_bytes=60 * 2**20
        ),
        name="attend_back",
    )(do, q, kv, of, lse, starts, *early)


def finish_kernel(reduce, count, shared, *refs):
    refs = list(refs)
    take = lambda n: [refs.pop(0) for _ in range(n)]
    dq_ref, dkv_ref, pre_ref, h_ref, gains, cos_ref, sin_ref, gain_ref, bc_ref, pick_ref, bd_ref = take(11)
    far = take(11)
    early = take(1) if reduce else []
    out_ref, block_ref = take(2)
    gout = take(4) if reduce else take(1)
    x, d_mid, n1, wq, wk, wv, ac, mid, down, down_x, cot = near = take(11)
    d_n, gb, dh_own, dh_other, dh_sum, sbuf, rbuf, gq = take(8)
    near_sems, dh_send, dh_recv, xsend, xrecv = take(5)
    sequences, inner, rows = dq_ref.shape
    width = out_ref.shape[2]
    kw = wk.shape[1]
    half_rows = sequences * RANK // 2
    me = lax.axis_index("ctx")
    across = {"tp": 1 - lax.axis_index("tp")}
    mine = pl.ds(pl.multiple_of(lax.axis_index("tp") * (width // 2), width // 2), width // 2)

    loads = [pltpu.make_async_copy(f, n, near_sems.at[i]) for i, (f, n) in enumerate(zip(far, near))]
    barrier = pltpu.get_barrier_semaphore()
    pl.semaphore_signal(barrier, inc=1, device_id=across, device_id_type=MESH)
    peers = 1
    if reduce:
        core_in, plane, z_in, plane_in = take(4)
        fin_outs, fin_ins = take(2), take(2)
        twin_sems, z_send, z_recv, plane_send, plane_recv, fin_send, fin_recv, last_sems = take(8)
        chips = count // 2
        chip, core = me // 2, lax.rem(me, 2)
        twin = {"ctx": 2 * chip + 1 - core}
        pl.semaphore_signal(barrier, inc=1, device_id=twin, device_id_type=MESH)

        def at_chip(k):
            return lax.rem(chip + k, chips)

        def greet(k, _):
            pl.semaphore_signal(barrier, inc=1, device_id={"ctx": 2 * at_chip(k) + core}, device_id_type=MESH)
            return 0

        lax.fori_loop(1, chips, greet, 0)
        peers += chips

        w_qkv = gq.shape[2]
        to_twin = remote(gq.at[1 - core], core_in, twin_sems.at[0], twin_sems.at[1], twin)
    for i in (3, 4, 5, 2, 6, 7, 8, 9, 10, 0, 1):
        loads[i].start()
    pl.semaphore_wait(barrier, peers)
    if reduce:
        deep = chips // 2
        z, y = chip // 2, lax.rem(chip, 2)

        def z_copy(other, sender):
            chunk = early[0].shape[1] // deep
            return remote(
                early[0].at[:, pl.ds(pl.multiple_of(other * chunk, 128), chunk)], z_in.at[sender], z_send.at[other],
                z_recv.at[sender], {"ctx": 4 * other + 2 * y + core},
            )

        def each_z(step):
            loop(1, deep, lambda k: step(lax.rem(z + k, deep)))

        each_z(lambda k: z_copy(k, z).start())

    cosine, sine = cos_ref[...], sin_ref[...]
    heads_k = kw // HEAD_DIM
    cuts = (slice(0, inner), slice(inner, inner + kw), slice(inner + kw, inner + 2 * kw))

    def prepare_back(pre, gains, c):
        u = pre.reshape(pre.shape[0] // HEAD_DIM, HEAD_DIM, rows)
        scale = lax.rsqrt(jnp.mean(u * u, axis=1, keepdims=True) + EPSILON)
        y = u * scale
        w = turn(c.reshape(u.shape).astype(F32), cosine, -sine) * gains
        return (scale * (w - y * jnp.mean(w * y, axis=1, keepdims=True))).reshape(pre.shape)

    def first_step(s):
        dkv = dkv_ref[s * heads_k : (s + 1) * heads_k].astype(F32)
        dkv = jnp.sum(dkv, axis=1).astype(BF) if dkv.shape[1] > 1 else dkv[:, 0].astype(BF)
        d_q = prepare_back(pre_ref[s, :inner, :], gains[0], dq_ref[s])
        d_k = prepare_back(pre_ref[s, inner:, :], gains[1], dkv[:, :HEAD_DIM, :].reshape(kw, rows))
        d_v = dkv[:, HEAD_DIM:, :].reshape(kw, rows).astype(F32)
        d = jnp.transpose(jnp.concatenate([d_q, d_k, d_v], axis=0)).astype(BF)
        d_n[s] = d
        dh = [mm_nt(d[:, c], bc_ref[s, :, c]) * 2.0 for c in cuts]
        dh_own[s] = jnp.concatenate(dh + [jnp.zeros((rows, 128 - 3 * RANK), F32)], axis=1).astype(BF)
        t = (jnp.transpose(h_ref[s].astype(F32)) * 2.0).astype(BF)
        gb[s] = jnp.concatenate([mm(t[i * RANK : (i + 1) * RANK], d[:, c]) for i, c in enumerate(cuts)], axis=1)

    def part_copy(s):
        return remote(sbuf.at[s], rbuf.at[s], xsend.at[s], xrecv.at[s], across)

    dh_copies = []

    def send_pair(p):
        pair = pl.ds(2 * p, 2)
        first_step(2 * p)
        first_step(2 * p + 1)
        dh_copies.append(remote(dh_own.at[pair], dh_other.at[pair], dh_send.at[p], dh_recv.at[p], across))
        dh_copies[-1].start()
        if p == 0:
            for i in (3, 4, 5):
                loads[i].wait()
        d = jnp.concatenate([d_n[2 * p], d_n[2 * p + 1]], axis=0)
        part = mm_nt(d[:, cuts[0]], wq[...]) + mm_nt(d[:, cuts[1]], wk[...]) + mm_nt(d[:, cuts[2]], wv[...])
        for i in (0, 1):
            sbuf[2 * p + i] = part[i * rows : (i + 1) * rows].astype(BF)
            part_copy(2 * p + i).start()

    def plane_copy(k, slot):
        chunk = plane.shape[1] // chips
        return remote(
            plane.at[:, pl.ds(pl.multiple_of(k * chunk, 128), chunk)], plane_in.at[slot], plane_send.at[k],
            plane_recv.at[slot], {"ctx": 2 * k + core},
        )

    def fin_copy(g, k, slot):
        return remote(
            fin_outs[g].at[k], fin_ins[g].at[slot], fin_send.at[g, k], fin_recv.at[g, slot], {"ctx": 2 * k + core}
        )

    def each_chip(step):
        loop(1, chips, lambda k: step(at_chip(k)))

    def to_plane():
        to_twin.wait_recv()
        plane[:, :w_qkv] = (gq[core].astype(F32) + core_in[...].astype(F32)).astype(BF)
        if plane.shape[1] > w_qkv:
            plane[:, w_qkv:] = jnp.zeros((half_rows, plane.shape[1] - w_qkv), BF)
        chunk = plane.shape[1] // chips
        each_chip(lambda k: plane_copy(k, chip).start())
        plane_in[chip] = plane[:, pl.ds(pl.multiple_of(chip * chunk, 128), chunk)]

    def to_owners(g):
        if g == 0:
            each_z(lambda k: z_copy(k, k).wait_recv())
            chunk = early[0].shape[1] // deep
            z_in[z] = early[0][:, pl.ds(pl.multiple_of(z * chunk, 128), chunk)]
        else:
            each_chip(lambda k: plane_copy(k, k).wait_recv())
        blocks = z_in if g == 0 else plane_in
        total = blocks[0].astype(F32)
        for k in range(1, blocks.shape[0]):
            total = total + blocks[k].astype(F32)
        for k in range(chips):
            fin_outs[g][k] = owner_rows(total, pick_ref, k, sequences)
        each_chip(lambda k: fin_copy(g, k, chip).start())
        fin_ins[g][chip] = fin_outs[g][chip]

    def rows_in(g):
        each_chip(lambda k: fin_copy(g, k, k).wait_recv())
        chunk = gout[g].shape[1] // chips
        for k in range(chips):
            unfold_rows(gout[g], (k % 2 * deep + k // 2 if g == 0 else k) * chunk, fin_ins[g][k])
        copy = remote(
            gout[g].at[:, shared[g][0] : shared[g][1]], gout[2 + g], last_sems.at[g], last_sems.at[2 + g], across
        )
        copy.start()
        return copy

    def last_step(s):
        part_copy(s).wait_recv()
        c = sbuf[s].astype(F32) + rbuf[s].astype(F32) + mm(dh_sum[s][:, : 3 * RANK], ac[s])
        out_ref[s] = (d_mid[s] + norm_back(x[s].astype(F32), gain_ref[...][None, :], c)).astype(BF)

    pairs = sequences // 2
    send_pair(0)
    for p in range(1, pairs):
        send_pair(p)
    for i in (2, 7, 8, 9, 10):
        loads[i].wait()
    blocks = []
    for s in range(sequences):
        total = down[s].astype(F32) + down_x[s].astype(F32)
        h = total[:, width : width + RANK].astype(BF) * 2
        block_ref[s] = (mid[s] + (total[:, :width] + mm(h, bd_ref[s * RANK : (s + 1) * RANK, :]))).astype(BF)
        wide = jnp.concatenate([h, jnp.zeros((rows, 128 - RANK), BF)], axis=1)
        gb_down = mm(jnp.transpose(wide.astype(F32)).astype(BF)[:RANK], cot[s, :, mine])
        if s % 2 == 0:
            dh_copies[s // 2].wait_recv()
        dh = (dh_own[s].astype(F32) + dh_other[s].astype(F32)).astype(BF)
        dh_sum[s] = dh
        t = jnp.transpose(dh.astype(F32)).astype(BF)
        wide = mm(t[: 3 * RANK], n1[s, :, mine])
        blocks.append(jnp.concatenate([wide[i * RANK : (i + 1) * RANK] for i in range(3)] + [gb_down, gb[s]], axis=1))
    everything = rank_halves(blocks)
    for b in (0, 1):
        gq[b] = everything[b * half_rows : (b + 1) * half_rows].astype(BF)
    if reduce:
        to_twin.start()
        to_plane()
        to_owners(0)
    for i in (6, 0, 1):
        loads[i].wait()
    if reduce:
        last_step(0)
        to_owners(1)
        shared_copies = [rows_in(0)]
        last_step(1)
        shared_copies.append(rows_in(1))
        for s in range(2, sequences):
            last_step(s)
        for c in shared_copies:
            c.wait()
        to_twin.wait_send()
        each_z(lambda k: z_copy(k, z).wait_send())
        each_chip(lambda k: plane_copy(k, chip).wait_send())
        for g in (0, 1):
            each_chip(lambda k, g=g: fin_copy(g, k, chip).wait_send())
    else:
        for s in range(sequences):
            last_step(s)
        gout[0][...] = gq[...]
    for c in dh_copies:
        c.wait_send()
    for s in range(sequences):
        part_copy(s).wait_send()


def finish(
    reduce, count, dq, dkv, pre, h, gains, tables, gain, bc, pick, bd, x, d_mid, n1, weights, ac, mid, down, down_x, cot,
    early, shared, collective_id,
):
    sequences, rows, width = x.shape
    inner, kw = weights[0].shape[1], weights[1].shape[1]
    w_qkv = 4 * (width // 2) + inner + 2 * kw
    half_rows = sequences * RANK // 2
    dma = pltpu.SemaphoreType.DMA
    far = (x, d_mid, n1) + tuple(weights) + (ac, mid, down, down_x, cot)
    gshape = (shape((2, half_rows, w_qkv), BF),)
    scratch = [pltpu.VMEM(a.shape, a.dtype) for a in far]
    scratch += [
        pltpu.VMEM((sequences, rows, inner + 2 * kw), BF),
        pltpu.VMEM((sequences, RANK, inner + 2 * kw), F32),
        pltpu.VMEM((sequences, rows, 128), BF),
        pltpu.VMEM((sequences, rows, 128), BF),
        pltpu.VMEM((sequences, rows, 128), BF),
        pltpu.VMEM(x.shape, BF),
        pltpu.VMEM(x.shape, BF),
        pltpu.VMEM((2, half_rows, w_qkv), BF),
        dma((11,)), dma((sequences // 2,)), dma((sequences // 2,)), dma((sequences,)), dma((sequences,)),
    ]
    if reduce:
        chips = count // 2
        totals = (2 * early[0].shape[1], padded(w_qkv, chips))
        gshape = tuple(shape((RANK // 2, n), F32) for n in totals)
        gshape += tuple(shape((RANK // 2, b - a), F32) for a, b in shared)
        scratch += [
            pltpu.VMEM((half_rows, w_qkv), BF),
            pltpu.VMEM((half_rows, totals[1]), BF),
            pltpu.VMEM((chips // 2, half_rows, totals[0] // chips), BF),
            pltpu.VMEM((chips, half_rows, totals[1] // chips), BF),
        ]
        scratch += [pltpu.VMEM((chips, RANK, n // chips // 2), BF) for n in totals] * 2
        scratch += [dma((2,)), dma((chips // 2,)), dma((chips // 2,)), dma((chips,)), dma((chips,))]
        scratch += [dma((2, chips))] * 2 + [dma((4,))]
    return pl.pallas_call(
        functools.partial(finish_kernel, reduce, count, shared),
        out_shape=(shape(x.shape, BF),) * 2 + gshape,
        in_specs=[VM] * 11 + [ANYWHERE] * 11 + [VM] * len(early),
        out_specs=(VM,) * (2 + len(gshape)),
        scratch_shapes=scratch,
        compiler_params=pltpu.CompilerParams(
            collective_id=collective_id, has_side_effects=True, vmem_limit_bytes=60 * 2**20
        ),
        name="finish",
    )(dq, dkv, pre, h, gains, *tables, gain, bc, pick, bd, *far, *early)


def unpack_kernel(hidden_units, tile, inner, kw, block, grad, first, second, first_x, second_x, block_out, grad_out, *outs):
    block_out[...] = block[...]
    grad_out[...] = grad[...]
    ga_query, gb_query, ga_key, gb_key, ga_value, gb_value, ga_out, gb_out, ga_gate, gb_gate, ga_up, gb_up, ga_down, gb_down = outs
    width = ga_query.shape[1]
    w = width // 2
    lower = lax.axis_index("tp") == 0

    def join(out, own, own_at, other, i):
        a = own[:, own_at + i * w : own_at + (i + 1) * w]
        b = other[:, i * w : (i + 1) * w]
        out[:, :w] = jnp.where(lower, a, b)
        out[:, w:] = jnp.where(lower, b, a)

    @pl.when(pl.program_id(0) == 0)
    def _():
        for f in range(hidden_units // tile):
            for n, out in enumerate((gb_gate, gb_up, ga_down)):
                out[:, f * tile : (f + 1) * tile] = first[:, (3 * f + n) * tile : (3 * f + n + 1) * tile]
        at = 3 * hidden_units
        ga_out[...] = first[:, at : at + inner]
        for i, out in enumerate((ga_gate, ga_up, gb_out)):
            join(out, first, at + inner, first_x, i)
        for i, out in enumerate((ga_query, ga_key, ga_value, gb_down)):
            join(out, second, 0, second_x, i)
        at = 4 * w
        gb_query[...] = second[:, at : at + inner]
        gb_key[...] = second[:, at + inner : at + inner + kw]
        gb_value[...] = second[:, at + inner + kw : at + inner + 2 * kw]


def unpack(block, grad, owned, hidden_units, tile, inner, kw):
    width, rows = block.shape[2], owned[0].shape[0]
    sizes = (width, inner, width, kw, width, kw, inner, width, width, hidden_units, width, hidden_units, hidden_units, width)
    outs = tuple(shape((rows, n), F32) for n in sizes)
    return pl.pallas_call(
        functools.partial(unpack_kernel, hidden_units, tile, inner, kw),
        grid=(block.shape[0],),
        out_shape=(shape(block.shape, BF),) * 2 + outs,
        in_specs=[stepped(block.shape, 1)] * 2 + [whole(a) for a in owned],
        out_specs=(stepped(block.shape, 1),) * 2 + tuple(whole(a) for a in outs),
        compiler_params=BIG,
        name="unpack",
    )(block, grad, *owned)


def rotary_tables(positions):
    half = HEAD_DIM // 2
    frequencies = THETA_BASE ** (-jnp.arange(half, dtype=F32) * 2.0 / HEAD_DIM)
    angles = frequencies[:, None] * positions.astype(F32)[None, :]
    return jnp.cos(angles), jnp.sin(angles)


def swap(values):
    return lax.ppermute(values, "tp", [(0, 1), (1, 0)])


def reduce_scatter_rows(grads, count):
    rows, columns = grads.shape
    index = lax.axis_index("ctx")
    held = grads.reshape(count, rows // count, columns)
    bit = 1
    while bit < count:
        mine = (index // bit) % 2
        pairs = held.reshape(held.shape[0] // 2, 2, held.shape[1], columns)
        kept = lax.dynamic_index_in_dim(pairs, mine, 1, keepdims=False)
        sent = lax.dynamic_index_in_dim(pairs, 1 - mine, 1, keepdims=False).astype(BF)
        held = kept.astype(F32) + lax.ppermute(sent, "ctx", [(i, i ^ bit) for i in range(count)]).astype(F32)
        bit *= 2
    return held[0]


def local(
    tokens, output_cotangent, segment_ids, variant, attn_gain, ffn_gain, q_gain, k_gain,
    query_matrix, key_matrix, value_matrix, output_matrix, gate_matrix, up_matrix, down_matrix,
    query_input_factor, query_output_factor, key_input_factor, key_output_factor,
    value_input_factor, value_output_factor, output_input_factor, output_output_factor,
    gate_input_factor, gate_output_factor, up_input_factor, up_output_factor,
    down_input_factor, down_output_factor,
):
    sequences, rows_here, width = tokens.shape
    count = lax.axis_size("ctx")
    index = lax.axis_index("ctx")
    inner, kw = query_matrix.shape[1], key_matrix.shape[1]
    key_heads = kw // HEAD_DIM
    units = sequences * key_heads
    parts = count // units
    stacked = query_input_factor.shape[0]
    reduce_here = stacked // count == RANK // 2
    tables = rotary_tables(index * rows_here + jnp.arange(rows_here, dtype=jnp.int32))
    weights = (query_matrix, key_matrix, value_matrix)
    ins = (query_input_factor, key_input_factor, value_input_factor)
    outs = (query_output_factor, key_output_factor, value_output_factor)

    output_matrix_other = swap(output_matrix)
    output_input_other = swap(output_input_factor)

    n1, h_one, pre, queries, keys_values, ac, bc, gains, pick, *chosen = project(
        variant, tokens, attn_gain, weights, ins, outs, q_gain, k_gain, tables,
        (
            gate_input_factor, up_input_factor, down_output_factor, gate_output_factor, up_output_factor, down_input_factor,
            output_output_factor, output_input_factor,
        ),
    )
    flat = lambda a: a.reshape(sequences * rows_here, -1)
    *kept, dh_down, attn, attn_other, d_hidden = attend(
        segment_ids, queries, keys_values, flat(output_cotangent), chosen[2], chosen[5], down_matrix, count, parts,
        key_heads, 0,
    )
    attn, attn_other = (a.reshape(sequences, inner, rows_here) for a in (attn, attn_other))
    mid, n2, h_out = middle(
        variant, tokens, attn, attn_other, ffn_gain, output_matrix, output_matrix_other,
        output_input_factor, output_input_other, output_output_factor,
    )

    cuts = tuple(rows_here * s for s in (0, sequences // 2, sequences))
    g_ffn, down, d_mid, d_attn, g_mid = feed(
        cuts, flat(n2), dh_down, *chosen[:2], *chosen[6:], output_matrix, ffn_gain, gate_matrix, up_matrix, down_matrix,
        *chosen[3:6], d_hidden, mid, output_cotangent, h_out, attn, 3,
    )
    d_attn = d_attn.reshape(queries.shape)
    d_attn, down = lax.optimization_barrier((d_attn, down))
    down_other = swap(down)
    early = (g_ffn, g_mid) if reduce_here else ()
    dq, dkv, *early = attend_back(d_attn, *kept, early, count, parts, 1)

    w = width // 2
    hidden_units = gate_matrix.shape[1]
    tile = feed_tile(hidden_units)
    at = 3 * hidden_units + inner
    shared = ((at, at + 3 * w), (0, 4 * w))
    input_grad, block_result, *ends = finish(
        reduce_here, count, dq.reshape(sequences, inner, rows_here), dkv.reshape(units, parts, 2 * HEAD_DIM, rows_here),
        pre, h_one, gains, tables, attn_gain, bc, pick, chosen[2], tokens, d_mid, n1, weights, ac,
        mid, down, down_other, output_cotangent, early, shared, 2,
    )
    if reduce_here:
        owned = ends
    else:
        per = RANK // 2
        pick = (jnp.arange(stacked // RANK, dtype=jnp.int32)[:, None] == variant[None, :]).astype(F32)
        owned, other = [], []
        for grads, (low, high) in zip((jnp.concatenate([g_ffn, g_mid], axis=1), ends[0]), shared):
            grads = grads.reshape(2, sequences, per, -1).astype(F32)
            dense = jnp.sum(pick[:, None, :, None, None] * grads[None], axis=2)
            owned.append(reduce_scatter_rows(dense.reshape(stacked, -1), count))
            other.append(swap(owned[-1][:, low:high]))
        owned = owned + other
    return tuple(unpack(block_result, input_grad, owned, hidden_units, tile, inner, kw))


def solution(mesh):
    rows, whole, columns = P(None, "ctx", None), P(), P(None, "tp")
    owned, owned_half = P("ctx", None), P("ctx", "tp")
    return jax.shard_map(
        local,
        mesh=mesh,
        in_specs=(rows, rows) + (whole,) * 6
        + (columns, columns, columns, P("tp", None), columns, columns, P("tp", None))
        + (whole, columns) * 3 + (columns, whole) + (whole, columns) * 2 + (columns, whole),
        out_specs=(
            rows, rows, owned, owned_half, owned, owned_half, owned, owned_half,
            owned_half, owned, owned, owned_half, owned, owned_half, owned_half, owned,
        ),
        check_vma=False,
    )
```

```python
import functools, jax, jax.numpy as jnp
from jax import lax
from jax.experimental import pallas as pl
from jax.experimental.pallas import tpu as pltpu
from jax.sharding import PartitionSpec as P

HEAD_DIM = 64
LOG2E = 1.4426950408889634
MESH = pl.DeviceIdType.MESH
SMEM = pl.BlockSpec(memory_space=pltpu.SMEM)
VM = pl.BlockSpec(memory_space=pltpu.VMEM)
RANK = 16
EPSILON = 1e-05
THETA_BASE = 1000000.0
BF = jnp.bfloat16
F32 = jnp.float32
NT = (((1,), (1,)), ((), ()))
BIG = pltpu.CompilerParams(vmem_limit_bytes=60 * 2**20)


def cost(rows, width, columns, products, moved):
    return pl.CostEstimate(flops=2 * products * rows * width * columns, bytes_accessed=moved, transcendentals=0)

ANYWHERE = pl.BlockSpec(memory_space=pl.ANY)


def mm(a, b):
    return jnp.dot(a, b, preferred_element_type=F32)


def mm_nt(a, b):
    return lax.dot_general(a, b, NT, preferred_element_type=F32)


def shape(dims, kind):
    return jax.ShapeDtypeStruct(dims, kind)


def remote(source, target, send, recv, device):
    return pltpu.make_async_remote_copy(
        src_ref=source, dst_ref=target, send_sem=send, recv_sem=recv, device_id=device, device_id_type=MESH
    )


def norm_back(u, gain, c):
    scale = lax.rsqrt(jnp.mean(u * u, axis=-1, keepdims=True) + EPSILON)
    y = u * scale
    w = c * gain
    return scale * (w - y * jnp.mean(w * y, axis=-1, keepdims=True))


def turn(values, cosine, sine):
    half = HEAD_DIM // 2
    a, b = values[:, :half], values[:, half:]
    return jnp.concatenate([a * cosine - b * sine, b * cosine + a * sine], axis=1)


def rank_halves(blocks):
    return jnp.concatenate([b[: RANK // 2] for b in blocks] + [b[RANK // 2 :] for b in blocks], axis=0)


def column(ref):
    return jnp.transpose(jnp.broadcast_to(ref[...][None, :], (128, ref.shape[0])))


def whole(array):
    return pl.BlockSpec(array.shape, lambda i: (0,) * len(array.shape), pipeline_mode=pl.Buffered(1))


def stepped(dims, per):
    return pl.BlockSpec((per,) + tuple(dims[1:]), lambda i: (i,) + (0,) * (len(dims) - 1))


def own_ranks(first, rows, ranks):
    row = lax.broadcasted_iota(jnp.int32, (rows, ranks), 0) // 128 + first // 128
    return row == lax.broadcasted_iota(jnp.int32, (rows, ranks), 1) // RANK


def feed_kernel(
    cuts, n2_ref, dhd_ref, ag, au, bo, ao, wo, gain_ref, wg_ref, wu_ref, wd_ref, bg_ref, bu_ref, ad_ref, dh_ref,
    mid_ref, cot_ref, hout_ref, attn_ref,
    grads_ref, down_ref, dmid_ref, dattn_ref, more_ref,
    hg, hu, hs, dn2_acc, dhg_acc, dhu_acc, down_acc, h_acc, hidden_s, dgate_s, dup_s, back_s, back_x, branch_s, more_s,
    send_sems, recv_sems,
):
    step = pl.program_id(0)
    rows, width = n2_ref.shape
    tiles, tile = hidden_s.shape[0], hidden_s.shape[2]
    seqs = rows // 128
    ranks = seqs * RANK
    chunks = len(cuts) - 1
    last = chunks * tiles
    f = lax.rem(step, tiles)
    across = {"tp": 1 - lax.axis_index("tp")}

    def compact(a, first=0):
        a = jnp.where(own_ranks(first, *a.shape), a, 0.0)
        return sum(a[:, i * RANK : (i + 1) * RANK] for i in range(seqs))

    def copy(c):
        there = pl.ds(cuts[c], cuts[c + 1] - cuts[c])
        return remote(back_s.at[there, :], back_x.at[there, :], send_sems.at[c], recv_sems.at[c], across)

    @pl.when(step == 0)
    def _():
        barrier = pltpu.get_barrier_semaphore()
        pl.semaphore_signal(barrier, inc=1, device_id=across, device_id_type=MESH)
        pl.semaphore_wait(barrier, 1)
        kept = own_ranks(0, rows, ranks)
        g = jnp.where(kept, mm_nt(n2_ref[...], ag[...]) * 2.0, 0.0)
        u = jnp.where(kept, mm_nt(n2_ref[...], au[...]) * 2.0, 0.0)
        hg[...] = g.astype(BF)
        hu[...] = u.astype(BF)
        for n, a in enumerate((g, u, dhd_ref[...].astype(F32))):
            turned = jnp.transpose(jnp.concatenate([a, jnp.zeros((rows, 128 - ranks), F32)], axis=1))
            rows_of = [turned[i * RANK : (i + 1) * RANK] for i in range(seqs)]
            hs[n] = rank_halves(rows_of).astype(BF)
        down_acc[...] = jnp.zeros_like(down_acc)
        h_acc[...] = jnp.zeros_like(h_acc)

    for c in range(chunks):
        first, part = cuts[c], cuts[c + 1] - cuts[c]
        here, top = slice(first, first + part), slice(0, part)

        @pl.when((step >= c * tiles) & (step < (c + 1) * tiles))
        def _(here=here, top=top):
            n2 = n2_ref[here, :]
            bg, bu = bg_ref[...], bu_ref[...]
            gate = mm(n2, wg_ref[...]) + mm(hg[here, :], bg)
            up = mm(n2, wu_ref[...]) + mm(hu[here, :], bu)
            sg = 1.0 / (1.0 + jnp.exp(-gate))
            silu = gate * sg
            hidden_s[f, here, :] = (silu * up).astype(BF)
            dh = dh_ref[here, :].astype(F32)
            dg = (dh * up * sg * (1.0 + gate * (1.0 - sg))).astype(BF)
            du = (dh * silu).astype(BF)
            dgate_s[f, here, :] = dg
            dup_s[f, here, :] = du
            terms = (
                (dn2_acc, mm_nt(dg, wg_ref[...]) + mm_nt(du, wu_ref[...])), (dhg_acc, mm_nt(dg, bg)), (dhu_acc, mm_nt(du, bu))
            )
            for acc, term in terms:
                acc[top, :] = jnp.where(f == 0, term, acc[top, :] + term)

        @pl.when(step == (c + 1) * tiles - 1)
        def _(c=c, here=here, top=top, first=first, part=part):
            back_s[here, :width] = dn2_acc[top, :].astype(BF)
            small = [compact(a[top, :], first) * 2 for a in (dhg_acc, dhu_acc)]
            back_s[here, width:] = jnp.concatenate(small + [jnp.zeros((part, 128 - 2 * RANK), F32)], axis=1).astype(BF)
            copy(c).start()

    @pl.when((step >= last) & (step < last + tiles))
    def _():
        hidden = hidden_s[f]
        down_acc[...] += mm(hidden, wd_ref[...])
        h_acc[...] += mm_nt(hidden, ad_ref[...])
        for n, kept in enumerate((dgate_s, dup_s, hidden_s)):
            grads_ref[:, n * tile : (n + 1) * tile] = mm(hs[n], kept[f]).astype(BF)

    for c in range(chunks):

        @pl.when(step == last + tiles + cuts[c] // 128)
        def _(c=c):
            copy(c).wait()

    @pl.when(step >= last + tiles)
    def _():
        s = step - last - tiles
        here = pl.ds(pl.multiple_of(s * 128, 128), 128)
        own = pl.ds(pl.multiple_of(s * RANK, RANK), RANK)
        mine = pl.ds(pl.multiple_of(lax.axis_index("tp") * (width // 2), width // 2), width // 2)
        down_ref[0, :, :width] = down_acc[here, :].astype(BF)
        h = jnp.where(own_ranks(s * 128, 128, ranks), h_acc[here, :], 0.0)
        h = sum(h[:, i * RANK : (i + 1) * RANK] for i in range(seqs))
        down_ref[0, :, width:] = jnp.concatenate([h, jnp.zeros((128, 128 - RANK), F32)], axis=1).astype(BF)
        total = back_s[here, :].astype(F32) + back_x[here, :].astype(F32)
        dh = total[:, width : width + 2 * RANK].astype(BF)
        c = total[:, :width] + mm(dh, jnp.concatenate([ag[own, :], au[own, :]], axis=0))
        d_mid = cot_ref[0].astype(F32) + norm_back(mid_ref[0], gain_ref[...][None, :], c)
        dmid_ref[0] = d_mid
        branch_s[...] = d_mid.astype(BF)
        dho = (mm_nt(branch_s[...], bo[own, :]) * 2.0).astype(BF)
        d_attn = mm_nt(branch_s[...], wo[...]) + mm(dho, ao[own, :])
        dattn_ref[0] = jnp.transpose(d_attn).astype(BF)
        wide = jnp.concatenate([dh, dho, hout_ref[0][:, :RANK] * 2, jnp.zeros((128, 128 - 4 * RANK), BF)], axis=1)
        t = jnp.transpose(wide.astype(F32)).astype(BF)
        both = mm(t[: 2 * RANK], n2_ref[here, mine])
        more_s[s] = jnp.concatenate(
            [
                mm_nt(t[2 * RANK : 3 * RANK], attn_ref[0]), both[:RANK], both[RANK:],
                mm(t[3 * RANK : 4 * RANK], branch_s[:, mine]),
            ],
            axis=1,
        )

    @pl.when(step == pl.num_programs(0) - 1)
    def _():
        more_ref[...] = rank_halves([more_s[i] for i in range(seqs)]).astype(BF)


def feed_tile(units):
    return 1152 if units % 1152 == 0 else units


def feed(cuts, n2, dhd, ag, au, bo, ao, wo, gain, wg, wu, wd, bg, bu, ad, dh, mid, cot, hout, attn, collective_id):
    rows, width = n2.shape
    stacked, units = bg.shape
    inner = wo.shape[0]
    tile = feed_tile(units)
    chunks, part = len(cuts) - 1, max(b - a for a, b in zip(cuts, cuts[1:]))
    seqs, tiles, ranks = rows // 128, units // tile, rows // 128 * RANK
    last = chunks * tiles
    early = lambda height: pl.BlockSpec((height, tile), lambda i: (0, jnp.where(i < last, lax.rem(i, tiles), tiles - 1)))
    late = lambda i: jnp.clip(i - last, 0, tiles - 1)
    by_seq = lambda dims: pl.BlockSpec((1,) + dims[1:], lambda i: (jnp.maximum(i - last - tiles, 0), 0, 0))
    vm, dma = pltpu.VMEM, pltpu.SemaphoreType.DMA
    more = shape((ranks, inner + 3 * (width // 2)), BF)
    wide = (seqs, 128, width + 128)
    return pl.pallas_call(
        functools.partial(feed_kernel, cuts),
        grid=(last + tiles + seqs,),
        out_shape=(shape((ranks, 3 * units), BF), shape(wide, BF), shape(mid.shape, F32), shape(attn.shape, BF), more),
        in_specs=[whole(a) for a in (n2, dhd, ag, au, bo, ao, wo, gain)]
        + [early(width), early(width), pl.BlockSpec((tile, width), lambda i: (late(i), 0)), early(stacked), early(stacked)]
        + [pl.BlockSpec((stacked, tile), lambda i: (0, late(i))), early(rows)]
        + [by_seq(a.shape) for a in (mid, cot, hout, attn)],
        out_specs=(
            pl.BlockSpec((ranks, 3 * tile), lambda i: (0, late(i))), by_seq(wide), by_seq(mid.shape), by_seq(attn.shape),
            whole(more),
        ),
        scratch_shapes=[vm((rows, ranks), BF)] * 2
        + [vm((3, ranks, rows), BF), vm((part, width), F32), vm((part, ranks), F32), vm((part, ranks), F32)]
        + [vm((rows, width), F32), vm((rows, ranks), F32)] + [vm((tiles, rows, tile), BF)] * 3
        + [vm((rows, width + 128), BF)] * 2 + [vm((128, width), BF), vm((seqs, RANK, more.shape[1]), F32)]
        + [dma((chunks,)), dma((chunks,))],
        compiler_params=pltpu.CompilerParams(
            collective_id=collective_id, has_side_effects=True, vmem_limit_bytes=63 * 2**20
        ),
        cost_estimate=cost(rows, width, units, 5, 12 * width * units),
        name="feed_forward",
    )(n2, dhd, ag, au, bo, ao, wo, gain, wg, wu, wd, bg, bu, ad, dh, mid, cot, hout, attn)


TILE = 512
BLOCKS = TILE // 128
SUB = 512
SCALE = HEAD_DIM**-0.5


def document_starts(seg_ref, seq, starts):
    sequences, length = seg_ref.shape
    blocks = length // 128
    number = lax.broadcasted_iota(jnp.int32, (sequences, length), 0)
    row = jnp.sum(jnp.where(number == seq, seg_ref[...], 0), axis=0, keepdims=True)
    segs = jnp.concatenate([row[:, b * 128 : (b + 1) * 128] for b in range(blocks)], axis=0)
    lane = lax.broadcasted_iota(jnp.int32, segs.shape, 1)
    position = lax.broadcasted_iota(jnp.int32, segs.shape, 0) * 128 + lane

    def down(a, n):
        return jnp.concatenate([jnp.zeros((n, 128), jnp.int32), a[: blocks - n]], axis=0)

    before = jnp.where(lane == 0, pltpu.roll(down(segs, 1), 1, 1), pltpu.roll(segs, 1, 1))
    start = jnp.where((segs != before) & (position > 0), position, 0)
    step = 1
    while step < 128:
        start = jnp.maximum(start, jnp.where(lane >= step, pltpu.roll(start, step, 1), 0))
        step *= 2
    carried = down(jnp.broadcast_to(start[:, 127:], segs.shape), 1)
    step = 1
    while step < blocks:
        carried = jnp.maximum(carried, down(carried, step))
        step *= 2
    start = jnp.maximum(start, carried)
    for b in range(blocks):
        starts[b] = start[b : b + 1]


def query_rows(starts, tile, stride, part):
    lanes = lax.broadcasted_iota(jnp.int32, (1, 128), 1)
    blocks = [(BLOCKS * tile + b) * stride + part for b in range(BLOCKS)]
    position = jnp.concatenate([b * 128 + lanes for b in blocks], axis=1)
    return position, jnp.concatenate([starts[b] for b in blocks], axis=1)


def key_range(tile, stride, part):
    return BLOCKS * tile * stride // BLOCKS + part // BLOCKS, ((BLOCKS * tile + BLOCKS - 1) * stride + part) // BLOCKS + 1


def keep_pairs(p, first, start, position, causal):
    key = lax.broadcasted_iota(jnp.int32, p.shape, 0)
    keep = key >= jnp.broadcast_to(start - first, p.shape)
    if causal:
        keep = keep & (key <= jnp.broadcast_to(position - first, p.shape))
    return jnp.where(keep, p, 0.0)


def across_blocks(ref, tile, rows):
    return jnp.concatenate([ref[BLOCKS * tile + b, rows, :] for b in range(BLOCKS)], axis=1)


def load_keys(kv_ref, kb, vt):
    def load(j, _):
        for b in range(BLOCKS):
            kb[j, b * 128 : (b + 1) * 128, :] = jnp.transpose(kv_ref[BLOCKS * j + b, :HEAD_DIM, :])
            vt[j, :HEAD_DIM, b * 128 : (b + 1) * 128] = kv_ref[BLOCKS * j + b, HEAD_DIM:, :]
        vt[j, HEAD_DIM:, :] = jnp.ones((16, TILE), BF)
        return 0

    lax.fori_loop(0, kv_ref.shape[0] // BLOCKS, load, 0)


def head_forward(h, stride, part, q_ref, starts, kb, vt, acc, of_ref, lse_ref, done):
    rows = pl.ds(h * HEAD_DIM, HEAD_DIM)

    def q_step(i, _):
        position, start = query_rows(starts, i, stride, part)
        qt = across_blocks(q_ref, i, rows)
        acc[...] = jnp.zeros_like(acc)

        def k_step(causal, j, _):
            total = acc[...]
            for c in range(TILE // SUB):
                keys = slice(c * SUB, (c + 1) * SUB)
                p = jnp.exp2(mm(kb[j, keys, :], qt) * (LOG2E * SCALE))
                p = keep_pairs(p, j * TILE + c * SUB, start, position, causal)
                total = total + mm(vt[j, :, keys], p.astype(BF))
            acc[...] = total
            return 0

        whole, end = key_range(i, stride, part)
        lax.fori_loop(0, whole, functools.partial(k_step, False), 0)
        lax.fori_loop(whole, end, functools.partial(k_step, True), 0)
        total = acc[HEAD_DIM : HEAD_DIM + 1, :]
        lse_ref[h, i] = jnp.broadcast_to(jnp.log2(total), (8, TILE))
        out = acc[:HEAD_DIM, :] / total
        for b in range(BLOCKS):
            of_ref[BLOCKS * i + b, rows, :] = out[:, b * 128 : (b + 1) * 128]
        done(i, out.astype(BF))
        return 0

    lax.fori_loop(0, q_ref.shape[0] // BLOCKS, q_step, 0)


def pair_backward(h, i, j, causal, stride, part, qt, q3, dot_t, do3, lse_ref, delta, starts, kb, vb, kt, dqt, dk, dv):
    position, start = query_rows(starts, i, stride, part)
    dq = dqt[h, i]
    for c in range(TILE // SUB):
        keys = slice(c * SUB, (c + 1) * SUB)
        p = jnp.exp2(mm(kb[j, keys, :], qt[h, i]) * (LOG2E * SCALE) - lse_ref[h, i, 0:1, :])
        p = keep_pairs(p, j * TILE + c * SUB, start, position, causal)
        dp = mm(vb[j, keys, :], dot_t[h, i])
        ds = (p * (dp - delta[h, i, 0:1, :])).astype(BF)
        dv[j, keys, :] += mm(p.astype(BF), do3[h, i])
        dk[j, keys, :] += mm(ds, q3[h, i])
        dq = dq + mm(kt[j, :, keys], ds)
    dqt[h, i] = dq


def head_rows(h):
    return pl.ds(h * HEAD_DIM, HEAD_DIM)


def loop(low, high, step):
    def body(k, _):
        step(k)
        return 0

    lax.fori_loop(low, high, body, 0)


def class_copy(count, parts, source, target, send, recv):
    def make(index, sender):
        return remote(
            source(index), target(sender), send.at[index], recv.at[sender],
            {"ctx": index * parts + lax.rem(lax.axis_index("ctx"), parts)},
        )

    return make


def owner_rows(total, pick_ref, k, sequences):
    per = RANK // 2
    row = jnp.zeros((per, total.shape[1]), F32)
    for s in range(sequences):
        row = row + total[s * per : (s + 1) * per] * pick_ref[k, s][:, :1]
    half = total.shape[1] // 2
    return jnp.concatenate([row[:, :half], row[:, half:]], axis=0).astype(BF)


def unfold_rows(rows_ref, at, block):
    per, half = RANK // 2, block.shape[1]
    rows_ref[:, at : at + half] = block[:per].astype(F32)
    rows_ref[:, at + half : at + 2 * half] = block[per:].astype(F32)


class EarlyReduction:
    def __init__(self, me, grads, y_sum, own, core_in, plane, y_in, loads, twin_sends, twin_recvs, y_sems):
        self.y_sum, self.own, self.core_in, self.plane, self.y_in = y_sum, own, core_in, plane, y_in
        chip, core = me // 2, lax.rem(me, 2)
        self.y = lax.rem(chip, 2)
        self.loads, self.to_twin, at = [], [], 0
        for i, ref in enumerate(grads):
            size, place = ref.shape[0] // 2, slice(at, at + ref.shape[1])
            at += ref.shape[1]
            half = lambda who, ref=ref, size=size: ref.at[pl.ds(pl.multiple_of(who * size, 16), size), :]
            self.loads.append(pltpu.make_async_copy(half(core), own.at[:, place], loads.at[i]))
            twin = {"ctx": 2 * chip + 1 - core}
            self.to_twin.append(remote(half(1 - core), core_in.at[:, place], twin_sends.at[i], twin_recvs.at[i], twin))
        self.known, self.width = at, plane.shape[1] // 2
        self.to_y = remote(
            plane.at[:, pl.ds(pl.multiple_of((1 - self.y) * self.width, 128), self.width)], y_in, y_sems.at[0],
            y_sems.at[1], {"ctx": 2 * (chip + 1 - 2 * self.y) + core},
        )

    def begin(self):
        for c in self.loads + self.to_twin:
            c.start()

    def over_cores(self):
        for c in self.loads:
            c.wait()
        for c in self.to_twin:
            c.wait_recv()
        self.plane[:, : self.known] = (self.own[...].astype(F32) + self.core_in[...].astype(F32)).astype(BF)
        rest = self.plane.shape[1] - self.known
        if rest:
            self.plane[:, self.known :] = jnp.zeros((self.plane.shape[0], rest), BF)
        self.to_y.start()

    def over_y(self):
        self.to_y.wait()
        mine = self.plane[:, pl.ds(pl.multiple_of(self.y * self.width, 128), self.width)]
        self.y_sum[...] = (mine.astype(F32) + self.y_in[...].astype(F32)).astype(BF)
        for c in self.to_twin:
            c.wait_send()


def early_scratch(grads, total):
    vm, dma = pltpu.VMEM, pltpu.SemaphoreType.DMA
    rows, known = grads[0].shape[0] // 2, sum(g.shape[1] for g in grads)
    return [vm((rows, known), BF), vm((rows, known), BF), vm((rows, total), BF), vm((rows, total // 2), BF)] + [dma((2,))] * 4


def padded(columns, chips):
    return -(-columns // (256 * chips)) * 256 * chips


def attend_back_kernel(count, parts, reduce, do_ref, q_all, kv_all, of_ref, lse_ref, starts, *refs):
    refs = list(refs)
    take = lambda n: [refs.pop(0) for _ in range(n)]
    grads = take(2) if reduce else []
    dq_home, dkv_home = take(2)
    early = EarlyReduction(lax.axis_index("ctx"), grads, *take(9)) if reduce else None
    attend_back_body(
        count, parts, early,
        do_ref, q_all, kv_all, of_ref, lse_ref, starts, dq_home, dkv_home, *refs,
    )


def attend_back_body(
    count, parts, early, do_ref, q_all, kv_all, of_ref, lse_ref, starts, dq_home, dkv_home,
    do_in, dq_buf, dkv_buf, kb, vb, kt, qt, q3, dot_t, do3, delta, dqt, dk, dv,
    do_send, do_recv, dq_send, dq_recv, dkv_send, dkv_recv, own_sems,
):
    me = lax.axis_index("ctx")
    units = count // parts
    unit, part = me // parts, lax.rem(me, parts)
    group, tiles, ktiles = q_all.shape[1] // HEAD_DIM, units // BLOCKS, count // BLOCKS
    barrier = pltpu.get_barrier_semaphore()
    loop(
        1, count,
        lambda k: pl.semaphore_signal(barrier, inc=1, device_id={"ctx": lax.rem(me + k, count)}, device_id_type=MESH),
    )
    own_do = pltpu.make_async_copy(do_ref.at[unit], do_in.at[unit], own_sems.at[0])
    own_do.start()
    pl.semaphore_wait(barrier, count - 1)
    if early:
        early.begin()

    def turn_of(k):
        return lax.rem(unit + k, units)

    do_copy = [
        class_copy(
            count, parts, lambda i, h=h: do_ref.at[i, head_rows(h), :], lambda i, h=h: do_in.at[i, head_rows(h), :],
            do_send.at[h], do_recv.at[h],
        )
        for h in range(group)
    ]
    dq_copy = [
        class_copy(
            count, parts, lambda i, h=h: dq_buf.at[h, i], lambda i, h=h: dq_home.at[i, head_rows(h), :],
            dq_send.at[h], dq_recv.at[h],
        )
        for h in range(group)
    ]

    def dkv_copy(device, sender):
        return remote(dkv_buf.at[device], dkv_home.at[sender], dkv_send.at[device], dkv_recv.at[sender], {"ctx": device})

    own_dkv = pltpu.make_async_copy(dkv_buf.at[me], dkv_home.at[me], own_sems.at[1])

    def own_dq(h):
        return pltpu.make_async_copy(dq_buf.at[h, unit], dq_home.at[unit, head_rows(h), :], own_sems.at[2 + h])

    for h in range(group):
        loop(1, units, lambda k, h=h: do_copy[h](turn_of(k), unit).start())

    def load_kv(j):
        for b in range(BLOCKS):
            lanes = slice(b * 128, (b + 1) * 128)
            kt[j, :, lanes] = kv_all[BLOCKS * j + b, :HEAD_DIM, :]
            kb[j, lanes, :] = jnp.transpose(kv_all[BLOCKS * j + b, :HEAD_DIM, :])
            vb[j, lanes, :] = jnp.transpose(kv_all[BLOCKS * j + b, HEAD_DIM:, :])

    def load_q(i):
        for h in range(group):
            for b in range(BLOCKS):
                lanes = slice(b * 128, (b + 1) * 128)
                q = q_all[BLOCKS * i + b, h * HEAD_DIM : (h + 1) * HEAD_DIM, :]
                qt[h, i, :, lanes] = q
                q3[h, i, lanes, :] = jnp.transpose(q)
            dqt[h, i] = jnp.zeros((HEAD_DIM, TILE), F32)

    def load_do(h, i):
        rows = slice(h * HEAD_DIM, (h + 1) * HEAD_DIM)
        for b in range(BLOCKS):
            lanes = slice(b * 128, (b + 1) * 128)
            g = do_in[BLOCKS * i + b, rows, :]
            dot_t[h, i, :, lanes] = g
            do3[h, i, lanes, :] = jnp.transpose(g)
            d = jnp.sum(g.astype(F32) * of_ref[BLOCKS * i + b, rows, :], axis=0, keepdims=True)
            delta[h, i, :, lanes] = jnp.broadcast_to(d, (8, 128))

    loop(0, ktiles, load_kv)
    loop(0, tiles, load_q)

    def last_tile(i):
        return key_range(i, parts, part)[1] - 1

    def run(h, j):
        low = jnp.maximum(BLOCKS * j - part + parts - 1, 0) // (BLOCKS * parts)
        full = jnp.minimum((BLOCKS * (j + 1) - part + BLOCKS * parts - 1) // (BLOCKS * parts), tiles)

        def pair(causal, i):
            pair_backward(
                h, i, j, causal, parts, part, qt, q3, dot_t, do3, lse_ref, delta, starts, kb, vb, kt, dqt, dk, dv
            )

        loop(low, full, functools.partial(pair, True))
        loop(full, tiles, functools.partial(pair, False))

    def emit_keys(j):
        for b in range(BLOCKS):
            rows = slice(b * 128, (b + 1) * 128)
            block = BLOCKS * j + b
            dkv_buf[block, :HEAD_DIM, :] = jnp.transpose(dk[j, rows, :] * SCALE).astype(BF)
            dkv_buf[block, HEAD_DIM:, :] = jnp.transpose(dv[j, rows, :]).astype(BF)

            @pl.when(block == me)
            def _():
                own_dkv.start()

            @pl.when(block != me)
            def _():
                dkv_copy(block, me).start()

    def emit_queries(h, j, i):
        @pl.when(last_tile(i) == j)
        def _():
            for b in range(BLOCKS):
                block = BLOCKS * i + b
                dq_buf[h, block] = (dqt[h, i, :, b * 128 : (b + 1) * 128] * SCALE).astype(BF)

                @pl.when(block == unit)
                def _():
                    own_dq(h).start()

                @pl.when(block != unit)
                def _():
                    dq_copy[h](block, unit).start()

    dk[...] = jnp.zeros_like(dk)
    dv[...] = jnp.zeros_like(dv)
    own_do.wait()
    if early:
        early.over_cores()
    for h in range(group):
        loop(1, units, lambda k, h=h: do_copy[h](unit, turn_of(k)).wait_recv())
        loop(0, tiles, functools.partial(load_do, h))

        def key_step(j, h=h):
            run(h, j)
            if h == group - 1:
                emit_keys(j)
            loop(0, tiles, functools.partial(emit_queries, h, j))

        loop(0, ktiles, key_step)
        if early and h == 1:
            early.over_y()
    for h in range(group):
        own_dq(h).wait()
    own_dkv.wait()

    def finish_full(k):
        other = lax.rem(me + k, count)
        dkv_copy(other, me).wait_send()
        dkv_copy(me, other).wait_recv()

    loop(1, count, finish_full)

    def finish_class(k):
        other = turn_of(k)
        for h in range(group):
            do_copy[h](other, unit).wait_send()
            dq_copy[h](other, unit).wait_send()
            dq_copy[h](unit, other).wait_recv()

    loop(1, units, finish_class)


def attend_back(do, q, kv, of, lse, starts, early, count, parts, collective_id):
    units, qrows, _ = q.shape
    group, tiles, ktiles = qrows // HEAD_DIM, units // BLOCKS, count // BLOCKS
    dma, vm = pltpu.SemaphoreType.DMA, pltpu.VMEM
    sums, scratch = (), []
    if early:
        total = padded(sum(g.shape[1] for g in early), count // 2)
        sums = (shape((early[0].shape[0] // 2, total // 2), BF),)
        scratch = early_scratch(early, total)
    return pl.pallas_call(
        functools.partial(attend_back_kernel, count, parts, bool(early)),
        out_shape=(shape(q.shape, BF), shape(kv.shape, BF)) + sums,
        in_specs=[ANYWHERE] + [VM] * 5 + [ANYWHERE] * len(early),
        out_specs=(ANYWHERE, ANYWHERE) + (VM,) * len(sums),
        scratch_shapes=scratch + [vm(q.shape, BF), vm((group, units, HEAD_DIM, 128), BF), vm(kv.shape, BF)]
        + [vm((ktiles, TILE, HEAD_DIM), BF)] * 2 + [vm((ktiles, HEAD_DIM, TILE), BF)]
        + [vm((group, tiles, HEAD_DIM, TILE), BF), vm((group, tiles, TILE, HEAD_DIM), BF)] * 2
        + [vm((group, tiles, 8, TILE), F32), vm((group, tiles, HEAD_DIM, TILE), F32)]
        + [vm((ktiles, TILE, HEAD_DIM), F32)] * 2
        + [dma((group, units))] * 4 + [dma((count,))] * 2 + [dma((2 + group,))],
        compiler_params=pltpu.CompilerParams(
            collective_id=collective_id, has_side_effects=True, vmem_limit_bytes=60 * 2**20
        ),
        name="attend_back",
    )(do, q, kv, of, lse, starts, *early)


class Names:
    def __init__(self, names, refs):
        assert len(names) == len(refs)
        self.__dict__.update(zip(names, refs))


FACTORS = ("ag", "au", "bd", "bg", "bu", "ad", "bo", "ao")
FORWARD_NEAR = ("variant", "x", "gain_one", "gain_two", "q_gain", "k_gain", "cosine", "sine", "segs") + (
    "wq", "wk", "wv", "aq", "ak", "av", "bq", "bk", "bv",
)
FORWARD_FAR = ("cot", "wd", "wo") + FACTORS
FORWARD_SMALL = ("h_one", "ac", "bc", "gains", "pick", "lse", "starts", "dhd", "h_out")
FORWARD_SAVED = ("n1", "pre", "q_all", "kv_all", "of", "home", "mid", "n2") + tuple("c_" + f for f in FACTORS)
FORWARD_OUT = FORWARD_SMALL + FORWARD_SAVED + ("dh",)
FORWARD_BUFFERS = ("cot_s", "wd_s", "wo_s", "wo_x", "ao_x", "dh_s", "q_msg", "kv_msg", "o_buf", "kb", "vt", "acc")
FORWARD_BUFFERS += ("home_x", "lhs", "lhs_x")
FORWARD_SEMS = ("far_sems", "save_sems", "dh_sems", "kv_send", "kv_recv", "q_send", "q_recv", "o_send", "o_recv")
FORWARD_SEMS += ("x_send", "x_recv", "own_sems", "w_send", "w_recv")


def forward_kernel(count, parts, *refs):
    names = FORWARD_NEAR + FORWARD_FAR + FORWARD_OUT
    names += tuple(f + "_s" for f in FACTORS) + tuple(n + "_s" for n in FORWARD_SAVED) + FORWARD_BUFFERS + FORWARD_SEMS
    r = Names(names, refs)
    me = lax.axis_index("ctx")
    units = count // parts
    unit, part = me // parts, lax.rem(me, parts)
    sequences, rows, width = r.x.shape
    qw, kw = r.wq.shape[1], r.wk.shape[1]
    heads_k = kw // HEAD_DIM
    group = qw // kw
    ranks = sequences * RANK
    across = {"tp": 1 - lax.axis_index("tp")}
    core = lax.rem(me, 2)
    twin = {"ctx": me + 1 - 2 * core}

    def turn_of(k):
        return lax.rem(unit + k, units)

    barrier = pltpu.get_barrier_semaphore()
    pl.semaphore_signal(barrier, inc=1, device_id=across, device_id_type=MESH)
    loop(
        1, count,
        lambda k: pl.semaphore_signal(barrier, inc=1, device_id={"ctx": lax.rem(me + k, count)}, device_id_type=MESH),
    )
    tiles, tile = r.wd_s.shape[0], r.wd_s.shape[1]
    far = [(r.cot, r.cot_s)] + [(r.wd.at[pl.ds(f * tile, tile), :], r.wd_s.at[f]) for f in range(tiles)]
    far += [(r.wo, r.wo_s)] + [(getattr(r, f), getattr(r, f + "_s")) for f in FACTORS]
    far = [pltpu.make_async_copy(a, b, r.far_sems.at[i]) for i, (a, b) in enumerate(far)]
    for c in far:
        c.start()
    saves = {
        n: pltpu.make_async_copy(getattr(r, n + "_s"), getattr(r, n), r.save_sems.at[i]) for i, n in enumerate(FORWARD_SAVED)
    }

    def kv_copy(index, to_part, sender):
        device = index * parts + to_part
        return remote(r.kv_msg.at[index], r.kv_all_s.at[sender], r.kv_send.at[device], r.kv_recv.at[sender], {"ctx": device})

    q_copy = [
        class_copy(
            count, parts, lambda i, h=h: r.q_msg.at[i, head_rows(h), :], lambda i, h=h: r.q_all_s.at[i, head_rows(h), :],
            r.q_send.at[h], r.q_recv.at[h],
        )
        for h in range(group)
    ]
    o_copy = [
        class_copy(
            count, parts, lambda i, h=h: r.o_buf.at[h, i], lambda i, h=h: r.home_s.at[i, head_rows(h), :],
            r.o_send.at[h], r.o_recv.at[h],
        )
        for h in range(group)
    ]

    def x_copy(h, i):
        place = (i, head_rows(h), slice(None))
        return remote(r.home_s.at[place], r.home_x.at[place], r.x_send.at[h, i], r.x_recv.at[h, i], across)

    column_of = lax.broadcasted_iota(jnp.int32, (RANK, r.aq.shape[0]), 1)
    rank_of = lax.broadcasted_iota(jnp.int32, (RANK, r.aq.shape[0]), 0)
    chooser = [jnp.where(column_of == r.variant[s] * RANK + rank_of, 1.0, 0.0).astype(BF) for s in range(sequences)]
    choosers = jnp.concatenate(chooser, axis=0)
    stacked = lax.broadcasted_iota(jnp.int32, (1, r.aq.shape[0]), 1) // RANK
    cosine, sine = r.cosine[...], r.sine[...]
    qg, kg = column(r.q_gain), column(r.k_gain)
    gain = r.gain_one[...][None, :]

    def prepare(t, gains):
        heads = t.reshape(t.shape[0] // HEAD_DIM, HEAD_DIM, rows)
        scale = lax.rsqrt(jnp.mean(heads * heads, axis=1, keepdims=True) + EPSILON)
        return turn(heads * scale * gains, cosine, sine).astype(BF)

    def project(p):
        for s in (2 * p, 2 * p + 1):
            x = r.x[s].astype(F32)
            scale = lax.rsqrt(jnp.mean(x * x, axis=-1, keepdims=True) + EPSILON)
            r.n1_s[s] = (x * scale * gain).astype(BF)
        n1 = jnp.concatenate([r.n1_s[2 * p], r.n1_s[2 * p + 1]], axis=0)
        low = [mm_nt(n1, a[...]) for a in (r.aq, r.ak, r.av)]
        base = [mm(n1, w[...]) for w in (r.wq, r.wk, r.wv)]
        for i in (0, 1):
            s = 2 * p + i
            half = slice(i * rows, (i + 1) * rows)
            own = jnp.where(stacked == r.variant[s], 1.0, 0.0)
            h = [(a[half] * own).astype(BF) for a in low]
            small = [mm_nt(a, chooser[s]) for a in h] + [jnp.zeros((rows, 128 - 3 * RANK), F32)]
            r.h_one[s] = jnp.concatenate(small, axis=1).astype(BF)
            q, k, val = (
                jnp.transpose(base[n][half] + mm(h[n] * 2, f[...])) for n, f in enumerate((r.bq, r.bk, r.bv))
            )
            r.pre_s[s, :qw, :] = q
            r.pre_s[s, qw:, :] = k
            here = slice(s * heads_k, (s + 1) * heads_k)
            r.q_msg[here] = prepare(q, qg).reshape(heads_k, group * HEAD_DIM, rows)
            r.kv_msg[here, :HEAD_DIM, :] = prepare(k, kg)
            r.kv_msg[here, HEAD_DIM:, :] = val.astype(BF).reshape(heads_k, HEAD_DIM, rows)

    def own_kv():
        return pltpu.make_async_copy(r.kv_msg.at[unit], r.kv_all_s.at[me], r.own_sems.at[0])

    def own_q():
        return pltpu.make_async_copy(r.q_msg.at[unit], r.q_all_s.at[unit], r.own_sems.at[1])

    per_pair = 2 * heads_k

    def send_keys(p):
        def step(k):
            index = p * per_pair + lax.rem(unit + k, per_pair)
            for t in range(parts):

                @pl.when(index * parts + t != me)
                def _():
                    kv_copy(index, t, me).start()

            @pl.when(index != unit)
            def _():
                q_copy[0](index, unit).start()

            @pl.when(index == unit)
            def _():
                own_kv().start()
                own_q().start()

        loop(0, per_pair, step)

    part_rows = r.wo_s.shape[0] // 2
    rows_of = lambda who: pl.ds(pl.multiple_of(who * part_rows, 16), part_rows)
    w_copies = [
        remote(r.wo_s.at[rows_of(core), :], r.wo_x.at[rows_of(core), :], r.w_send.at[0], r.w_recv.at[0], across),
        remote(r.wo_x.at[rows_of(core), :], r.wo_x.at[rows_of(core), :], r.w_send.at[1], r.w_recv.at[1], twin),
        remote(r.c_ao_s, r.ao_x, r.w_send.at[2], r.w_recv.at[2], across),
    ]

    project(0)
    pl.semaphore_wait(barrier, count)
    send_keys(0)
    for p in range(1, sequences // 2):
        project(p)
        send_keys(p)
    for h in range(1, group):
        loop(1, units, lambda k, h=h: q_copy[h](turn_of(k), unit).start())
    for n in ("n1", "pre"):
        saves[n].start()
    far[1 + tiles].wait()
    w_copies[0].start()

    def choose(names):
        for f in names:
            far[2 + tiles + FACTORS.index(f)].wait()
            getattr(r, "c_" + f + "_s")[...] = mm(choosers, getattr(r, f + "_s")[...]).astype(BF)
            saves["c_" + f].start()

    document_starts(r.segs, unit // heads_k, r.starts)
    choose(("ao", "bd", "ad"))
    w_copies[2].start()
    far[0].wait()
    d = mm_nt(r.cot_s[...], r.c_bd_s[...]) * 2.0
    r.dhd[...] = jnp.where(own_ranks(0, *d.shape), d, 0.0).astype(BF)
    dh_saves = []
    for f in range(tiles):
        far[1 + f].wait()
        columns = slice(f * tile, (f + 1) * tile)
        r.dh_s[:, columns] = (mm_nt(r.cot_s[...], r.wd_s[f]) + mm(r.dhd[...], r.c_ad_s[:, columns])).astype(BF)
        dh_saves.append(pltpu.make_async_copy(r.dh_s.at[:, columns], r.dh.at[:, columns], r.dh_sems.at[f]))
        dh_saves[-1].start()

    own_kv().wait()
    own_q().wait()
    loop(1, count, lambda k: kv_copy(unit, part, lax.rem(me + k, count)).wait_recv())
    load_keys(r.kv_all_s, r.kb, r.vt)
    saves["kv_all"].start()

    def keep_own(h):
        return pltpu.make_async_copy(r.o_buf.at[h, unit], r.home_s.at[unit, head_rows(h), :], r.own_sems.at[2 + h])

    def pass_on(h, low, high):
        if low == 0:
            keep_own(h).wait()
            x_copy(h, unit).start()

        def relay(k):
            other = turn_of(units - k)
            o_copy[h](unit, other).wait_recv()
            x_copy(h, other).start()

        loop(max(low, 1), high, relay)

    tiles_q = units // BLOCKS
    for h in range(group):
        loop(1, units, lambda k, h=h: q_copy[h](unit, turn_of(k)).wait_recv())
        if h == group - 1:
            saves["q_all"].start()

        def done(i, out, h=h):
            for b in range(BLOCKS):
                block = BLOCKS * i + b
                r.o_buf[h, block] = out[:, b * 128 : (b + 1) * 128]

                @pl.when(block == unit)
                def _():
                    keep_own(h).start()

                @pl.when(block != unit)
                def _():
                    o_copy[h](block, unit).start()

            if h > 0:
                for n in (1, 2):

                    @pl.when(i == tiles_q - 3 + n)
                    def _():
                        pass_on(h - 1, (n - 1) * units // 2, n * units // 2)

        head_forward(h, parts, part, r.q_all_s, r.starts, r.kb, r.vt, r.acc, r.of_s, r.lse, done)
        if h == 0:
            w_copies[0].wait_recv()
            w_copies[1].start()
    saves["of"].start()
    choose(("ag", "au", "bg", "bu", "bo"))
    pass_on(group - 1, 0, units)
    for s in range(sequences):
        r.ac[s] = jnp.concatenate([mm(chooser[s], a[...]) for a in (r.aq, r.ak, r.av)], axis=0).astype(BF)
        r.bc[s] = jnp.concatenate([mm(chooser[s], b[...]) for b in (r.bq, r.bk, r.bv)], axis=1).astype(BF)
        for v in range(r.pick.shape[0]):
            r.pick[v, s] = jnp.full((8, 128), jnp.where(r.variant[s] == v, 1.0, 0.0), F32)
    r.gains[0], r.gains[1] = qg, kg
    saves["home"].start()
    w_copies[1].wait_recv()
    w_copies[2].wait_recv()
    for h in range(group):
        loop(0, units, lambda i, h=h: x_copy(h, i).wait_recv())

    gain = r.gain_two[...][None, :]
    for p in range(sequences // 2):
        for i in (0, 1):
            half = slice(i * rows, (i + 1) * rows)
            for lhs, home in ((r.lhs, r.home_s), (r.lhs_x, r.home_x)):
                blocks = home[(2 * p + i) * heads_k : (2 * p + i + 1) * heads_k]
                lhs[half, :] = jnp.transpose(blocks.reshape(qw, rows))
        out = mm(r.lhs[...], r.wo_s[...]) + mm(r.lhs_x[...], r.wo_x[...])
        for i in (0, 1):
            s = 2 * p + i
            half, own = slice(i * rows, (i + 1) * rows), slice(s * RANK, (s + 1) * RANK)
            h = (mm_nt(r.lhs[half, :], r.c_ao_s[own, :]) + mm_nt(r.lhs_x[half, :], r.ao_x[own, :])).astype(BF)
            r.h_out[s] = jnp.concatenate([h, jnp.zeros((rows, 128 - RANK), BF)], axis=1)
            mid = r.x[s].astype(F32) + (out[half] + mm(h * 2, r.c_bo_s[own, :]))
            r.mid_s[s] = mid
            scale = lax.rsqrt(jnp.mean(mid * mid, axis=-1, keepdims=True) + EPSILON)
            r.n2_s[s] = (mid * scale * gain).astype(BF)
    saves["mid"].start()
    saves["n2"].start()

    for c in list(saves.values()) + dh_saves:
        c.wait()
    for c in w_copies:
        c.wait_send()

    def finish_full(k):
        other = lax.rem(me + k, count)
        kv_copy(other // parts, lax.rem(other, parts), me).wait_send()

    loop(1, count, finish_full)
    for h in range(group):

        def finish_block(k, h=h):
            q_copy[h](turn_of(k), unit).wait_send()
            o_copy[h](turn_of(k), unit).wait_send()

        loop(1, units, finish_block)
        loop(0, units, lambda i, h=h: x_copy(h, i).wait_send())


def forward(near, far, count, parts, collective_id):
    n = Names(FORWARD_NEAR + FORWARD_FAR, tuple(near) + tuple(far))
    sequences, rows, width = n.x.shape
    qw, kw = n.wq.shape[1], n.wk.shape[1]
    units, group = count // parts, qw // kw
    tiles, ktiles = units // BLOCKS, count // BLOCKS
    hidden_units, tile = n.wd.shape[0], feed_tile(n.wd.shape[0])
    spare, ranks = hidden_units // tile, sequences * RANK
    q_shape, kv_shape = (units, group * HEAD_DIM, rows), (count, 2 * HEAD_DIM, rows)
    small = (
        shape((sequences, rows, 128), BF), shape((sequences, 3 * RANK, width), BF), shape((sequences, RANK, qw + 2 * kw), BF),
        shape((2, HEAD_DIM, rows), F32), shape((n.aq.shape[0] // RANK, sequences, 8, 128), F32),
        shape((group, tiles, 8, TILE), F32), shape((count, 1, 128), jnp.int32), shape((sequences * rows, ranks), BF),
        shape((sequences, rows, 128), BF),
    )
    saved = (
        shape(n.x.shape, BF), shape((sequences, qw + kw, rows), F32), shape(q_shape, BF), shape(kv_shape, BF),
        shape(q_shape, F32), shape(q_shape, BF), shape(n.x.shape, F32), shape(n.x.shape, BF),
    ) + tuple(shape((ranks, getattr(n, f).shape[1]), BF) for f in FACTORS)
    dma, vm = pltpu.SemaphoreType.DMA, pltpu.VMEM
    buffers = [vm(getattr(n, f).shape, BF) for f in FACTORS] + [vm(s.shape, s.dtype) for s in saved]
    buffers += [
        vm(n.cot.shape, BF), vm((spare, tile, width), BF), vm(n.wo.shape, BF), vm(n.wo.shape, BF), vm((ranks, qw), BF),
        vm((sequences * rows, hidden_units), BF), vm(q_shape, BF), vm((units,) + kv_shape[1:], BF),
        vm((group, units, HEAD_DIM, 128), BF), vm((ktiles, TILE, HEAD_DIM), BF), vm((ktiles, HEAD_DIM + 16, TILE), BF),
        vm((HEAD_DIM + 16, TILE), F32), vm(q_shape, BF), vm((2 * rows, qw), BF), vm((2 * rows, qw), BF),
    ]
    sems = [dma((2 + spare + len(FACTORS),)), dma((len(saved),)), dma((spare,)), dma((count,)), dma((count,))]
    sems += [dma((group, units))] * 6 + [dma((2 + group,)), dma((3,)), dma((3,))]
    outs = pl.pallas_call(
        functools.partial(forward_kernel, count, parts),
        out_shape=small + saved + (shape((sequences * rows, hidden_units), BF),),
        in_specs=[SMEM] + [VM] * (len(FORWARD_NEAR) - 1) + [ANYWHERE] * len(FORWARD_FAR),
        out_specs=(VM,) * len(small) + (ANYWHERE,) * (len(saved) + 1),
        scratch_shapes=buffers + sems,
        compiler_params=pltpu.CompilerParams(
            collective_id=collective_id, has_side_effects=True, vmem_limit_bytes=62 * 2**20
        ),
        name="forward",
    )(*near, *far)
    return Names(FORWARD_OUT, outs)


def finish_kernel(reduce, count, shared, *refs):
    refs = list(refs)
    take = lambda n: [refs.pop(0) for _ in range(n)]
    dq_ref, dkv_ref, pre_ref, h_ref, gains, cos_ref, sin_ref, gain_ref, bc_ref, pick_ref, bd_ref = take(11)
    far = take(11)
    early = take(1) if reduce else []
    out_ref, block_ref = take(2)
    gout = take(4) if reduce else take(1)
    x, d_mid, n1, wq, wk, wv, ac, mid, down, down_x, cot = near = take(11)
    d_n, gb, dh_own, dh_other, dh_sum, sbuf, rbuf, gq = take(8)
    near_sems, dh_send, dh_recv, xsend, xrecv = take(5)
    sequences, inner, rows = dq_ref.shape
    width = out_ref.shape[2]
    kw = wk.shape[1]
    half_rows = sequences * RANK // 2
    me = lax.axis_index("ctx")
    across = {"tp": 1 - lax.axis_index("tp")}
    mine = pl.ds(pl.multiple_of(lax.axis_index("tp") * (width // 2), width // 2), width // 2)

    loads = [pltpu.make_async_copy(f, n, near_sems.at[i]) for i, (f, n) in enumerate(zip(far, near))]
    barrier = pltpu.get_barrier_semaphore()
    pl.semaphore_signal(barrier, inc=1, device_id=across, device_id_type=MESH)
    peers = 1
    if reduce:
        core_in, plane, z_in, plane_in = take(4)
        fin_outs, fin_ins, shared_out = take(2), take(2), take(2)
        twin_sems, z_send, z_recv, plane_send, plane_recv, fin_send, fin_recv, last_sems = take(8)
        chips = count // 2
        chip, core = me // 2, lax.rem(me, 2)
        twin = {"ctx": 2 * chip + 1 - core}
        pl.semaphore_signal(barrier, inc=1, device_id=twin, device_id_type=MESH)

        def at_chip(k):
            return lax.rem(chip + k, chips)

        def greet(k, _):
            pl.semaphore_signal(barrier, inc=1, device_id={"ctx": 2 * at_chip(k) + core}, device_id_type=MESH)
            return 0

        lax.fori_loop(1, chips, greet, 0)
        peers += chips

        w_qkv = gq.shape[2]
        to_twin = remote(gq.at[1 - core], core_in, twin_sems.at[0], twin_sems.at[1], twin)
    for i in (3, 4, 5, 2, 6, 7, 8, 9, 10, 0, 1):
        loads[i].start()
    pl.semaphore_wait(barrier, peers)
    if reduce:
        deep = chips // 2
        z, y = chip // 2, lax.rem(chip, 2)

        def z_copy(other, sender):
            chunk = early[0].shape[1] // deep
            return remote(
                early[0].at[:, pl.ds(pl.multiple_of(other * chunk, 128), chunk)], z_in.at[sender], z_send.at[other],
                z_recv.at[sender], {"ctx": 4 * other + 2 * y + core},
            )

        def each_z(step):
            loop(1, deep, lambda k: step(lax.rem(z + k, deep)))

        each_z(lambda k: z_copy(k, z).start())

    cosine, sine = cos_ref[...], sin_ref[...]
    heads_k = kw // HEAD_DIM
    cuts = (slice(0, inner), slice(inner, inner + kw), slice(inner + kw, inner + 2 * kw))

    def prepare_back(pre, gains, c):
        u = pre.reshape(pre.shape[0] // HEAD_DIM, HEAD_DIM, rows)
        scale = lax.rsqrt(jnp.mean(u * u, axis=1, keepdims=True) + EPSILON)
        y = u * scale
        w = turn(c.reshape(u.shape).astype(F32), cosine, -sine) * gains
        return (scale * (w - y * jnp.mean(w * y, axis=1, keepdims=True))).reshape(pre.shape)

    def first_step(s):
        dkv = dkv_ref[s * heads_k : (s + 1) * heads_k].astype(F32)
        dkv = jnp.sum(dkv, axis=1).astype(BF) if dkv.shape[1] > 1 else dkv[:, 0].astype(BF)
        d_q = prepare_back(pre_ref[s, :inner, :], gains[0], dq_ref[s])
        d_k = prepare_back(pre_ref[s, inner:, :], gains[1], dkv[:, :HEAD_DIM, :].reshape(kw, rows))
        d_v = dkv[:, HEAD_DIM:, :].reshape(kw, rows).astype(F32)
        d = jnp.transpose(jnp.concatenate([d_q, d_k, d_v], axis=0)).astype(BF)
        d_n[s] = d
        dh = [mm_nt(d[:, c], bc_ref[s, :, c]) * 2.0 for c in cuts]
        dh = jnp.transpose(jnp.concatenate(dh + [jnp.zeros((rows, 128 - 3 * RANK), F32)], axis=1))
        dh_own[s] = dh[: 3 * RANK].astype(BF)
        t = (jnp.transpose(h_ref[s].astype(F32)) * 2.0).astype(BF)
        gb[s] = jnp.concatenate([mm(t[i * RANK : (i + 1) * RANK], d[:, c]) for i, c in enumerate(cuts)], axis=1)

    def part_copy(s):
        return remote(sbuf.at[s], rbuf.at[s], xsend.at[s], xrecv.at[s], across)

    dh_copy = remote(dh_own, dh_other, dh_send.at[0], dh_recv.at[0], across)

    def send_pair(p):
        d = jnp.concatenate([d_n[2 * p], d_n[2 * p + 1]], axis=0)
        part = mm_nt(d[:, cuts[0]], wq[...]) + mm_nt(d[:, cuts[1]], wk[...]) + mm_nt(d[:, cuts[2]], wv[...])
        for i in (0, 1):
            sbuf[2 * p + i] = part[i * rows : (i + 1) * rows].astype(BF)
            part_copy(2 * p + i).start()

    def plane_copy(k, slot):
        chunk = plane.shape[1] // chips
        return remote(
            plane.at[:, pl.ds(pl.multiple_of(k * chunk, 128), chunk)], plane_in.at[slot], plane_send.at[k],
            plane_recv.at[slot], {"ctx": 2 * k + core},
        )

    def fin_copy(g, k, slot):
        return remote(
            fin_outs[g].at[k], fin_ins[g].at[slot], fin_send.at[g, k], fin_recv.at[g, slot], {"ctx": 2 * k + core}
        )

    def each_chip(step):
        loop(1, chips, lambda k: step(at_chip(k)))

    def to_plane():
        to_twin.wait_recv()
        plane[:, :w_qkv] = (gq[core].astype(F32) + core_in[...].astype(F32)).astype(BF)
        if plane.shape[1] > w_qkv:
            plane[:, w_qkv:] = jnp.zeros((half_rows, plane.shape[1] - w_qkv), BF)
        chunk = plane.shape[1] // chips
        each_chip(lambda k: plane_copy(k, chip).start())
        plane_in[chip] = plane[:, pl.ds(pl.multiple_of(chip * chunk, 128), chunk)]

    def to_owners(g):
        if g == 0:
            each_z(lambda k: z_copy(k, k).wait_recv())
            chunk = early[0].shape[1] // deep
            z_in[z] = early[0][:, pl.ds(pl.multiple_of(z * chunk, 128), chunk)]
        else:
            each_chip(lambda k: plane_copy(k, k).wait_recv())
        blocks = z_in if g == 0 else plane_in
        total = blocks[0].astype(F32)
        for k in range(1, blocks.shape[0]):
            total = total + blocks[k].astype(F32)
        for k in range(chips):
            fin_outs[g][k] = owner_rows(total, pick_ref, k, sequences)
        each_chip(lambda k: fin_copy(g, k, chip).start())
        fin_ins[g][chip] = fin_outs[g][chip]

    def rows_in(g):
        each_chip(lambda k: fin_copy(g, k, k).wait_recv())
        chunk = gout[g].shape[1] // chips
        for k in range(chips):
            unfold_rows(gout[g], (k % 2 * deep + k // 2 if g == 0 else k) * chunk, fin_ins[g][k])
        low, high = shared[g]
        middle = (low + high) // 2
        shared_out[g][...] = jnp.concatenate([gout[g][:, low:middle], gout[g][:, middle:high]], axis=0).astype(BF)
        copy = remote(shared_out[g], gout[2 + g], last_sems.at[g], last_sems.at[2 + g], across)
        copy.start()
        return copy

    def last_step(s):
        part_copy(s).wait_recv()
        c = sbuf[s].astype(F32) + rbuf[s].astype(F32) + mm(dh_sum[s][:, : 3 * RANK], ac[s])
        out_ref[s] = (d_mid[s] + norm_back(x[s].astype(F32), gain_ref[...][None, :], c)).astype(BF)

    for s in range(sequences):
        first_step(s)
    dh_copy.start()
    for i in (3, 4, 5):
        loads[i].wait()
    for p in range(sequences // 2):
        send_pair(p)
    dh_copy.wait()
    for i in (2, 7, 8, 9, 10):
        loads[i].wait()
    blocks = []
    for s in range(sequences):
        total = down[s].astype(F32) + down_x[s].astype(F32)
        h = total[:, width : width + RANK].astype(BF) * 2
        block_ref[s] = (mid[s] + (total[:, :width] + mm(h, bd_ref[s * RANK : (s + 1) * RANK, :]))).astype(BF)
        wide = jnp.concatenate([h, jnp.zeros((rows, 128 - RANK), BF)], axis=1)
        gb_down = mm(jnp.transpose(wide.astype(F32)).astype(BF)[:RANK], cot[s, :, mine])
        dh = (dh_own[s].astype(F32) + dh_other[s].astype(F32)).astype(BF)
        dh_sum[s] = jnp.transpose(jnp.concatenate([dh.astype(F32), jnp.zeros((128 - 3 * RANK, rows), F32)], axis=0)).astype(BF)
        wide = mm(dh, n1[s, :, mine])
        blocks.append(jnp.concatenate([wide[i * RANK : (i + 1) * RANK] for i in range(3)] + [gb_down, gb[s]], axis=1))
    everything = rank_halves(blocks)
    for b in (0, 1):
        gq[b] = everything[b * half_rows : (b + 1) * half_rows].astype(BF)
    if reduce:
        to_twin.start()
        to_plane()
        to_owners(0)
    for i in (6, 0, 1):
        loads[i].wait()
    if reduce:
        last_step(0)
        to_owners(1)
        shared_copies = [rows_in(0)]
        last_step(1)
        shared_copies.append(rows_in(1))
        for s in range(2, sequences):
            last_step(s)
        for c in shared_copies:
            c.wait()
        to_twin.wait_send()
        each_z(lambda k: z_copy(k, z).wait_send())
        each_chip(lambda k: plane_copy(k, chip).wait_send())
        for g in (0, 1):
            each_chip(lambda k, g=g: fin_copy(g, k, chip).wait_send())
    else:
        for s in range(sequences):
            last_step(s)
        gout[0][...] = gq[...]
    for s in range(sequences):
        part_copy(s).wait_send()


def finish(
    reduce, count, dq, dkv, pre, h, gains, tables, gain, bc, pick, bd, x, d_mid, n1, weights, ac, mid, down, down_x, cot,
    early, shared, collective_id,
):
    sequences, rows, width = x.shape
    inner, kw = weights[0].shape[1], weights[1].shape[1]
    w_qkv = 4 * (width // 2) + inner + 2 * kw
    half_rows = sequences * RANK // 2
    dma = pltpu.SemaphoreType.DMA
    far = (x, d_mid, n1) + tuple(weights) + (ac, mid, down, down_x, cot)
    gshape = (shape((2, half_rows, w_qkv), BF),)
    scratch = [pltpu.VMEM(a.shape, a.dtype) for a in far]
    scratch += [
        pltpu.VMEM((sequences, rows, inner + 2 * kw), BF),
        pltpu.VMEM((sequences, RANK, inner + 2 * kw), F32),
        pltpu.VMEM((sequences, 3 * RANK, rows), BF),
        pltpu.VMEM((sequences, 3 * RANK, rows), BF),
        pltpu.VMEM((sequences, rows, 128), BF),
        pltpu.VMEM(x.shape, BF),
        pltpu.VMEM(x.shape, BF),
        pltpu.VMEM((2, half_rows, w_qkv), BF),
        dma((11,)), dma((1,)), dma((1,)), dma((sequences,)), dma((sequences,)),
    ]
    if reduce:
        chips = count // 2
        totals = (2 * early[0].shape[1], padded(w_qkv, chips))
        gshape = tuple(shape((RANK // 2, n), F32) for n in totals)
        gshape += tuple(shape((RANK, (b - a) // 2), BF) for a, b in shared)
        scratch += [
            pltpu.VMEM((half_rows, w_qkv), BF),
            pltpu.VMEM((half_rows, totals[1]), BF),
            pltpu.VMEM((chips // 2, half_rows, totals[0] // chips), BF),
            pltpu.VMEM((chips, half_rows, totals[1] // chips), BF),
        ]
        scratch += [pltpu.VMEM((chips, RANK, n // chips // 2), BF) for n in totals] * 2
        scratch += [pltpu.VMEM((RANK, (b - a) // 2), BF) for a, b in shared]
        scratch += [dma((2,)), dma((chips // 2,)), dma((chips // 2,)), dma((chips,)), dma((chips,))]
        scratch += [dma((2, chips))] * 2 + [dma((4,))]
    return pl.pallas_call(
        functools.partial(finish_kernel, reduce, count, shared),
        out_shape=(shape(x.shape, BF),) * 2 + gshape,
        in_specs=[VM] * 11 + [ANYWHERE] * 11 + [VM] * len(early),
        out_specs=(VM,) * (2 + len(gshape)),
        scratch_shapes=scratch,
        compiler_params=pltpu.CompilerParams(
            collective_id=collective_id, has_side_effects=True, vmem_limit_bytes=60 * 2**20
        ),
        name="finish",
    )(dq, dkv, pre, h, gains, *tables, gain, bc, pick, bd, *far, *early)


def unpack_kernel(hidden_units, tile, inner, kw, block, grad, first, second, first_x, second_x, block_out, grad_out, *outs):
    block_out[...] = block[...]
    grad_out[...] = grad[...]
    ga_query, gb_query, ga_key, gb_key, ga_value, gb_value, ga_out, gb_out, ga_gate, gb_gate, ga_up, gb_up, ga_down, gb_down = outs
    width = ga_query.shape[1]
    w = width // 2
    lower = lax.axis_index("tp") == 0

    def join(out, own, own_at, other, i):
        a = own[:, own_at + i * w : own_at + (i + 1) * w]
        b = other[:, i * w : (i + 1) * w]
        out[:, :w] = jnp.where(lower, a, b)
        out[:, w:] = jnp.where(lower, b, a)

    @pl.when(pl.program_id(0) == 0)
    def _():
        for f in range(hidden_units // tile):
            for n, out in enumerate((gb_gate, gb_up, ga_down)):
                out[:, f * tile : (f + 1) * tile] = first[:, (3 * f + n) * tile : (3 * f + n + 1) * tile]
        at = 3 * hidden_units
        ga_out[...] = first[:, at : at + inner]
        rows = first.shape[0]
        unfold = lambda x: jnp.concatenate([x[:rows].astype(F32), x[rows:].astype(F32)], axis=1)
        other = unfold(first_x[...])
        for i, out in enumerate((ga_gate, ga_up, gb_out)):
            join(out, first, at + inner, other, i)
        other = unfold(second_x[...])
        for i, out in enumerate((ga_query, ga_key, ga_value, gb_down)):
            join(out, second, 0, other, i)
        at = 4 * w
        gb_query[...] = second[:, at : at + inner]
        gb_key[...] = second[:, at + inner : at + inner + kw]
        gb_value[...] = second[:, at + inner + kw : at + inner + 2 * kw]


def unpack(block, grad, owned, hidden_units, tile, inner, kw):
    width, rows = block.shape[2], owned[0].shape[0]
    sizes = (width, inner, width, kw, width, kw, inner, width, width, hidden_units, width, hidden_units, hidden_units, width)
    outs = tuple(shape((rows, n), F32) for n in sizes)
    return pl.pallas_call(
        functools.partial(unpack_kernel, hidden_units, tile, inner, kw),
        grid=(block.shape[0],),
        out_shape=(shape(block.shape, BF),) * 2 + outs,
        in_specs=[stepped(block.shape, 1)] * 2 + [whole(a) for a in owned],
        out_specs=(stepped(block.shape, 1),) * 2 + tuple(whole(a) for a in outs),
        compiler_params=BIG,
        name="unpack",
    )(block, grad, *owned)


def rotary_tables(positions):
    half = HEAD_DIM // 2
    frequencies = THETA_BASE ** (-jnp.arange(half, dtype=F32) * 2.0 / HEAD_DIM)
    angles = frequencies[:, None] * positions.astype(F32)[None, :]
    return jnp.cos(angles), jnp.sin(angles)


def swap(values):
    return lax.ppermute(values, "tp", [(0, 1), (1, 0)])


def reduce_scatter_rows(grads, count):
    rows, columns = grads.shape
    index = lax.axis_index("ctx")
    held = grads.reshape(count, rows // count, columns)
    bit = 1
    while bit < count:
        mine = (index // bit) % 2
        pairs = held.reshape(held.shape[0] // 2, 2, held.shape[1], columns)
        kept = lax.dynamic_index_in_dim(pairs, mine, 1, keepdims=False)
        sent = lax.dynamic_index_in_dim(pairs, 1 - mine, 1, keepdims=False).astype(BF)
        held = kept.astype(F32) + lax.ppermute(sent, "ctx", [(i, i ^ bit) for i in range(count)]).astype(F32)
        bit *= 2
    return held[0]


def local(
    tokens, output_cotangent, segment_ids, variant, attn_gain, ffn_gain, q_gain, k_gain,
    query_matrix, key_matrix, value_matrix, output_matrix, gate_matrix, up_matrix, down_matrix,
    query_input_factor, query_output_factor, key_input_factor, key_output_factor,
    value_input_factor, value_output_factor, output_input_factor, output_output_factor,
    gate_input_factor, gate_output_factor, up_input_factor, up_output_factor,
    down_input_factor, down_output_factor,
):
    sequences, rows_here, width = tokens.shape
    count = lax.axis_size("ctx")
    index = lax.axis_index("ctx")
    inner, kw = query_matrix.shape[1], key_matrix.shape[1]
    key_heads = kw // HEAD_DIM
    units = sequences * key_heads
    parts = count // units
    stacked = query_input_factor.shape[0]
    reduce_here = stacked // count == RANK // 2
    tables = rotary_tables(index * rows_here + jnp.arange(rows_here, dtype=jnp.int32))
    weights = (query_matrix, key_matrix, value_matrix)
    ins = (query_input_factor, key_input_factor, value_input_factor)
    outs = (query_output_factor, key_output_factor, value_output_factor)

    flat = lambda a: a.reshape(sequences * rows_here, -1)
    p = forward(
        (variant, tokens, attn_gain, ffn_gain, q_gain, k_gain, *tables, segment_ids, *weights, *ins, *outs),
        (
            flat(output_cotangent), down_matrix, output_matrix, gate_input_factor, up_input_factor, down_output_factor,
            gate_output_factor, up_output_factor, down_input_factor, output_output_factor, output_input_factor,
        ),
        count, parts, 0,
    )
    attn = p.home.reshape(sequences, inner, rows_here)

    cuts = tuple(rows_here * s for s in (0, sequences // 2, sequences))
    g_ffn, down, d_mid, d_attn, g_mid = feed(
        cuts, flat(p.n2), p.dhd, p.c_ag, p.c_au, p.c_bo, p.c_ao, output_matrix, ffn_gain, gate_matrix, up_matrix,
        down_matrix, p.c_bg, p.c_bu, p.c_ad, p.dh, p.mid, output_cotangent, p.h_out, attn, 3,
    )
    d_attn = d_attn.reshape(p.q_all.shape)
    d_attn, down = lax.optimization_barrier((d_attn, down))
    down_other = swap(down)
    early = (g_ffn, g_mid) if reduce_here else ()
    dq, dkv, *early = attend_back(d_attn, p.q_all, p.kv_all, p.of, p.lse, p.starts, early, count, parts, 1)

    w = width // 2
    hidden_units = gate_matrix.shape[1]
    tile = feed_tile(hidden_units)
    at = 3 * hidden_units + inner
    shared = ((at, at + 3 * w), (0, 4 * w))
    input_grad, block_result, *ends = finish(
        reduce_here, count, dq.reshape(sequences, inner, rows_here), dkv.reshape(units, parts, 2 * HEAD_DIM, rows_here),
        p.pre, p.h_one, p.gains, tables, attn_gain, p.bc, p.pick, p.c_bd, tokens, d_mid, p.n1, weights, p.ac,
        p.mid, down, down_other, output_cotangent, early, shared, 2,
    )
    if reduce_here:
        owned = ends
    else:
        per = RANK // 2
        pick = (jnp.arange(stacked // RANK, dtype=jnp.int32)[:, None] == variant[None, :]).astype(F32)
        owned, other = [], []
        for grads, (low, high) in zip((jnp.concatenate([g_ffn, g_mid], axis=1), ends[0]), shared):
            grads = grads.reshape(2, sequences, per, -1).astype(F32)
            dense = jnp.sum(pick[:, None, :, None, None] * grads[None], axis=2)
            owned.append(reduce_scatter_rows(dense.reshape(stacked, -1), count))
            half = swap(owned[-1][:, low:high])
            other.append(jnp.concatenate(jnp.split(half, 2, axis=1), axis=0))
        owned = owned + other
    return tuple(unpack(block_result, input_grad, owned, hidden_units, tile, inner, kw))


def solution(mesh):
    rows, whole, columns = P(None, "ctx", None), P(), P(None, "tp")
    owned, owned_half = P("ctx", None), P("ctx", "tp")
    return jax.shard_map(
        local,
        mesh=mesh,
        in_specs=(rows, rows) + (whole,) * 6
        + (columns, columns, columns, P("tp", None), columns, columns, P("tp", None))
        + (whole, columns) * 3 + (columns, whole) + (whole, columns) * 2 + (columns, whole),
        out_specs=(
            rows, rows, owned, owned_half, owned, owned_half, owned, owned_half,
            owned_half, owned, owned, owned_half, owned, owned_half, owned_half, owned,
        ),
        check_vma=False,
    )
```

```python
import functools, jax, jax.numpy as jnp
from jax import lax
from jax.experimental import pallas as pl
from jax.experimental.pallas import tpu as pltpu
from jax.sharding import PartitionSpec as P

HEAD_DIM = 64
LOG2E = 1.4426950408889634
MESH = pl.DeviceIdType.MESH
SMEM = pl.BlockSpec(memory_space=pltpu.SMEM)
VM = pl.BlockSpec(memory_space=pltpu.VMEM)
RANK = 16
EPSILON = 1e-05
THETA_BASE = 1000000.0
BF = jnp.bfloat16
F32 = jnp.float32
NT = (((1,), (1,)), ((), ()))
BIG = pltpu.CompilerParams(vmem_limit_bytes=60 * 2**20)


def cost(rows, width, columns, products, moved):
    return pl.CostEstimate(flops=2 * products * rows * width * columns, bytes_accessed=moved, transcendentals=0)

ANYWHERE = pl.BlockSpec(memory_space=pl.ANY)


def mm(a, b):
    return jnp.dot(a, b, preferred_element_type=F32)


def mm_nt(a, b):
    return lax.dot_general(a, b, NT, preferred_element_type=F32)


def shape(dims, kind):
    return jax.ShapeDtypeStruct(dims, kind)


def remote(source, target, send, recv, device):
    return pltpu.make_async_remote_copy(
        src_ref=source, dst_ref=target, send_sem=send, recv_sem=recv, device_id=device, device_id_type=MESH
    )


def norm_back(u, gain, c):
    scale = lax.rsqrt(jnp.mean(u * u, axis=-1, keepdims=True) + EPSILON)
    y = u * scale
    w = c * gain
    return scale * (w - y * jnp.mean(w * y, axis=-1, keepdims=True))


def turn(values, cosine, sine):
    half = HEAD_DIM // 2
    a, b = values[:, :half], values[:, half:]
    return jnp.concatenate([a * cosine - b * sine, b * cosine + a * sine], axis=1)


def rank_halves(blocks):
    return jnp.concatenate([b[: RANK // 2] for b in blocks] + [b[RANK // 2 :] for b in blocks], axis=0)


def column(ref):
    return jnp.transpose(jnp.broadcast_to(ref[...][None, :], (128, ref.shape[0])))


def whole(array):
    return pl.BlockSpec(array.shape, lambda i: (0,) * len(array.shape), pipeline_mode=pl.Buffered(1))


def stepped(dims, per):
    return pl.BlockSpec((per,) + tuple(dims[1:]), lambda i: (i,) + (0,) * (len(dims) - 1))


def own_ranks(first, rows, ranks):
    row = lax.broadcasted_iota(jnp.int32, (rows, ranks), 0) // 128 + first // 128
    return row == lax.broadcasted_iota(jnp.int32, (rows, ranks), 1) // RANK


def feed_kernel(
    cuts, n2_ref, dhd_ref, ag, au, bo, ao, wo, gain_ref, wd_ref, bg_ref, bu_ref, ad_ref, dh_ref,
    mid_ref, cot_ref, hout_ref, attn_ref, wg_ref, wu_ref,
    grads_ref, down_ref, dmid_ref, dattn_ref, more_ref,
    hg, hu, hs, dn2_acc, dhg_acc, dhu_acc, down_acc, h_acc, hidden_s, dgu_s, w_s, back_s, back_x, branch_s, more_s,
    send_sems, recv_sems, w_sems,
):
    step = pl.program_id(0)
    rows, width = n2_ref.shape
    tiles, tile = hidden_s.shape[0], hidden_s.shape[2]
    seqs = rows // 128
    ranks = seqs * RANK
    chunks = len(cuts) - 1
    last = chunks * tiles
    f = lax.rem(step, tiles)
    across = {"tp": 1 - lax.axis_index("tp")}

    def compact(a, first=0):
        a = jnp.where(own_ranks(first, *a.shape), a, 0.0)
        return sum(a[:, i * RANK : (i + 1) * RANK] for i in range(seqs))

    def copy(c):
        there = pl.ds(cuts[c], cuts[c + 1] - cuts[c])
        return remote(back_s.at[there, :], back_x.at[there, :], send_sems.at[c], recv_sems.at[c], across)

    def weights(i):
        columns, slot = pl.ds(pl.multiple_of(lax.rem(i, tiles) * tile, 128), tile), lax.rem(i, 2)
        return [
            pltpu.make_async_copy(w.at[:, columns], w_s.at[slot, :, n * tile : (n + 1) * tile], w_sems.at[slot, n])
            for n, w in enumerate((wg_ref, wu_ref))
        ]

    @pl.when(step == 0)
    def _():
        for i in (0, 1):
            for load in weights(i):
                load.start()
        barrier = pltpu.get_barrier_semaphore()
        pl.semaphore_signal(barrier, inc=1, device_id=across, device_id_type=MESH)
        pl.semaphore_wait(barrier, 1)
        kept = own_ranks(0, rows, ranks)
        g = jnp.where(kept, mm_nt(n2_ref[...], ag[...]) * 2.0, 0.0)
        u = jnp.where(kept, mm_nt(n2_ref[...], au[...]) * 2.0, 0.0)
        hg[...] = g.astype(BF)
        hu[...] = u.astype(BF)
        for n, a in enumerate((g, u, dhd_ref[...].astype(F32))):
            turned = jnp.transpose(jnp.concatenate([a, jnp.zeros((rows, 128 - ranks), F32)], axis=1))
            rows_of = [turned[i * RANK : (i + 1) * RANK] for i in range(seqs)]
            hs[n] = rank_halves(rows_of).astype(BF)
        down_acc[...] = jnp.zeros_like(down_acc)
        h_acc[...] = jnp.zeros_like(h_acc)

    @pl.when(step < last)
    def _():
        for load in weights(step):
            load.wait()

    slot = lax.rem(step, 2)
    for c in range(chunks):
        first, part = cuts[c], cuts[c + 1] - cuts[c]
        here, top = slice(first, first + part), slice(0, part)

        @pl.when((step >= c * tiles) & (step < (c + 1) * tiles))
        def _(here=here, top=top):
            n2 = n2_ref[here, :]
            bg, bu = bg_ref[...], bu_ref[...]
            both = mm(n2, w_s[slot])
            gate = both[:, :tile] + mm(hg[here, :], bg)
            up = both[:, tile:] + mm(hu[here, :], bu)
            sg = 1.0 / (1.0 + jnp.exp(-gate))
            silu = gate * sg
            hidden_s[f, here, :] = (silu * up).astype(BF)
            dh = dh_ref[here, :].astype(F32)
            dg = (dh * up * sg * (1.0 + gate * (1.0 - sg))).astype(BF)
            du = (dh * silu).astype(BF)
            dgu_s[f, here, :tile] = dg
            dgu_s[f, here, tile:] = du
            terms = ((dn2_acc, mm_nt(dgu_s[f, here, :], w_s[slot])), (dhg_acc, mm_nt(dg, bg)), (dhu_acc, mm_nt(du, bu)))
            for acc, term in terms:
                acc[top, :] = jnp.where(f == 0, term, acc[top, :] + term)

        @pl.when(step == (c + 1) * tiles - 1)
        def _(c=c, here=here, top=top, first=first, part=part):
            back_s[here, :width] = dn2_acc[top, :].astype(BF)
            small = [compact(a[top, :], first) * 2 for a in (dhg_acc, dhu_acc)]
            back_s[here, width:] = jnp.concatenate(small + [jnp.zeros((part, 128 - 2 * RANK), F32)], axis=1).astype(BF)
            copy(c).start()

    @pl.when(step < last - 2)
    def _():
        for load in weights(step + 2):
            load.start()

    @pl.when((step >= last) & (step < last + tiles))
    def _():
        hidden = hidden_s[f]
        down_acc[...] += mm(hidden, wd_ref[...])
        h_acc[...] += mm_nt(hidden, ad_ref[...])
        for n, kept in enumerate((dgu_s[f, :, :tile], dgu_s[f, :, tile:], hidden)):
            grads_ref[:, n * tile : (n + 1) * tile] = mm(hs[n], kept).astype(BF)

    for c in range(chunks):

        @pl.when(step == last + tiles + cuts[c] // 128)
        def _(c=c):
            copy(c).wait()

    @pl.when(step >= last + tiles)
    def _():
        s = step - last - tiles
        here = pl.ds(pl.multiple_of(s * 128, 128), 128)
        own = pl.ds(pl.multiple_of(s * RANK, RANK), RANK)
        mine = pl.ds(pl.multiple_of(lax.axis_index("tp") * (width // 2), width // 2), width // 2)
        down_ref[0, :, :width] = down_acc[here, :].astype(BF)
        h = jnp.where(own_ranks(s * 128, 128, ranks), h_acc[here, :], 0.0)
        h = sum(h[:, i * RANK : (i + 1) * RANK] for i in range(seqs))
        down_ref[0, :, width:] = jnp.concatenate([h, jnp.zeros((128, 128 - RANK), F32)], axis=1).astype(BF)
        total = back_s[here, :].astype(F32) + back_x[here, :].astype(F32)
        dh = total[:, width : width + 2 * RANK].astype(BF)
        c = total[:, :width] + mm(dh, jnp.concatenate([ag[own, :], au[own, :]], axis=0))
        d_mid = cot_ref[0].astype(F32) + norm_back(mid_ref[0], gain_ref[...][None, :], c)
        dmid_ref[0] = d_mid
        branch_s[...] = d_mid.astype(BF)
        dho = (mm_nt(branch_s[...], bo[own, :]) * 2.0).astype(BF)
        d_attn = mm_nt(branch_s[...], wo[...]) + mm(dho, ao[own, :])
        dattn_ref[:, 0] = jnp.transpose(d_attn).astype(BF).reshape(dattn_ref.shape[0], *dattn_ref.shape[2:])
        wide = jnp.concatenate([dh, dho, hout_ref[0][:, :RANK] * 2, jnp.zeros((128, 128 - 4 * RANK), BF)], axis=1)
        t = jnp.transpose(wide.astype(F32)).astype(BF)
        both = mm(t[: 2 * RANK], n2_ref[here, mine])
        more_s[s] = jnp.concatenate(
            [
                mm_nt(t[2 * RANK : 3 * RANK], attn_ref[:, 0].reshape(wo.shape[0], 128)), both[:RANK], both[RANK:],
                mm(t[3 * RANK : 4 * RANK], branch_s[:, mine]),
            ],
            axis=1,
        )

    @pl.when(step == pl.num_programs(0) - 1)
    def _():
        more_ref[...] = rank_halves([more_s[i] for i in range(seqs)]).astype(BF)


def feed_tile(units):
    return 1152 if units % 1152 == 0 else units


def feed(cuts, n2, dhd, ag, au, bo, ao, wo, gain, wg, wu, wd, bg, bu, ad, dh, mid, cot, hout, attn, collective_id):
    rows, width = n2.shape
    stacked, units = bg.shape
    inner = wo.shape[0]
    tile = feed_tile(units)
    chunks, part = len(cuts) - 1, max(b - a for a, b in zip(cuts, cuts[1:]))
    seqs, tiles, ranks = rows // 128, units // tile, rows // 128 * RANK
    last = chunks * tiles
    early = lambda height: pl.BlockSpec((height, tile), lambda i: (0, jnp.where(i < last, lax.rem(i, tiles), tiles - 1)))
    late = lambda i: jnp.clip(i - last, 0, tiles - 1)
    by_seq = lambda dims: pl.BlockSpec((1,) + dims[1:], lambda i: (jnp.maximum(i - last - tiles, 0), 0, 0))
    by_head = pl.BlockSpec(
        attn.shape[:1] + (1,) + attn.shape[2:], lambda i: (0, jnp.maximum(i - last - tiles, 0), 0, 0)
    )
    vm, dma = pltpu.VMEM, pltpu.SemaphoreType.DMA
    more = shape((ranks, inner + 3 * (width // 2)), BF)
    wide = (seqs, 128, width + 128)
    return pl.pallas_call(
        functools.partial(feed_kernel, cuts),
        grid=(last + tiles + seqs,),
        out_shape=(shape((ranks, 3 * units), BF), shape(wide, BF), shape(mid.shape, F32), shape(attn.shape, BF), more),
        in_specs=[whole(a) for a in (n2, dhd, ag, au, bo, ao, wo, gain)]
        + [pl.BlockSpec((tile, width), lambda i: (late(i), 0)), early(stacked), early(stacked)]
        + [pl.BlockSpec((stacked, tile), lambda i: (0, late(i))), early(rows)]
        + [by_seq(a.shape) for a in (mid, cot, hout)] + [by_head, ANYWHERE, ANYWHERE],
        out_specs=(
            pl.BlockSpec((ranks, 3 * tile), lambda i: (0, late(i))), by_seq(wide), by_seq(mid.shape), by_head,
            whole(more),
        ),
        scratch_shapes=[vm((rows, ranks), BF)] * 2
        + [vm((3, ranks, rows), BF), vm((part, width), F32), vm((part, ranks), F32), vm((part, ranks), F32)]
        + [vm((rows, width), F32), vm((rows, ranks), F32)] + [vm((tiles, rows, tile), BF), vm((tiles, rows, 2 * tile), BF)]
        + [vm((2, width, 2 * tile), BF)] + [vm((rows, width + 128), BF)] * 2 + [vm((128, width), BF), vm((seqs, RANK, more.shape[1]), F32)]
        + [dma((chunks,)), dma((chunks,)), dma((2, 2))],
        compiler_params=pltpu.CompilerParams(
            collective_id=collective_id, has_side_effects=True, vmem_limit_bytes=63 * 2**20
        ),
        cost_estimate=cost(rows, width, units, 5, 12 * width * units),
        name="feed_forward",
    )(n2, dhd, ag, au, bo, ao, wo, gain, wd, bg, bu, ad, dh, mid, cot, hout, attn, wg, wu)


TILE = 512
BLOCKS = TILE // 128
SUB = 512
SCALE = HEAD_DIM**-0.5


def document_starts(seg_ref, seq, starts):
    sequences, length = seg_ref.shape
    blocks = length // 128
    number = lax.broadcasted_iota(jnp.int32, (sequences, length), 0)
    row = jnp.sum(jnp.where(number == seq, seg_ref[...], 0), axis=0, keepdims=True)
    segs = jnp.concatenate([row[:, b * 128 : (b + 1) * 128] for b in range(blocks)], axis=0)
    lane = lax.broadcasted_iota(jnp.int32, segs.shape, 1)
    position = lax.broadcasted_iota(jnp.int32, segs.shape, 0) * 128 + lane

    def down(a, n):
        return jnp.concatenate([jnp.zeros((n, 128), jnp.int32), a[: blocks - n]], axis=0)

    before = jnp.where(lane == 0, pltpu.roll(down(segs, 1), 1, 1), pltpu.roll(segs, 1, 1))
    start = jnp.where((segs != before) & (position > 0), position, 0)
    step = 1
    while step < 128:
        start = jnp.maximum(start, jnp.where(lane >= step, pltpu.roll(start, step, 1), 0))
        step *= 2
    carried = down(jnp.broadcast_to(start[:, 127:], segs.shape), 1)
    step = 1
    while step < blocks:
        carried = jnp.maximum(carried, down(carried, step))
        step *= 2
    start = jnp.maximum(start, carried)
    for b in range(blocks):
        starts[b] = start[b : b + 1]


def query_rows(starts, tile, stride, part):
    lanes = lax.broadcasted_iota(jnp.int32, (1, 128), 1)
    blocks = [(BLOCKS * tile + b) * stride + part for b in range(BLOCKS)]
    position = jnp.concatenate([b * 128 + lanes for b in blocks], axis=1)
    return position, jnp.concatenate([starts[b] for b in blocks], axis=1)


def key_range(tile, stride, part):
    return BLOCKS * tile * stride // BLOCKS + part // BLOCKS, ((BLOCKS * tile + BLOCKS - 1) * stride + part) // BLOCKS + 1


def keep_pairs(p, first, start, position, causal):
    key = lax.broadcasted_iota(jnp.int32, p.shape, 0)
    keep = key >= jnp.broadcast_to(start - first, p.shape)
    if causal:
        keep = keep & (key <= jnp.broadcast_to(position - first, p.shape))
    return jnp.where(keep, p, 0.0)


def across_blocks(ref, tile, rows):
    return jnp.concatenate([ref[BLOCKS * tile + b, rows, :] for b in range(BLOCKS)], axis=1)


def load_keys(kv_ref, kb, vt):
    def load(j, _):
        for b in range(BLOCKS):
            kb[j, b * 128 : (b + 1) * 128, :] = jnp.transpose(kv_ref[BLOCKS * j + b, :HEAD_DIM, :])
            vt[j, :HEAD_DIM, b * 128 : (b + 1) * 128] = kv_ref[BLOCKS * j + b, HEAD_DIM:, :]
        vt[j, HEAD_DIM:, :] = jnp.ones((16, TILE), BF)
        return 0

    lax.fori_loop(0, kv_ref.shape[0] // BLOCKS, load, 0)


def head_forward(h, stride, part, first, q_ref, starts, kb, vt, acc, of_ref, lse_ref, done):
    rows = pl.ds(h * HEAD_DIM, HEAD_DIM)

    tiles = q_ref.shape[0] // BLOCKS

    def q_step(n, _):
        i = lax.rem(first + n, tiles)
        position, start = query_rows(starts, i, stride, part)
        qt = across_blocks(q_ref, i, rows)
        acc[...] = jnp.zeros_like(acc)

        def k_step(causal, j, _):
            total = acc[...]
            for c in range(TILE // SUB):
                keys = slice(c * SUB, (c + 1) * SUB)
                p = jnp.exp2(mm(kb[j, keys, :], qt) * (LOG2E * SCALE))
                p = keep_pairs(p, j * TILE + c * SUB, start, position, causal)
                total = total + mm(vt[j, :, keys], p.astype(BF))
            acc[...] = total
            return 0

        whole, end = key_range(i, stride, part)
        lax.fori_loop(0, whole, functools.partial(k_step, False), 0)
        lax.fori_loop(whole, end, functools.partial(k_step, True), 0)
        total = acc[HEAD_DIM : HEAD_DIM + 1, :]
        lse_ref[h, i] = jnp.broadcast_to(jnp.log2(total), (8, TILE))
        out = acc[:HEAD_DIM, :] / total
        for b in range(BLOCKS):
            of_ref[BLOCKS * i + b, rows, :] = out[:, b * 128 : (b + 1) * 128]
        done(n, i, out.astype(BF))
        return 0

    lax.fori_loop(0, tiles, q_step, 0)


def pair_backward(h, i, j, causal, stride, part, qt, q3, dot_t, do3, lse_ref, delta, starts, kb, vb, kt, dqt, dk, dv):
    position, start = query_rows(starts, i, stride, part)
    dq = dqt[h, i]
    for c in range(TILE // SUB):
        keys = slice(c * SUB, (c + 1) * SUB)
        p = jnp.exp2(mm(kb[j, keys, :], qt[h, i]) * (LOG2E * SCALE) - lse_ref[h, i, 0:1, :])
        p = keep_pairs(p, j * TILE + c * SUB, start, position, causal)
        dp = mm(vb[j, keys, :], dot_t[h, i])
        ds = (p * (dp - delta[h, i, 0:1, :])).astype(BF)
        dv[j, keys, :] += mm(p.astype(BF), do3[h, i])
        dk[j, keys, :] += mm(ds, q3[h, i])
        dq = dq + mm(kt[j, :, keys], ds)
    dqt[h, i] = dq


def head_rows(h):
    return pl.ds(h * HEAD_DIM, HEAD_DIM)


def loop(low, high, step):
    def body(k, _):
        step(k)
        return 0

    lax.fori_loop(low, high, body, 0)


def class_copy(count, parts, source, target, send, recv):
    def make(index, sender):
        return remote(
            source(index), target(sender), send.at[index], recv.at[sender],
            {"ctx": index * parts + lax.rem(lax.axis_index("ctx"), parts)},
        )

    return make


def owner_rows(total, pick_ref, k, sequences):
    per = RANK // 2
    row = jnp.zeros((per, total.shape[1]), F32)
    for s in range(sequences):
        row = row + total[s * per : (s + 1) * per] * pick_ref[k, s][:, :1]
    half = total.shape[1] // 2
    return jnp.concatenate([row[:, :half], row[:, half:]], axis=0).astype(BF)


def unfold_rows(rows_ref, at, block):
    per, half = RANK // 2, block.shape[1]
    rows_ref[:, at : at + half] = block[:per].astype(F32)
    rows_ref[:, at + half : at + 2 * half] = block[per:].astype(F32)


class EarlyReduction:
    def __init__(self, me, grads, y_sum, own, core_in, plane, y_in, loads, twin_sends, twin_recvs, y_sems):
        self.y_sum, self.own, self.core_in, self.plane, self.y_in = y_sum, own, core_in, plane, y_in
        chip, core = me // 2, lax.rem(me, 2)
        self.y = lax.rem(chip, 2)
        self.loads, self.to_twin, at = [], [], 0
        for i, ref in enumerate(grads):
            size, place = ref.shape[0] // 2, slice(at, at + ref.shape[1])
            at += ref.shape[1]
            half = lambda who, ref=ref, size=size: ref.at[pl.ds(pl.multiple_of(who * size, 16), size), :]
            self.loads.append(pltpu.make_async_copy(half(core), own.at[:, place], loads.at[i]))
            twin = {"ctx": 2 * chip + 1 - core}
            self.to_twin.append(remote(half(1 - core), core_in.at[:, place], twin_sends.at[i], twin_recvs.at[i], twin))
        self.known, self.width = at, plane.shape[1] // 2
        self.to_y = remote(
            plane.at[:, pl.ds(pl.multiple_of((1 - self.y) * self.width, 128), self.width)], y_in, y_sems.at[0],
            y_sems.at[1], {"ctx": 2 * (chip + 1 - 2 * self.y) + core},
        )

    def begin(self):
        for c in self.loads + self.to_twin:
            c.start()

    def over_cores(self):
        for c in self.loads:
            c.wait()
        for c in self.to_twin:
            c.wait_recv()
        self.plane[:, : self.known] = (self.own[...].astype(F32) + self.core_in[...].astype(F32)).astype(BF)
        rest = self.plane.shape[1] - self.known
        if rest:
            self.plane[:, self.known :] = jnp.zeros((self.plane.shape[0], rest), BF)
        self.to_y.start()

    def over_y(self):
        self.to_y.wait()
        mine = self.plane[:, pl.ds(pl.multiple_of(self.y * self.width, 128), self.width)]
        self.y_sum[...] = (mine.astype(F32) + self.y_in[...].astype(F32)).astype(BF)
        for c in self.to_twin:
            c.wait_send()


def early_scratch(grads, total):
    vm, dma = pltpu.VMEM, pltpu.SemaphoreType.DMA
    rows, known = grads[0].shape[0] // 2, sum(g.shape[1] for g in grads)
    return [vm((rows, known), BF), vm((rows, known), BF), vm((rows, total), BF), vm((rows, total // 2), BF)] + [dma((2,))] * 4


def padded(columns, chips):
    return -(-columns // (256 * chips)) * 256 * chips


def attend_back_kernel(count, parts, reduce, do_ref, q_all, kv_all, of_ref, lse_ref, starts, *refs):
    refs = list(refs)
    take = lambda n: [refs.pop(0) for _ in range(n)]
    grads = take(2) if reduce else []
    dq_home, dkv_home = take(2)
    early = EarlyReduction(lax.axis_index("ctx"), grads, *take(9)) if reduce else None
    attend_back_body(
        count, parts, early,
        do_ref, q_all, kv_all, of_ref, lse_ref, starts, dq_home, dkv_home, *refs,
    )


def attend_back_body(
    count, parts, early, do_ref, q_all, kv_all, of_ref, lse_ref, starts, dq_home, dkv_home,
    do_in, dq_buf, dkv_buf, kb, vb, kt, qt, q3, dot_t, do3, delta, dqt, dk, dv,
    do_send, do_recv, dq_send, dq_recv, dkv_send, dkv_recv, own_sems,
):
    me = lax.axis_index("ctx")
    units = count // parts
    unit, part = me // parts, lax.rem(me, parts)
    group, tiles, ktiles = q_all.shape[1] // HEAD_DIM, units // BLOCKS, count // BLOCKS
    barrier = pltpu.get_barrier_semaphore()
    loop(
        1, count,
        lambda k: pl.semaphore_signal(barrier, inc=1, device_id={"ctx": lax.rem(me + k, count)}, device_id_type=MESH),
    )
    own_do = pltpu.make_async_copy(do_ref.at[unit], do_in.at[unit], own_sems.at[0])
    own_do.start()
    pl.semaphore_wait(barrier, count - 1)
    if early:
        early.begin()

    def turn_of(k):
        return lax.rem(unit + k, units)

    do_copy = [
        class_copy(
            count, parts, lambda i, h=h: do_ref.at[i, head_rows(h), :], lambda i, h=h: do_in.at[i, head_rows(h), :],
            do_send.at[h], do_recv.at[h],
        )
        for h in range(group)
    ]
    dq_copy = [
        class_copy(
            count, parts, lambda i, h=h: dq_buf.at[h, i], lambda i, h=h: dq_home.at[i, head_rows(h), :],
            dq_send.at[h], dq_recv.at[h],
        )
        for h in range(group)
    ]

    def dkv_copy(device, sender):
        return remote(dkv_buf.at[device], dkv_home.at[sender], dkv_send.at[device], dkv_recv.at[sender], {"ctx": device})

    own_dkv = pltpu.make_async_copy(dkv_buf.at[me], dkv_home.at[me], own_sems.at[1])

    def own_dq(h):
        return pltpu.make_async_copy(dq_buf.at[h, unit], dq_home.at[unit, head_rows(h), :], own_sems.at[2 + h])

    for h in range(group):
        loop(1, units, lambda k, h=h: do_copy[h](turn_of(k), unit).start())

    def load_kv(j):
        for b in range(BLOCKS):
            lanes = slice(b * 128, (b + 1) * 128)
            kt[j, :, lanes] = kv_all[BLOCKS * j + b, :HEAD_DIM, :]
            kb[j, lanes, :] = jnp.transpose(kv_all[BLOCKS * j + b, :HEAD_DIM, :])
            vb[j, lanes, :] = jnp.transpose(kv_all[BLOCKS * j + b, HEAD_DIM:, :])

    def load_q(i):
        for h in range(group):
            for b in range(BLOCKS):
                lanes = slice(b * 128, (b + 1) * 128)
                q = q_all[BLOCKS * i + b, h * HEAD_DIM : (h + 1) * HEAD_DIM, :]
                qt[h, i, :, lanes] = q
                q3[h, i, lanes, :] = jnp.transpose(q)
            dqt[h, i] = jnp.zeros((HEAD_DIM, TILE), F32)

    def load_do(h, i):
        rows = slice(h * HEAD_DIM, (h + 1) * HEAD_DIM)
        for b in range(BLOCKS):
            lanes = slice(b * 128, (b + 1) * 128)
            g = do_in[BLOCKS * i + b, rows, :]
            dot_t[h, i, :, lanes] = g
            do3[h, i, lanes, :] = jnp.transpose(g)
            d = jnp.sum(g.astype(F32) * of_ref[BLOCKS * i + b, rows, :], axis=0, keepdims=True)
            delta[h, i, :, lanes] = jnp.broadcast_to(d, (8, 128))

    loop(0, ktiles, load_kv)
    loop(0, tiles, load_q)

    def run(h, j):
        low = jnp.maximum(BLOCKS * j - part + parts - 1, 0) // (BLOCKS * parts)
        full = jnp.minimum((BLOCKS * (j + 1) - part + BLOCKS * parts - 1) // (BLOCKS * parts), tiles)

        def pair(causal, i):
            pair_backward(
                h, i, j, causal, parts, part, qt, q3, dot_t, do3, lse_ref, delta, starts, kb, vb, kt, dqt, dk, dv
            )

        loop(low, full, functools.partial(pair, True))
        loop(full, tiles, functools.partial(pair, False))

    def emit_keys(j):
        for b in range(BLOCKS):
            rows = slice(b * 128, (b + 1) * 128)
            block = BLOCKS * j + b
            dkv_buf[block, :HEAD_DIM, :] = jnp.transpose(dk[j, rows, :] * SCALE).astype(BF)
            dkv_buf[block, HEAD_DIM:, :] = jnp.transpose(dv[j, rows, :]).astype(BF)

            @pl.when(block == me)
            def _():
                own_dkv.start()

            @pl.when(block != me)
            def _():
                dkv_copy(block, me).start()

    def emit_queries(h, n):
        i = lax.rem(unit + n, tiles)
        for b in range(BLOCKS):
            block = BLOCKS * i + b
            dq_buf[h, block] = (dqt[h, i, :, b * 128 : (b + 1) * 128] * SCALE).astype(BF)

            @pl.when(block == unit)
            def _():
                own_dq(h).start()

            @pl.when(block != unit)
            def _():
                dq_copy[h](block, unit).start()

    dk[...] = jnp.zeros_like(dk)
    dv[...] = jnp.zeros_like(dv)
    own_do.wait()
    if early:
        early.over_cores()
    for h in range(group):
        loop(1, units, lambda k, h=h: do_copy[h](unit, turn_of(k)).wait_recv())
        loop(0, tiles, functools.partial(load_do, h))

        def key_step(n, h=h):
            j = lax.rem(unit + n, ktiles)
            run(h, j)
            if h == group - 1:
                emit_keys(j)

        loop(0, ktiles, key_step)
        loop(0, tiles, functools.partial(emit_queries, h))
        if early and h == 1:
            early.over_y()
    for h in range(group):
        own_dq(h).wait()
    own_dkv.wait()

    def finish_full(k):
        other = lax.rem(me + k, count)
        dkv_copy(other, me).wait_send()
        dkv_copy(me, other).wait_recv()

    loop(1, count, finish_full)

    def finish_class(k):
        other = turn_of(k)
        for h in range(group):
            do_copy[h](other, unit).wait_send()
            dq_copy[h](other, unit).wait_send()
            dq_copy[h](unit, other).wait_recv()

    loop(1, units, finish_class)


def attend_back(do, q, kv, of, lse, starts, early, count, parts, collective_id):
    units, qrows, _ = q.shape
    group, tiles, ktiles = qrows // HEAD_DIM, units // BLOCKS, count // BLOCKS
    dma, vm = pltpu.SemaphoreType.DMA, pltpu.VMEM
    sums, scratch = (), []
    if early:
        total = padded(sum(g.shape[1] for g in early), count // 2)
        sums = (shape((early[0].shape[0] // 2, total // 2), BF),)
        scratch = early_scratch(early, total)
    return pl.pallas_call(
        functools.partial(attend_back_kernel, count, parts, bool(early)),
        out_shape=(shape(q.shape, BF), shape(kv.shape, BF)) + sums,
        in_specs=[ANYWHERE] + [VM] * 5 + [ANYWHERE] * len(early),
        out_specs=(ANYWHERE, ANYWHERE) + (VM,) * len(sums),
        scratch_shapes=scratch + [vm(q.shape, BF), vm((group, units, HEAD_DIM, 128), BF), vm(kv.shape, BF)]
        + [vm((ktiles, TILE, HEAD_DIM), BF)] * 2 + [vm((ktiles, HEAD_DIM, TILE), BF)]
        + [vm((group, tiles, HEAD_DIM, TILE), BF), vm((group, tiles, TILE, HEAD_DIM), BF)] * 2
        + [vm((group, tiles, 8, TILE), F32), vm((group, tiles, HEAD_DIM, TILE), F32)]
        + [vm((ktiles, TILE, HEAD_DIM), F32)] * 2
        + [dma((group, units))] * 4 + [dma((count,))] * 2 + [dma((2 + group,))],
        compiler_params=pltpu.CompilerParams(
            collective_id=collective_id, has_side_effects=True, vmem_limit_bytes=60 * 2**20
        ),
        name="attend_back",
    )(do, q, kv, of, lse, starts, *early)


class Names:
    def __init__(self, names, refs):
        assert len(names) == len(refs)
        self.__dict__.update(zip(names, refs))


FACTORS = ("ag", "au", "bd", "bg", "bu", "ad", "bo", "ao")
FORWARD_NEAR = ("variant", "x", "gain_one", "gain_two", "q_gain", "k_gain", "cosine", "sine", "segs") + (
    "wq", "wk", "wv", "aq", "ak", "av", "bq", "bk", "bv",
)
FORWARD_FAR = ("cot", "wd", "wo") + FACTORS
FORWARD_SMALL = ("h_one", "ac", "bc", "gains", "pick", "lse", "starts", "dhd", "h_out")
FORWARD_SAVED = ("n1", "pre", "q_all", "kv_all", "of", "home", "mid", "n2") + tuple("c_" + f for f in FACTORS)
FORWARD_OUT = FORWARD_SMALL + FORWARD_SAVED + ("dh",)
FORWARD_BUFFERS = ("cot_s", "wd_s", "wo_s", "wo_x", "ao_x", "dh_s", "q_msg", "kv_msg", "o_buf", "kb", "vt", "acc")
FORWARD_BUFFERS += ("home_x", "lhs", "lhs_x")
FORWARD_SEMS = ("far_sems", "save_sems", "dh_sems", "kv_send", "kv_recv", "q_send", "q_recv", "o_send", "o_recv")
FORWARD_SEMS += ("x_send", "x_recv", "own_sems", "w_send", "w_recv")


LAG = 4


def forward_kernel(count, parts, *refs):
    names = FORWARD_NEAR + FORWARD_FAR + FORWARD_OUT
    names += tuple(f + "_s" for f in FACTORS) + tuple(n + "_s" for n in FORWARD_SAVED) + FORWARD_BUFFERS + FORWARD_SEMS
    r = Names(names, refs)
    me = lax.axis_index("ctx")
    units = count // parts
    unit, part = me // parts, lax.rem(me, parts)
    sequences, rows, width = r.x.shape
    qw, kw = r.wq.shape[1], r.wk.shape[1]
    heads_k = kw // HEAD_DIM
    group = qw // kw
    ranks = sequences * RANK
    across = {"tp": 1 - lax.axis_index("tp")}
    core = lax.rem(me, 2)
    twin = {"ctx": me + 1 - 2 * core}

    def turn_of(k):
        return lax.rem(unit + k, units)

    barrier = pltpu.get_barrier_semaphore()
    pl.semaphore_signal(barrier, inc=1, device_id=across, device_id_type=MESH)
    loop(
        1, count,
        lambda k: pl.semaphore_signal(barrier, inc=1, device_id={"ctx": lax.rem(me + k, count)}, device_id_type=MESH),
    )
    tiles, tile = r.wd_s.shape[0], r.wd_s.shape[1]
    far = [(r.cot, r.cot_s)] + [(r.wd.at[pl.ds(f * tile, tile), :], r.wd_s.at[f]) for f in range(tiles)]
    far += [(r.wo, r.wo_s)] + [(getattr(r, f), getattr(r, f + "_s")) for f in FACTORS]
    far = [pltpu.make_async_copy(a, b, r.far_sems.at[i]) for i, (a, b) in enumerate(far)]
    for c in far:
        c.start()
    saves = {
        n: pltpu.make_async_copy(getattr(r, n + "_s"), getattr(r, n), r.save_sems.at[i]) for i, n in enumerate(FORWARD_SAVED)
    }

    def kv_copy(index, to_part, sender):
        device = index * parts + to_part
        return remote(r.kv_msg.at[index], r.kv_all_s.at[sender], r.kv_send.at[device], r.kv_recv.at[sender], {"ctx": device})

    q_copy = [
        class_copy(
            count, parts, lambda i, h=h: r.q_msg.at[i, head_rows(h), :], lambda i, h=h: r.q_all_s.at[i, head_rows(h), :],
            r.q_send.at[h], r.q_recv.at[h],
        )
        for h in range(group)
    ]
    o_copy = [
        class_copy(
            count, parts, lambda i, h=h: r.o_buf.at[h, i], lambda i, h=h: r.home_s.at[i, head_rows(h), :],
            r.o_send.at[h], r.o_recv.at[h],
        )
        for h in range(group)
    ]

    def x_copy(h, i):
        place = (i, head_rows(h), slice(None))
        return remote(r.home_s.at[place], r.home_x.at[place], r.x_send.at[h, i], r.x_recv.at[h, i], across)

    column_of = lax.broadcasted_iota(jnp.int32, (RANK, r.aq.shape[0]), 1)
    rank_of = lax.broadcasted_iota(jnp.int32, (RANK, r.aq.shape[0]), 0)
    chooser = [jnp.where(column_of == r.variant[s] * RANK + rank_of, 1.0, 0.0).astype(BF) for s in range(sequences)]
    choosers = jnp.concatenate(chooser, axis=0)
    stacked = lax.broadcasted_iota(jnp.int32, (1, r.aq.shape[0]), 1) // RANK
    cosine, sine = r.cosine[...], r.sine[...]
    qg, kg = column(r.q_gain), column(r.k_gain)
    gain = r.gain_one[...][None, :]

    def prepare(t, gains):
        heads = t.reshape(t.shape[0] // HEAD_DIM, HEAD_DIM, rows)
        scale = lax.rsqrt(jnp.mean(heads * heads, axis=1, keepdims=True) + EPSILON)
        return turn(heads * scale * gains, cosine, sine).astype(BF)

    def project(p):
        for s in (2 * p, 2 * p + 1):
            x = r.x[s].astype(F32)
            scale = lax.rsqrt(jnp.mean(x * x, axis=-1, keepdims=True) + EPSILON)
            r.n1_s[s] = (x * scale * gain).astype(BF)
        n1 = jnp.concatenate([r.n1_s[2 * p], r.n1_s[2 * p + 1]], axis=0)
        low = [mm_nt(n1, a[...]) for a in (r.aq, r.ak, r.av)]
        base = [mm(n1, w[...]) for w in (r.wq, r.wk, r.wv)]
        for i in (0, 1):
            s = 2 * p + i
            half = slice(i * rows, (i + 1) * rows)
            own = jnp.where(stacked == r.variant[s], 1.0, 0.0)
            h = [(a[half] * own).astype(BF) for a in low]
            small = [mm_nt(a, chooser[s]) for a in h] + [jnp.zeros((rows, 128 - 3 * RANK), F32)]
            r.h_one[s] = jnp.concatenate(small, axis=1).astype(BF)
            q, k, val = (
                jnp.transpose(base[n][half] + mm(h[n] * 2, f[...])) for n, f in enumerate((r.bq, r.bk, r.bv))
            )
            r.pre_s[s, :qw, :] = q
            r.pre_s[s, qw:, :] = k
            q = prepare(q, qg).reshape(heads_k, group * HEAD_DIM, rows)
            k, val = prepare(k, kg), val.astype(BF).reshape(heads_k, HEAD_DIM, rows)
            for n in range(heads_k):
                r.q_msg[n * sequences + s] = q[n]
                r.kv_msg[n * sequences + s, :HEAD_DIM, :] = k[n]
                r.kv_msg[n * sequences + s, HEAD_DIM:, :] = val[n]

    def own_kv():
        return pltpu.make_async_copy(r.kv_msg.at[unit], r.kv_all_s.at[me], r.own_sems.at[0])

    def own_q():
        return pltpu.make_async_copy(r.q_msg.at[unit], r.q_all_s.at[unit], r.own_sems.at[1])

    per_pair = 2 * heads_k

    def send_keys(p):
        def step(k):
            turned = lax.rem(unit + k, per_pair)
            index = turned // 2 * sequences + 2 * p + lax.rem(turned, 2)
            for t in range(parts):

                @pl.when(index * parts + t != me)
                def _():
                    kv_copy(index, t, me).start()

            @pl.when(index != unit)
            def _():
                q_copy[0](index, unit).start()

            @pl.when(index == unit)
            def _():
                own_kv().start()
                own_q().start()

        loop(0, per_pair, step)

    part_rows = r.wo_s.shape[0] // 2
    rows_of = lambda who: pl.ds(pl.multiple_of(who * part_rows, 16), part_rows)
    w_copies = [
        remote(r.wo_s.at[rows_of(core), :], r.wo_x.at[rows_of(core), :], r.w_send.at[0], r.w_recv.at[0], across),
        remote(r.wo_x.at[rows_of(core), :], r.wo_x.at[rows_of(core), :], r.w_send.at[1], r.w_recv.at[1], twin),
        remote(r.c_ao_s, r.ao_x, r.w_send.at[2], r.w_recv.at[2], across),
    ]

    project(0)
    pl.semaphore_wait(barrier, count)
    send_keys(0)
    for p in range(1, sequences // 2):
        project(p)
        send_keys(p)
    for h in range(1, group):
        loop(1, units, lambda k, h=h: q_copy[h](turn_of(k), unit).start())
    for n in ("n1", "pre"):
        saves[n].start()
    far[1 + tiles].wait()
    w_copies[0].start()

    def choose(names):
        for f in names:
            far[2 + tiles + FACTORS.index(f)].wait()
            getattr(r, "c_" + f + "_s")[...] = mm(choosers, getattr(r, f + "_s")[...]).astype(BF)
            saves["c_" + f].start()

    document_starts(r.segs, lax.rem(unit, sequences), r.starts)
    choose(("ao", "bd", "ad"))
    w_copies[2].start()
    far[0].wait()
    d = mm_nt(r.cot_s[...], r.c_bd_s[...]) * 2.0
    r.dhd[...] = jnp.where(own_ranks(0, *d.shape), d, 0.0).astype(BF)
    dh_saves = []
    for f in range(tiles):
        far[1 + f].wait()
        columns = slice(f * tile, (f + 1) * tile)
        r.dh_s[:, columns] = (mm_nt(r.cot_s[...], r.wd_s[f]) + mm(r.dhd[...], r.c_ad_s[:, columns])).astype(BF)
        dh_saves.append(pltpu.make_async_copy(r.dh_s.at[:, columns], r.dh.at[:, columns], r.dh_sems.at[f]))
        dh_saves[-1].start()

    own_kv().wait()
    own_q().wait()
    loop(1, count, lambda k: kv_copy(unit, part, lax.rem(me + k, count)).wait_recv())
    load_keys(r.kv_all_s, r.kb, r.vt)
    saves["kv_all"].start()

    def keep_own(h):
        return pltpu.make_async_copy(r.o_buf.at[h, unit], r.home_s.at[unit, head_rows(h), :], r.own_sems.at[2 + h])

    tiles_q = units // BLOCKS
    my_tile = unit // BLOCKS

    def pass_on(h, n):
        def relay(v):
            other = v * tiles_q + lax.rem(my_tile - n + tiles_q, tiles_q)

            @pl.when(other == unit)
            def _():
                keep_own(h).wait()
                x_copy(h, other).start()

            @pl.when(other != unit)
            def _():
                o_copy[h](unit, other).wait_recv()
                x_copy(h, other).start()

        loop(0, units // tiles_q, relay)

    for h in range(group):
        loop(1, units, lambda k, h=h: q_copy[h](unit, turn_of(k)).wait_recv())
        if h == group - 1:
            saves["q_all"].start()

        def done(n, i, out, h=h):
            for b in range(BLOCKS):
                block = BLOCKS * i + b
                r.o_buf[h, block] = out[:, b * 128 : (b + 1) * 128]

                @pl.when(block == unit)
                def _():
                    keep_own(h).start()

                @pl.when(block != unit)
                def _():
                    o_copy[h](block, unit).start()

            for m in range(tiles_q):
                if m >= LAG or h > 0:

                    @pl.when(n == m)
                    def _(m=m):
                        pass_on(h if m >= LAG else h - 1, m - LAG if m >= LAG else m - LAG + tiles_q)

        head_forward(h, parts, part, unit, r.q_all_s, r.starts, r.kb, r.vt, r.acc, r.of_s, r.lse, done)
        if h == 0:
            w_copies[0].wait_recv()
            w_copies[1].start()
    saves["of"].start()
    choose(("ag", "au", "bg", "bu", "bo"))
    for n in range(tiles_q - LAG, tiles_q):
        pass_on(group - 1, n)
    for s in range(sequences):
        r.ac[s] = jnp.concatenate([mm(chooser[s], a[...]) for a in (r.aq, r.ak, r.av)], axis=0).astype(BF)
        r.bc[s] = jnp.concatenate([mm(chooser[s], b[...]) for b in (r.bq, r.bk, r.bv)], axis=1).astype(BF)
        for v in range(r.pick.shape[0]):
            r.pick[v, s] = jnp.full((8, 128), jnp.where(r.variant[s] == v, 1.0, 0.0), F32)
    r.gains[0], r.gains[1] = qg, kg
    saves["home"].start()
    w_copies[1].wait_recv()
    w_copies[2].wait_recv()
    for h in range(group):
        loop(0, units, lambda i, h=h: x_copy(h, i).wait_recv())

    gain = r.gain_two[...][None, :]
    for p in range(sequences // 2):
        for i in (0, 1):
            half = slice(i * rows, (i + 1) * rows)
            for lhs, home in ((r.lhs, r.home_s), (r.lhs_x, r.home_x)):
                blocks = [home[n * sequences + 2 * p + i] for n in range(heads_k)]
                lhs[half, :] = jnp.transpose(jnp.concatenate(blocks, axis=0))
        out = mm(r.lhs[...], r.wo_s[...]) + mm(r.lhs_x[...], r.wo_x[...])
        for i in (0, 1):
            s = 2 * p + i
            half, own = slice(i * rows, (i + 1) * rows), slice(s * RANK, (s + 1) * RANK)
            h = (mm_nt(r.lhs[half, :], r.c_ao_s[own, :]) + mm_nt(r.lhs_x[half, :], r.ao_x[own, :])).astype(BF)
            r.h_out[s] = jnp.concatenate([h, jnp.zeros((rows, 128 - RANK), BF)], axis=1)
            mid = r.x[s].astype(F32) + (out[half] + mm(h * 2, r.c_bo_s[own, :]))
            r.mid_s[s] = mid
            scale = lax.rsqrt(jnp.mean(mid * mid, axis=-1, keepdims=True) + EPSILON)
            r.n2_s[s] = (mid * scale * gain).astype(BF)
    saves["mid"].start()
    saves["n2"].start()

    for c in list(saves.values()) + dh_saves:
        c.wait()
    for c in w_copies:
        c.wait_send()

    def finish_full(k):
        other = lax.rem(me + k, count)
        kv_copy(other // parts, lax.rem(other, parts), me).wait_send()

    loop(1, count, finish_full)
    for h in range(group):

        def finish_block(k, h=h):
            q_copy[h](turn_of(k), unit).wait_send()
            o_copy[h](turn_of(k), unit).wait_send()

        loop(1, units, finish_block)
        loop(0, units, lambda i, h=h: x_copy(h, i).wait_send())


def forward(near, far, count, parts, collective_id):
    n = Names(FORWARD_NEAR + FORWARD_FAR, tuple(near) + tuple(far))
    sequences, rows, width = n.x.shape
    qw, kw = n.wq.shape[1], n.wk.shape[1]
    units, group = count // parts, qw // kw
    tiles, ktiles = units // BLOCKS, count // BLOCKS
    hidden_units, tile = n.wd.shape[0], feed_tile(n.wd.shape[0])
    spare, ranks = hidden_units // tile, sequences * RANK
    q_shape, kv_shape = (units, group * HEAD_DIM, rows), (count, 2 * HEAD_DIM, rows)
    small = (
        shape((sequences, rows, 128), BF), shape((sequences, 3 * RANK, width), BF), shape((sequences, RANK, qw + 2 * kw), BF),
        shape((2, HEAD_DIM, rows), F32), shape((n.aq.shape[0] // RANK, sequences, 8, 128), F32),
        shape((group, tiles, 8, TILE), F32), shape((count, 1, 128), jnp.int32), shape((sequences * rows, ranks), BF),
        shape((sequences, rows, 128), BF),
    )
    saved = (
        shape(n.x.shape, BF), shape((sequences, qw + kw, rows), F32), shape(q_shape, BF), shape(kv_shape, BF),
        shape(q_shape, F32), shape(q_shape, BF), shape(n.x.shape, F32), shape(n.x.shape, BF),
    ) + tuple(shape((ranks, getattr(n, f).shape[1]), BF) for f in FACTORS)
    dma, vm = pltpu.SemaphoreType.DMA, pltpu.VMEM
    buffers = [vm(getattr(n, f).shape, BF) for f in FACTORS] + [vm(s.shape, s.dtype) for s in saved]
    buffers += [
        vm(n.cot.shape, BF), vm((spare, tile, width), BF), vm(n.wo.shape, BF), vm(n.wo.shape, BF), vm((ranks, qw), BF),
        vm((sequences * rows, hidden_units), BF), vm(q_shape, BF), vm((units,) + kv_shape[1:], BF),
        vm((group, units, HEAD_DIM, 128), BF), vm((ktiles, TILE, HEAD_DIM), BF), vm((ktiles, HEAD_DIM + 16, TILE), BF),
        vm((HEAD_DIM + 16, TILE), F32), vm(q_shape, BF), vm((2 * rows, qw), BF), vm((2 * rows, qw), BF),
    ]
    sems = [dma((2 + spare + len(FACTORS),)), dma((len(saved),)), dma((spare,)), dma((count,)), dma((count,))]
    sems += [dma((group, units))] * 6 + [dma((2 + group,)), dma((3,)), dma((3,))]
    outs = pl.pallas_call(
        functools.partial(forward_kernel, count, parts),
        out_shape=small + saved + (shape((sequences * rows, hidden_units), BF),),
        in_specs=[SMEM] + [VM] * (len(FORWARD_NEAR) - 1) + [ANYWHERE] * len(FORWARD_FAR),
        out_specs=(VM,) * len(small) + (ANYWHERE,) * (len(saved) + 1),
        scratch_shapes=buffers + sems,
        compiler_params=pltpu.CompilerParams(
            collective_id=collective_id, has_side_effects=True, vmem_limit_bytes=62 * 2**20
        ),
        name="forward",
    )(*near, *far)
    return Names(FORWARD_OUT, outs)


def finish_kernel(reduce, count, shared, *refs):
    refs = list(refs)
    take = lambda n: [refs.pop(0) for _ in range(n)]
    dq_ref, dkv_ref, pre_ref, h_ref, gains, cos_ref, sin_ref, gain_ref, bc_ref, pick_ref, bd_ref = take(11)
    far = take(11)
    early = take(1) if reduce else []
    out_ref, block_ref = take(2)
    gout = take(4) if reduce else take(1)
    x, d_mid, n1, wq, wk, wv, ac, mid, down, down_x, cot = near = take(11)
    d_n, gb, dh_own, dh_other, dh_sum, sbuf, rbuf, gq = take(8)
    near_sems, dh_send, dh_recv, xsend, xrecv = take(5)
    sequences, rows = dq_ref.shape[1], dq_ref.shape[3]
    inner = dq_ref.shape[0] * dq_ref.shape[2]
    width = out_ref.shape[2]
    kw = wk.shape[1]
    half_rows = sequences * RANK // 2
    me = lax.axis_index("ctx")
    across = {"tp": 1 - lax.axis_index("tp")}
    mine = pl.ds(pl.multiple_of(lax.axis_index("tp") * (width // 2), width // 2), width // 2)

    loads = [pltpu.make_async_copy(f, n, near_sems.at[i]) for i, (f, n) in enumerate(zip(far, near))]
    barrier = pltpu.get_barrier_semaphore()
    pl.semaphore_signal(barrier, inc=1, device_id=across, device_id_type=MESH)
    peers = 1
    if reduce:
        core_in, plane, z_in, plane_in = take(4)
        fin_outs, fin_ins, shared_out = take(2), take(2), take(2)
        twin_sems, z_send, z_recv, plane_send, plane_recv, fin_send, fin_recv, last_sems = take(8)
        chips = count // 2
        chip, core = me // 2, lax.rem(me, 2)
        twin = {"ctx": 2 * chip + 1 - core}
        pl.semaphore_signal(barrier, inc=1, device_id=twin, device_id_type=MESH)

        def at_chip(k):
            return lax.rem(chip + k, chips)

        def greet(k, _):
            pl.semaphore_signal(barrier, inc=1, device_id={"ctx": 2 * at_chip(k) + core}, device_id_type=MESH)
            return 0

        lax.fori_loop(1, chips, greet, 0)
        peers += chips

        w_qkv = gq.shape[2]
        to_twin = remote(gq.at[1 - core], core_in, twin_sems.at[0], twin_sems.at[1], twin)
    for i in (3, 4, 5, 2, 6, 7, 8, 9, 10, 0, 1):
        loads[i].start()
    pl.semaphore_wait(barrier, peers)
    if reduce:
        deep = chips // 2
        z, y = chip // 2, lax.rem(chip, 2)

        def z_copy(other, sender):
            chunk = early[0].shape[1] // deep
            return remote(
                early[0].at[:, pl.ds(pl.multiple_of(other * chunk, 128), chunk)], z_in.at[sender], z_send.at[other],
                z_recv.at[sender], {"ctx": 4 * other + 2 * y + core},
            )

        def each_z(step):
            loop(1, deep, lambda k: step(lax.rem(z + k, deep)))

        each_z(lambda k: z_copy(k, z).start())

    cosine, sine = cos_ref[...], sin_ref[...]
    heads_k = kw // HEAD_DIM
    cuts = (slice(0, inner), slice(inner, inner + kw), slice(inner + kw, inner + 2 * kw))

    def prepare_back(pre, gains, c):
        u = pre.reshape(pre.shape[0] // HEAD_DIM, HEAD_DIM, rows)
        scale = lax.rsqrt(jnp.mean(u * u, axis=1, keepdims=True) + EPSILON)
        y = u * scale
        w = turn(c.reshape(u.shape).astype(F32), cosine, -sine) * gains
        return (scale * (w - y * jnp.mean(w * y, axis=1, keepdims=True))).reshape(pre.shape)

    def first_step(s):
        dkv = dkv_ref[:, s].astype(F32)
        dkv = jnp.sum(dkv, axis=1).astype(BF) if dkv.shape[1] > 1 else dkv[:, 0].astype(BF)
        d_q = prepare_back(pre_ref[s, :inner, :], gains[0], dq_ref[:, s].reshape(inner, rows))
        d_k = prepare_back(pre_ref[s, inner:, :], gains[1], dkv[:, :HEAD_DIM, :].reshape(kw, rows))
        d_v = dkv[:, HEAD_DIM:, :].reshape(kw, rows).astype(F32)
        d = jnp.transpose(jnp.concatenate([d_q, d_k, d_v], axis=0)).astype(BF)
        d_n[s] = d
        dh = [mm_nt(d[:, c], bc_ref[s, :, c]) * 2.0 for c in cuts]
        dh = jnp.transpose(jnp.concatenate(dh + [jnp.zeros((rows, 128 - 3 * RANK), F32)], axis=1))
        dh_own[s] = dh[: 3 * RANK].astype(BF)
        t = (jnp.transpose(h_ref[s].astype(F32)) * 2.0).astype(BF)
        gb[s] = jnp.concatenate([mm(t[i * RANK : (i + 1) * RANK], d[:, c]) for i, c in enumerate(cuts)], axis=1)

    def part_copy(s):
        return remote(sbuf.at[s], rbuf.at[s], xsend.at[s], xrecv.at[s], across)

    dh_copy = remote(dh_own, dh_other, dh_send.at[0], dh_recv.at[0], across)

    def send_pair(p):
        d = jnp.concatenate([d_n[2 * p], d_n[2 * p + 1]], axis=0)
        part = mm_nt(d[:, cuts[0]], wq[...]) + mm_nt(d[:, cuts[1]], wk[...]) + mm_nt(d[:, cuts[2]], wv[...])
        for i in (0, 1):
            sbuf[2 * p + i] = part[i * rows : (i + 1) * rows].astype(BF)
            part_copy(2 * p + i).start()

    def plane_copy(k, slot):
        chunk = plane.shape[1] // chips
        return remote(
            plane.at[:, pl.ds(pl.multiple_of(k * chunk, 128), chunk)], plane_in.at[slot], plane_send.at[k],
            plane_recv.at[slot], {"ctx": 2 * k + core},
        )

    def fin_copy(g, k, slot):
        return remote(
            fin_outs[g].at[k], fin_ins[g].at[slot], fin_send.at[g, k], fin_recv.at[g, slot], {"ctx": 2 * k + core}
        )

    def each_chip(step):
        loop(1, chips, lambda k: step(at_chip(k)))

    def to_plane():
        to_twin.wait_recv()
        plane[:, :w_qkv] = (gq[core].astype(F32) + core_in[...].astype(F32)).astype(BF)
        if plane.shape[1] > w_qkv:
            plane[:, w_qkv:] = jnp.zeros((half_rows, plane.shape[1] - w_qkv), BF)
        chunk = plane.shape[1] // chips
        each_chip(lambda k: plane_copy(k, chip).start())
        plane_in[chip] = plane[:, pl.ds(pl.multiple_of(chip * chunk, 128), chunk)]

    def to_owners(g):
        if g == 0:
            each_z(lambda k: z_copy(k, k).wait_recv())
            chunk = early[0].shape[1] // deep
            z_in[z] = early[0][:, pl.ds(pl.multiple_of(z * chunk, 128), chunk)]
        else:
            each_chip(lambda k: plane_copy(k, k).wait_recv())
        blocks = z_in if g == 0 else plane_in
        total = blocks[0].astype(F32)
        for k in range(1, blocks.shape[0]):
            total = total + blocks[k].astype(F32)
        for k in range(chips):
            fin_outs[g][k] = owner_rows(total, pick_ref, k, sequences)
        each_chip(lambda k: fin_copy(g, k, chip).start())
        fin_ins[g][chip] = fin_outs[g][chip]

    def rows_in(g):
        each_chip(lambda k: fin_copy(g, k, k).wait_recv())
        chunk = gout[g].shape[1] // chips
        for k in range(chips):
            unfold_rows(gout[g], (k % 2 * deep + k // 2 if g == 0 else k) * chunk, fin_ins[g][k])
        low, high = shared[g]
        middle = (low + high) // 2
        shared_out[g][...] = jnp.concatenate([gout[g][:, low:middle], gout[g][:, middle:high]], axis=0).astype(BF)
        copy = remote(shared_out[g], gout[2 + g], last_sems.at[g], last_sems.at[2 + g], across)
        copy.start()
        return copy

    def last_step(s):
        part_copy(s).wait_recv()
        c = sbuf[s].astype(F32) + rbuf[s].astype(F32) + mm(dh_sum[s][:, : 3 * RANK], ac[s])
        out_ref[s] = (d_mid[s] + norm_back(x[s].astype(F32), gain_ref[...][None, :], c)).astype(BF)

    for s in range(sequences):
        first_step(s)
    dh_copy.start()
    for i in (3, 4, 5):
        loads[i].wait()
    for p in range(sequences // 2):
        send_pair(p)
    dh_copy.wait()
    for i in (2, 7, 8, 9, 10):
        loads[i].wait()
    blocks = []
    for s in range(sequences):
        total = down[s].astype(F32) + down_x[s].astype(F32)
        h = total[:, width : width + RANK].astype(BF) * 2
        block_ref[s] = (mid[s] + (total[:, :width] + mm(h, bd_ref[s * RANK : (s + 1) * RANK, :]))).astype(BF)
        wide = jnp.concatenate([h, jnp.zeros((rows, 128 - RANK), BF)], axis=1)
        gb_down = mm(jnp.transpose(wide.astype(F32)).astype(BF)[:RANK], cot[s, :, mine])
        dh = (dh_own[s].astype(F32) + dh_other[s].astype(F32)).astype(BF)
        dh_sum[s] = jnp.transpose(jnp.concatenate([dh.astype(F32), jnp.zeros((128 - 3 * RANK, rows), F32)], axis=0)).astype(BF)
        wide = mm(dh, n1[s, :, mine])
        blocks.append(jnp.concatenate([wide[i * RANK : (i + 1) * RANK] for i in range(3)] + [gb_down, gb[s]], axis=1))
    everything = rank_halves(blocks)
    for b in (0, 1):
        gq[b] = everything[b * half_rows : (b + 1) * half_rows].astype(BF)
    if reduce:
        to_twin.start()
        to_plane()
        to_owners(0)
    for i in (6, 0, 1):
        loads[i].wait()
    if reduce:
        last_step(0)
        to_owners(1)
        shared_copies = [rows_in(0)]
        last_step(1)
        shared_copies.append(rows_in(1))
        for s in range(2, sequences):
            last_step(s)
        for c in shared_copies:
            c.wait()
        to_twin.wait_send()
        each_z(lambda k: z_copy(k, z).wait_send())
        each_chip(lambda k: plane_copy(k, chip).wait_send())
        for g in (0, 1):
            each_chip(lambda k, g=g: fin_copy(g, k, chip).wait_send())
    else:
        for s in range(sequences):
            last_step(s)
        gout[0][...] = gq[...]
    for s in range(sequences):
        part_copy(s).wait_send()


def finish(
    reduce, count, dq, dkv, pre, h, gains, tables, gain, bc, pick, bd, x, d_mid, n1, weights, ac, mid, down, down_x, cot,
    early, shared, collective_id,
):
    sequences, rows, width = x.shape
    inner, kw = weights[0].shape[1], weights[1].shape[1]
    w_qkv = 4 * (width // 2) + inner + 2 * kw
    half_rows = sequences * RANK // 2
    dma = pltpu.SemaphoreType.DMA
    far = (x, d_mid, n1) + tuple(weights) + (ac, mid, down, down_x, cot)
    gshape = (shape((2, half_rows, w_qkv), BF),)
    scratch = [pltpu.VMEM(a.shape, a.dtype) for a in far]
    scratch += [
        pltpu.VMEM((sequences, rows, inner + 2 * kw), BF),
        pltpu.VMEM((sequences, RANK, inner + 2 * kw), F32),
        pltpu.VMEM((sequences, 3 * RANK, rows), BF),
        pltpu.VMEM((sequences, 3 * RANK, rows), BF),
        pltpu.VMEM((sequences, rows, 128), BF),
        pltpu.VMEM(x.shape, BF),
        pltpu.VMEM(x.shape, BF),
        pltpu.VMEM((2, half_rows, w_qkv), BF),
        dma((11,)), dma((1,)), dma((1,)), dma((sequences,)), dma((sequences,)),
    ]
    if reduce:
        chips = count // 2
        totals = (2 * early[0].shape[1], padded(w_qkv, chips))
        gshape = tuple(shape((RANK // 2, n), F32) for n in totals)
        gshape += tuple(shape((RANK, (b - a) // 2), BF) for a, b in shared)
        scratch += [
            pltpu.VMEM((half_rows, w_qkv), BF),
            pltpu.VMEM((half_rows, totals[1]), BF),
            pltpu.VMEM((chips // 2, half_rows, totals[0] // chips), BF),
            pltpu.VMEM((chips, half_rows, totals[1] // chips), BF),
        ]
        scratch += [pltpu.VMEM((chips, RANK, n // chips // 2), BF) for n in totals] * 2
        scratch += [pltpu.VMEM((RANK, (b - a) // 2), BF) for a, b in shared]
        scratch += [dma((2,)), dma((chips // 2,)), dma((chips // 2,)), dma((chips,)), dma((chips,))]
        scratch += [dma((2, chips))] * 2 + [dma((4,))]
    return pl.pallas_call(
        functools.partial(finish_kernel, reduce, count, shared),
        out_shape=(shape(x.shape, BF),) * 2 + gshape,
        in_specs=[VM] * 11 + [ANYWHERE] * 11 + [VM] * len(early),
        out_specs=(VM,) * (2 + len(gshape)),
        scratch_shapes=scratch,
        compiler_params=pltpu.CompilerParams(
            collective_id=collective_id, has_side_effects=True, vmem_limit_bytes=60 * 2**20
        ),
        name="finish",
    )(dq, dkv, pre, h, gains, *tables, gain, bc, pick, bd, *far, *early)


def unpack_kernel(hidden_units, tile, inner, kw, block, grad, first, second, first_x, second_x, block_out, grad_out, *outs):
    block_out[...] = block[...]
    grad_out[...] = grad[...]
    ga_query, gb_query, ga_key, gb_key, ga_value, gb_value, ga_out, gb_out, ga_gate, gb_gate, ga_up, gb_up, ga_down, gb_down = outs
    width = ga_query.shape[1]
    w = width // 2
    lower = lax.axis_index("tp") == 0

    def join(out, own, own_at, other, i):
        a = own[:, own_at + i * w : own_at + (i + 1) * w]
        b = other[:, i * w : (i + 1) * w]
        out[:, :w] = jnp.where(lower, a, b)
        out[:, w:] = jnp.where(lower, b, a)

    @pl.when(pl.program_id(0) == 0)
    def _():
        for f in range(hidden_units // tile):
            for n, out in enumerate((gb_gate, gb_up, ga_down)):
                out[:, f * tile : (f + 1) * tile] = first[:, (3 * f + n) * tile : (3 * f + n + 1) * tile]
        at = 3 * hidden_units
        ga_out[...] = first[:, at : at + inner]
        rows = first.shape[0]
        unfold = lambda x: jnp.concatenate([x[:rows].astype(F32), x[rows:].astype(F32)], axis=1)
        other = unfold(first_x[...])
        for i, out in enumerate((ga_gate, ga_up, gb_out)):
            join(out, first, at + inner, other, i)
        other = unfold(second_x[...])
        for i, out in enumerate((ga_query, ga_key, ga_value, gb_down)):
            join(out, second, 0, other, i)
        at = 4 * w
        gb_query[...] = second[:, at : at + inner]
        gb_key[...] = second[:, at + inner : at + inner + kw]
        gb_value[...] = second[:, at + inner + kw : at + inner + 2 * kw]


def unpack(block, grad, owned, hidden_units, tile, inner, kw):
    width, rows = block.shape[2], owned[0].shape[0]
    sizes = (width, inner, width, kw, width, kw, inner, width, width, hidden_units, width, hidden_units, hidden_units, width)
    outs = tuple(shape((rows, n), F32) for n in sizes)
    return pl.pallas_call(
        functools.partial(unpack_kernel, hidden_units, tile, inner, kw),
        grid=(block.shape[0],),
        out_shape=(shape(block.shape, BF),) * 2 + outs,
        in_specs=[stepped(block.shape, 1)] * 2 + [whole(a) for a in owned],
        out_specs=(stepped(block.shape, 1),) * 2 + tuple(whole(a) for a in outs),
        compiler_params=BIG,
        name="unpack",
    )(block, grad, *owned)


def rotary_tables(positions):
    half = HEAD_DIM // 2
    frequencies = THETA_BASE ** (-jnp.arange(half, dtype=F32) * 2.0 / HEAD_DIM)
    angles = frequencies[:, None] * positions.astype(F32)[None, :]
    return jnp.cos(angles), jnp.sin(angles)


def swap(values):
    return lax.ppermute(values, "tp", [(0, 1), (1, 0)])


def reduce_scatter_rows(grads, count):
    rows, columns = grads.shape
    index = lax.axis_index("ctx")
    held = grads.reshape(count, rows // count, columns)
    bit = 1
    while bit < count:
        mine = (index // bit) % 2
        pairs = held.reshape(held.shape[0] // 2, 2, held.shape[1], columns)
        kept = lax.dynamic_index_in_dim(pairs, mine, 1, keepdims=False)
        sent = lax.dynamic_index_in_dim(pairs, 1 - mine, 1, keepdims=False).astype(BF)
        held = kept.astype(F32) + lax.ppermute(sent, "ctx", [(i, i ^ bit) for i in range(count)]).astype(F32)
        bit *= 2
    return held[0]


def local(
    tokens, output_cotangent, segment_ids, variant, attn_gain, ffn_gain, q_gain, k_gain,
    query_matrix, key_matrix, value_matrix, output_matrix, gate_matrix, up_matrix, down_matrix,
    query_input_factor, query_output_factor, key_input_factor, key_output_factor,
    value_input_factor, value_output_factor, output_input_factor, output_output_factor,
    gate_input_factor, gate_output_factor, up_input_factor, up_output_factor,
    down_input_factor, down_output_factor,
):
    sequences, rows_here, width = tokens.shape
    count = lax.axis_size("ctx")
    index = lax.axis_index("ctx")
    inner, kw = query_matrix.shape[1], key_matrix.shape[1]
    key_heads = kw // HEAD_DIM
    units = sequences * key_heads
    parts = count // units
    stacked = query_input_factor.shape[0]
    reduce_here = stacked // count == RANK // 2
    tables = rotary_tables(index * rows_here + jnp.arange(rows_here, dtype=jnp.int32))
    weights = (query_matrix, key_matrix, value_matrix)
    ins = (query_input_factor, key_input_factor, value_input_factor)
    outs = (query_output_factor, key_output_factor, value_output_factor)

    flat = lambda a: a.reshape(sequences * rows_here, -1)
    p = forward(
        (variant, tokens, attn_gain, ffn_gain, q_gain, k_gain, *tables, segment_ids, *weights, *ins, *outs),
        (
            flat(output_cotangent), down_matrix, output_matrix, gate_input_factor, up_input_factor, down_output_factor,
            gate_output_factor, up_output_factor, down_input_factor, output_output_factor, output_input_factor,
        ),
        count, parts, 0,
    )
    by_head = (key_heads, sequences)
    attn = p.home.reshape(by_head + p.home.shape[1:])

    cuts = tuple(rows_here * s for s in (0, sequences // 2, sequences))
    g_ffn, down, d_mid, d_attn, g_mid = feed(
        cuts, flat(p.n2), p.dhd, p.c_ag, p.c_au, p.c_bo, p.c_ao, output_matrix, ffn_gain, gate_matrix, up_matrix,
        down_matrix, p.c_bg, p.c_bu, p.c_ad, p.dh, p.mid, output_cotangent, p.h_out, attn, 3,
    )
    d_attn = d_attn.reshape(p.q_all.shape)
    d_attn, down = lax.optimization_barrier((d_attn, down))
    down_other = swap(down)
    early = (g_ffn, g_mid) if reduce_here else ()
    dq, dkv, *early = attend_back(d_attn, p.q_all, p.kv_all, p.of, p.lse, p.starts, early, count, parts, 1)

    w = width // 2
    hidden_units = gate_matrix.shape[1]
    tile = feed_tile(hidden_units)
    at = 3 * hidden_units + inner
    shared = ((at, at + 3 * w), (0, 4 * w))
    input_grad, block_result, *ends = finish(
        reduce_here, count, dq.reshape(by_head + dq.shape[1:]), dkv.reshape(by_head + (parts,) + dkv.shape[1:]),
        p.pre, p.h_one, p.gains, tables, attn_gain, p.bc, p.pick, p.c_bd, tokens, d_mid, p.n1, weights, p.ac,
        p.mid, down, down_other, output_cotangent, early, shared, 2,
    )
    if reduce_here:
        owned = ends
    else:
        per = RANK // 2
        pick = (jnp.arange(stacked // RANK, dtype=jnp.int32)[:, None] == variant[None, :]).astype(F32)
        owned, other = [], []
        for grads, (low, high) in zip((jnp.concatenate([g_ffn, g_mid], axis=1), ends[0]), shared):
            grads = grads.reshape(2, sequences, per, -1).astype(F32)
            dense = jnp.sum(pick[:, None, :, None, None] * grads[None], axis=2)
            owned.append(reduce_scatter_rows(dense.reshape(stacked, -1), count))
            half = swap(owned[-1][:, low:high])
            other.append(jnp.concatenate(jnp.split(half, 2, axis=1), axis=0))
        owned = owned + other
    return tuple(unpack(block_result, input_grad, owned, hidden_units, tile, inner, kw))


def solution(mesh):
    rows, whole, columns = P(None, "ctx", None), P(), P(None, "tp")
    owned, owned_half = P("ctx", None), P("ctx", "tp")
    return jax.shard_map(
        local,
        mesh=mesh,
        in_specs=(rows, rows) + (whole,) * 6
        + (columns, columns, columns, P("tp", None), columns, columns, P("tp", None))
        + (whole, columns) * 3 + (columns, whole) + (whole, columns) * 2 + (columns, whole),
        out_specs=(
            rows, rows, owned, owned_half, owned, owned_half, owned, owned_half,
            owned_half, owned, owned, owned_half, owned, owned_half, owned_half, owned,
        ),
        check_vma=False,
    )
```

```python
import functools, jax, jax.numpy as jnp
from jax import lax
from jax.experimental import pallas as pl
from jax.experimental.pallas import tpu as pltpu
from jax.sharding import PartitionSpec as P

HEAD_DIM = 64
LOG2E = 1.4426950408889634
MESH = pl.DeviceIdType.MESH
SMEM = pl.BlockSpec(memory_space=pltpu.SMEM)
VM = pl.BlockSpec(memory_space=pltpu.VMEM)
RANK = 16
EPSILON = 1e-05
THETA_BASE = 1000000.0
BF = jnp.bfloat16
F32 = jnp.float32
NT = (((1,), (1,)), ((), ()))
BIG = pltpu.CompilerParams(vmem_limit_bytes=60 * 2**20)


def cost(rows, width, columns, products, moved):
    return pl.CostEstimate(flops=2 * products * rows * width * columns, bytes_accessed=moved, transcendentals=0)

ANYWHERE = pl.BlockSpec(memory_space=pl.ANY)


def mm(a, b):
    return jnp.dot(a, b, preferred_element_type=F32)


def mm_nt(a, b):
    return lax.dot_general(a, b, NT, preferred_element_type=F32)


def shape(dims, kind):
    return jax.ShapeDtypeStruct(dims, kind)


def remote(source, target, send, recv, device):
    return pltpu.make_async_remote_copy(
        src_ref=source, dst_ref=target, send_sem=send, recv_sem=recv, device_id=device, device_id_type=MESH
    )


def norm_back(u, gain, c):
    scale = lax.rsqrt(jnp.mean(u * u, axis=-1, keepdims=True) + EPSILON)
    y = u * scale
    w = c * gain
    return scale * (w - y * jnp.mean(w * y, axis=-1, keepdims=True))


def turn(values, cosine, sine):
    half = HEAD_DIM // 2
    a, b = values[:, :half], values[:, half:]
    return jnp.concatenate([a * cosine - b * sine, b * cosine + a * sine], axis=1)


def rank_halves(blocks):
    return jnp.concatenate([b[: RANK // 2] for b in blocks] + [b[RANK // 2 :] for b in blocks], axis=0)


def column(ref):
    return jnp.transpose(jnp.broadcast_to(ref[...][None, :], (128, ref.shape[0])))


def whole(array):
    return pl.BlockSpec(array.shape, lambda i: (0,) * len(array.shape), pipeline_mode=pl.Buffered(1))


def stepped(dims, per):
    return pl.BlockSpec((per,) + tuple(dims[1:]), lambda i: (i,) + (0,) * (len(dims) - 1))


def own_ranks(first, rows, ranks):
    row = lax.broadcasted_iota(jnp.int32, (rows, ranks), 0) // 128 + first // 128
    return row == lax.broadcasted_iota(jnp.int32, (rows, ranks), 1) // RANK


def feed_kernel(
    cuts, n2_ref, dhd_ref, ag, au, bo, ao, wo, gain_ref, wd_ref, bg_ref, bu_ref, ad_ref, dh_ref,
    mid_ref, cot_ref, hout_ref, attn_ref, wg_ref, wu_ref,
    grads_ref, down_ref, dmid_ref, dattn_ref, more_ref,
    hg, hu, hs, dn2_acc, dhg_acc, dhu_acc, down_acc, h_acc, hidden_s, dgu_s, w_s, back_s, back_x, branch_s, more_s,
    send_sems, recv_sems, w_sems,
):
    step = pl.program_id(0)
    rows, width = n2_ref.shape
    tiles, tile = hidden_s.shape[0], hidden_s.shape[2]
    seqs = rows // 128
    ranks = seqs * RANK
    chunks = len(cuts) - 1
    last = chunks * tiles
    f = lax.rem(step, tiles)
    across = {"tp": 1 - lax.axis_index("tp")}

    def compact(a, first=0):
        a = jnp.where(own_ranks(first, *a.shape), a, 0.0)
        return sum(a[:, i * RANK : (i + 1) * RANK] for i in range(seqs))

    def copy(s):
        there = pl.ds(s * 128, 128)
        return remote(back_s.at[there, :], back_x.at[there, :], send_sems.at[s], recv_sems.at[s], across)

    def weights(i):
        columns, slot = pl.ds(pl.multiple_of(lax.rem(i, tiles) * tile, 128), tile), lax.rem(i, 2)
        return [
            pltpu.make_async_copy(w.at[:, columns], w_s.at[slot, :, n * tile : (n + 1) * tile], w_sems.at[slot, n])
            for n, w in enumerate((wg_ref, wu_ref))
        ]

    @pl.when(step == 0)
    def _():
        for i in (0, 1):
            for load in weights(i):
                load.start()
        barrier = pltpu.get_barrier_semaphore()
        pl.semaphore_signal(barrier, inc=1, device_id=across, device_id_type=MESH)
        pl.semaphore_wait(barrier, 1)
        kept = own_ranks(0, rows, ranks)
        g = jnp.where(kept, mm_nt(n2_ref[...], ag[...]) * 2.0, 0.0)
        u = jnp.where(kept, mm_nt(n2_ref[...], au[...]) * 2.0, 0.0)
        hg[...] = g.astype(BF)
        hu[...] = u.astype(BF)
        for n, a in enumerate((g, u, dhd_ref[...].astype(F32))):
            turned = jnp.transpose(jnp.concatenate([a, jnp.zeros((rows, 128 - ranks), F32)], axis=1))
            rows_of = [turned[i * RANK : (i + 1) * RANK] for i in range(seqs)]
            hs[n] = rank_halves(rows_of).astype(BF)
        down_acc[...] = jnp.zeros_like(down_acc)
        h_acc[...] = jnp.zeros_like(h_acc)

    @pl.when(step < last)
    def _():
        for load in weights(step):
            load.wait()

    slot = lax.rem(step, 2)
    for c in range(chunks):
        first, part = cuts[c], cuts[c + 1] - cuts[c]
        here, top = slice(first, first + part), slice(0, part)

        @pl.when((step >= c * tiles) & (step < (c + 1) * tiles))
        def _(here=here, top=top):
            n2 = n2_ref[here, :]
            bg, bu = bg_ref[...], bu_ref[...]
            both = mm(n2, w_s[slot])
            gate = both[:, :tile] + mm(hg[here, :], bg)
            up = both[:, tile:] + mm(hu[here, :], bu)
            sg = 1.0 / (1.0 + jnp.exp(-gate))
            silu = gate * sg
            hidden_s[f, here, :] = (silu * up).astype(BF)
            dh = dh_ref[here, :].astype(F32)
            dg = (dh * up * sg * (1.0 + gate * (1.0 - sg))).astype(BF)
            du = (dh * silu).astype(BF)
            dgu_s[f, here, :tile] = dg
            dgu_s[f, here, tile:] = du
            terms = ((dn2_acc, mm_nt(dgu_s[f, here, :], w_s[slot])), (dhg_acc, mm_nt(dg, bg)), (dhu_acc, mm_nt(du, bu)))
            for acc, term in terms:
                acc[top, :] = jnp.where(f == 0, term, acc[top, :] + term)

        @pl.when(step == (c + 1) * tiles - 1)
        def _(c=c, here=here, top=top, first=first, part=part):
            back_s[here, :width] = dn2_acc[top, :].astype(BF)
            small = [compact(a[top, :], first) * 2 for a in (dhg_acc, dhu_acc)]
            back_s[here, width:] = jnp.concatenate(small + [jnp.zeros((part, 128 - 2 * RANK), F32)], axis=1).astype(BF)
            for s in range(first // 128, (first + part) // 128):
                copy(s).start()

    @pl.when(step < last - 2)
    def _():
        for load in weights(step + 2):
            load.start()

    @pl.when((step >= last) & (step < last + tiles))
    def _():
        hidden = hidden_s[f]
        down_acc[...] += mm(hidden, wd_ref[...])
        h_acc[...] += mm_nt(hidden, ad_ref[...])
        for n, kept in enumerate((dgu_s[f, :, :tile], dgu_s[f, :, tile:], hidden)):
            grads_ref[:, n * tile : (n + 1) * tile] = mm(hs[n], kept).astype(BF)

    for s in range(seqs):

        @pl.when(step == last + tiles + s)
        def _(s=s):
            copy(s).wait()

    @pl.when(step >= last + tiles)
    def _():
        s = step - last - tiles
        here = pl.ds(pl.multiple_of(s * 128, 128), 128)
        own = pl.ds(pl.multiple_of(s * RANK, RANK), RANK)
        mine = pl.ds(pl.multiple_of(lax.axis_index("tp") * (width // 2), width // 2), width // 2)
        down_ref[0, :, :width] = down_acc[here, :].astype(BF)
        h = jnp.where(own_ranks(s * 128, 128, ranks), h_acc[here, :], 0.0)
        h = sum(h[:, i * RANK : (i + 1) * RANK] for i in range(seqs))
        down_ref[0, :, width:] = jnp.concatenate([h, jnp.zeros((128, 128 - RANK), F32)], axis=1).astype(BF)
        total = back_s[here, :].astype(F32) + back_x[here, :].astype(F32)
        dh = total[:, width : width + 2 * RANK].astype(BF)
        c = total[:, :width] + mm(dh, jnp.concatenate([ag[own, :], au[own, :]], axis=0))
        d_mid = cot_ref[0].astype(F32) + norm_back(mid_ref[0], gain_ref[...][None, :], c)
        dmid_ref[0] = d_mid
        branch_s[...] = d_mid.astype(BF)
        dho = (mm_nt(branch_s[...], bo[own, :]) * 2.0).astype(BF)
        d_attn = mm_nt(branch_s[...], wo[...]) + mm(dho, ao[own, :])
        dattn_ref[:, 0] = jnp.transpose(d_attn).astype(BF).reshape(dattn_ref.shape[0], *dattn_ref.shape[2:])
        wide = jnp.concatenate([dh, dho, hout_ref[0][:, :RANK] * 2, jnp.zeros((128, 128 - 4 * RANK), BF)], axis=1)
        t = jnp.transpose(wide.astype(F32)).astype(BF)
        both = mm(t[: 2 * RANK], n2_ref[here, mine])
        more_s[s] = jnp.concatenate(
            [
                mm_nt(t[2 * RANK : 3 * RANK], attn_ref[:, 0].reshape(wo.shape[0], 128)), both[:RANK], both[RANK:],
                mm(t[3 * RANK : 4 * RANK], branch_s[:, mine]),
            ],
            axis=1,
        )

    @pl.when(step == pl.num_programs(0) - 1)
    def _():
        more_ref[...] = rank_halves([more_s[i] for i in range(seqs)]).astype(BF)


def feed_tile(units):
    return 1152 if units % 1152 == 0 else units


def feed(cuts, n2, dhd, ag, au, bo, ao, wo, gain, wg, wu, wd, bg, bu, ad, dh, mid, cot, hout, attn, collective_id):
    rows, width = n2.shape
    stacked, units = bg.shape
    inner = wo.shape[0]
    tile = feed_tile(units)
    chunks, part = len(cuts) - 1, max(b - a for a, b in zip(cuts, cuts[1:]))
    seqs, tiles, ranks = rows // 128, units // tile, rows // 128 * RANK
    last = chunks * tiles
    early = lambda height: pl.BlockSpec((height, tile), lambda i: (0, jnp.where(i < last, lax.rem(i, tiles), tiles - 1)))
    late = lambda i: jnp.clip(i - last, 0, tiles - 1)
    by_seq = lambda dims: pl.BlockSpec((1,) + dims[1:], lambda i: (jnp.maximum(i - last - tiles, 0), 0, 0))
    by_head = pl.BlockSpec(
        attn.shape[:1] + (1,) + attn.shape[2:], lambda i: (0, jnp.maximum(i - last - tiles, 0), 0, 0)
    )
    vm, dma = pltpu.VMEM, pltpu.SemaphoreType.DMA
    more = shape((ranks, inner + 3 * (width // 2)), BF)
    wide = (seqs, 128, width + 128)
    return pl.pallas_call(
        functools.partial(feed_kernel, cuts),
        grid=(last + tiles + seqs,),
        out_shape=(shape((ranks, 3 * units), BF), shape(wide, BF), shape(mid.shape, F32), shape(attn.shape, BF), more),
        in_specs=[whole(a) for a in (n2, dhd, ag, au, bo, ao, wo, gain)]
        + [pl.BlockSpec((tile, width), lambda i: (late(i), 0)), early(stacked), early(stacked)]
        + [pl.BlockSpec((stacked, tile), lambda i: (0, late(i))), early(rows)]
        + [by_seq(a.shape) for a in (mid, cot, hout)] + [by_head, ANYWHERE, ANYWHERE],
        out_specs=(
            pl.BlockSpec((ranks, 3 * tile), lambda i: (0, late(i))), by_seq(wide), by_seq(mid.shape), by_head,
            whole(more),
        ),
        scratch_shapes=[vm((rows, ranks), BF)] * 2
        + [vm((3, ranks, rows), BF), vm((part, width), F32), vm((part, ranks), F32), vm((part, ranks), F32)]
        + [vm((rows, width), F32), vm((rows, ranks), F32)] + [vm((tiles, rows, tile), BF), vm((tiles, rows, 2 * tile), BF)]
        + [vm((2, width, 2 * tile), BF)] + [vm((rows, width + 128), BF)] * 2 + [vm((128, width), BF), vm((seqs, RANK, more.shape[1]), F32)]
        + [dma((seqs,)), dma((seqs,)), dma((2, 2))],
        compiler_params=pltpu.CompilerParams(
            collective_id=collective_id, has_side_effects=True, vmem_limit_bytes=63 * 2**20
        ),
        cost_estimate=cost(rows, width, units, 5, 12 * width * units),
        name="feed_forward",
    )(n2, dhd, ag, au, bo, ao, wo, gain, wd, bg, bu, ad, dh, mid, cot, hout, attn, wg, wu)


TILE = 512
BLOCKS = TILE // 128
SUB = 512
SCALE = HEAD_DIM**-0.5


def document_starts(seg_ref, seq, starts):
    sequences, length = seg_ref.shape
    blocks = length // 128
    number = lax.broadcasted_iota(jnp.int32, (sequences, length), 0)
    row = jnp.sum(jnp.where(number == seq, seg_ref[...], 0), axis=0, keepdims=True)
    segs = jnp.concatenate([row[:, b * 128 : (b + 1) * 128] for b in range(blocks)], axis=0)
    lane = lax.broadcasted_iota(jnp.int32, segs.shape, 1)
    position = lax.broadcasted_iota(jnp.int32, segs.shape, 0) * 128 + lane

    def down(a, n):
        return jnp.concatenate([jnp.zeros((n, 128), jnp.int32), a[: blocks - n]], axis=0)

    before = jnp.where(lane == 0, pltpu.roll(down(segs, 1), 1, 1), pltpu.roll(segs, 1, 1))
    start = jnp.where((segs != before) & (position > 0), position, 0)
    step = 1
    while step < 128:
        start = jnp.maximum(start, jnp.where(lane >= step, pltpu.roll(start, step, 1), 0))
        step *= 2
    carried = down(jnp.broadcast_to(start[:, 127:], segs.shape), 1)
    step = 1
    while step < blocks:
        carried = jnp.maximum(carried, down(carried, step))
        step *= 2
    start = jnp.maximum(start, carried)
    for b in range(blocks):
        starts[b] = start[b : b + 1]


def query_rows(starts, tile, stride, part):
    lanes = lax.broadcasted_iota(jnp.int32, (1, 128), 1)
    blocks = [(BLOCKS * tile + b) * stride + part for b in range(BLOCKS)]
    position = jnp.concatenate([b * 128 + lanes for b in blocks], axis=1)
    return position, jnp.concatenate([starts[b] for b in blocks], axis=1)


def key_range(tile, stride, part):
    return BLOCKS * tile * stride // BLOCKS + part // BLOCKS, ((BLOCKS * tile + BLOCKS - 1) * stride + part) // BLOCKS + 1


def keep_pairs(p, first, start, position, causal):
    key = lax.broadcasted_iota(jnp.int32, p.shape, 0)
    keep = key >= jnp.broadcast_to(start - first, p.shape)
    if causal:
        keep = keep & (key <= jnp.broadcast_to(position - first, p.shape))
    return jnp.where(keep, p, 0.0)


def across_blocks(ref, tile, rows):
    return jnp.concatenate([ref[BLOCKS * tile + b, rows, :] for b in range(BLOCKS)], axis=1)


def load_keys(kv_ref, kb, vt):
    def load(j, _):
        for b in range(BLOCKS):
            kb[j, b * 128 : (b + 1) * 128, :] = jnp.transpose(kv_ref[BLOCKS * j + b, :HEAD_DIM, :])
            vt[j, :HEAD_DIM, b * 128 : (b + 1) * 128] = kv_ref[BLOCKS * j + b, HEAD_DIM:, :]
        vt[j, HEAD_DIM:, :] = jnp.ones((16, TILE), BF)
        return 0

    lax.fori_loop(0, kv_ref.shape[0] // BLOCKS, load, 0)


def head_forward(h, stride, part, first, q_ref, starts, kb, vt, acc, of_ref, lse_ref, done):
    rows = pl.ds(h * HEAD_DIM, HEAD_DIM)

    tiles = q_ref.shape[0] // BLOCKS

    def q_step(n, _):
        i = lax.rem(first + n, tiles)
        position, start = query_rows(starts, i, stride, part)
        qt = across_blocks(q_ref, i, rows)
        acc[...] = jnp.zeros_like(acc)

        def k_step(causal, j, _):
            total = acc[...]
            for c in range(TILE // SUB):
                keys = slice(c * SUB, (c + 1) * SUB)
                p = jnp.exp2(mm(kb[j, keys, :], qt) * (LOG2E * SCALE))
                p = keep_pairs(p, j * TILE + c * SUB, start, position, causal)
                total = total + mm(vt[j, :, keys], p.astype(BF))
            acc[...] = total
            return 0

        whole, end = key_range(i, stride, part)
        lax.fori_loop(0, whole, functools.partial(k_step, False), 0)
        lax.fori_loop(whole, end, functools.partial(k_step, True), 0)
        total = acc[HEAD_DIM : HEAD_DIM + 1, :]
        lse_ref[h, i] = jnp.broadcast_to(jnp.log2(total), (8, TILE))
        out = acc[:HEAD_DIM, :] / total
        for b in range(BLOCKS):
            of_ref[BLOCKS * i + b, rows, :] = out[:, b * 128 : (b + 1) * 128]
        done(n, i, out.astype(BF))
        return 0

    lax.fori_loop(0, tiles, q_step, 0)


def pair_backward(h, i, j, causal, stride, part, qt, q3, dot_t, do3, lse_ref, delta, starts, kb, vb, kt, dqt, dk, dv):
    position, start = query_rows(starts, i, stride, part)
    dq = dqt[h, i]
    for c in range(TILE // SUB):
        keys = slice(c * SUB, (c + 1) * SUB)
        p = jnp.exp2(mm(kb[j, keys, :], qt[h, i]) * (LOG2E * SCALE) - lse_ref[h, i, 0:1, :])
        p = keep_pairs(p, j * TILE + c * SUB, start, position, causal)
        dp = mm(vb[j, keys, :], dot_t[h, i])
        ds = (p * (dp - delta[h, i, 0:1, :])).astype(BF)
        dv[j, keys, :] += mm(p.astype(BF), do3[h, i])
        dk[j, keys, :] += mm(ds, q3[h, i])
        dq = dq + mm(kt[j, :, keys], ds)
    dqt[h, i] = dq


def head_rows(h):
    return pl.ds(h * HEAD_DIM, HEAD_DIM)


def loop(low, high, step):
    def body(k, _):
        step(k)
        return 0

    lax.fori_loop(low, high, body, 0)


def class_copy(count, parts, source, target, send, recv):
    def make(index, sender):
        return remote(
            source(index), target(sender), send.at[index], recv.at[sender],
            {"ctx": index * parts + lax.rem(lax.axis_index("ctx"), parts)},
        )

    return make


def owner_rows(total, pick_ref, k, sequences):
    per = RANK // 2
    row = jnp.zeros((per, total.shape[1]), F32)
    for s in range(sequences):
        row = row + total[s * per : (s + 1) * per] * pick_ref[k, s][:, :1]
    half = total.shape[1] // 2
    return jnp.concatenate([row[:, :half], row[:, half:]], axis=0).astype(BF)


def unfold_rows(rows_ref, at, block):
    per, half = RANK // 2, block.shape[1]
    rows_ref[:, at : at + half] = block[:per].astype(F32)
    rows_ref[:, at + half : at + 2 * half] = block[per:].astype(F32)


class EarlyReduction:
    def __init__(self, me, grads, y_sum, own, core_in, plane, y_in, loads, twin_sends, twin_recvs, y_sems):
        self.y_sum, self.own, self.core_in, self.plane, self.y_in = y_sum, own, core_in, plane, y_in
        chip, core = me // 2, lax.rem(me, 2)
        self.y = lax.rem(chip, 2)
        self.loads, self.to_twin, at = [], [], 0
        for i, ref in enumerate(grads):
            size, place = ref.shape[0] // 2, slice(at, at + ref.shape[1])
            at += ref.shape[1]
            half = lambda who, ref=ref, size=size: ref.at[pl.ds(pl.multiple_of(who * size, 16), size), :]
            self.loads.append(pltpu.make_async_copy(half(core), own.at[:, place], loads.at[i]))
            twin = {"ctx": 2 * chip + 1 - core}
            self.to_twin.append(remote(half(1 - core), core_in.at[:, place], twin_sends.at[i], twin_recvs.at[i], twin))
        self.known, self.width = at, plane.shape[1] // 2
        self.to_y = remote(
            plane.at[:, pl.ds(pl.multiple_of((1 - self.y) * self.width, 128), self.width)], y_in, y_sems.at[0],
            y_sems.at[1], {"ctx": 2 * (chip + 1 - 2 * self.y) + core},
        )

    def begin(self):
        for c in self.loads + self.to_twin:
            c.start()

    def over_cores(self):
        for c in self.loads:
            c.wait()
        for c in self.to_twin:
            c.wait_recv()
        self.plane[:, : self.known] = (self.own[...].astype(F32) + self.core_in[...].astype(F32)).astype(BF)
        rest = self.plane.shape[1] - self.known
        if rest:
            self.plane[:, self.known :] = jnp.zeros((self.plane.shape[0], rest), BF)
        self.to_y.start()

    def over_y(self):
        self.to_y.wait()
        mine = self.plane[:, pl.ds(pl.multiple_of(self.y * self.width, 128), self.width)]
        self.y_sum[...] = (mine.astype(F32) + self.y_in[...].astype(F32)).astype(BF)
        for c in self.to_twin:
            c.wait_send()


def early_scratch(grads, total):
    vm, dma = pltpu.VMEM, pltpu.SemaphoreType.DMA
    rows, known = grads[0].shape[0] // 2, sum(g.shape[1] for g in grads)
    return [vm((rows, known), BF), vm((rows, known), BF), vm((rows, total), BF), vm((rows, total // 2), BF)] + [dma((2,))] * 4


def padded(columns, chips):
    return -(-columns // (256 * chips)) * 256 * chips


def attend_back_kernel(count, parts, reduce, do_ref, q_all, kv_all, of_ref, lse_ref, starts, *refs):
    refs = list(refs)
    take = lambda n: [refs.pop(0) for _ in range(n)]
    grads = take(2) if reduce else []
    dq_home, dkv_home = take(2)
    early = EarlyReduction(lax.axis_index("ctx"), grads, *take(9)) if reduce else None
    attend_back_body(
        count, parts, early,
        do_ref, q_all, kv_all, of_ref, lse_ref, starts, dq_home, dkv_home, *refs,
    )


def attend_back_body(
    count, parts, early, do_ref, q_all, kv_all, of_ref, lse_ref, starts, dq_home, dkv_home,
    q_all_s, kv_all_s, of_s, in_sems, do_in, dq_buf, dkv_buf, kb, vb, kt, qt, q3, dot_t, do3, delta, dqt, dk, dv,
    do_send, do_recv, dq_send, dq_recv, dkv_send, dkv_recv, own_sems,
):
    me = lax.axis_index("ctx")
    units = count // parts
    unit, part = me // parts, lax.rem(me, parts)
    group, tiles, ktiles = q_all.shape[1] // HEAD_DIM, units // BLOCKS, count // BLOCKS
    barrier = pltpu.get_barrier_semaphore()
    loop(
        1, count,
        lambda k: pl.semaphore_signal(barrier, inc=1, device_id={"ctx": lax.rem(me + k, count)}, device_id_type=MESH),
    )
    own_do = pltpu.make_async_copy(do_ref.at[unit], do_in.at[unit], own_sems.at[0])
    own_do.start()
    kept = [
        pltpu.make_async_copy(a, b, in_sems.at[i]) for i, (a, b) in enumerate(((kv_all, kv_all_s), (q_all, q_all_s), (of_ref, of_s)))
    ]
    for c in kept:
        c.start()
    q_all, kv_all, of_ref = q_all_s, kv_all_s, of_s
    pl.semaphore_wait(barrier, count - 1)
    if early:
        early.begin()

    def turn_of(k):
        return lax.rem(unit + k, units)

    do_copy = [
        class_copy(
            count, parts, lambda i, h=h: do_ref.at[i, head_rows(h), :], lambda i, h=h: do_in.at[i, head_rows(h), :],
            do_send.at[h], do_recv.at[h],
        )
        for h in range(group)
    ]
    dq_copy = [
        class_copy(
            count, parts, lambda i, h=h: dq_buf.at[h, i], lambda i, h=h: dq_home.at[i, head_rows(h), :],
            dq_send.at[h], dq_recv.at[h],
        )
        for h in range(group)
    ]

    def dkv_copy(device, sender):
        return remote(dkv_buf.at[device], dkv_home.at[sender], dkv_send.at[device], dkv_recv.at[sender], {"ctx": device})

    own_dkv = pltpu.make_async_copy(dkv_buf.at[me], dkv_home.at[me], own_sems.at[1])

    def own_dq(h):
        return pltpu.make_async_copy(dq_buf.at[h, unit], dq_home.at[unit, head_rows(h), :], own_sems.at[2 + h])

    for h in range(group):
        loop(1, units, lambda k, h=h: do_copy[h](turn_of(k), unit).start())

    def load_kv(j):
        for b in range(BLOCKS):
            lanes = slice(b * 128, (b + 1) * 128)
            kt[j, :, lanes] = kv_all[BLOCKS * j + b, :HEAD_DIM, :]
            kb[j, lanes, :] = jnp.transpose(kv_all[BLOCKS * j + b, :HEAD_DIM, :])
            vb[j, lanes, :] = jnp.transpose(kv_all[BLOCKS * j + b, HEAD_DIM:, :])

    def load_q(i):
        for h in range(group):
            for b in range(BLOCKS):
                lanes = slice(b * 128, (b + 1) * 128)
                q = q_all[BLOCKS * i + b, h * HEAD_DIM : (h + 1) * HEAD_DIM, :]
                qt[h, i, :, lanes] = q
                q3[h, i, lanes, :] = jnp.transpose(q)
            dqt[h, i] = jnp.zeros((HEAD_DIM, TILE), F32)

    def load_do(h, i):
        rows = slice(h * HEAD_DIM, (h + 1) * HEAD_DIM)
        for b in range(BLOCKS):
            lanes = slice(b * 128, (b + 1) * 128)
            g = do_in[BLOCKS * i + b, rows, :]
            dot_t[h, i, :, lanes] = g
            do3[h, i, lanes, :] = jnp.transpose(g)
            d = jnp.sum(g.astype(F32) * of_ref[BLOCKS * i + b, rows, :], axis=0, keepdims=True)
            delta[h, i, :, lanes] = jnp.broadcast_to(d, (8, 128))

    kept[0].wait()
    loop(0, ktiles, load_kv)
    kept[1].wait()
    loop(0, tiles, load_q)
    kept[2].wait()

    def run(h, j):
        low = jnp.maximum(BLOCKS * j - part + parts - 1, 0) // (BLOCKS * parts)
        full = jnp.minimum((BLOCKS * (j + 1) - part + BLOCKS * parts - 1) // (BLOCKS * parts), tiles)

        def pair(causal, i):
            pair_backward(
                h, i, j, causal, parts, part, qt, q3, dot_t, do3, lse_ref, delta, starts, kb, vb, kt, dqt, dk, dv
            )

        loop(low, full, functools.partial(pair, True))
        loop(full, tiles, functools.partial(pair, False))

    def emit_keys(j):
        for b in range(BLOCKS):
            rows = slice(b * 128, (b + 1) * 128)
            block = BLOCKS * j + b
            dkv_buf[block, :HEAD_DIM, :] = jnp.transpose(dk[j, rows, :] * SCALE).astype(BF)
            dkv_buf[block, HEAD_DIM:, :] = jnp.transpose(dv[j, rows, :]).astype(BF)

            @pl.when(block == me)
            def _():
                own_dkv.start()

            @pl.when(block != me)
            def _():
                dkv_copy(block, me).start()

    def emit_queries(h, n):
        i = lax.rem(unit + n, tiles)
        for b in range(BLOCKS):
            block = BLOCKS * i + b
            dq_buf[h, block] = (dqt[h, i, :, b * 128 : (b + 1) * 128] * SCALE).astype(BF)

            @pl.when(block == unit)
            def _():
                own_dq(h).start()

            @pl.when(block != unit)
            def _():
                dq_copy[h](block, unit).start()

    dk[...] = jnp.zeros_like(dk)
    dv[...] = jnp.zeros_like(dv)
    own_do.wait()
    if early:
        early.over_cores()
    for h in range(group):
        loop(1, units, lambda k, h=h: do_copy[h](unit, turn_of(k)).wait_recv())
        loop(0, tiles, functools.partial(load_do, h))

        def key_step(n, h=h):
            j = lax.rem(unit + n, ktiles)
            run(h, j)
            if h == group - 1:
                emit_keys(j)

        loop(0, ktiles, key_step)
        loop(0, tiles, functools.partial(emit_queries, h))
        if early and h == 1:
            early.over_y()
    for h in range(group):
        own_dq(h).wait()
    own_dkv.wait()

    def finish_full(k):
        other = lax.rem(me + k, count)
        dkv_copy(other, me).wait_send()
        dkv_copy(me, other).wait_recv()

    loop(1, count, finish_full)

    def finish_class(k):
        other = turn_of(k)
        for h in range(group):
            do_copy[h](other, unit).wait_send()
            dq_copy[h](other, unit).wait_send()
            dq_copy[h](unit, other).wait_recv()

    loop(1, units, finish_class)


def attend_back(do, q, kv, of, lse, starts, early, count, parts, collective_id):
    units, qrows, _ = q.shape
    group, tiles, ktiles = qrows // HEAD_DIM, units // BLOCKS, count // BLOCKS
    dma, vm = pltpu.SemaphoreType.DMA, pltpu.VMEM
    sums, scratch = (), []
    if early:
        total = padded(sum(g.shape[1] for g in early), count // 2)
        sums = (shape((early[0].shape[0] // 2, total // 2), BF),)
        scratch = early_scratch(early, total)
    return pl.pallas_call(
        functools.partial(attend_back_kernel, count, parts, bool(early)),
        out_shape=(shape(q.shape, BF), shape(kv.shape, BF)) + sums,
        in_specs=[ANYWHERE] * 4 + [VM] * 2 + [ANYWHERE] * len(early),
        out_specs=(ANYWHERE, ANYWHERE) + (VM,) * len(sums),
        scratch_shapes=scratch + [vm(q.shape, BF), vm(kv.shape, BF), vm(of.shape, F32), dma((3,)), vm(q.shape, BF), vm((group, units, HEAD_DIM, 128), BF), vm(kv.shape, BF)]
        + [vm((ktiles, TILE, HEAD_DIM), BF)] * 2 + [vm((ktiles, HEAD_DIM, TILE), BF)]
        + [vm((group, tiles, HEAD_DIM, TILE), BF), vm((group, tiles, TILE, HEAD_DIM), BF)] * 2
        + [vm((group, tiles, 8, TILE), F32), vm((group, tiles, HEAD_DIM, TILE), F32)]
        + [vm((ktiles, TILE, HEAD_DIM), F32)] * 2
        + [dma((group, units))] * 4 + [dma((count,))] * 2 + [dma((2 + group,))],
        compiler_params=pltpu.CompilerParams(
            collective_id=collective_id, has_side_effects=True, vmem_limit_bytes=60 * 2**20
        ),
        name="attend_back",
    )(do, q, kv, of, lse, starts, *early)


class Names:
    def __init__(self, names, refs):
        assert len(names) == len(refs)
        self.__dict__.update(zip(names, refs))


FACTORS = ("ag", "au", "bd", "bg", "bu", "ad", "bo", "ao")
FORWARD_NEAR = ("variant", "x", "gain_one", "gain_two", "q_gain", "k_gain", "cosine", "sine", "segs") + (
    "wq", "wk", "wv", "aq", "ak", "av", "bq", "bk", "bv",
)
FORWARD_FAR = ("cot", "wd", "wo") + FACTORS
FORWARD_SMALL = ("h_one", "ac", "bc", "gains", "pick", "lse", "starts", "dhd", "h_out")
FORWARD_SAVED = ("n1", "pre", "q_all", "kv_all", "of", "home", "mid", "n2") + tuple("c_" + f for f in FACTORS)
FORWARD_OUT = FORWARD_SMALL + FORWARD_SAVED + ("dh",)
FORWARD_BUFFERS = ("cot_s", "wd_s", "wo_s", "wo_x", "ao_x", "dh_s", "q_msg", "kv_msg", "o_buf", "kb", "vt", "acc")
FORWARD_BUFFERS += ("home_x", "lhs", "lhs_x")
FORWARD_SEMS = ("far_sems", "save_sems", "dh_sems", "kv_send", "kv_recv", "q_send", "q_recv", "o_send", "o_recv")
FORWARD_SEMS += ("x_send", "x_recv", "own_sems", "w_send", "w_recv")


LAG = 4


def forward_kernel(count, parts, *refs):
    names = FORWARD_NEAR + FORWARD_FAR + FORWARD_OUT
    names += tuple(f + "_s" for f in FACTORS) + tuple(n + "_s" for n in FORWARD_SAVED) + FORWARD_BUFFERS + FORWARD_SEMS
    r = Names(names, refs)
    me = lax.axis_index("ctx")
    units = count // parts
    unit, part = me // parts, lax.rem(me, parts)
    sequences, rows, width = r.x.shape
    qw, kw = r.wq.shape[1], r.wk.shape[1]
    heads_k = kw // HEAD_DIM
    group = qw // kw
    ranks = sequences * RANK
    across = {"tp": 1 - lax.axis_index("tp")}
    core = lax.rem(me, 2)
    twin = {"ctx": me + 1 - 2 * core}

    def turn_of(k):
        return lax.rem(unit + k, units)

    barrier = pltpu.get_barrier_semaphore()
    pl.semaphore_signal(barrier, inc=1, device_id=across, device_id_type=MESH)
    loop(
        1, count,
        lambda k: pl.semaphore_signal(barrier, inc=1, device_id={"ctx": lax.rem(me + k, count)}, device_id_type=MESH),
    )
    tiles, tile = r.wd_s.shape[0], r.wd_s.shape[1]
    far = [(r.cot, r.cot_s)] + [(r.wd.at[pl.ds(f * tile, tile), :], r.wd_s.at[f]) for f in range(tiles)]
    far += [(r.wo, r.wo_s)] + [(getattr(r, f), getattr(r, f + "_s")) for f in FACTORS]
    far = [pltpu.make_async_copy(a, b, r.far_sems.at[i]) for i, (a, b) in enumerate(far)]
    for c in far:
        c.start()
    saves = {
        n: pltpu.make_async_copy(getattr(r, n + "_s"), getattr(r, n), r.save_sems.at[i]) for i, n in enumerate(FORWARD_SAVED)
    }

    def kv_copy(index, to_part, sender):
        device = index * parts + to_part
        return remote(r.kv_msg.at[index], r.kv_all_s.at[sender], r.kv_send.at[device], r.kv_recv.at[sender], {"ctx": device})

    q_copy = [
        class_copy(
            count, parts, lambda i, h=h: r.q_msg.at[i, head_rows(h), :], lambda i, h=h: r.q_all_s.at[i, head_rows(h), :],
            r.q_send.at[h], r.q_recv.at[h],
        )
        for h in range(group)
    ]
    o_copy = [
        class_copy(
            count, parts, lambda i, h=h: r.o_buf.at[h, i], lambda i, h=h: r.home_s.at[i, head_rows(h), :],
            r.o_send.at[h], r.o_recv.at[h],
        )
        for h in range(group)
    ]

    def x_copy(h, i):
        place = (i, head_rows(h), slice(None))
        return remote(r.home_s.at[place], r.home_x.at[place], r.x_send.at[h, i], r.x_recv.at[h, i], across)

    column_of = lax.broadcasted_iota(jnp.int32, (RANK, r.aq.shape[0]), 1)
    rank_of = lax.broadcasted_iota(jnp.int32, (RANK, r.aq.shape[0]), 0)
    chooser = [jnp.where(column_of == r.variant[s] * RANK + rank_of, 1.0, 0.0).astype(BF) for s in range(sequences)]
    choosers = jnp.concatenate(chooser, axis=0)
    stacked = lax.broadcasted_iota(jnp.int32, (1, r.aq.shape[0]), 1) // RANK
    cosine, sine = r.cosine[...], r.sine[...]
    qg, kg = column(r.q_gain), column(r.k_gain)
    gain = r.gain_one[...][None, :]

    def prepare(t, gains):
        heads = t.reshape(t.shape[0] // HEAD_DIM, HEAD_DIM, rows)
        scale = lax.rsqrt(jnp.mean(heads * heads, axis=1, keepdims=True) + EPSILON)
        return turn(heads * scale * gains, cosine, sine).astype(BF)

    def project(p):
        for s in (2 * p, 2 * p + 1):
            x = r.x[s].astype(F32)
            scale = lax.rsqrt(jnp.mean(x * x, axis=-1, keepdims=True) + EPSILON)
            r.n1_s[s] = (x * scale * gain).astype(BF)
        n1 = jnp.concatenate([r.n1_s[2 * p], r.n1_s[2 * p + 1]], axis=0)
        low = [mm_nt(n1, a[...]) for a in (r.aq, r.ak, r.av)]
        base = [mm(n1, w[...]) for w in (r.wq, r.wk, r.wv)]
        for i in (0, 1):
            s = 2 * p + i
            half = slice(i * rows, (i + 1) * rows)
            own = jnp.where(stacked == r.variant[s], 1.0, 0.0)
            h = [(a[half] * own).astype(BF) for a in low]
            small = [mm_nt(a, chooser[s]) for a in h] + [jnp.zeros((rows, 128 - 3 * RANK), F32)]
            r.h_one[s] = jnp.concatenate(small, axis=1).astype(BF)
            q, k, val = (
                jnp.transpose(base[n][half] + mm(h[n] * 2, f[...])) for n, f in enumerate((r.bq, r.bk, r.bv))
            )
            r.pre_s[s, :qw, :] = q
            r.pre_s[s, qw:, :] = k
            q = prepare(q, qg).reshape(heads_k, group * HEAD_DIM, rows)
            k, val = prepare(k, kg), val.astype(BF).reshape(heads_k, HEAD_DIM, rows)
            for n in range(heads_k):
                r.q_msg[n * sequences + s] = q[n]
                r.kv_msg[n * sequences + s, :HEAD_DIM, :] = k[n]
                r.kv_msg[n * sequences + s, HEAD_DIM:, :] = val[n]

    def own_kv():
        return pltpu.make_async_copy(r.kv_msg.at[unit], r.kv_all_s.at[me], r.own_sems.at[0])

    def own_q():
        return pltpu.make_async_copy(r.q_msg.at[unit], r.q_all_s.at[unit], r.own_sems.at[1])

    per_pair = 2 * heads_k

    def send_keys(p):
        def step(k):
            turned = lax.rem(unit + k, per_pair)
            index = turned // 2 * sequences + 2 * p + lax.rem(turned, 2)
            for t in range(parts):

                @pl.when(index * parts + t != me)
                def _():
                    kv_copy(index, t, me).start()

            @pl.when(index != unit)
            def _():
                q_copy[0](index, unit).start()

            @pl.when(index == unit)
            def _():
                own_kv().start()
                own_q().start()

        loop(0, per_pair, step)

    part_rows = r.wo_s.shape[0] // 2
    rows_of = lambda who: pl.ds(pl.multiple_of(who * part_rows, 16), part_rows)
    w_copies = [
        remote(r.wo_s.at[rows_of(core), :], r.wo_x.at[rows_of(core), :], r.w_send.at[0], r.w_recv.at[0], across),
        remote(r.wo_x.at[rows_of(core), :], r.wo_x.at[rows_of(core), :], r.w_send.at[1], r.w_recv.at[1], twin),
        remote(r.c_ao_s, r.ao_x, r.w_send.at[2], r.w_recv.at[2], across),
    ]

    project(0)
    pl.semaphore_wait(barrier, count)
    send_keys(0)
    for p in range(1, sequences // 2):
        project(p)
        send_keys(p)
    for h in range(1, group):
        loop(1, units, lambda k, h=h: q_copy[h](turn_of(k), unit).start())
    for n in ("n1", "pre"):
        saves[n].start()
    far[1 + tiles].wait()
    w_copies[0].start()

    def choose(names):
        for f in names:
            far[2 + tiles + FACTORS.index(f)].wait()
            getattr(r, "c_" + f + "_s")[...] = mm(choosers, getattr(r, f + "_s")[...]).astype(BF)
            saves["c_" + f].start()

    document_starts(r.segs, lax.rem(unit, sequences), r.starts)
    choose(("ao", "bd", "ad"))
    w_copies[2].start()
    far[0].wait()
    d = mm_nt(r.cot_s[...], r.c_bd_s[...]) * 2.0
    r.dhd[...] = jnp.where(own_ranks(0, *d.shape), d, 0.0).astype(BF)
    dh_saves = []
    for f in range(tiles):
        far[1 + f].wait()
        columns = slice(f * tile, (f + 1) * tile)
        r.dh_s[:, columns] = (mm_nt(r.cot_s[...], r.wd_s[f]) + mm(r.dhd[...], r.c_ad_s[:, columns])).astype(BF)
        dh_saves.append(pltpu.make_async_copy(r.dh_s.at[:, columns], r.dh.at[:, columns], r.dh_sems.at[f]))
        dh_saves[-1].start()

    own_kv().wait()
    own_q().wait()
    loop(1, count, lambda k: kv_copy(unit, part, lax.rem(me + k, count)).wait_recv())
    load_keys(r.kv_all_s, r.kb, r.vt)
    saves["kv_all"].start()

    def keep_own(h):
        return pltpu.make_async_copy(r.o_buf.at[h, unit], r.home_s.at[unit, head_rows(h), :], r.own_sems.at[2 + h])

    tiles_q = units // BLOCKS
    my_tile = unit // BLOCKS

    def pass_on(h, n):
        def relay(v):
            other = v * tiles_q + lax.rem(my_tile - n + tiles_q, tiles_q)

            @pl.when(other == unit)
            def _():
                keep_own(h).wait()
                x_copy(h, other).start()

            @pl.when(other != unit)
            def _():
                o_copy[h](unit, other).wait_recv()
                x_copy(h, other).start()

        loop(0, units // tiles_q, relay)

    for h in range(group):
        loop(1, units, lambda k, h=h: q_copy[h](unit, turn_of(k)).wait_recv())
        if h == group - 1:
            saves["q_all"].start()

        def done(n, i, out, h=h):
            for b in range(BLOCKS):
                block = BLOCKS * i + b
                r.o_buf[h, block] = out[:, b * 128 : (b + 1) * 128]

                @pl.when(block == unit)
                def _():
                    keep_own(h).start()

                @pl.when(block != unit)
                def _():
                    o_copy[h](block, unit).start()

            for m in range(tiles_q):
                if m >= LAG or h > 0:

                    @pl.when(n == m)
                    def _(m=m):
                        pass_on(h if m >= LAG else h - 1, m - LAG if m >= LAG else m - LAG + tiles_q)

        head_forward(h, parts, part, unit, r.q_all_s, r.starts, r.kb, r.vt, r.acc, r.of_s, r.lse, done)
        if h == 0:
            w_copies[0].wait_recv()
            w_copies[1].start()
    saves["of"].start()
    choose(("ag", "au", "bg", "bu", "bo"))
    for n in range(tiles_q - LAG, tiles_q):
        pass_on(group - 1, n)
    for s in range(sequences):
        r.ac[s] = jnp.concatenate([mm(chooser[s], a[...]) for a in (r.aq, r.ak, r.av)], axis=0).astype(BF)
        r.bc[s] = jnp.concatenate([mm(chooser[s], b[...]) for b in (r.bq, r.bk, r.bv)], axis=1).astype(BF)
        for v in range(r.pick.shape[0]):
            r.pick[v, s] = jnp.full((8, 128), jnp.where(r.variant[s] == v, 1.0, 0.0), F32)
    r.gains[0], r.gains[1] = qg, kg
    saves["home"].start()
    w_copies[1].wait_recv()
    w_copies[2].wait_recv()
    for h in range(group):
        loop(0, units, lambda i, h=h: x_copy(h, i).wait_recv())

    gain = r.gain_two[...][None, :]
    for p in range(sequences // 2):
        for i in (0, 1):
            half = slice(i * rows, (i + 1) * rows)
            for lhs, home in ((r.lhs, r.home_s), (r.lhs_x, r.home_x)):
                blocks = [home[n * sequences + 2 * p + i] for n in range(heads_k)]
                lhs[half, :] = jnp.transpose(jnp.concatenate(blocks, axis=0))
        out = mm(r.lhs[...], r.wo_s[...]) + mm(r.lhs_x[...], r.wo_x[...])
        for i in (0, 1):
            s = 2 * p + i
            half, own = slice(i * rows, (i + 1) * rows), slice(s * RANK, (s + 1) * RANK)
            h = (mm_nt(r.lhs[half, :], r.c_ao_s[own, :]) + mm_nt(r.lhs_x[half, :], r.ao_x[own, :])).astype(BF)
            r.h_out[s] = jnp.concatenate([h, jnp.zeros((rows, 128 - RANK), BF)], axis=1)
            mid = r.x[s].astype(F32) + (out[half] + mm(h * 2, r.c_bo_s[own, :]))
            r.mid_s[s] = mid
            scale = lax.rsqrt(jnp.mean(mid * mid, axis=-1, keepdims=True) + EPSILON)
            r.n2_s[s] = (mid * scale * gain).astype(BF)
    saves["mid"].start()
    saves["n2"].start()

    for c in list(saves.values()) + dh_saves:
        c.wait()
    for c in w_copies:
        c.wait_send()

    def finish_full(k):
        other = lax.rem(me + k, count)
        kv_copy(other // parts, lax.rem(other, parts), me).wait_send()

    loop(1, count, finish_full)
    for h in range(group):

        def finish_block(k, h=h):
            q_copy[h](turn_of(k), unit).wait_send()
            o_copy[h](turn_of(k), unit).wait_send()

        loop(1, units, finish_block)
        loop(0, units, lambda i, h=h: x_copy(h, i).wait_send())


def forward(near, far, count, parts, collective_id):
    n = Names(FORWARD_NEAR + FORWARD_FAR, tuple(near) + tuple(far))
    sequences, rows, width = n.x.shape
    qw, kw = n.wq.shape[1], n.wk.shape[1]
    units, group = count // parts, qw // kw
    tiles, ktiles = units // BLOCKS, count // BLOCKS
    hidden_units, tile = n.wd.shape[0], feed_tile(n.wd.shape[0])
    spare, ranks = hidden_units // tile, sequences * RANK
    q_shape, kv_shape = (units, group * HEAD_DIM, rows), (count, 2 * HEAD_DIM, rows)
    small = (
        shape((sequences, rows, 128), BF), shape((sequences, 3 * RANK, width), BF), shape((sequences, RANK, qw + 2 * kw), BF),
        shape((2, HEAD_DIM, rows), F32), shape((n.aq.shape[0] // RANK, sequences, 8, 128), F32),
        shape((group, tiles, 8, TILE), F32), shape((count, 1, 128), jnp.int32), shape((sequences * rows, ranks), BF),
        shape((sequences, rows, 128), BF),
    )
    saved = (
        shape(n.x.shape, BF), shape((sequences, qw + kw, rows), F32), shape(q_shape, BF), shape(kv_shape, BF),
        shape(q_shape, F32), shape(q_shape, BF), shape(n.x.shape, F32), shape(n.x.shape, BF),
    ) + tuple(shape((ranks, getattr(n, f).shape[1]), BF) for f in FACTORS)
    dma, vm = pltpu.SemaphoreType.DMA, pltpu.VMEM
    buffers = [vm(getattr(n, f).shape, BF) for f in FACTORS] + [vm(s.shape, s.dtype) for s in saved]
    buffers += [
        vm(n.cot.shape, BF), vm((spare, tile, width), BF), vm(n.wo.shape, BF), vm(n.wo.shape, BF), vm((ranks, qw), BF),
        vm((sequences * rows, hidden_units), BF), vm(q_shape, BF), vm((units,) + kv_shape[1:], BF),
        vm((group, units, HEAD_DIM, 128), BF), vm((ktiles, TILE, HEAD_DIM), BF), vm((ktiles, HEAD_DIM + 16, TILE), BF),
        vm((HEAD_DIM + 16, TILE), F32), vm(q_shape, BF), vm((2 * rows, qw), BF), vm((2 * rows, qw), BF),
    ]
    sems = [dma((2 + spare + len(FACTORS),)), dma((len(saved),)), dma((spare,)), dma((count,)), dma((count,))]
    sems += [dma((group, units))] * 6 + [dma((2 + group,)), dma((3,)), dma((3,))]
    outs = pl.pallas_call(
        functools.partial(forward_kernel, count, parts),
        out_shape=small + saved + (shape((sequences * rows, hidden_units), BF),),
        in_specs=[SMEM] + [VM] * (len(FORWARD_NEAR) - 1) + [ANYWHERE] * len(FORWARD_FAR),
        out_specs=(VM,) * len(small) + (ANYWHERE,) * (len(saved) + 1),
        scratch_shapes=buffers + sems,
        compiler_params=pltpu.CompilerParams(
            collective_id=collective_id, has_side_effects=True, vmem_limit_bytes=62 * 2**20
        ),
        name="forward",
    )(*near, *far)
    return Names(FORWARD_OUT, outs)


def finish_kernel(reduce, count, shared, *refs):
    refs = list(refs)
    take = lambda n: [refs.pop(0) for _ in range(n)]
    dq_ref, dkv_ref, pre_ref, h_ref, gains, cos_ref, sin_ref, gain_ref, bc_ref, pick_ref, bd_ref = take(11)
    far = take(11)
    early = take(1) if reduce else []
    out_ref, block_ref = take(2)
    gout = take(4) if reduce else take(1)
    x, d_mid, n1, wq, wk, wv, ac, mid, down, down_x, cot = near = take(11)
    d_n, gb, dh_own, dh_other, dh_sum, sbuf, rbuf, gq = take(8)
    near_sems, dh_send, dh_recv, xsend, xrecv = take(5)
    sequences, rows = dq_ref.shape[1], dq_ref.shape[3]
    inner = dq_ref.shape[0] * dq_ref.shape[2]
    width = out_ref.shape[2]
    kw = wk.shape[1]
    half_rows = sequences * RANK // 2
    me = lax.axis_index("ctx")
    across = {"tp": 1 - lax.axis_index("tp")}
    mine = pl.ds(pl.multiple_of(lax.axis_index("tp") * (width // 2), width // 2), width // 2)

    loads = [pltpu.make_async_copy(f, n, near_sems.at[i]) for i, (f, n) in enumerate(zip(far, near))]
    barrier = pltpu.get_barrier_semaphore()
    pl.semaphore_signal(barrier, inc=1, device_id=across, device_id_type=MESH)
    peers = 1
    if reduce:
        core_in, plane, z_in, plane_in = take(4)
        fin_outs, fin_ins, shared_out = take(2), take(2), take(2)
        twin_sems, z_send, z_recv, plane_send, plane_recv, fin_send, fin_recv, last_sems = take(8)
        chips = count // 2
        chip, core = me // 2, lax.rem(me, 2)
        twin = {"ctx": 2 * chip + 1 - core}
        pl.semaphore_signal(barrier, inc=1, device_id=twin, device_id_type=MESH)

        def at_chip(k):
            return lax.rem(chip + k, chips)

        def greet(k, _):
            pl.semaphore_signal(barrier, inc=1, device_id={"ctx": 2 * at_chip(k) + core}, device_id_type=MESH)
            return 0

        lax.fori_loop(1, chips, greet, 0)
        peers += chips

        w_qkv = gq.shape[2]
        to_twin = remote(gq.at[1 - core], core_in, twin_sems.at[0], twin_sems.at[1], twin)
    for i in (3, 4, 5, 2, 6, 7, 8, 9, 10, 0, 1):
        loads[i].start()
    pl.semaphore_wait(barrier, peers)
    if reduce:
        deep = chips // 2
        z, y = chip // 2, lax.rem(chip, 2)

        def z_copy(other, sender):
            chunk = early[0].shape[1] // deep
            return remote(
                early[0].at[:, pl.ds(pl.multiple_of(other * chunk, 128), chunk)], z_in.at[sender], z_send.at[other],
                z_recv.at[sender], {"ctx": 4 * other + 2 * y + core},
            )

        def each_z(step):
            loop(1, deep, lambda k: step(lax.rem(z + k, deep)))

        each_z(lambda k: z_copy(k, z).start())

    cosine, sine = cos_ref[...], sin_ref[...]
    heads_k = kw // HEAD_DIM
    cuts = (slice(0, inner), slice(inner, inner + kw), slice(inner + kw, inner + 2 * kw))

    def prepare_back(pre, gains, c):
        u = pre.reshape(pre.shape[0] // HEAD_DIM, HEAD_DIM, rows)
        scale = lax.rsqrt(jnp.mean(u * u, axis=1, keepdims=True) + EPSILON)
        y = u * scale
        w = turn(c.reshape(u.shape).astype(F32), cosine, -sine) * gains
        return (scale * (w - y * jnp.mean(w * y, axis=1, keepdims=True))).reshape(pre.shape)

    def first_step(s):
        dkv = dkv_ref[:, s].astype(F32)
        dkv = jnp.sum(dkv, axis=1).astype(BF) if dkv.shape[1] > 1 else dkv[:, 0].astype(BF)
        d_q = prepare_back(pre_ref[s, :inner, :], gains[0], dq_ref[:, s].reshape(inner, rows))
        d_k = prepare_back(pre_ref[s, inner:, :], gains[1], dkv[:, :HEAD_DIM, :].reshape(kw, rows))
        d_v = dkv[:, HEAD_DIM:, :].reshape(kw, rows).astype(F32)
        d = jnp.transpose(jnp.concatenate([d_q, d_k, d_v], axis=0)).astype(BF)
        d_n[s] = d
        dh = [mm_nt(d[:, c], bc_ref[s, :, c]) * 2.0 for c in cuts]
        dh = jnp.transpose(jnp.concatenate(dh + [jnp.zeros((rows, 128 - 3 * RANK), F32)], axis=1))
        dh_own[s] = dh[: 3 * RANK].astype(BF)
        t = (jnp.transpose(h_ref[s].astype(F32)) * 2.0).astype(BF)
        gb[s] = jnp.concatenate([mm(t[i * RANK : (i + 1) * RANK], d[:, c]) for i, c in enumerate(cuts)], axis=1)

    def part_copy(s):
        return remote(sbuf.at[s], rbuf.at[s], xsend.at[s], xrecv.at[s], across)

    def dh_copy(p):
        pair = pl.ds(2 * p, 2)
        return remote(dh_own.at[pair], dh_other.at[pair], dh_send.at[p], dh_recv.at[p], across)

    def work_pair(p):
        d = jnp.concatenate([d_n[2 * p], d_n[2 * p + 1]], axis=0)
        part = mm_nt(d[:, cuts[0]], wq[...]) + mm_nt(d[:, cuts[1]], wk[...]) + mm_nt(d[:, cuts[2]], wv[...])
        for i in (0, 1):
            sbuf[2 * p + i] = part[i * rows : (i + 1) * rows].astype(BF)

    def plane_copy(k, slot):
        chunk = plane.shape[1] // chips
        return remote(
            plane.at[:, pl.ds(pl.multiple_of(k * chunk, 128), chunk)], plane_in.at[slot], plane_send.at[k],
            plane_recv.at[slot], {"ctx": 2 * k + core},
        )

    def fin_copy(g, k, slot):
        return remote(
            fin_outs[g].at[k], fin_ins[g].at[slot], fin_send.at[g, k], fin_recv.at[g, slot], {"ctx": 2 * k + core}
        )

    def each_chip(step):
        loop(1, chips, lambda k: step(at_chip(k)))

    def to_plane():
        to_twin.wait_recv()
        plane[:, :w_qkv] = (gq[core].astype(F32) + core_in[...].astype(F32)).astype(BF)
        if plane.shape[1] > w_qkv:
            plane[:, w_qkv:] = jnp.zeros((half_rows, plane.shape[1] - w_qkv), BF)
        chunk = plane.shape[1] // chips
        each_chip(lambda k: plane_copy(k, chip).start())
        plane_in[chip] = plane[:, pl.ds(pl.multiple_of(chip * chunk, 128), chunk)]

    def to_owners(g):
        if g == 0:
            each_z(lambda k: z_copy(k, k).wait_recv())
            chunk = early[0].shape[1] // deep
            z_in[z] = early[0][:, pl.ds(pl.multiple_of(z * chunk, 128), chunk)]
        else:
            each_chip(lambda k: plane_copy(k, k).wait_recv())
        blocks = z_in if g == 0 else plane_in
        total = blocks[0].astype(F32)
        for k in range(1, blocks.shape[0]):
            total = total + blocks[k].astype(F32)
        for k in range(chips):
            fin_outs[g][k] = owner_rows(total, pick_ref, k, sequences)
        each_chip(lambda k: fin_copy(g, k, chip).start())
        fin_ins[g][chip] = fin_outs[g][chip]

    def rows_in(g):
        each_chip(lambda k: fin_copy(g, k, k).wait_recv())
        chunk = gout[g].shape[1] // chips
        for k in range(chips):
            unfold_rows(gout[g], (k % 2 * deep + k // 2 if g == 0 else k) * chunk, fin_ins[g][k])
        low, high = shared[g]
        middle = (low + high) // 2
        shared_out[g][...] = jnp.concatenate([gout[g][:, low:middle], gout[g][:, middle:high]], axis=0).astype(BF)
        copy = remote(shared_out[g], gout[2 + g], last_sems.at[g], last_sems.at[2 + g], across)
        copy.start()
        return copy

    def last_step(s):
        part_copy(s).wait_recv()
        c = sbuf[s].astype(F32) + rbuf[s].astype(F32) + mm(dh_sum[s][:, : 3 * RANK], ac[s])
        out_ref[s] = (d_mid[s] + norm_back(x[s].astype(F32), gain_ref[...][None, :], c)).astype(BF)

    pairs = sequences // 2
    for p in range(pairs):
        first_step(2 * p)
        first_step(2 * p + 1)
        dh_copy(p).start()
        if p == 0:
            for i in (3, 4, 5):
                loads[i].wait()
            work_pair(0)
            part_copy(0).start()
    part_copy(1).start()
    for p in range(1, pairs):
        work_pair(p)
        part_copy(2 * p).start()
        part_copy(2 * p + 1).start()
    for p in range(pairs):
        dh_copy(p).wait()
    for i in (2, 7, 8, 9, 10):
        loads[i].wait()
    blocks = []
    for s in range(sequences):
        total = down[s].astype(F32) + down_x[s].astype(F32)
        h = total[:, width : width + RANK].astype(BF) * 2
        block_ref[s] = (mid[s] + (total[:, :width] + mm(h, bd_ref[s * RANK : (s + 1) * RANK, :]))).astype(BF)
        wide = jnp.concatenate([h, jnp.zeros((rows, 128 - RANK), BF)], axis=1)
        gb_down = mm(jnp.transpose(wide.astype(F32)).astype(BF)[:RANK], cot[s, :, mine])
        dh = (dh_own[s].astype(F32) + dh_other[s].astype(F32)).astype(BF)
        dh_sum[s] = jnp.transpose(jnp.concatenate([dh.astype(F32), jnp.zeros((128 - 3 * RANK, rows), F32)], axis=0)).astype(BF)
        wide = mm(dh, n1[s, :, mine])
        blocks.append(jnp.concatenate([wide[i * RANK : (i + 1) * RANK] for i in range(3)] + [gb_down, gb[s]], axis=1))
    everything = rank_halves(blocks)
    for b in (0, 1):
        gq[b] = everything[b * half_rows : (b + 1) * half_rows].astype(BF)
    if reduce:
        to_twin.start()
        to_plane()
        to_owners(0)
    for i in (6, 0, 1):
        loads[i].wait()
    if reduce:
        last_step(0)
        to_owners(1)
        shared_copies = [rows_in(0)]
        last_step(1)
        shared_copies.append(rows_in(1))
        for s in range(2, sequences):
            last_step(s)
        for c in shared_copies:
            c.wait()
        to_twin.wait_send()
        each_z(lambda k: z_copy(k, z).wait_send())
        each_chip(lambda k: plane_copy(k, chip).wait_send())
        for g in (0, 1):
            each_chip(lambda k, g=g: fin_copy(g, k, chip).wait_send())
    else:
        for s in range(sequences):
            last_step(s)
        gout[0][...] = gq[...]
    for s in range(sequences):
        part_copy(s).wait_send()


def finish(
    reduce, count, dq, dkv, pre, h, gains, tables, gain, bc, pick, bd, x, d_mid, n1, weights, ac, mid, down, down_x, cot,
    early, shared, collective_id,
):
    sequences, rows, width = x.shape
    inner, kw = weights[0].shape[1], weights[1].shape[1]
    w_qkv = 4 * (width // 2) + inner + 2 * kw
    half_rows = sequences * RANK // 2
    dma = pltpu.SemaphoreType.DMA
    far = (x, d_mid, n1) + tuple(weights) + (ac, mid, down, down_x, cot)
    gshape = (shape((2, half_rows, w_qkv), BF),)
    scratch = [pltpu.VMEM(a.shape, a.dtype) for a in far]
    scratch += [
        pltpu.VMEM((sequences, rows, inner + 2 * kw), BF),
        pltpu.VMEM((sequences, RANK, inner + 2 * kw), F32),
        pltpu.VMEM((sequences, 3 * RANK, rows), BF),
        pltpu.VMEM((sequences, 3 * RANK, rows), BF),
        pltpu.VMEM((sequences, rows, 128), BF),
        pltpu.VMEM(x.shape, BF),
        pltpu.VMEM(x.shape, BF),
        pltpu.VMEM((2, half_rows, w_qkv), BF),
        dma((11,)), dma((sequences // 2,)), dma((sequences // 2,)), dma((sequences,)), dma((sequences,)),
    ]
    if reduce:
        chips = count // 2
        totals = (2 * early[0].shape[1], padded(w_qkv, chips))
        gshape = tuple(shape((RANK // 2, n), F32) for n in totals)
        gshape += tuple(shape((RANK, (b - a) // 2), BF) for a, b in shared)
        scratch += [
            pltpu.VMEM((half_rows, w_qkv), BF),
            pltpu.VMEM((half_rows, totals[1]), BF),
            pltpu.VMEM((chips // 2, half_rows, totals[0] // chips), BF),
            pltpu.VMEM((chips, half_rows, totals[1] // chips), BF),
        ]
        scratch += [pltpu.VMEM((chips, RANK, n // chips // 2), BF) for n in totals] * 2
        scratch += [pltpu.VMEM((RANK, (b - a) // 2), BF) for a, b in shared]
        scratch += [dma((2,)), dma((chips // 2,)), dma((chips // 2,)), dma((chips,)), dma((chips,))]
        scratch += [dma((2, chips))] * 2 + [dma((4,))]
    return pl.pallas_call(
        functools.partial(finish_kernel, reduce, count, shared),
        out_shape=(shape(x.shape, BF),) * 2 + gshape,
        in_specs=[VM] * 11 + [ANYWHERE] * 11 + [VM] * len(early),
        out_specs=(VM,) * (2 + len(gshape)),
        scratch_shapes=scratch,
        compiler_params=pltpu.CompilerParams(
            collective_id=collective_id, has_side_effects=True, vmem_limit_bytes=60 * 2**20
        ),
        name="finish",
    )(dq, dkv, pre, h, gains, *tables, gain, bc, pick, bd, *far, *early)


def unpack_kernel(hidden_units, tile, inner, kw, block, grad, first, second, first_x, second_x, block_out, grad_out, *outs):
    block_out[...] = block[...]
    grad_out[...] = grad[...]
    ga_query, gb_query, ga_key, gb_key, ga_value, gb_value, ga_out, gb_out, ga_gate, gb_gate, ga_up, gb_up, ga_down, gb_down = outs
    width = ga_query.shape[1]
    w = width // 2
    lower = lax.axis_index("tp") == 0

    def join(out, own, own_at, other, i):
        a = own[:, own_at + i * w : own_at + (i + 1) * w]
        b = other[:, i * w : (i + 1) * w]
        out[:, :w] = jnp.where(lower, a, b)
        out[:, w:] = jnp.where(lower, b, a)

    @pl.when(pl.program_id(0) == 0)
    def _():
        for f in range(hidden_units // tile):
            for n, out in enumerate((gb_gate, gb_up, ga_down)):
                out[:, f * tile : (f + 1) * tile] = first[:, (3 * f + n) * tile : (3 * f + n + 1) * tile]
        at = 3 * hidden_units
        ga_out[...] = first[:, at : at + inner]
        rows = first.shape[0]
        unfold = lambda x: jnp.concatenate([x[:rows].astype(F32), x[rows:].astype(F32)], axis=1)
        other = unfold(first_x[...])
        for i, out in enumerate((ga_gate, ga_up, gb_out)):
            join(out, first, at + inner, other, i)
        other = unfold(second_x[...])
        for i, out in enumerate((ga_query, ga_key, ga_value, gb_down)):
            join(out, second, 0, other, i)
        at = 4 * w
        gb_query[...] = second[:, at : at + inner]
        gb_key[...] = second[:, at + inner : at + inner + kw]
        gb_value[...] = second[:, at + inner + kw : at + inner + 2 * kw]


def unpack(block, grad, owned, hidden_units, tile, inner, kw):
    width, rows = block.shape[2], owned[0].shape[0]
    sizes = (width, inner, width, kw, width, kw, inner, width, width, hidden_units, width, hidden_units, hidden_units, width)
    outs = tuple(shape((rows, n), F32) for n in sizes)
    return pl.pallas_call(
        functools.partial(unpack_kernel, hidden_units, tile, inner, kw),
        grid=(block.shape[0] // 2,),
        out_shape=(shape(block.shape, BF),) * 2 + outs,
        in_specs=[stepped(block.shape, 2)] * 2 + [whole(a) for a in owned],
        out_specs=(stepped(block.shape, 2),) * 2 + tuple(whole(a) for a in outs),
        compiler_params=BIG,
        name="unpack",
    )(block, grad, *owned)


def rotary_tables(positions):
    half = HEAD_DIM // 2
    frequencies = THETA_BASE ** (-jnp.arange(half, dtype=F32) * 2.0 / HEAD_DIM)
    angles = frequencies[:, None] * positions.astype(F32)[None, :]
    return jnp.cos(angles), jnp.sin(angles)


def swap(values):
    return lax.ppermute(values, "tp", [(0, 1), (1, 0)])


def reduce_scatter_rows(grads, count):
    rows, columns = grads.shape
    index = lax.axis_index("ctx")
    held = grads.reshape(count, rows // count, columns)
    bit = 1
    while bit < count:
        mine = (index // bit) % 2
        pairs = held.reshape(held.shape[0] // 2, 2, held.shape[1], columns)
        kept = lax.dynamic_index_in_dim(pairs, mine, 1, keepdims=False)
        sent = lax.dynamic_index_in_dim(pairs, 1 - mine, 1, keepdims=False).astype(BF)
        held = kept.astype(F32) + lax.ppermute(sent, "ctx", [(i, i ^ bit) for i in range(count)]).astype(F32)
        bit *= 2
    return held[0]


def local(
    tokens, output_cotangent, segment_ids, variant, attn_gain, ffn_gain, q_gain, k_gain,
    query_matrix, key_matrix, value_matrix, output_matrix, gate_matrix, up_matrix, down_matrix,
    query_input_factor, query_output_factor, key_input_factor, key_output_factor,
    value_input_factor, value_output_factor, output_input_factor, output_output_factor,
    gate_input_factor, gate_output_factor, up_input_factor, up_output_factor,
    down_input_factor, down_output_factor,
):
    sequences, rows_here, width = tokens.shape
    count = lax.axis_size("ctx")
    index = lax.axis_index("ctx")
    inner, kw = query_matrix.shape[1], key_matrix.shape[1]
    key_heads = kw // HEAD_DIM
    units = sequences * key_heads
    parts = count // units
    stacked = query_input_factor.shape[0]
    reduce_here = stacked // count == RANK // 2
    tables = rotary_tables(index * rows_here + jnp.arange(rows_here, dtype=jnp.int32))
    weights = (query_matrix, key_matrix, value_matrix)
    ins = (query_input_factor, key_input_factor, value_input_factor)
    outs = (query_output_factor, key_output_factor, value_output_factor)

    flat = lambda a: a.reshape(sequences * rows_here, -1)
    p = forward(
        (variant, tokens, attn_gain, ffn_gain, q_gain, k_gain, *tables, segment_ids, *weights, *ins, *outs),
        (
            flat(output_cotangent), down_matrix, output_matrix, gate_input_factor, up_input_factor, down_output_factor,
            gate_output_factor, up_output_factor, down_input_factor, output_output_factor, output_input_factor,
        ),
        count, parts, 0,
    )
    by_head = (key_heads, sequences)
    attn = p.home.reshape(by_head + p.home.shape[1:])

    cuts = tuple(rows_here * s for s in (0, sequences // 2, sequences))
    g_ffn, down, d_mid, d_attn, g_mid = feed(
        cuts, flat(p.n2), p.dhd, p.c_ag, p.c_au, p.c_bo, p.c_ao, output_matrix, ffn_gain, gate_matrix, up_matrix,
        down_matrix, p.c_bg, p.c_bu, p.c_ad, p.dh, p.mid, output_cotangent, p.h_out, attn, 3,
    )
    d_attn = d_attn.reshape(p.q_all.shape)
    d_attn, down = lax.optimization_barrier((d_attn, down))
    down_other = swap(down)
    early = (g_ffn, g_mid) if reduce_here else ()
    dq, dkv, *early = attend_back(d_attn, p.q_all, p.kv_all, p.of, p.lse, p.starts, early, count, parts, 1)

    w = width // 2
    hidden_units = gate_matrix.shape[1]
    tile = feed_tile(hidden_units)
    at = 3 * hidden_units + inner
    shared = ((at, at + 3 * w), (0, 4 * w))
    input_grad, block_result, *ends = finish(
        reduce_here, count, dq.reshape(by_head + dq.shape[1:]), dkv.reshape(by_head + (parts,) + dkv.shape[1:]),
        p.pre, p.h_one, p.gains, tables, attn_gain, p.bc, p.pick, p.c_bd, tokens, d_mid, p.n1, weights, p.ac,
        p.mid, down, down_other, output_cotangent, early, shared, 2,
    )
    if reduce_here:
        owned = ends
    else:
        per = RANK // 2
        pick = (jnp.arange(stacked // RANK, dtype=jnp.int32)[:, None] == variant[None, :]).astype(F32)
        owned, other = [], []
        for grads, (low, high) in zip((jnp.concatenate([g_ffn, g_mid], axis=1), ends[0]), shared):
            grads = grads.reshape(2, sequences, per, -1).astype(F32)
            dense = jnp.sum(pick[:, None, :, None, None] * grads[None], axis=2)
            owned.append(reduce_scatter_rows(dense.reshape(stacked, -1), count))
            half = swap(owned[-1][:, low:high])
            other.append(jnp.concatenate(jnp.split(half, 2, axis=1), axis=0))
        owned = owned + other
    return tuple(unpack(block_result, input_grad, owned, hidden_units, tile, inner, kw))


def solution(mesh):
    rows, whole, columns = P(None, "ctx", None), P(), P(None, "tp")
    owned, owned_half = P("ctx", None), P("ctx", "tp")
    return jax.shard_map(
        local,
        mesh=mesh,
        in_specs=(rows, rows) + (whole,) * 6
        + (columns, columns, columns, P("tp", None), columns, columns, P("tp", None))
        + (whole, columns) * 3 + (columns, whole) + (whole, columns) * 2 + (columns, whole),
        out_specs=(
            rows, rows, owned, owned_half, owned, owned_half, owned, owned_half,
            owned_half, owned, owned, owned_half, owned, owned_half, owned_half, owned,
        ),
        check_vma=False,
    )
```

```python
import functools, jax, jax.numpy as jnp
from jax import lax
from jax.experimental import pallas as pl
from jax.experimental.pallas import tpu as pltpu
from jax.sharding import PartitionSpec as P

HEAD_DIM = 64
LOG2E = 1.4426950408889634
MESH = pl.DeviceIdType.MESH
SMEM = pl.BlockSpec(memory_space=pltpu.SMEM)
VM = pl.BlockSpec(memory_space=pltpu.VMEM)
RANK = 16
EPSILON = 1e-05
THETA_BASE = 1000000.0
BF = jnp.bfloat16
F32 = jnp.float32
NT = (((1,), (1,)), ((), ()))
BIG = pltpu.CompilerParams(vmem_limit_bytes=60 * 2**20)


def cost(rows, width, columns, products, moved):
    return pl.CostEstimate(flops=2 * products * rows * width * columns, bytes_accessed=moved, transcendentals=0)

ANYWHERE = pl.BlockSpec(memory_space=pl.ANY)


def mm(a, b):
    return jnp.dot(a, b, preferred_element_type=F32)


def mm_nt(a, b):
    return lax.dot_general(a, b, NT, preferred_element_type=F32)


def shape(dims, kind):
    return jax.ShapeDtypeStruct(dims, kind)


def remote(source, target, send, recv, device):
    return pltpu.make_async_remote_copy(
        src_ref=source, dst_ref=target, send_sem=send, recv_sem=recv, device_id=device, device_id_type=MESH
    )


def norm_back(u, gain, c):
    scale = lax.rsqrt(jnp.mean(u * u, axis=-1, keepdims=True) + EPSILON)
    y = u * scale
    w = c * gain
    return scale * (w - y * jnp.mean(w * y, axis=-1, keepdims=True))


def turn(values, cosine, sine):
    half = HEAD_DIM // 2
    a, b = values[:, :half], values[:, half:]
    return jnp.concatenate([a * cosine - b * sine, b * cosine + a * sine], axis=1)


def rank_halves(blocks):
    return jnp.concatenate([b[: RANK // 2] for b in blocks] + [b[RANK // 2 :] for b in blocks], axis=0)


def column(ref):
    return jnp.transpose(jnp.broadcast_to(ref[...][None, :], (128, ref.shape[0])))


def whole(array):
    return pl.BlockSpec(array.shape, lambda i: (0,) * len(array.shape), pipeline_mode=pl.Buffered(1))


def stepped(dims, per):
    return pl.BlockSpec((per,) + tuple(dims[1:]), lambda i: (i,) + (0,) * (len(dims) - 1))


def own_ranks(first, rows, ranks):
    row = lax.broadcasted_iota(jnp.int32, (rows, ranks), 0) // 128 + first // 128
    return row == lax.broadcasted_iota(jnp.int32, (rows, ranks), 1) // RANK


def feed_kernel(
    cuts, n2_ref, dhd_ref, ag, au, bo, ao, wo, gain_ref, wd_ref, bg_ref, bu_ref, ad_ref, dh_ref,
    mid_ref, cot_ref, hout_ref, attn_ref, wg_ref, wu_ref,
    grads_ref, down_ref, dmid_ref, dattn_ref, more_ref,
    hg, hu, hs, dn2_acc, dhg_acc, dhu_acc, down_acc, h_acc, hidden_s, dgu_s, w_s, back_s, back_x, branch_s, more_s,
    send_sems, recv_sems, w_sems,
):
    step = pl.program_id(0)
    rows, width = n2_ref.shape
    tiles, tile = hidden_s.shape[0], hidden_s.shape[2]
    seqs = rows // 128
    ranks = seqs * RANK
    chunks = len(cuts) - 1
    last = chunks * tiles
    f = lax.rem(step, tiles)
    across = {"tp": 1 - lax.axis_index("tp")}

    def compact(a, first=0):
        a = jnp.where(own_ranks(first, *a.shape), a, 0.0)
        return sum(a[:, i * RANK : (i + 1) * RANK] for i in range(seqs))

    def copy(s):
        there = pl.ds(s * 128, 128)
        return remote(back_s.at[there, :], back_x.at[there, :], send_sems.at[s], recv_sems.at[s], across)

    def weights(i):
        columns, slot = pl.ds(pl.multiple_of(lax.rem(i, tiles) * tile, 128), tile), lax.rem(i, 2)
        return [
            pltpu.make_async_copy(w.at[:, columns], w_s.at[slot, :, n * tile : (n + 1) * tile], w_sems.at[slot, n])
            for n, w in enumerate((wg_ref, wu_ref))
        ]

    @pl.when(step == 0)
    def _():
        for i in (0, 1):
            for load in weights(i):
                load.start()
        barrier = pltpu.get_barrier_semaphore()
        pl.semaphore_signal(barrier, inc=1, device_id=across, device_id_type=MESH)
        pl.semaphore_wait(barrier, 1)
        kept = own_ranks(0, rows, ranks)
        g = jnp.where(kept, mm_nt(n2_ref[...], ag[...]) * 2.0, 0.0)
        u = jnp.where(kept, mm_nt(n2_ref[...], au[...]) * 2.0, 0.0)
        hg[...] = g.astype(BF)
        hu[...] = u.astype(BF)
        for n, a in enumerate((g, u, dhd_ref[...].astype(F32))):
            turned = jnp.transpose(jnp.concatenate([a, jnp.zeros((rows, 128 - ranks), F32)], axis=1))
            rows_of = [turned[i * RANK : (i + 1) * RANK] for i in range(seqs)]
            hs[n] = rank_halves(rows_of).astype(BF)
        down_acc[...] = jnp.zeros_like(down_acc)
        h_acc[...] = jnp.zeros_like(h_acc)

    @pl.when(step < last)
    def _():
        for load in weights(step):
            load.wait()

    slot = lax.rem(step, 2)
    for c in range(chunks):
        first, part = cuts[c], cuts[c + 1] - cuts[c]
        here, top = slice(first, first + part), slice(0, part)

        @pl.when((step >= c * tiles) & (step < (c + 1) * tiles))
        def _(here=here, top=top):
            n2 = n2_ref[here, :]
            bg, bu = bg_ref[...], bu_ref[...]
            both = mm(n2, w_s[slot])
            gate = both[:, :tile] + mm(hg[here, :], bg)
            up = both[:, tile:] + mm(hu[here, :], bu)
            sg = 1.0 / (1.0 + jnp.exp(-gate))
            silu = gate * sg
            hidden_s[f, here, :] = (silu * up).astype(BF)
            dh = dh_ref[here, :].astype(F32)
            dg = (dh * up * sg * (1.0 + gate * (1.0 - sg))).astype(BF)
            du = (dh * silu).astype(BF)
            dgu_s[f, here, :tile] = dg
            dgu_s[f, here, tile:] = du
            terms = ((dn2_acc, mm_nt(dgu_s[f, here, :], w_s[slot])), (dhg_acc, mm_nt(dg, bg)), (dhu_acc, mm_nt(du, bu)))
            for acc, term in terms:
                acc[top, :] = jnp.where(f == 0, term, acc[top, :] + term)

        @pl.when(step == (c + 1) * tiles - 1)
        def _(c=c, here=here, top=top, first=first, part=part):
            back_s[here, :width] = dn2_acc[top, :].astype(BF)
            small = [compact(a[top, :], first) * 2 for a in (dhg_acc, dhu_acc)]
            back_s[here, width:] = jnp.concatenate(small + [jnp.zeros((part, 128 - 2 * RANK), F32)], axis=1).astype(BF)
            for s in range(first // 128, (first + part) // 128):
                copy(s).start()

    @pl.when(step < last - 2)
    def _():
        for load in weights(step + 2):
            load.start()

    @pl.when((step >= last) & (step < last + tiles))
    def _():
        hidden = hidden_s[f]
        down_acc[...] += mm(hidden, wd_ref[...])
        h_acc[...] += mm_nt(hidden, ad_ref[...])
        for n, kept in enumerate((dgu_s[f, :, :tile], dgu_s[f, :, tile:], hidden)):
            grads_ref[:, n * tile : (n + 1) * tile] = mm(hs[n], kept).astype(BF)

    for s in range(seqs):

        @pl.when(step == last + tiles + s)
        def _(s=s):
            copy(s).wait()

    @pl.when(step >= last + tiles)
    def _():
        s = step - last - tiles
        here = pl.ds(pl.multiple_of(s * 128, 128), 128)
        own = pl.ds(pl.multiple_of(s * RANK, RANK), RANK)
        mine = pl.ds(pl.multiple_of(lax.axis_index("tp") * (width // 2), width // 2), width // 2)
        down_ref[0, :, :width] = down_acc[here, :].astype(BF)
        h = jnp.where(own_ranks(s * 128, 128, ranks), h_acc[here, :], 0.0)
        h = sum(h[:, i * RANK : (i + 1) * RANK] for i in range(seqs))
        down_ref[0, :, width:] = jnp.concatenate([h, jnp.zeros((128, 128 - RANK), F32)], axis=1).astype(BF)
        total = back_s[here, :].astype(F32) + back_x[here, :].astype(F32)
        dh = total[:, width : width + 2 * RANK].astype(BF)
        c = total[:, :width] + mm(dh, jnp.concatenate([ag[own, :], au[own, :]], axis=0))
        d_mid = cot_ref[0].astype(F32) + norm_back(mid_ref[0], gain_ref[...][None, :], c)
        dmid_ref[0] = d_mid
        branch_s[...] = d_mid.astype(BF)
        dho = (mm_nt(branch_s[...], bo[own, :]) * 2.0).astype(BF)
        d_attn = mm_nt(branch_s[...], wo[...]) + mm(dho, ao[own, :])
        dattn_ref[:, 0] = jnp.transpose(d_attn).astype(BF).reshape(dattn_ref.shape[0], *dattn_ref.shape[2:])
        wide = jnp.concatenate([dh, dho, hout_ref[0][:, :RANK] * 2, jnp.zeros((128, 128 - 4 * RANK), BF)], axis=1)
        t = jnp.transpose(wide.astype(F32)).astype(BF)
        both = mm(t[: 2 * RANK], n2_ref[here, mine])
        more_s[s] = jnp.concatenate(
            [
                mm_nt(t[2 * RANK : 3 * RANK], attn_ref[:, 0].reshape(wo.shape[0], 128)), both[:RANK], both[RANK:],
                mm(t[3 * RANK : 4 * RANK], branch_s[:, mine]),
            ],
            axis=1,
        )

    @pl.when(step == pl.num_programs(0) - 1)
    def _():
        more_ref[...] = rank_halves([more_s[i] for i in range(seqs)]).astype(BF)


def feed_tile(units):
    return 1152 if units % 1152 == 0 else units


def feed(cuts, n2, dhd, ag, au, bo, ao, wo, gain, wg, wu, wd, bg, bu, ad, dh, mid, cot, hout, attn, collective_id):
    rows, width = n2.shape
    stacked, units = bg.shape
    inner = wo.shape[0]
    tile = feed_tile(units)
    chunks, part = len(cuts) - 1, max(b - a for a, b in zip(cuts, cuts[1:]))
    seqs, tiles, ranks = rows // 128, units // tile, rows // 128 * RANK
    last = chunks * tiles
    early = lambda height: pl.BlockSpec((height, tile), lambda i: (0, jnp.where(i < last, lax.rem(i, tiles), tiles - 1)))
    late = lambda i: jnp.clip(i - last, 0, tiles - 1)
    by_seq = lambda dims: pl.BlockSpec((1,) + dims[1:], lambda i: (jnp.maximum(i - last - tiles, 0), 0, 0))
    by_head = pl.BlockSpec(
        attn.shape[:1] + (1,) + attn.shape[2:], lambda i: (0, jnp.maximum(i - last - tiles, 0), 0, 0)
    )
    vm, dma = pltpu.VMEM, pltpu.SemaphoreType.DMA
    more = shape((ranks, inner + 3 * (width // 2)), BF)
    wide = (seqs, 128, width + 128)
    return pl.pallas_call(
        functools.partial(feed_kernel, cuts),
        grid=(last + tiles + seqs,),
        out_shape=(shape((ranks, 3 * units), BF), shape(wide, BF), shape(mid.shape, F32), shape(attn.shape, BF), more),
        in_specs=[whole(a) for a in (n2, dhd, ag, au, bo, ao, wo, gain)]
        + [pl.BlockSpec((tile, width), lambda i: (late(i), 0)), early(stacked), early(stacked)]
        + [pl.BlockSpec((stacked, tile), lambda i: (0, late(i))), early(rows)]
        + [by_seq(a.shape) for a in (mid, cot, hout)] + [by_head, ANYWHERE, ANYWHERE],
        out_specs=(
            pl.BlockSpec((ranks, 3 * tile), lambda i: (0, late(i))), by_seq(wide), by_seq(mid.shape), by_head,
            whole(more),
        ),
        scratch_shapes=[vm((rows, ranks), BF)] * 2
        + [vm((3, ranks, rows), BF), vm((part, width), F32), vm((part, ranks), F32), vm((part, ranks), F32)]
        + [vm((rows, width), F32), vm((rows, ranks), F32)] + [vm((tiles, rows, tile), BF), vm((tiles, rows, 2 * tile), BF)]
        + [vm((2, width, 2 * tile), BF)] + [vm((rows, width + 128), BF)] * 2 + [vm((128, width), BF), vm((seqs, RANK, more.shape[1]), F32)]
        + [dma((seqs,)), dma((seqs,)), dma((2, 2))],
        compiler_params=pltpu.CompilerParams(
            collective_id=collective_id, has_side_effects=True, vmem_limit_bytes=63 * 2**20
        ),
        cost_estimate=cost(rows, width, units, 5, 12 * width * units),
        name="feed_forward",
    )(n2, dhd, ag, au, bo, ao, wo, gain, wd, bg, bu, ad, dh, mid, cot, hout, attn, wg, wu)


TILE = 512
BLOCKS = TILE // 128
SUB = 512
SCALE = HEAD_DIM**-0.5


def document_starts(seg_ref, seq, starts):
    sequences, length = seg_ref.shape
    blocks = length // 128
    number = lax.broadcasted_iota(jnp.int32, (sequences, length), 0)
    row = jnp.sum(jnp.where(number == seq, seg_ref[...], 0), axis=0, keepdims=True)
    segs = jnp.concatenate([row[:, b * 128 : (b + 1) * 128] for b in range(blocks)], axis=0)
    lane = lax.broadcasted_iota(jnp.int32, segs.shape, 1)
    position = lax.broadcasted_iota(jnp.int32, segs.shape, 0) * 128 + lane

    def down(a, n):
        return jnp.concatenate([jnp.zeros((n, 128), jnp.int32), a[: blocks - n]], axis=0)

    before = jnp.where(lane == 0, pltpu.roll(down(segs, 1), 1, 1), pltpu.roll(segs, 1, 1))
    start = jnp.where((segs != before) & (position > 0), position, 0)
    step = 1
    while step < 128:
        start = jnp.maximum(start, jnp.where(lane >= step, pltpu.roll(start, step, 1), 0))
        step *= 2
    carried = down(jnp.broadcast_to(start[:, 127:], segs.shape), 1)
    step = 1
    while step < blocks:
        carried = jnp.maximum(carried, down(carried, step))
        step *= 2
    start = jnp.maximum(start, carried)
    for b in range(blocks):
        starts[b] = start[b : b + 1]


def query_rows(starts, tile, stride, part):
    lanes = lax.broadcasted_iota(jnp.int32, (1, 128), 1)
    blocks = [(BLOCKS * tile + b) * stride + part for b in range(BLOCKS)]
    position = jnp.concatenate([b * 128 + lanes for b in blocks], axis=1)
    return position, jnp.concatenate([starts[b] for b in blocks], axis=1)


def key_range(tile, stride, part):
    return BLOCKS * tile * stride // BLOCKS + part // BLOCKS, ((BLOCKS * tile + BLOCKS - 1) * stride + part) // BLOCKS + 1


def keep_pairs(p, first, start, position, causal):
    key = lax.broadcasted_iota(jnp.int32, p.shape, 0)
    keep = key >= jnp.broadcast_to(start - first, p.shape)
    if causal:
        keep = keep & (key <= jnp.broadcast_to(position - first, p.shape))
    return jnp.where(keep, p, 0.0)


def across_blocks(ref, tile, rows):
    return jnp.concatenate([ref[BLOCKS * tile + b, rows, :] for b in range(BLOCKS)], axis=1)


def load_keys(kv_ref, kb, vt):
    def load(j, _):
        for b in range(BLOCKS):
            kb[j, b * 128 : (b + 1) * 128, :] = jnp.transpose(kv_ref[BLOCKS * j + b, :HEAD_DIM, :])
            vt[j, :HEAD_DIM, b * 128 : (b + 1) * 128] = kv_ref[BLOCKS * j + b, HEAD_DIM:, :]
        vt[j, HEAD_DIM:, :] = jnp.ones((16, TILE), BF)
        return 0

    lax.fori_loop(0, kv_ref.shape[0] // BLOCKS, load, 0)


def head_forward(h, stride, part, first, q_ref, starts, kb, vt, acc, of_ref, lse_ref, done):
    rows = pl.ds(h * HEAD_DIM, HEAD_DIM)

    tiles = q_ref.shape[0] // BLOCKS

    def q_step(n, _):
        i = lax.rem(first + n, tiles)
        position, start = query_rows(starts, i, stride, part)
        qt = across_blocks(q_ref, i, rows)
        acc[...] = jnp.zeros_like(acc)

        def k_step(causal, j, _):
            total = acc[...]
            for c in range(TILE // SUB):
                keys = slice(c * SUB, (c + 1) * SUB)
                p = jnp.exp2(mm(kb[j, keys, :], qt) * (LOG2E * SCALE))
                p = keep_pairs(p, j * TILE + c * SUB, start, position, causal)
                total = total + mm(vt[j, :, keys], p.astype(BF))
            acc[...] = total
            return 0

        whole, end = key_range(i, stride, part)
        lax.fori_loop(0, whole, functools.partial(k_step, False), 0)
        lax.fori_loop(whole, end, functools.partial(k_step, True), 0)
        total = acc[HEAD_DIM : HEAD_DIM + 1, :]
        lse_ref[h, i] = jnp.broadcast_to(jnp.log2(total), (8, TILE))
        out = acc[:HEAD_DIM, :] / total
        for b in range(BLOCKS):
            of_ref[BLOCKS * i + b, rows, :] = out[:, b * 128 : (b + 1) * 128]
        done(n, i, out.astype(BF))
        return 0

    lax.fori_loop(0, tiles, q_step, 0)


def pair_backward(h, i, j, causal, stride, part, qt, q3, dot_t, do3, lse_ref, delta, starts, kb, vb, kt, dqt, dk, dv):
    position, start = query_rows(starts, i, stride, part)
    dq = dqt[h, i]
    for c in range(TILE // SUB):
        keys = slice(c * SUB, (c + 1) * SUB)
        p = jnp.exp2(mm(kb[j, keys, :], qt[h, i]) * (LOG2E * SCALE) - lse_ref[h, i, 0:1, :])
        p = keep_pairs(p, j * TILE + c * SUB, start, position, causal)
        dp = mm(vb[j, keys, :], dot_t[h, i])
        ds = (p * (dp - delta[h, i, 0:1, :])).astype(BF)
        dv[j, keys, :] += mm(p.astype(BF), do3[h, i])
        dk[j, keys, :] += mm(ds, q3[h, i])
        dq = dq + mm(kt[j, :, keys], ds)
    dqt[h, i] = dq


def head_rows(h):
    return pl.ds(h * HEAD_DIM, HEAD_DIM)


def loop(low, high, step):
    def body(k, _):
        step(k)
        return 0

    lax.fori_loop(low, high, body, 0)


def class_copy(count, parts, source, target, send, recv):
    def make(index, sender):
        return remote(
            source(index), target(sender), send.at[index], recv.at[sender],
            {"ctx": index * parts + lax.rem(lax.axis_index("ctx"), parts)},
        )

    return make


def owner_rows(total, pick_ref, k, sequences):
    per = RANK // 2
    row = jnp.zeros((per, total.shape[1]), F32)
    for s in range(sequences):
        row = row + total[s * per : (s + 1) * per] * pick_ref[k, s][:, :1]
    half = total.shape[1] // 2
    return jnp.concatenate([row[:, :half], row[:, half:]], axis=0).astype(BF)


def unfold_rows(rows_ref, at, block):
    per, half = RANK // 2, block.shape[1]
    rows_ref[:, at : at + half] = block[:per].astype(F32)
    rows_ref[:, at + half : at + 2 * half] = block[per:].astype(F32)


class EarlyReduction:
    def __init__(self, me, grads, y_sum, own, core_in, plane, y_in, loads, twin_sends, twin_recvs, y_sems):
        self.y_sum, self.own, self.core_in, self.plane, self.y_in = y_sum, own, core_in, plane, y_in
        chip, core = me // 2, lax.rem(me, 2)
        self.y = lax.rem(chip, 2)
        self.loads, self.to_twin, at = [], [], 0
        for i, ref in enumerate(grads):
            size, place = ref.shape[0] // 2, slice(at, at + ref.shape[1])
            at += ref.shape[1]
            half = lambda who, ref=ref, size=size: ref.at[pl.ds(pl.multiple_of(who * size, 16), size), :]
            self.loads.append(pltpu.make_async_copy(half(core), own.at[:, place], loads.at[i]))
            twin = {"ctx": 2 * chip + 1 - core}
            self.to_twin.append(remote(half(1 - core), core_in.at[:, place], twin_sends.at[i], twin_recvs.at[i], twin))
        self.known, self.width = at, plane.shape[1] // 2
        self.to_y = remote(
            plane.at[:, pl.ds(pl.multiple_of((1 - self.y) * self.width, 128), self.width)], y_in, y_sems.at[0],
            y_sems.at[1], {"ctx": 2 * (chip + 1 - 2 * self.y) + core},
        )

    def begin(self):
        for c in self.loads + self.to_twin:
            c.start()

    def over_cores(self):
        for c in self.loads:
            c.wait()
        for c in self.to_twin:
            c.wait_recv()
        self.plane[:, : self.known] = (self.own[...].astype(F32) + self.core_in[...].astype(F32)).astype(BF)
        rest = self.plane.shape[1] - self.known
        if rest:
            self.plane[:, self.known :] = jnp.zeros((self.plane.shape[0], rest), BF)
        self.to_y.start()

    def over_y(self):
        self.to_y.wait()
        mine = self.plane[:, pl.ds(pl.multiple_of(self.y * self.width, 128), self.width)]
        self.y_sum[...] = (mine.astype(F32) + self.y_in[...].astype(F32)).astype(BF)
        for c in self.to_twin:
            c.wait_send()


def early_scratch(grads, total):
    vm, dma = pltpu.VMEM, pltpu.SemaphoreType.DMA
    rows, known = grads[0].shape[0] // 2, sum(g.shape[1] for g in grads)
    return [vm((rows, known), BF), vm((rows, known), BF), vm((rows, total), BF), vm((rows, total // 2), BF)] + [dma((2,))] * 4


def padded(columns, chips):
    return -(-columns // (256 * chips)) * 256 * chips


def attend_back_kernel(count, parts, reduce, do_ref, q_all, kv_all, of_ref, lse_ref, starts, *refs):
    refs = list(refs)
    take = lambda n: [refs.pop(0) for _ in range(n)]
    grads = take(2) if reduce else []
    dq_home, dkv_home = take(2)
    early = EarlyReduction(lax.axis_index("ctx"), grads, *take(9)) if reduce else None
    attend_back_body(
        count, parts, early,
        do_ref, q_all, kv_all, of_ref, lse_ref, starts, dq_home, dkv_home, *refs,
    )


def attend_back_body(
    count, parts, early, do_ref, q_all, kv_all, of_ref, lse_ref, starts, dq_home, dkv_home,
    q_all_s, kv_all_s, of_s, in_sems, do_in, dq_buf, dkv_buf, kb, vb, kt, qt, q3, dot_t, do3, delta, dqt, dk, dv,
    do_send, do_recv, dq_send, dq_recv, dkv_send, dkv_recv, own_sems,
):
    me = lax.axis_index("ctx")
    units = count // parts
    unit, part = me // parts, lax.rem(me, parts)
    group, tiles, ktiles = q_all.shape[1] // HEAD_DIM, units // BLOCKS, count // BLOCKS
    barrier = pltpu.get_barrier_semaphore()
    loop(
        1, count,
        lambda k: pl.semaphore_signal(barrier, inc=1, device_id={"ctx": lax.rem(me + k, count)}, device_id_type=MESH),
    )
    own_do = pltpu.make_async_copy(do_ref.at[unit], do_in.at[unit], own_sems.at[0])
    own_do.start()
    kept = [
        pltpu.make_async_copy(a, b, in_sems.at[i]) for i, (a, b) in enumerate(((kv_all, kv_all_s), (q_all, q_all_s), (of_ref, of_s)))
    ]
    for c in kept:
        c.start()
    q_all, kv_all, of_ref = q_all_s, kv_all_s, of_s
    pl.semaphore_wait(barrier, count - 1)
    if early:
        early.begin()

    def turn_of(k):
        return lax.rem(unit + k, units)

    do_copy = [
        class_copy(
            count, parts, lambda i, h=h: do_ref.at[i, head_rows(h), :], lambda i, h=h: do_in.at[i, head_rows(h), :],
            do_send.at[h], do_recv.at[h],
        )
        for h in range(group)
    ]
    dq_copy = [
        class_copy(
            count, parts, lambda i, h=h: dq_buf.at[h, i], lambda i, h=h: dq_home.at[i, head_rows(h), :],
            dq_send.at[h], dq_recv.at[h],
        )
        for h in range(group)
    ]

    def dkv_copy(device, sender):
        return remote(dkv_buf.at[device], dkv_home.at[sender], dkv_send.at[device], dkv_recv.at[sender], {"ctx": device})

    own_dkv = pltpu.make_async_copy(dkv_buf.at[me], dkv_home.at[me], own_sems.at[1])

    def own_dq(h):
        return pltpu.make_async_copy(dq_buf.at[h, unit], dq_home.at[unit, head_rows(h), :], own_sems.at[2 + h])

    for h in range(group):
        loop(1, units, lambda k, h=h: do_copy[h](turn_of(k), unit).start())

    def load_kv(j):
        for b in range(BLOCKS):
            lanes = slice(b * 128, (b + 1) * 128)
            kt[j, :, lanes] = kv_all[BLOCKS * j + b, :HEAD_DIM, :]
            kb[j, lanes, :] = jnp.transpose(kv_all[BLOCKS * j + b, :HEAD_DIM, :])
            vb[j, lanes, :] = jnp.transpose(kv_all[BLOCKS * j + b, HEAD_DIM:, :])

    def load_q(i):
        for h in range(group):
            for b in range(BLOCKS):
                lanes = slice(b * 128, (b + 1) * 128)
                q = q_all[BLOCKS * i + b, h * HEAD_DIM : (h + 1) * HEAD_DIM, :]
                qt[h, i, :, lanes] = q
                q3[h, i, lanes, :] = jnp.transpose(q)
            dqt[h, i] = jnp.zeros((HEAD_DIM, TILE), F32)

    def load_do(h, i):
        rows = slice(h * HEAD_DIM, (h + 1) * HEAD_DIM)
        for b in range(BLOCKS):
            lanes = slice(b * 128, (b + 1) * 128)
            g = do_in[BLOCKS * i + b, rows, :]
            dot_t[h, i, :, lanes] = g
            do3[h, i, lanes, :] = jnp.transpose(g)
            d = jnp.sum(g.astype(F32) * of_ref[BLOCKS * i + b, rows, :], axis=0, keepdims=True)
            delta[h, i, :, lanes] = jnp.broadcast_to(d, (8, 128))

    kept[0].wait()
    loop(0, ktiles, load_kv)
    kept[1].wait()
    loop(0, tiles, load_q)
    kept[2].wait()

    def run(h, j):
        low = jnp.maximum(BLOCKS * j - part + parts - 1, 0) // (BLOCKS * parts)
        full = jnp.minimum((BLOCKS * (j + 1) - part + BLOCKS * parts - 1) // (BLOCKS * parts), tiles)

        def pair(causal, i):
            pair_backward(
                h, i, j, causal, parts, part, qt, q3, dot_t, do3, lse_ref, delta, starts, kb, vb, kt, dqt, dk, dv
            )

        loop(low, full, functools.partial(pair, True))
        loop(full, tiles, functools.partial(pair, False))

    def emit_keys(j):
        for b in range(BLOCKS):
            rows = slice(b * 128, (b + 1) * 128)
            block = BLOCKS * j + b
            dkv_buf[block, :HEAD_DIM, :] = jnp.transpose(dk[j, rows, :] * SCALE).astype(BF)
            dkv_buf[block, HEAD_DIM:, :] = jnp.transpose(dv[j, rows, :]).astype(BF)

            @pl.when(block == me)
            def _():
                own_dkv.start()

            @pl.when(block != me)
            def _():
                dkv_copy(block, me).start()

    def emit_queries(h, n):
        i = lax.rem(unit + n, tiles)
        for b in range(BLOCKS):
            block = BLOCKS * i + b
            dq_buf[h, block] = (dqt[h, i, :, b * 128 : (b + 1) * 128] * SCALE).astype(BF)

            @pl.when(block == unit)
            def _():
                own_dq(h).start()

            @pl.when(block != unit)
            def _():
                dq_copy[h](block, unit).start()

    dk[...] = jnp.zeros_like(dk)
    dv[...] = jnp.zeros_like(dv)
    own_do.wait()
    if early:
        early.over_cores()
    for h in range(group):
        loop(1, units, lambda k, h=h: do_copy[h](unit, turn_of(k)).wait_recv())
        loop(0, tiles, functools.partial(load_do, h))

        def key_step(n, h=h):
            j = lax.rem(unit + n, ktiles)
            run(h, j)
            if h == group - 1:
                emit_keys(j)

        loop(0, ktiles, key_step)
        loop(0, tiles, functools.partial(emit_queries, h))
        if early and h == 1:
            early.over_y()
    for h in range(group):
        own_dq(h).wait()
    own_dkv.wait()

    def finish_full(k):
        other = lax.rem(me + k, count)
        dkv_copy(other, me).wait_send()
        dkv_copy(me, other).wait_recv()

    loop(1, count, finish_full)

    def finish_class(k):
        other = turn_of(k)
        for h in range(group):
            do_copy[h](other, unit).wait_send()
            dq_copy[h](other, unit).wait_send()
            dq_copy[h](unit, other).wait_recv()

    loop(1, units, finish_class)


def attend_back(do, q, kv, of, lse, starts, early, count, parts, collective_id):
    units, qrows, _ = q.shape
    group, tiles, ktiles = qrows // HEAD_DIM, units // BLOCKS, count // BLOCKS
    dma, vm = pltpu.SemaphoreType.DMA, pltpu.VMEM
    sums, scratch = (), []
    if early:
        total = padded(sum(g.shape[1] for g in early), count // 2)
        sums = (shape((early[0].shape[0] // 2, total // 2), BF),)
        scratch = early_scratch(early, total)
    return pl.pallas_call(
        functools.partial(attend_back_kernel, count, parts, bool(early)),
        out_shape=(shape(q.shape, BF), shape(kv.shape, BF)) + sums,
        in_specs=[ANYWHERE] * 4 + [VM] * 2 + [ANYWHERE] * len(early),
        out_specs=(ANYWHERE, ANYWHERE) + (VM,) * len(sums),
        scratch_shapes=scratch + [vm(q.shape, BF), vm(kv.shape, BF), vm(of.shape, F32), dma((3,)), vm(q.shape, BF), vm((group, units, HEAD_DIM, 128), BF), vm(kv.shape, BF)]
        + [vm((ktiles, TILE, HEAD_DIM), BF)] * 2 + [vm((ktiles, HEAD_DIM, TILE), BF)]
        + [vm((group, tiles, HEAD_DIM, TILE), BF), vm((group, tiles, TILE, HEAD_DIM), BF)] * 2
        + [vm((group, tiles, 8, TILE), F32), vm((group, tiles, HEAD_DIM, TILE), F32)]
        + [vm((ktiles, TILE, HEAD_DIM), F32)] * 2
        + [dma((group, units))] * 4 + [dma((count,))] * 2 + [dma((2 + group,))],
        compiler_params=pltpu.CompilerParams(
            collective_id=collective_id, has_side_effects=True, vmem_limit_bytes=60 * 2**20
        ),
        name="attend_back",
    )(do, q, kv, of, lse, starts, *early)


class Names:
    def __init__(self, names, refs):
        assert len(names) == len(refs)
        self.__dict__.update(zip(names, refs))


FACTORS = ("ag", "au", "bd", "bg", "bu", "ad", "bo", "ao")
FORWARD_NEAR = ("variant", "x", "gain_one", "gain_two", "q_gain", "k_gain", "cosine", "sine", "segs") + (
    "wq", "wk", "wv", "aq", "ak", "av", "bq", "bk", "bv",
)
FORWARD_FAR = ("cot", "wd", "wo") + FACTORS
FORWARD_SMALL = ("h_one", "ac", "bc", "gains", "pick", "lse", "starts", "dhd", "h_out")
FORWARD_SAVED = ("n1", "pre", "q_all", "kv_all", "of", "home", "mid", "n2") + tuple("c_" + f for f in FACTORS)
FORWARD_OUT = FORWARD_SMALL + FORWARD_SAVED + ("dh",)
FORWARD_BUFFERS = ("cot_s", "wd_s", "wo_s", "wo_x", "ao_x", "dh_s", "q_msg", "kv_msg", "o_buf", "kb", "vt", "acc")
FORWARD_BUFFERS += ("home_x", "lhs", "lhs_x")
FORWARD_SEMS = ("far_sems", "save_sems", "dh_sems", "kv_send", "kv_recv", "q_send", "q_recv", "o_send", "o_recv")
FORWARD_SEMS += ("x_send", "x_recv", "own_sems", "w_send", "w_recv", "tail_sems")


LAG = 4


def forward_kernel(count, parts, *refs):
    names = FORWARD_NEAR + FORWARD_FAR + FORWARD_OUT
    names += tuple(f + "_s" for f in FACTORS) + tuple(n + "_s" for n in FORWARD_SAVED) + FORWARD_BUFFERS + FORWARD_SEMS
    r = Names(names, refs)
    me = lax.axis_index("ctx")
    units = count // parts
    unit, part = me // parts, lax.rem(me, parts)
    sequences, rows, width = r.x.shape
    qw, kw = r.wq.shape[1], r.wk.shape[1]
    heads_k = kw // HEAD_DIM
    group = qw // kw
    ranks = sequences * RANK
    across = {"tp": 1 - lax.axis_index("tp")}
    core = lax.rem(me, 2)
    twin = {"ctx": me + 1 - 2 * core}

    def turn_of(k):
        return lax.rem(unit + k, units)

    barrier = pltpu.get_barrier_semaphore()
    pl.semaphore_signal(barrier, inc=1, device_id=across, device_id_type=MESH)
    loop(
        1, count,
        lambda k: pl.semaphore_signal(barrier, inc=1, device_id={"ctx": lax.rem(me + k, count)}, device_id_type=MESH),
    )
    tiles, tile = r.wd_s.shape[0], r.wd_s.shape[1]
    far = [(r.cot, r.cot_s)] + [(r.wd.at[pl.ds(f * tile, tile), :], r.wd_s.at[f]) for f in range(tiles)]
    far += [(r.wo, r.wo_s)] + [(getattr(r, f), getattr(r, f + "_s")) for f in FACTORS]
    far = [pltpu.make_async_copy(a, b, r.far_sems.at[i]) for i, (a, b) in enumerate(far)]
    for c in far:
        c.start()
    saves = {
        n: pltpu.make_async_copy(getattr(r, n + "_s"), getattr(r, n), r.save_sems.at[i]) for i, n in enumerate(FORWARD_SAVED) if n not in ("mid", "n2")
    }

    def kv_copy(index, to_part, sender):
        device = index * parts + to_part
        return remote(r.kv_msg.at[index], r.kv_all_s.at[sender], r.kv_send.at[device], r.kv_recv.at[sender], {"ctx": device})

    q_copy = [
        class_copy(
            count, parts, lambda i, h=h: r.q_msg.at[i, head_rows(h), :], lambda i, h=h: r.q_all_s.at[i, head_rows(h), :],
            r.q_send.at[h], r.q_recv.at[h],
        )
        for h in range(group)
    ]
    o_copy = [
        class_copy(
            count, parts, lambda i, h=h: r.o_buf.at[h, i], lambda i, h=h: r.home_s.at[i, head_rows(h), :],
            r.o_send.at[h], r.o_recv.at[h],
        )
        for h in range(group)
    ]

    def x_copy(h, i):
        place = (i, head_rows(h), slice(None))
        return remote(r.home_s.at[place], r.home_x.at[place], r.x_send.at[h, i], r.x_recv.at[h, i], across)

    column_of = lax.broadcasted_iota(jnp.int32, (RANK, r.aq.shape[0]), 1)
    rank_of = lax.broadcasted_iota(jnp.int32, (RANK, r.aq.shape[0]), 0)
    chooser = [jnp.where(column_of == r.variant[s] * RANK + rank_of, 1.0, 0.0).astype(BF) for s in range(sequences)]
    choosers = jnp.concatenate(chooser, axis=0)
    stacked = lax.broadcasted_iota(jnp.int32, (1, r.aq.shape[0]), 1) // RANK
    cosine, sine = r.cosine[...], r.sine[...]
    qg, kg = column(r.q_gain), column(r.k_gain)
    gain = r.gain_one[...][None, :]

    def prepare(t, gains):
        heads = t.reshape(t.shape[0] // HEAD_DIM, HEAD_DIM, rows)
        scale = lax.rsqrt(jnp.mean(heads * heads, axis=1, keepdims=True) + EPSILON)
        return turn(heads * scale * gains, cosine, sine).astype(BF)

    def project(p):
        for s in (2 * p, 2 * p + 1):
            x = r.x[s].astype(F32)
            scale = lax.rsqrt(jnp.mean(x * x, axis=-1, keepdims=True) + EPSILON)
            r.n1_s[s] = (x * scale * gain).astype(BF)
        n1 = jnp.concatenate([r.n1_s[2 * p], r.n1_s[2 * p + 1]], axis=0)
        low = [mm_nt(n1, a[...]) for a in (r.aq, r.ak, r.av)]
        base = [mm(n1, w[...]) for w in (r.wq, r.wk, r.wv)]
        for i in (0, 1):
            s = 2 * p + i
            half = slice(i * rows, (i + 1) * rows)
            own = jnp.where(stacked == r.variant[s], 1.0, 0.0)
            h = [(a[half] * own).astype(BF) for a in low]
            small = [mm_nt(a, chooser[s]) for a in h] + [jnp.zeros((rows, 128 - 3 * RANK), F32)]
            r.h_one[s] = jnp.concatenate(small, axis=1).astype(BF)
            q, k, val = (
                jnp.transpose(base[n][half] + mm(h[n] * 2, f[...])) for n, f in enumerate((r.bq, r.bk, r.bv))
            )
            r.pre_s[s, :qw, :] = q
            r.pre_s[s, qw:, :] = k
            q = prepare(q, qg).reshape(heads_k, group * HEAD_DIM, rows)
            k, val = prepare(k, kg), val.astype(BF).reshape(heads_k, HEAD_DIM, rows)
            for n in range(heads_k):
                r.q_msg[n * sequences + s] = q[n]
                r.kv_msg[n * sequences + s, :HEAD_DIM, :] = k[n]
                r.kv_msg[n * sequences + s, HEAD_DIM:, :] = val[n]

    def own_kv():
        return pltpu.make_async_copy(r.kv_msg.at[unit], r.kv_all_s.at[me], r.own_sems.at[0])

    def own_q():
        return pltpu.make_async_copy(r.q_msg.at[unit], r.q_all_s.at[unit], r.own_sems.at[1])

    per_pair = 2 * heads_k

    def send_keys(p):
        def step(k):
            turned = lax.rem(unit + k, per_pair)
            index = turned // 2 * sequences + 2 * p + lax.rem(turned, 2)
            for t in range(parts):

                @pl.when(index * parts + t != me)
                def _():
                    kv_copy(index, t, me).start()

            @pl.when(index != unit)
            def _():
                q_copy[0](index, unit).start()

            @pl.when(index == unit)
            def _():
                own_kv().start()
                own_q().start()

        loop(0, per_pair, step)

    part_rows = r.wo_s.shape[0] // 2
    rows_of = lambda who: pl.ds(pl.multiple_of(who * part_rows, 16), part_rows)
    w_copies = [
        remote(r.wo_s.at[rows_of(core), :], r.wo_x.at[rows_of(core), :], r.w_send.at[0], r.w_recv.at[0], across),
        remote(r.wo_x.at[rows_of(core), :], r.wo_x.at[rows_of(core), :], r.w_send.at[1], r.w_recv.at[1], twin),
        remote(r.c_ao_s, r.ao_x, r.w_send.at[2], r.w_recv.at[2], across),
    ]

    project(0)
    pl.semaphore_wait(barrier, count)
    send_keys(0)
    for p in range(1, sequences // 2):
        project(p)
        send_keys(p)
    for h in range(1, group):
        loop(1, units, lambda k, h=h: q_copy[h](turn_of(k), unit).start())
    for n in ("n1", "pre"):
        saves[n].start()
    far[1 + tiles].wait()
    w_copies[0].start()

    def choose(names):
        for f in names:
            far[2 + tiles + FACTORS.index(f)].wait()
            getattr(r, "c_" + f + "_s")[...] = mm(choosers, getattr(r, f + "_s")[...]).astype(BF)
            saves["c_" + f].start()

    document_starts(r.segs, lax.rem(unit, sequences), r.starts)
    choose(("ao", "bd", "ad"))
    w_copies[2].start()
    far[0].wait()
    d = mm_nt(r.cot_s[...], r.c_bd_s[...]) * 2.0
    r.dhd[...] = jnp.where(own_ranks(0, *d.shape), d, 0.0).astype(BF)
    dh_saves = []
    for f in range(tiles):
        far[1 + f].wait()
        columns = slice(f * tile, (f + 1) * tile)
        r.dh_s[:, columns] = (mm_nt(r.cot_s[...], r.wd_s[f]) + mm(r.dhd[...], r.c_ad_s[:, columns])).astype(BF)
        dh_saves.append(pltpu.make_async_copy(r.dh_s.at[:, columns], r.dh.at[:, columns], r.dh_sems.at[f]))
        dh_saves[-1].start()

    own_kv().wait()
    own_q().wait()
    loop(1, count, lambda k: kv_copy(unit, part, lax.rem(me + k, count)).wait_recv())
    load_keys(r.kv_all_s, r.kb, r.vt)
    saves["kv_all"].start()

    def keep_own(h):
        return pltpu.make_async_copy(r.o_buf.at[h, unit], r.home_s.at[unit, head_rows(h), :], r.own_sems.at[2 + h])

    tiles_q = units // BLOCKS
    my_tile = unit // BLOCKS

    def pass_on(h, n):
        def relay(v):
            other = v * tiles_q + lax.rem(my_tile - n + tiles_q, tiles_q)

            @pl.when(other == unit)
            def _():
                keep_own(h).wait()
                x_copy(h, other).start()

            @pl.when(other != unit)
            def _():
                o_copy[h](unit, other).wait_recv()
                x_copy(h, other).start()

        loop(0, units // tiles_q, relay)

    for h in range(group):
        loop(1, units, lambda k, h=h: q_copy[h](unit, turn_of(k)).wait_recv())
        if h == group - 1:
            saves["q_all"].start()

        def done(n, i, out, h=h):
            for b in range(BLOCKS):
                block = BLOCKS * i + b
                r.o_buf[h, block] = out[:, b * 128 : (b + 1) * 128]

                @pl.when(block == unit)
                def _():
                    keep_own(h).start()

                @pl.when(block != unit)
                def _():
                    o_copy[h](block, unit).start()

            for m in range(tiles_q):
                if m >= LAG or h > 0:

                    @pl.when(n == m)
                    def _(m=m):
                        pass_on(h if m >= LAG else h - 1, m - LAG if m >= LAG else m - LAG + tiles_q)

        head_forward(h, parts, part, unit, r.q_all_s, r.starts, r.kb, r.vt, r.acc, r.of_s, r.lse, done)
        if h == 0:
            w_copies[0].wait_recv()
            w_copies[1].start()
    saves["of"].start()
    choose(("ag", "au", "bg", "bu", "bo"))
    for n in range(tiles_q - LAG, tiles_q):
        pass_on(group - 1, n)
    for s in range(sequences):
        r.ac[s] = jnp.concatenate([mm(chooser[s], a[...]) for a in (r.aq, r.ak, r.av)], axis=0).astype(BF)
        r.bc[s] = jnp.concatenate([mm(chooser[s], b[...]) for b in (r.bq, r.bk, r.bv)], axis=1).astype(BF)
        for v in range(r.pick.shape[0]):
            r.pick[v, s] = jnp.full((8, 128), jnp.where(r.variant[s] == v, 1.0, 0.0), F32)
    r.gains[0], r.gains[1] = qg, kg
    saves["home"].start()
    w_copies[1].wait_recv()
    w_copies[2].wait_recv()
    for h in range(group):
        loop(0, units, lambda i, h=h: x_copy(h, i).wait_recv())

    gain = r.gain_two[...][None, :]
    for p in range(sequences // 2):
        for i in (0, 1):
            half = slice(i * rows, (i + 1) * rows)
            for lhs, home in ((r.lhs, r.home_s), (r.lhs_x, r.home_x)):
                blocks = [home[n * sequences + 2 * p + i] for n in range(heads_k)]
                lhs[half, :] = jnp.transpose(jnp.concatenate(blocks, axis=0))
        out = mm(r.lhs[...], r.wo_s[...]) + mm(r.lhs_x[...], r.wo_x[...])
        for i in (0, 1):
            s = 2 * p + i
            half, own = slice(i * rows, (i + 1) * rows), slice(s * RANK, (s + 1) * RANK)
            h = (mm_nt(r.lhs[half, :], r.c_ao_s[own, :]) + mm_nt(r.lhs_x[half, :], r.ao_x[own, :])).astype(BF)
            r.h_out[s] = jnp.concatenate([h, jnp.zeros((rows, 128 - RANK), BF)], axis=1)
            mid = r.x[s].astype(F32) + (out[half] + mm(h * 2, r.c_bo_s[own, :]))
            r.mid_s[s] = mid
            scale = lax.rsqrt(jnp.mean(mid * mid, axis=-1, keepdims=True) + EPSILON)
            r.n2_s[s] = (mid * scale * gain).astype(BF)
        pair = pl.ds(2 * p, 2)
        for i, n in enumerate(("mid", "n2")):
            saves[n, p] = pltpu.make_async_copy(
                getattr(r, n + "_s").at[pair], getattr(r, n).at[pair], r.tail_sems.at[i, p]
            )
            saves[n, p].start()

    for c in list(saves.values()) + dh_saves:
        c.wait()
    for c in w_copies:
        c.wait_send()

    def finish_full(k):
        other = lax.rem(me + k, count)
        kv_copy(other // parts, lax.rem(other, parts), me).wait_send()

    loop(1, count, finish_full)
    for h in range(group):

        def finish_block(k, h=h):
            q_copy[h](turn_of(k), unit).wait_send()
            o_copy[h](turn_of(k), unit).wait_send()

        loop(1, units, finish_block)
        loop(0, units, lambda i, h=h: x_copy(h, i).wait_send())


def forward(near, far, count, parts, collective_id):
    n = Names(FORWARD_NEAR + FORWARD_FAR, tuple(near) + tuple(far))
    sequences, rows, width = n.x.shape
    qw, kw = n.wq.shape[1], n.wk.shape[1]
    units, group = count // parts, qw // kw
    tiles, ktiles = units // BLOCKS, count // BLOCKS
    hidden_units, tile = n.wd.shape[0], feed_tile(n.wd.shape[0])
    spare, ranks = hidden_units // tile, sequences * RANK
    q_shape, kv_shape = (units, group * HEAD_DIM, rows), (count, 2 * HEAD_DIM, rows)
    small = (
        shape((sequences, rows, 128), BF), shape((sequences, 3 * RANK, width), BF), shape((sequences, RANK, qw + 2 * kw), BF),
        shape((2, HEAD_DIM, rows), F32), shape((n.aq.shape[0] // RANK, sequences, 8, 128), F32),
        shape((group, tiles, 8, TILE), F32), shape((count, 1, 128), jnp.int32), shape((sequences * rows, ranks), BF),
        shape((sequences, rows, 128), BF),
    )
    saved = (
        shape(n.x.shape, BF), shape((sequences, qw + kw, rows), F32), shape(q_shape, BF), shape(kv_shape, BF),
        shape(q_shape, F32), shape(q_shape, BF), shape(n.x.shape, F32), shape(n.x.shape, BF),
    ) + tuple(shape((ranks, getattr(n, f).shape[1]), BF) for f in FACTORS)
    dma, vm = pltpu.SemaphoreType.DMA, pltpu.VMEM
    buffers = [vm(getattr(n, f).shape, BF) for f in FACTORS] + [vm(s.shape, s.dtype) for s in saved]
    buffers += [
        vm(n.cot.shape, BF), vm((spare, tile, width), BF), vm(n.wo.shape, BF), vm(n.wo.shape, BF), vm((ranks, qw), BF),
        vm((sequences * rows, hidden_units), BF), vm(q_shape, BF), vm((units,) + kv_shape[1:], BF),
        vm((group, units, HEAD_DIM, 128), BF), vm((ktiles, TILE, HEAD_DIM), BF), vm((ktiles, HEAD_DIM + 16, TILE), BF),
        vm((HEAD_DIM + 16, TILE), F32), vm(q_shape, BF), vm((2 * rows, qw), BF), vm((2 * rows, qw), BF),
    ]
    sems = [dma((2 + spare + len(FACTORS),)), dma((len(saved),)), dma((spare,)), dma((count,)), dma((count,))]
    sems += [dma((group, units))] * 6 + [dma((2 + group,)), dma((3,)), dma((3,)), dma((2, sequences // 2))]
    outs = pl.pallas_call(
        functools.partial(forward_kernel, count, parts),
        out_shape=small + saved + (shape((sequences * rows, hidden_units), BF),),
        in_specs=[SMEM] + [VM] * (len(FORWARD_NEAR) - 1) + [ANYWHERE] * len(FORWARD_FAR),
        out_specs=(VM,) * len(small) + (ANYWHERE,) * (len(saved) + 1),
        scratch_shapes=buffers + sems,
        compiler_params=pltpu.CompilerParams(
            collective_id=collective_id, has_side_effects=True, vmem_limit_bytes=62 * 2**20
        ),
        name="forward",
    )(*near, *far)
    return Names(FORWARD_OUT, outs)


def finish_kernel(reduce, count, shared, *refs):
    refs = list(refs)
    take = lambda n: [refs.pop(0) for _ in range(n)]
    dq_ref, dkv_ref, pre_ref, h_ref, gains, cos_ref, sin_ref, gain_ref, bc_ref, pick_ref, bd_ref = take(11)
    far = take(11)
    early = take(1) if reduce else []
    out_ref, block_ref = take(2)
    gout = take(4) if reduce else take(1)
    x, d_mid, n1, wq, wk, wv, ac, mid, down, down_x, cot = near = take(11)
    d_n, gb, dh_own, dh_other, dh_sum, sbuf, rbuf, gq = take(8)
    near_sems, dh_send, dh_recv, xsend, xrecv = take(5)
    sequences, rows = dq_ref.shape[1], dq_ref.shape[3]
    inner = dq_ref.shape[0] * dq_ref.shape[2]
    width = out_ref.shape[2]
    kw = wk.shape[1]
    half_rows = sequences * RANK // 2
    me = lax.axis_index("ctx")
    across = {"tp": 1 - lax.axis_index("tp")}
    mine = pl.ds(pl.multiple_of(lax.axis_index("tp") * (width // 2), width // 2), width // 2)

    loads = [pltpu.make_async_copy(f, n, near_sems.at[i]) for i, (f, n) in enumerate(zip(far, near))]
    barrier = pltpu.get_barrier_semaphore()
    pl.semaphore_signal(barrier, inc=1, device_id=across, device_id_type=MESH)
    peers = 1
    if reduce:
        core_in, plane, z_in, plane_in = take(4)
        fin_outs, fin_ins, shared_out = take(2), take(2), take(2)
        twin_sems, z_send, z_recv, plane_send, plane_recv, fin_send, fin_recv, last_sems = take(8)
        chips = count // 2
        chip, core = me // 2, lax.rem(me, 2)
        twin = {"ctx": 2 * chip + 1 - core}
        pl.semaphore_signal(barrier, inc=1, device_id=twin, device_id_type=MESH)

        def at_chip(k):
            return lax.rem(chip + k, chips)

        def greet(k, _):
            pl.semaphore_signal(barrier, inc=1, device_id={"ctx": 2 * at_chip(k) + core}, device_id_type=MESH)
            return 0

        lax.fori_loop(1, chips, greet, 0)
        peers += chips

        w_qkv = gq.shape[2]
        to_twin = remote(gq.at[1 - core], core_in, twin_sems.at[0], twin_sems.at[1], twin)
    for i in (3, 4, 5, 2, 6, 7, 8, 9, 10, 0, 1):
        loads[i].start()
    pl.semaphore_wait(barrier, peers)
    if reduce:
        deep = chips // 2
        z, y = chip // 2, lax.rem(chip, 2)

        def z_copy(other, sender):
            chunk = early[0].shape[1] // deep
            return remote(
                early[0].at[:, pl.ds(pl.multiple_of(other * chunk, 128), chunk)], z_in.at[sender], z_send.at[other],
                z_recv.at[sender], {"ctx": 4 * other + 2 * y + core},
            )

        def each_z(step):
            loop(1, deep, lambda k: step(lax.rem(z + k, deep)))

        each_z(lambda k: z_copy(k, z).start())

    cosine, sine = cos_ref[...], sin_ref[...]
    heads_k = kw // HEAD_DIM
    cuts = (slice(0, inner), slice(inner, inner + kw), slice(inner + kw, inner + 2 * kw))

    def prepare_back(pre, gains, c):
        u = pre.reshape(pre.shape[0] // HEAD_DIM, HEAD_DIM, rows)
        scale = lax.rsqrt(jnp.mean(u * u, axis=1, keepdims=True) + EPSILON)
        y = u * scale
        w = turn(c.reshape(u.shape).astype(F32), cosine, -sine) * gains
        return (scale * (w - y * jnp.mean(w * y, axis=1, keepdims=True))).reshape(pre.shape)

    def first_step(s):
        dkv = dkv_ref[:, s].astype(F32)
        dkv = jnp.sum(dkv, axis=1).astype(BF) if dkv.shape[1] > 1 else dkv[:, 0].astype(BF)
        d_q = prepare_back(pre_ref[s, :inner, :], gains[0], dq_ref[:, s].reshape(inner, rows))
        d_k = prepare_back(pre_ref[s, inner:, :], gains[1], dkv[:, :HEAD_DIM, :].reshape(kw, rows))
        d_v = dkv[:, HEAD_DIM:, :].reshape(kw, rows).astype(F32)
        d = jnp.transpose(jnp.concatenate([d_q, d_k, d_v], axis=0)).astype(BF)
        d_n[s] = d
        dh = [mm_nt(d[:, c], bc_ref[s, :, c]) * 2.0 for c in cuts]
        dh = jnp.transpose(jnp.concatenate(dh + [jnp.zeros((rows, 128 - 3 * RANK), F32)], axis=1))
        dh_own[s] = dh[: 3 * RANK].astype(BF)
        t = (jnp.transpose(h_ref[s].astype(F32)) * 2.0).astype(BF)
        gb[s] = jnp.concatenate([mm(t[i * RANK : (i + 1) * RANK], d[:, c]) for i, c in enumerate(cuts)], axis=1)

    def part_copy(s):
        return remote(sbuf.at[s], rbuf.at[s], xsend.at[s], xrecv.at[s], across)

    def dh_copy(p):
        pair = pl.ds(2 * p, 2)
        return remote(dh_own.at[pair], dh_other.at[pair], dh_send.at[p], dh_recv.at[p], across)

    def work_pair(p):
        d = jnp.concatenate([d_n[2 * p], d_n[2 * p + 1]], axis=0)
        part = mm_nt(d[:, cuts[0]], wq[...]) + mm_nt(d[:, cuts[1]], wk[...]) + mm_nt(d[:, cuts[2]], wv[...])
        for i in (0, 1):
            sbuf[2 * p + i] = part[i * rows : (i + 1) * rows].astype(BF)

    def plane_copy(k, slot):
        chunk = plane.shape[1] // chips
        return remote(
            plane.at[:, pl.ds(pl.multiple_of(k * chunk, 128), chunk)], plane_in.at[slot], plane_send.at[k],
            plane_recv.at[slot], {"ctx": 2 * k + core},
        )

    def fin_copy(g, k, slot):
        return remote(
            fin_outs[g].at[k], fin_ins[g].at[slot], fin_send.at[g, k], fin_recv.at[g, slot], {"ctx": 2 * k + core}
        )

    def each_chip(step):
        loop(1, chips, lambda k: step(at_chip(k)))

    def to_plane():
        to_twin.wait_recv()
        plane[:, :w_qkv] = (gq[core].astype(F32) + core_in[...].astype(F32)).astype(BF)
        if plane.shape[1] > w_qkv:
            plane[:, w_qkv:] = jnp.zeros((half_rows, plane.shape[1] - w_qkv), BF)
        chunk = plane.shape[1] // chips
        each_chip(lambda k: plane_copy(k, chip).start())
        plane_in[chip] = plane[:, pl.ds(pl.multiple_of(chip * chunk, 128), chunk)]

    def to_owners(g):
        if g == 0:
            each_z(lambda k: z_copy(k, k).wait_recv())
            chunk = early[0].shape[1] // deep
            z_in[z] = early[0][:, pl.ds(pl.multiple_of(z * chunk, 128), chunk)]
        else:
            each_chip(lambda k: plane_copy(k, k).wait_recv())
        blocks = z_in if g == 0 else plane_in
        total = blocks[0].astype(F32)
        for k in range(1, blocks.shape[0]):
            total = total + blocks[k].astype(F32)
        for k in range(chips):
            fin_outs[g][k] = owner_rows(total, pick_ref, k, sequences)
        each_chip(lambda k: fin_copy(g, k, chip).start())
        fin_ins[g][chip] = fin_outs[g][chip]

    def rows_in(g):
        each_chip(lambda k: fin_copy(g, k, k).wait_recv())
        chunk = gout[g].shape[1] // chips
        for k in range(chips):
            unfold_rows(gout[g], (k % 2 * deep + k // 2 if g == 0 else k) * chunk, fin_ins[g][k])
        low, high = shared[g]
        middle = (low + high) // 2
        shared_out[g][...] = jnp.concatenate([gout[g][:, low:middle], gout[g][:, middle:high]], axis=0).astype(BF)
        copy = remote(shared_out[g], gout[2 + g], last_sems.at[g], last_sems.at[2 + g], across)
        copy.start()
        return copy

    def last_step(s):
        part_copy(s).wait_recv()
        c = sbuf[s].astype(F32) + rbuf[s].astype(F32) + mm(dh_sum[s][:, : 3 * RANK], ac[s])
        out_ref[s] = (d_mid[s] + norm_back(x[s].astype(F32), gain_ref[...][None, :], c)).astype(BF)

    pairs = sequences // 2
    for p in range(pairs):
        first_step(2 * p)
        first_step(2 * p + 1)
        dh_copy(p).start()
        if p == 0:
            for i in (3, 4, 5):
                loads[i].wait()
            work_pair(0)
            part_copy(0).start()
    part_copy(1).start()
    for p in range(1, pairs):
        work_pair(p)
        part_copy(2 * p).start()
        part_copy(2 * p + 1).start()
    for p in range(pairs):
        dh_copy(p).wait()
    for i in (2, 7, 8, 9, 10):
        loads[i].wait()
    blocks = []
    for s in range(sequences):
        total = down[s].astype(F32) + down_x[s].astype(F32)
        h = total[:, width : width + RANK].astype(BF) * 2
        block_ref[s] = (mid[s] + (total[:, :width] + mm(h, bd_ref[s * RANK : (s + 1) * RANK, :]))).astype(BF)
        wide = jnp.concatenate([h, jnp.zeros((rows, 128 - RANK), BF)], axis=1)
        gb_down = mm(jnp.transpose(wide.astype(F32)).astype(BF)[:RANK], cot[s, :, mine])
        dh = (dh_own[s].astype(F32) + dh_other[s].astype(F32)).astype(BF)
        dh_sum[s] = jnp.transpose(jnp.concatenate([dh.astype(F32), jnp.zeros((128 - 3 * RANK, rows), F32)], axis=0)).astype(BF)
        wide = mm(dh, n1[s, :, mine])
        blocks.append(jnp.concatenate([wide[i * RANK : (i + 1) * RANK] for i in range(3)] + [gb_down, gb[s]], axis=1))
    everything = rank_halves(blocks)
    for b in (0, 1):
        gq[b] = everything[b * half_rows : (b + 1) * half_rows].astype(BF)
    if reduce:
        to_twin.start()
        to_plane()
        to_owners(0)
    for i in (6, 0, 1):
        loads[i].wait()
    if reduce:
        last_step(0)
        to_owners(1)
        shared_copies = [rows_in(0)]
        last_step(1)
        shared_copies.append(rows_in(1))
        for s in range(2, sequences):
            last_step(s)
        for c in shared_copies:
            c.wait()
        to_twin.wait_send()
        each_z(lambda k: z_copy(k, z).wait_send())
        each_chip(lambda k: plane_copy(k, chip).wait_send())
        for g in (0, 1):
            each_chip(lambda k, g=g: fin_copy(g, k, chip).wait_send())
    else:
        for s in range(sequences):
            last_step(s)
        gout[0][...] = gq[...]
    for s in range(sequences):
        part_copy(s).wait_send()


def finish(
    reduce, count, dq, dkv, pre, h, gains, tables, gain, bc, pick, bd, x, d_mid, n1, weights, ac, mid, down, down_x, cot,
    early, shared, collective_id,
):
    sequences, rows, width = x.shape
    inner, kw = weights[0].shape[1], weights[1].shape[1]
    w_qkv = 4 * (width // 2) + inner + 2 * kw
    half_rows = sequences * RANK // 2
    dma = pltpu.SemaphoreType.DMA
    far = (x, d_mid, n1) + tuple(weights) + (ac, mid, down, down_x, cot)
    gshape = (shape((2, half_rows, w_qkv), BF),)
    scratch = [pltpu.VMEM(a.shape, a.dtype) for a in far]
    scratch += [
        pltpu.VMEM((sequences, rows, inner + 2 * kw), BF),
        pltpu.VMEM((sequences, RANK, inner + 2 * kw), F32),
        pltpu.VMEM((sequences, 3 * RANK, rows), BF),
        pltpu.VMEM((sequences, 3 * RANK, rows), BF),
        pltpu.VMEM((sequences, rows, 128), BF),
        pltpu.VMEM(x.shape, BF),
        pltpu.VMEM(x.shape, BF),
        pltpu.VMEM((2, half_rows, w_qkv), BF),
        dma((11,)), dma((sequences // 2,)), dma((sequences // 2,)), dma((sequences,)), dma((sequences,)),
    ]
    if reduce:
        chips = count // 2
        totals = (2 * early[0].shape[1], padded(w_qkv, chips))
        gshape = tuple(shape((RANK // 2, n), F32) for n in totals)
        gshape += tuple(shape((RANK, (b - a) // 2), BF) for a, b in shared)
        scratch += [
            pltpu.VMEM((half_rows, w_qkv), BF),
            pltpu.VMEM((half_rows, totals[1]), BF),
            pltpu.VMEM((chips // 2, half_rows, totals[0] // chips), BF),
            pltpu.VMEM((chips, half_rows, totals[1] // chips), BF),
        ]
        scratch += [pltpu.VMEM((chips, RANK, n // chips // 2), BF) for n in totals] * 2
        scratch += [pltpu.VMEM((RANK, (b - a) // 2), BF) for a, b in shared]
        scratch += [dma((2,)), dma((chips // 2,)), dma((chips // 2,)), dma((chips,)), dma((chips,))]
        scratch += [dma((2, chips))] * 2 + [dma((4,))]
    return pl.pallas_call(
        functools.partial(finish_kernel, reduce, count, shared),
        out_shape=(shape(x.shape, BF),) * 2 + gshape,
        in_specs=[VM] * 11 + [ANYWHERE] * 11 + [VM] * len(early),
        out_specs=(VM,) * (2 + len(gshape)),
        scratch_shapes=scratch,
        compiler_params=pltpu.CompilerParams(
            collective_id=collective_id, has_side_effects=True, vmem_limit_bytes=63 * 2**20
        ),
        name="finish",
    )(dq, dkv, pre, h, gains, *tables, gain, bc, pick, bd, *far, *early)


def unpack_kernel(hidden_units, tile, inner, kw, block, grad, first, second, first_x, second_x, block_out, grad_out, *outs):
    block_out[...] = block[...]
    grad_out[...] = grad[...]
    ga_query, gb_query, ga_key, gb_key, ga_value, gb_value, ga_out, gb_out, ga_gate, gb_gate, ga_up, gb_up, ga_down, gb_down = outs
    width = ga_query.shape[1]
    w = width // 2
    lower = lax.axis_index("tp") == 0

    def join(out, own, own_at, other, i):
        a = own[:, own_at + i * w : own_at + (i + 1) * w]
        b = other[:, i * w : (i + 1) * w]
        out[:, :w] = jnp.where(lower, a, b)
        out[:, w:] = jnp.where(lower, b, a)

    @pl.when(pl.program_id(0) == 0)
    def _():
        for f in range(hidden_units // tile):
            for n, out in enumerate((gb_gate, gb_up, ga_down)):
                out[:, f * tile : (f + 1) * tile] = first[:, (3 * f + n) * tile : (3 * f + n + 1) * tile]
        at = 3 * hidden_units
        ga_out[...] = first[:, at : at + inner]
        rows = first.shape[0]
        unfold = lambda x: jnp.concatenate([x[:rows].astype(F32), x[rows:].astype(F32)], axis=1)
        other = unfold(first_x[...])
        for i, out in enumerate((ga_gate, ga_up, gb_out)):
            join(out, first, at + inner, other, i)
        other = unfold(second_x[...])
        for i, out in enumerate((ga_query, ga_key, ga_value, gb_down)):
            join(out, second, 0, other, i)
        at = 4 * w
        gb_query[...] = second[:, at : at + inner]
        gb_key[...] = second[:, at + inner : at + inner + kw]
        gb_value[...] = second[:, at + inner + kw : at + inner + 2 * kw]


def unpack(block, grad, owned, hidden_units, tile, inner, kw):
    width, rows = block.shape[2], owned[0].shape[0]
    sizes = (width, inner, width, kw, width, kw, inner, width, width, hidden_units, width, hidden_units, hidden_units, width)
    outs = tuple(shape((rows, n), F32) for n in sizes)
    return pl.pallas_call(
        functools.partial(unpack_kernel, hidden_units, tile, inner, kw),
        grid=(block.shape[0] // 2,),
        out_shape=(shape(block.shape, BF),) * 2 + outs,
        in_specs=[stepped(block.shape, 2)] * 2 + [whole(a) for a in owned],
        out_specs=(stepped(block.shape, 2),) * 2 + tuple(whole(a) for a in outs),
        compiler_params=BIG,
        name="unpack",
    )(block, grad, *owned)


def rotary_tables(positions):
    half = HEAD_DIM // 2
    frequencies = THETA_BASE ** (-jnp.arange(half, dtype=F32) * 2.0 / HEAD_DIM)
    angles = frequencies[:, None] * positions.astype(F32)[None, :]
    return jnp.cos(angles), jnp.sin(angles)


def swap(values):
    return lax.ppermute(values, "tp", [(0, 1), (1, 0)])


def reduce_scatter_rows(grads, count):
    rows, columns = grads.shape
    index = lax.axis_index("ctx")
    held = grads.reshape(count, rows // count, columns)
    bit = 1
    while bit < count:
        mine = (index // bit) % 2
        pairs = held.reshape(held.shape[0] // 2, 2, held.shape[1], columns)
        kept = lax.dynamic_index_in_dim(pairs, mine, 1, keepdims=False)
        sent = lax.dynamic_index_in_dim(pairs, 1 - mine, 1, keepdims=False).astype(BF)
        held = kept.astype(F32) + lax.ppermute(sent, "ctx", [(i, i ^ bit) for i in range(count)]).astype(F32)
        bit *= 2
    return held[0]


def local(
    tokens, output_cotangent, segment_ids, variant, attn_gain, ffn_gain, q_gain, k_gain,
    query_matrix, key_matrix, value_matrix, output_matrix, gate_matrix, up_matrix, down_matrix,
    query_input_factor, query_output_factor, key_input_factor, key_output_factor,
    value_input_factor, value_output_factor, output_input_factor, output_output_factor,
    gate_input_factor, gate_output_factor, up_input_factor, up_output_factor,
    down_input_factor, down_output_factor,
):
    sequences, rows_here, width = tokens.shape
    count = lax.axis_size("ctx")
    index = lax.axis_index("ctx")
    inner, kw = query_matrix.shape[1], key_matrix.shape[1]
    key_heads = kw // HEAD_DIM
    units = sequences * key_heads
    parts = count // units
    stacked = query_input_factor.shape[0]
    reduce_here = stacked // count == RANK // 2
    tables = rotary_tables(index * rows_here + jnp.arange(rows_here, dtype=jnp.int32))
    weights = (query_matrix, key_matrix, value_matrix)
    ins = (query_input_factor, key_input_factor, value_input_factor)
    outs = (query_output_factor, key_output_factor, value_output_factor)

    flat = lambda a: a.reshape(sequences * rows_here, -1)
    p = forward(
        (variant, tokens, attn_gain, ffn_gain, q_gain, k_gain, *tables, segment_ids, *weights, *ins, *outs),
        (
            flat(output_cotangent), down_matrix, output_matrix, gate_input_factor, up_input_factor, down_output_factor,
            gate_output_factor, up_output_factor, down_input_factor, output_output_factor, output_input_factor,
        ),
        count, parts, 0,
    )
    by_head = (key_heads, sequences)
    attn = p.home.reshape(by_head + p.home.shape[1:])

    cuts = tuple(rows_here * s for s in (0, sequences // 2, sequences))
    g_ffn, down, d_mid, d_attn, g_mid = feed(
        cuts, flat(p.n2), p.dhd, p.c_ag, p.c_au, p.c_bo, p.c_ao, output_matrix, ffn_gain, gate_matrix, up_matrix,
        down_matrix, p.c_bg, p.c_bu, p.c_ad, p.dh, p.mid, output_cotangent, p.h_out, attn, 3,
    )
    d_attn = d_attn.reshape(p.q_all.shape)
    d_attn, down = lax.optimization_barrier((d_attn, down))
    down_other = swap(down)
    early = (g_ffn, g_mid) if reduce_here else ()
    dq, dkv, *early = attend_back(d_attn, p.q_all, p.kv_all, p.of, p.lse, p.starts, early, count, parts, 1)

    w = width // 2
    hidden_units = gate_matrix.shape[1]
    tile = feed_tile(hidden_units)
    at = 3 * hidden_units + inner
    shared = ((at, at + 3 * w), (0, 4 * w))
    input_grad, block_result, *ends = finish(
        reduce_here, count, dq.reshape(by_head + dq.shape[1:]), dkv.reshape(by_head + (parts,) + dkv.shape[1:]),
        p.pre, p.h_one, p.gains, tables, attn_gain, p.bc, p.pick, p.c_bd, tokens, d_mid, p.n1, weights, p.ac,
        p.mid, down, down_other, output_cotangent, early, shared, 2,
    )
    if reduce_here:
        owned = ends
    else:
        per = RANK // 2
        pick = (jnp.arange(stacked // RANK, dtype=jnp.int32)[:, None] == variant[None, :]).astype(F32)
        owned, other = [], []
        for grads, (low, high) in zip((jnp.concatenate([g_ffn, g_mid], axis=1), ends[0]), shared):
            grads = grads.reshape(2, sequences, per, -1).astype(F32)
            dense = jnp.sum(pick[:, None, :, None, None] * grads[None], axis=2)
            owned.append(reduce_scatter_rows(dense.reshape(stacked, -1), count))
            half = swap(owned[-1][:, low:high])
            other.append(jnp.concatenate(jnp.split(half, 2, axis=1), axis=0))
        owned = owned + other
    return tuple(unpack(block_result, input_grad, owned, hidden_units, tile, inner, kw))


def solution(mesh):
    rows, whole, columns = P(None, "ctx", None), P(), P(None, "tp")
    owned, owned_half = P("ctx", None), P("ctx", "tp")
    return jax.shard_map(
        local,
        mesh=mesh,
        in_specs=(rows, rows) + (whole,) * 6
        + (columns, columns, columns, P("tp", None), columns, columns, P("tp", None))
        + (whole, columns) * 3 + (columns, whole) + (whole, columns) * 2 + (columns, whole),
        out_specs=(
            rows, rows, owned, owned_half, owned, owned_half, owned, owned_half,
            owned_half, owned, owned, owned_half, owned, owned_half, owned_half, owned,
        ),
        check_vma=False,
    )
```
